32 devices in a mesh: dp: 8 (over z, x), tensor: 4 (over y, core).
Axes of the slice: x: 2, y: 2, z: 4, core: 2. Of those that a mesh axis runs over, the one named last changes fastest.
Arguments:
- token_ids: int32 [8, 2048], P('dp'), may hold values from 0 to 30527
- seq_lengths: int32 [8], replicated, may hold values from 1024 to 2048, as said below
- mask_slots: int32 [8, 4, 40], replicated, may hold values from 0 to 511, as said below
- mask_targets: int32 [8, 4, 40], P('dp'), may hold values from 0 to 30527
- positive_rows: int32 [8], replicated, may hold values from 0 to 1023
- doc_ids: int32 [8], replicated, may hold values from 0 to 255
- false_pairs: int32 [8, 4], replicated, may hold values from 0 to 1023
- queue_docs: int32 [1024], replicated, may hold values from 0 to 255
- queue_embed: bfloat16 [1024, 768], P('dp'), may hold values from -6 to 6
- attend_weight: float32 [768, 3072], P('dp')
- attend_moment: float32 [768, 3072], P('dp'), may hold values from -5.340576e-05 to 5.340576e-05
- gate_up: float32 [768, 2, 3072], P('dp', None, 'tensor'), may hold values from -0.21875 to 0.21875
- gate_up_moment: float32 [768, 2, 3072], P('dp', None, 'tensor'), may hold values from -5.340576e-05 to 5.340576e-05
- down_weight: float32 [768, 3072], P('dp', 'tensor'), may hold values from -0.109375 to 0.109375
- down_moment: float32 [768, 3072], P('dp', 'tensor'), may hold values from -5.340576e-05 to 5.340576e-05
- embed_table: float32 [768, 30528], P('dp', 'tensor')
- embed_moment: float32 [768, 30528], P('dp', 'tensor'), may hold values from -5.340576e-05 to 5.340576e-05
- gains: float32 [3, 768], replicated, may hold values from 0.5 to 1.5
- gains_moment: float32 [3, 768], replicated, may hold values from -0.00024414062 to 0.00024414062
- attend_error: float32 [8, 768, 3072], P('dp', None, 'tensor'), may hold values from -0.00024414062 to 0.00024414062
- gate_up_error: float32 [8, 768, 2, 3072], P('dp', None, None, 'tensor'), may hold values from -0.00024414062 to 0.00024414062
- down_error: float32 [8, 768, 3072], P('dp', None, 'tensor'), may hold values from -0.00024414062 to 0.00024414062
- embed_error: float32 [8, 768, 30528], P('dp', None, 'tensor'), may hold values from -0.00024414062 to 0.00024414062
- factors: float32 [5, 768, 32], P(None, None, 'tensor'), may hold values from -6 to 6
Outputs:
- new_attend: float32 [768, 3072], P('dp')
- new_attend_moment: float32 [768, 3072], P('dp')
- new_gate_up: float32 [768, 2, 3072], P('dp', None, 'tensor')
- new_gate_up_moment: float32 [768, 2, 3072], P('dp', None, 'tensor')
- new_down: float32 [768, 3072], P('dp', 'tensor')
- new_down_moment: float32 [768, 3072], P('dp', 'tensor')
- new_table: float32 [768, 30528], P('dp', 'tensor')
- new_table_moment: float32 [768, 30528], P('dp', 'tensor')
- new_gains: float32 [3, 768], replicated
- new_gains_moment: float32 [3, 768], replicated
- new_attend_error: float32 [8, 768, 3072], P('dp', None, 'tensor')
- new_gate_up_error: float32 [8, 768, 2, 3072], P('dp', None, None, 'tensor')
- new_down_error: float32 [8, 768, 3072], P('dp', None, 'tensor')
- new_table_error: float32 [8, 768, 30528], P('dp', None, 'tensor')
- new_factors: float32 [5, 768, 32], P(None, None, 'tensor')
- clip_norm: float32 [], replicated
- masked_sum: float32 [], replicated
- mask_count: float32 [], replicated
- contrast_loss: float32 [], replicated
The draws below stay inside these ranges and needn't reach their ends.
Inputs may be any that keep to these rules, and one draw needn't show every extreme that they name: `seq_lengths`: the first sequence is full: its length is 2048. `mask_slots`: the 40 slots of one device of one group are distinct.
All inputs are finite; a program needn't handle non-finite values.
Results may differ from the reference program's by a relative error of at most 0.01405.
The reference program's roundings to bfloat16 on the way (of `table_b`, `probs`, `activated` and `keys_hat`) count: a program that leaves them out, or rounds other values in their place, can miss the bound.
Values may be sent and summed in bfloat16 or wider, within the bound.
No kernel may reach another device: no remote copies, remote signals or barrier semaphores. Data moves between devices by JAX's collectives and lax.ppermute only.
A program may use at most 448 MiB of HBM per device.

```python
import math
import jax
import jax.numpy as jnp
import numpy as np
from jax import lax

D = 768
HEADS = 12
HEAD_DIM = 64
FF = 3072
VOCAB = 30528
LEN = 2048
SEQ_GROUP = 1
MASK_DEV = 40
FALSE_PAIRS = 4
RANK = 8
SEQS = 8
ROWS_T = 512
QUEUE = 1024
N_DP = 8
N_TENSOR = 4


def draw_seq_lengths(key, part):
    key = jax.random.fold_in(key, 11)
    values = jax.random.randint(key, (SEQS,), LEN // 2, LEN + 1, dtype=jnp.int32)
    return values.at[0].set(LEN)


def draw_mask_slots(key, part):
    key = jax.random.fold_in(key, 23)
    keys = jax.random.split(key, N_DP * N_TENSOR)
    picks = jax.vmap(lambda single: jax.random.permutation(single, ROWS_T)[:MASK_DEV])(keys)
    return picks.reshape(N_DP, N_TENSOR, MASK_DEV).astype(jnp.int32)


def draw_attend_weight(key, part):
    key = jax.random.fold_in(key, 37)
    raw = jax.random.normal(key, (D, 4 * D), jnp.float32)
    column = jnp.arange(4 * D)
    factor = jnp.where(column < 3 * D, 1.0, (LEN / 4.0) ** 0.5) * D ** (-0.5)
    return raw * factor[None, :]


def draw_embed_table(key, part):
    key = jax.random.fold_in(key, 53)
    place = jnp.arange(VOCAB).astype(jnp.float32) / (VOCAB - 1)
    raw = jnp.clip(jax.random.normal(key, (D, VOCAB), jnp.float32), -6.0, 6.0)
    factor = 3.0 ** place
    return raw * (factor * D ** (-0.5))[None, :]


def with_ends(array, own_key, least, largest):
    spot = [jax.random.randint(jax.random.fold_in(own_key, axis), (), 0, length) for axis, length in enumerate(array.shape)]
    main_axis = array.shape.index(max(array.shape))
    beside = spot[:main_axis] + [(spot[main_axis] + 1) % array.shape[main_axis]] + spot[main_axis + 1:]
    return array.at[tuple(spot)].set(least).at[tuple(beside)].set(largest)


def steps_of(stream_key, extent, cuts, least, top_value):
    factor_of, own = 1.0, jax.random.fold_in(stream_key, 6)
    for axis_at, blocks in cuts:
        draws = jnp.exp(jax.random.uniform(jax.random.fold_in(own, axis_at), (blocks,), jnp.float32, least / len(cuts), top_value / len(cuts)))
        factor_of = factor_of * jnp.repeat(draws, extent[axis_at] // blocks).reshape([-1 if axis == axis_at else 1 for axis in range(len(extent))])
    return factor_of


def rank_bounds(count, slope):
    loads = [(1 << 20) // math.isqrt(rank ** slope) + 1 for rank in range(1, count + 1)]
    scale = 1 + sum(loads) // (1 << 30)
    return np.cumsum(np.array([max(1, weight // scale) for weight in loads]))


def ranked_ids(rng, dims, amount, slope):
    table = rank_bounds(amount, slope)
    lot = jax.random.randint(jax.random.fold_in(rng, 1), dims, 0, int(table[amount - 1]))
    grade = jnp.searchsorted(jnp.asarray(table, jnp.int32), lot, side="right")
    return jax.random.permutation(jax.random.fold_in(rng, 2), amount)[grade].astype(jnp.int32)


def normal_values(key, extent, deviation, reach, cuts=(), kind=jnp.bfloat16):
    result = deviation * jax.random.normal(key, extent, jnp.float32)
    if cuts:
        result = result * steps_of(key, extent, cuts, -0.22, 0.18)
    return jnp.clip(result, -reach, reach).astype(kind)


def setup_inputs(seed: int = 0) -> dict:
    streams_of = jax.random.split(jax.random.key(seed), 25)
    token_ids = with_ends(ranked_ids(streams_of[0], (SEQS, LEN), VOCAB, 2), jax.random.fold_in(streams_of[0], 3), 0, VOCAB - 1).astype(jnp.int32)
    seq_lengths = draw_seq_lengths(jax.random.fold_in(streams_of[24], 71), 0)
    mask_slots = draw_mask_slots(jax.random.fold_in(streams_of[24], 71), 0)
    mask_targets = with_ends(ranked_ids(streams_of[3], (N_DP, N_TENSOR, MASK_DEV), VOCAB, 2), jax.random.fold_in(streams_of[3], 3), 0, VOCAB - 1).astype(jnp.int32)
    positive_rows = with_ends(jax.random.randint(streams_of[4], (SEQS,), 0, QUEUE), jax.random.fold_in(streams_of[4], 1), 0, QUEUE - 1).astype(jnp.int32)
    doc_ids = with_ends(jax.random.randint(streams_of[5], (SEQS,), 0, QUEUE // 4), jax.random.fold_in(streams_of[5], 1), 0, (QUEUE // 4) - 1).astype(jnp.int32)
    false_pairs = with_ends(jax.random.randint(streams_of[6], (SEQS, FALSE_PAIRS), 0, QUEUE), jax.random.fold_in(streams_of[6], 1), 0, QUEUE - 1).astype(jnp.int32)
    queue_docs = with_ends(jax.random.randint(streams_of[7], (QUEUE,), 0, QUEUE // 4), jax.random.fold_in(streams_of[7], 1), 0, (QUEUE // 4) - 1).astype(jnp.int32)
    queue_embed = normal_values(streams_of[8], (QUEUE, D), 1.0, 6.0, ((0, 8),))
    attend_weight = draw_attend_weight(jax.random.fold_in(streams_of[24], 71), 0)
    attend_moment = normal_values(streams_of[10], (D, 4 * D), (0.02 / (D * (4 * D + 3 * FF + VOCAB)) ** 0.5), 5.340576171875e-05, ((0, 8),), jnp.float32)
    gate_up = normal_values(streams_of[11], (D, 2, FF), D ** -0.5, 0.21875, ((0, 8), (2, 4)), jnp.float32)
    gate_up_moment = normal_values(streams_of[12], (D, 2, FF), (0.02 / (D * (4 * D + 3 * FF + VOCAB)) ** 0.5), 5.340576171875e-05, ((0, 8), (2, 4)), jnp.float32)
    down_weight = normal_values(streams_of[13], (D, FF), FF ** -0.5, 0.109375, ((0, 8), (1, 4)), jnp.float32)
    down_moment = normal_values(streams_of[14], (D, FF), (0.02 / (D * (4 * D + 3 * FF + VOCAB)) ** 0.5), 5.340576171875e-05, ((0, 8), (1, 4)), jnp.float32)
    embed_table = draw_embed_table(jax.random.fold_in(streams_of[24], 71), 0)
    embed_moment = normal_values(streams_of[16], (D, VOCAB), (0.02 / (D * (4 * D + 3 * FF + VOCAB)) ** 0.5), 5.340576171875e-05, ((0, 8), (1, 4)), jnp.float32)
    gains = jnp.clip(1.0 + 0.1 * jax.random.normal(streams_of[17], (3, D), jnp.float32), 0.5, 1.5)
    gains_moment = normal_values(streams_of[18], (3, D), (0.1 / (D * (4 * D + 3 * FF + VOCAB)) ** 0.5), 0.00024414062, (), jnp.float32)
    attend_error = normal_values(streams_of[19], (N_DP, D, 4 * D), (0.3 / (N_DP * D * (4 * D + 3 * FF + VOCAB)) ** 0.5), 0.00024414062, ((0, 8), (2, 4)), jnp.float32)
    gate_up_error = normal_values(streams_of[20], (N_DP, D, 2, FF), (0.3 / (N_DP * D * (4 * D + 3 * FF + VOCAB)) ** 0.5), 0.00024414062, ((0, 8), (3, 4)), jnp.float32)
    down_error = normal_values(streams_of[21], (N_DP, D, FF), (0.3 / (N_DP * D * (4 * D + 3 * FF + VOCAB)) ** 0.5), 0.00024414062, ((0, 8), (2, 4)), jnp.float32)
    embed_error = normal_values(streams_of[22], (N_DP, D, VOCAB), (0.3 / (N_DP * D * (4 * D + 3 * FF + VOCAB)) ** 0.5), 0.00024414062, ((0, 8), (2, 4)), jnp.float32)
    factors = normal_values(streams_of[23], (5, D, RANK * N_TENSOR), 1.0, 6.0, ((2, 4),), jnp.float32)
    return dict(token_ids=token_ids, seq_lengths=seq_lengths, mask_slots=mask_slots, mask_targets=mask_targets, positive_rows=positive_rows, doc_ids=doc_ids, false_pairs=false_pairs, queue_docs=queue_docs, queue_embed=queue_embed, attend_weight=attend_weight, attend_moment=attend_moment, gate_up=gate_up, gate_up_moment=gate_up_moment, down_weight=down_weight, down_moment=down_moment, embed_table=embed_table, embed_moment=embed_moment, gains=gains, gains_moment=gains_moment, attend_error=attend_error, gate_up_error=gate_up_error, down_error=down_error, embed_error=embed_error, factors=factors)


EPS = 1e-05
ROPE_BASE = 1000.0
TAU = 0.02
LAMBDA = 1.0
CLIP = 0.02
LRATE = 5000.0
MOMENTUM = 0.9
HIGH = lax.Precision.HIGHEST

@jax.custom_vjp
def low(v):
    return lax.optimization_barrier(v.astype(jnp.bfloat16)).astype(jnp.float32)

@jax.custom_vjp
def low_back(v):
    return v

def low_keep(v):
    return (low(v), None)

def low_pass(kept, grad):
    return (grad,)

def back_keep(v):
    return (v, None)

def back_low(kept, grad):
    return (low(grad),)
low.defvjp(low_keep, low_pass)
low_back.defvjp(back_keep, back_low)

def product(left, right):
    return jnp.dot(left, right, precision=HIGH, preferred_element_type=jnp.float32)

def layer_norm(values, gain):
    mean = lax.optimization_barrier(jnp.mean(values, axis=-1, keepdims=True))
    centred = values - mean
    spread = lax.optimization_barrier(jnp.mean(centred * centred, axis=-1, keepdims=True))
    return centred * lax.rsqrt(spread + EPS) * gain

def rotary_tables(total_rows, seq_len):
    half = HEAD_DIM // 2
    column = (jnp.arange(HEADS * HEAD_DIM) % HEAD_DIM % half).astype(jnp.float32)
    freq = ROPE_BASE ** (-2.0 * column / HEAD_DIM)
    places = (jnp.arange(total_rows) % seq_len).astype(jnp.float32)
    angle = places[:, None] * freq[None, :]
    return (jnp.cos(angle), jnp.sin(angle))

def rotate(flat, cosine, sine):
    count_rows = flat.shape[0]
    split = flat.reshape(count_rows, HEADS, 2, HEAD_DIM // 2)
    swapped = jnp.stack([-split[:, :, 1], split[:, :, 0]], axis=2).reshape(count_rows, -1)
    return flat * cosine + swapped * sine

def encode(tokens, length, attend_b, gate_b, down_b, table_b, gains, cosine, sine):
    embedded = jnp.take(table_b, tokens, axis=1).T
    x_zero = layer_norm(embedded, gains[0])
    projected = low_back(product(low(x_zero), attend_b[:, :3 * D]))
    queries = low(rotate(projected[:, :D], cosine, sine)).reshape(LEN, HEADS, HEAD_DIM)
    keys = low(rotate(projected[:, D:2 * D], cosine, sine)).reshape(LEN, HEADS, HEAD_DIM)
    values = low(projected[:, 2 * D:]).reshape(LEN, HEADS, HEAD_DIM)
    keep = jnp.arange(LEN) < length
    block = min(512, LEN)

    def one_block(query_block):
        scores = jnp.einsum('qhd,khd->hqk', query_block, keys, precision=HIGH) * HEAD_DIM ** (-0.5)
        scores = jnp.where(keep[None, None, :], low_back(scores), -1e+30)
        top = lax.optimization_barrier(jnp.max(scores, axis=-1, keepdims=True))
        powers = jnp.exp(scores - top)
        probs = low(powers / lax.optimization_barrier(jnp.sum(powers, axis=-1, keepdims=True)))
        return jnp.einsum('hqk,khd->qhd', probs, values, precision=HIGH).reshape(block, D)
    attended = lax.map(jax.checkpoint(one_block), queries.reshape(LEN // block, block, HEADS, HEAD_DIM)).reshape(LEN, D)
    branch = low_back(product(low(low_back(attended)), attend_b[:, 3 * D:]))
    hidden_in = layer_norm(x_zero + branch, gains[1])
    gate_val = low_back(jnp.einsum('ld,dgf->lgf', low(hidden_in), gate_b, precision=HIGH))
    activated = jax.nn.silu(gate_val[:, 0]) * gate_val[:, 1]
    ffn = low_back(product(low(activated), down_b.T))
    return layer_norm(hidden_in + ffn, gains[2])

def replica_loss(params, replica, token_ids, seq_lengths, slots, targets, valid, count, keys_hat, excluded, positive_rows):
    attend, gate_up, down, table, gains = params
    attend_b, gate_b, down_b, table_b = (low(attend), low(gate_up), low(down), low(table))
    cosine, sine = rotary_tables(LEN, LEN)
    tokens = lax.dynamic_slice_in_dim(token_ids, replica * SEQ_GROUP, SEQ_GROUP, 0)
    lengths = lax.dynamic_slice_in_dim(seq_lengths, replica * SEQ_GROUP, SEQ_GROUP, 0)
    outputs = lax.map(lambda item: encode(item[0], item[1], attend_b, gate_b, down_b, table_b, gains, cosine, sine), (tokens, lengths))
    flat = outputs.reshape(SEQ_GROUP * LEN, D)
    my_slots = lax.dynamic_index_in_dim(slots, replica, 0, keepdims=False).reshape(-1)
    picked = jnp.take(low(flat), my_slots, axis=0)
    logits = low_back(product(picked, table_b))
    top = lax.optimization_barrier(jnp.max(logits, axis=-1, keepdims=True))
    log_total = top[:, 0] + jnp.log(lax.optimization_barrier(jnp.sum(jnp.exp(logits - top), axis=-1)))
    my_targets = lax.dynamic_index_in_dim(targets, replica, 0, keepdims=False).reshape(-1)
    target_logit = jnp.take_along_axis(logits, my_targets[:, None], axis=1)[:, 0]
    my_valid = lax.dynamic_index_in_dim(valid, replica, 0, keepdims=False).reshape(-1)
    masked_sum = jnp.sum(my_valid * (log_total - target_logit))
    keep = (jnp.arange(LEN)[None, :] < lengths[:, None]).astype(jnp.float32)
    pooled = lax.optimization_barrier(jnp.sum(outputs * keep[:, :, None], axis=1)) / lengths[:, None].astype(jnp.float32)
    embedding = pooled * lax.rsqrt(lax.optimization_barrier(jnp.sum(pooled * pooled, axis=-1, keepdims=True)) + EPS)
    scores = low_back(product(low(embedding), keys_hat.T)) / TAU
    blocked = lax.dynamic_slice_in_dim(excluded, replica * SEQ_GROUP, SEQ_GROUP, 0)
    masked = jnp.where(blocked, -1e+30, scores)
    top_c = lax.optimization_barrier(jnp.max(masked, axis=-1, keepdims=True))
    log_c = top_c[:, 0] + jnp.log(lax.optimization_barrier(jnp.sum(jnp.exp(masked - top_c), axis=-1)))
    chosen = lax.dynamic_slice_in_dim(positive_rows, replica * SEQ_GROUP, SEQ_GROUP, 0)
    chosen_score = jnp.take_along_axis(scores, chosen[:, None], axis=1)[:, 0]
    contrast = LAMBDA * jnp.sum(log_c - chosen_score) / SEQS
    return (masked_sum / count + contrast, (masked_sum, contrast))

def orthonormal(matrix):
    finished = []
    for index in range(RANK):
        column = matrix[:, index]
        for earlier in finished:
            column = column - jnp.sum(earlier * column) * earlier
        column = column * lax.rsqrt(jnp.sum(column * column))
        finished.append(column)
    return jnp.stack(finished, axis=1)

def compress(local, factor):
    projected = jnp.einsum('rdn,dk->rnk', local, factor, precision=HIGH)
    basis = orthonormal(lax.optimization_barrier(jnp.sum(projected, axis=0)))
    back = jnp.einsum('rdn,nk->rdk', local, basis, precision=HIGH)
    total = lax.optimization_barrier(jnp.sum(back, axis=0))
    grad = jnp.dot(total, basis.T, precision=HIGH)
    errors = local - jnp.einsum('rdk,nk->rdn', back, basis, precision=HIGH)
    return (grad, errors, total)

def slices(full):
    count_dp, count_rows, count_cols = full.shape
    return jnp.moveaxis(full.reshape(count_dp, count_rows, N_TENSOR, count_cols // N_TENSOR), 2, 0)

def joined(grad):
    return jnp.moveaxis(grad, 0, 1).reshape(grad.shape[1], -1)

def joined_errors(errors):
    return jnp.moveaxis(errors, 0, 2).reshape(errors.shape[1], errors.shape[2], -1)

def reference(token_ids, seq_lengths, mask_slots, mask_targets, positive_rows, doc_ids, false_pairs, queue_docs, queue_embed, attend_weight, attend_moment, gate_up, gate_up_moment, down_weight, down_moment, embed_table, embed_moment, gains, gains_moment, attend_error, gate_up_error, down_error, embed_error, factors):
    group_rows = mask_slots + ROWS_T * jnp.arange(N_TENSOR, dtype=jnp.int32)[None, :, None]
    seq_index = jnp.arange(N_DP, dtype=jnp.int32)[:, None, None] * SEQ_GROUP + group_rows // LEN
    valid = (group_rows % LEN < jnp.take(seq_lengths, seq_index)).astype(jnp.float32)
    count = jnp.sum(valid)
    keys = queue_embed.astype(jnp.float32)
    keys_hat = low(keys * lax.rsqrt(lax.optimization_barrier(jnp.sum(keys * keys, axis=-1, keepdims=True)) + EPS))
    columns = jnp.arange(QUEUE, dtype=jnp.int32)
    excluded = (queue_docs[None, :] == doc_ids[:, None]) | jnp.any(false_pairs[:, :, None] == columns[None, None, :], axis=1)
    excluded = excluded & (columns[None, :] != positive_rows[:, None])
    params = (attend_weight, gate_up, down_weight, embed_table, gains)

    def one_replica(replica):
        value, pull, parts = jax.vjp(lambda p: replica_loss(p, replica, token_ids, seq_lengths, group_rows, mask_targets, valid, count, keys_hat, excluded, positive_rows), params, has_aux=True)
        return (parts, pull(jnp.ones_like(value))[0])
    values, grads = lax.map(one_replica, jnp.arange(N_DP, dtype=jnp.int32))
    grad_attend, grad_gate_up, grad_down, grad_table, grad_gains = grads
    stacked = jnp.moveaxis(factors.reshape(5, D, N_TENSOR, RANK), 2, 0)
    locals_all = [grad_attend + attend_error, grad_gate_up[:, :, 0] + gate_up_error[:, :, 0], grad_gate_up[:, :, 1] + gate_up_error[:, :, 1], grad_down + down_error, grad_table + embed_error]
    results = [jax.vmap(compress)(slices(full), stacked[:, index]) for index, full in enumerate(locals_all)]
    reduced_attend = joined(results[0][0])
    reduced_gate_up = jnp.stack([joined(results[1][0]), joined(results[2][0])], axis=1)
    reduced_down = joined(results[3][0])
    reduced_table = joined(results[4][0])
    reduced_gains = lax.optimization_barrier(jnp.sum(grad_gains, axis=0))
    squares = jnp.sum(reduced_attend * reduced_attend) + jnp.sum(reduced_gate_up * reduced_gate_up) + jnp.sum(reduced_down * reduced_down) + jnp.sum(reduced_table * reduced_table) + jnp.sum(reduced_gains * reduced_gains)
    clip_norm = jnp.sqrt(squares)
    shrink = CLIP / jnp.maximum(clip_norm, CLIP)

    def advance(weight, moment, grad):
        fresh = MOMENTUM * moment + shrink * grad
        return (weight - LRATE * fresh, fresh)
    new_attend, new_attend_moment = advance(attend_weight, attend_moment, reduced_attend)
    new_gate_up, new_gate_up_moment = advance(gate_up, gate_up_moment, reduced_gate_up)
    new_down, new_down_moment = advance(down_weight, down_moment, reduced_down)
    new_table, new_table_moment = advance(embed_table, embed_moment, reduced_table)
    new_gains, new_gains_moment = advance(gains, gains_moment, reduced_gains)
    new_attend_error = joined_errors(results[0][1])
    new_gate_up_error = jnp.stack([joined_errors(results[1][1]), joined_errors(results[2][1])], axis=2)
    new_down_error = joined_errors(results[3][1])
    new_table_error = joined_errors(results[4][1])
    totals = jnp.stack([item[2] for item in results], axis=1)
    new_factors = jnp.moveaxis(totals, 0, 2).reshape(5, D, N_TENSOR * RANK)
    masked_sum = jnp.sum(values[0])
    contrast_loss = jnp.sum(values[1])
    return (new_attend, new_attend_moment, new_gate_up, new_gate_up_moment, new_down, new_down_moment, new_table, new_table_moment, new_gains, new_gains_moment, new_attend_error, new_gate_up_error, new_down_error, new_table_error, new_factors, clip_norm, masked_sum, count, contrast_loss)
```

```python
import functools

import jax
import jax.numpy as jnp
from jax import lax
from jax.experimental import pallas as pl
from jax.experimental.pallas import tpu as pltpu
from jax.sharding import PartitionSpec as P

HEADS = 12
HEAD_DIM = 64
RANK = 8
PAIR = 2 * HEAD_DIM
TILE = 512

EPS = 1e-05
ROPE_BASE = 1000.0
TAU = 0.02
LAMBDA = 1.0
CLIP = 0.02
LRATE = 5000.0
MOMENTUM = 0.9
WIDE = jnp.float32
NARROW = jnp.bfloat16
HIGH = lax.Precision.HIGHEST
NEGATIVE = -1e30
VMEM_BYTES = 56 * 1024 * 1024


def params():
    return pltpu.CompilerParams(vmem_limit_bytes=VMEM_BYTES)


def axis_bits(axis):
    size = lax.axis_size(axis)
    return [1 << place for place in range(size.bit_length() - 1)]


def swap(value, axis, bit):
    size = lax.axis_size(axis)
    return lax.ppermute(value, axis, [(index, index ^ bit) for index in range(size)])


def spread_blocks(value, axis):
    held = {0: value}
    for bit in reversed(axis_bits(axis)):
        for key in sorted(held):
            held[key ^ bit] = swap(held[key], axis, bit)
    return [held[key] for key in range(len(held))]


def summed_block(blocks, axis, kind):
    held = dict(enumerate(blocks))
    for bit in axis_bits(axis):
        for key in sorted((k for k in held if not k & bit), reverse=True):
            if key in held:
                got = swap(held.pop(key ^ bit).astype(kind), axis, bit)
                held[key] = held[key].astype(WIDE) + got.astype(WIDE)
    return held[0]


def summed_all(value, axis):
    for bit in axis_bits(axis):
        value = value + swap(value, axis, bit)
    return value


def picked_blocks(blocks, order):
    stacked = blocks if isinstance(blocks, jax.Array) else jnp.stack(blocks)
    return jnp.stack(
        [
            lax.dynamic_index_in_dim(stacked, order[k], 0, keepdims=False)
            for k in range(stacked.shape[0])
        ]
    )


def row_blocks(value, count):
    rows = value.shape[0] // count
    return [value[k * rows : (k + 1) * rows] for k in range(count)]


def layer_norm(values, gain):
    mean = jnp.mean(values, axis=-1, keepdims=True)
    centred = values - mean
    spread = jnp.mean(centred * centred, axis=-1, keepdims=True)
    return centred * lax.rsqrt(spread + EPS) * gain


def swiglu(gate, up):
    return jax.nn.silu(gate) * up


def dot_in(left, right, axes, precision=None):
    return lax.dot_general(
        left, right, (axes, ((), ())), precision=precision, preferred_element_type=WIDE
    )


def contract_rows(left, right):
    return dot_in(left, right, ((0,), (0,)))


def contract_cols(left, right):
    return dot_in(left, right, ((1,), (1,)))


def halves(value):
    high = value.astype(NARROW)
    return high, (value - high.astype(WIDE)).astype(NARROW)


def turn(piece, cosine, sine):
    lane = lax.broadcasted_iota(jnp.int32, piece.shape, 1) % HEAD_DIM
    half = HEAD_DIM // 2
    ahead = pltpu.roll(piece, PAIR - half, 1)
    behind = pltpu.roll(piece, half, 1)
    return piece * cosine + jnp.where(lane < half, -ahead, behind) * sine


def rotary_tables(places):
    half = HEAD_DIM // 2
    column = (jnp.arange(PAIR) % half).astype(WIDE)
    freq = ROPE_BASE ** (-2.0 * column / HEAD_DIM)
    angle = places.astype(WIDE)[:, None] * freq[None, :]
    return (jnp.cos(angle), jnp.sin(angle))


def project_kernel(scale, x_ref, w_ref, cos_ref, sin_ref, out_ref):
    flat = jnp.dot(x_ref[...], w_ref[...], preferred_element_type=WIDE)
    cosine, sine = cos_ref[...], sin_ref[...]
    for start in range(0, flat.shape[1], PAIR):
        piece = turn(flat[:, start : start + PAIR], cosine, sine).astype(NARROW)
        if scale != 1.0:
            piece = (piece.astype(WIDE) * scale).astype(NARROW)
        out_ref[:, start : start + PAIR] = piece


def project(x, weight, cosine, sine, scale):
    rows, width = x.shape
    columns = weight.shape[1]
    block, span = min(512, rows), 256
    return pl.pallas_call(
        functools.partial(project_kernel, scale),
        grid=(rows // block, columns // span),
        in_specs=[
            pl.BlockSpec((block, width), lambda i, j: (i, 0)),
            pl.BlockSpec((width, span), lambda i, j: (0, j)),
            pl.BlockSpec((block, PAIR), lambda i, j: (i, 0)),
            pl.BlockSpec((block, PAIR), lambda i, j: (i, 0)),
        ],
        out_specs=pl.BlockSpec((block, span), lambda i, j: (i, j)),
        out_shape=jax.ShapeDtypeStruct((rows, columns), NARROW),
        compiler_params=params(),
        cost_estimate=pl.CostEstimate(
            flops=2 * rows * width * columns,
            bytes_accessed=2 * (rows * width + width * columns + rows * columns),
            transcendentals=0,
        ),
    )(x, weight, cosine, sine)


def head_lanes(head):
    lane = lax.broadcasted_iota(jnp.int32, (1, PAIR), 1)
    return (lane // HEAD_DIM) == head, lane == HEAD_DIM * (1 - head)


def attend_kernel(q_ref, k_ref, v_ref, bias_ref, out_ref, log_ref, s_ref):
    head = pl.program_id(1)
    mine, spare = head_lanes(head)
    length = k_ref.shape[0]
    step = min(TILE, length)
    query = jnp.where(spare, 1.0, jnp.where(mine, q_ref[...].astype(WIDE), 0.0)).astype(NARROW)
    top = None
    for start in range(0, length, step):
        rows = pl.ds(start, step)
        key = jnp.where(spare, bias_ref[rows, :].astype(WIDE), k_ref[rows, :].astype(WIDE))
        scores = contract_cols(key.astype(NARROW), query)
        s_ref[rows, :] = scores
        peak = jnp.max(scores, axis=0, keepdims=True)
        top = peak if top is None else jnp.maximum(top, peak)
    total = None
    for start in range(0, length, step):
        rows = pl.ds(start, step)
        powers = jnp.exp(s_ref[rows, :] - top)
        s_ref[rows, :] = powers
        part = jnp.sum(powers, axis=0, keepdims=True)
        total = part if total is None else total + part
    share = 1.0 / total
    result = None
    for start in range(0, length, step):
        rows = pl.ds(start, step)
        probs = (s_ref[rows, :] * share).astype(NARROW)
        part = dot_in(v_ref[rows, :], probs, ((0,), (0,)))
        result = part if result is None else result + part
    log_ref[0, pl.ds(head, 1), :] = top + jnp.log(total)

    @pl.when(head == 0)
    def _():
        out_ref[...] = result

    @pl.when(head == 1)
    def _():
        out_ref[HEAD_DIM:, :] = result[HEAD_DIM:, :]


def attention_forward(queries, keys, values, bias):
    rows, width = queries.shape
    length = keys.shape[0]
    pairs = width // PAIR
    lanes = lambda i, h: (0, i)
    return pl.pallas_call(
        attend_kernel,
        grid=(pairs, 2),
        in_specs=[
            pl.BlockSpec((rows, PAIR), lanes),
            pl.BlockSpec((length, PAIR), lanes),
            pl.BlockSpec((length, PAIR), lanes),
            pl.BlockSpec((length, PAIR), lambda i, h: (0, 0)),
        ],
        out_specs=[
            pl.BlockSpec((PAIR, rows), lambda i, h: (i, 0)),
            pl.BlockSpec((1, 2, rows), lambda i, h: (i, 0, 0)),
        ],
        out_shape=[
            jax.ShapeDtypeStruct((width, rows), WIDE),
            jax.ShapeDtypeStruct((pairs, 2, rows), WIDE),
        ],
        scratch_shapes=[pltpu.VMEM((length, rows), WIDE)],
        compiler_params=params(),
        cost_estimate=pl.CostEstimate(
            flops=4 * rows * length * width,
            bytes_accessed=4 * length * width + 8 * rows * width,
            transcendentals=rows * length * HEADS,
        ),
    )(queries, keys, values, bias)


def attend_back_kernel(
    q_ref, k_ref, v_ref, bias_ref, grad_ref, out_ref, log_ref, cos_ref, sin_ref, cos_q_ref, sin_q_ref,
    dq_ref, dk_ref, dv_ref, dk_sum, dv_sum, dq_sum,
):
    head = pl.program_id(1)
    mine, spare = head_lanes(head)
    length, scale = k_ref.shape[0], HEAD_DIM ** (-0.5)
    step = min(TILE, length)
    own = jnp.where(mine, q_ref[...].astype(WIDE), 0.0)
    query = own.astype(NARROW)
    asked = jnp.where(spare, 1.0, own).astype(NARROW)
    grad_wide = jnp.where(mine, grad_ref[...].astype(WIDE), 0.0)
    grad = grad_wide.astype(NARROW)
    delta = jnp.sum(grad_wide.T * out_ref[...], axis=0, keepdims=True)
    log_total = log_ref[0, pl.ds(head, 1), :]
    dq = None
    for start in range(0, length, step):
        rows = pl.ds(start, step)
        key_block = k_ref[rows, :]
        key = jnp.where(spare, bias_ref[rows, :].astype(WIDE), key_block.astype(WIDE))
        scores = contract_cols(key.astype(NARROW), asked)
        probs = jnp.exp(scores - log_total)
        dprobs = contract_cols(v_ref[rows, :], grad)
        dv = jnp.dot(probs.astype(NARROW), grad, preferred_element_type=WIDE)
        dscores = (probs * (dprobs - delta)).astype(NARROW)
        dk = jnp.dot(dscores, query, preferred_element_type=WIDE)
        part = dot_in(key_block, dscores, ((0,), (0,)))
        dq = part if dq is None else dq + part

        @pl.when(head == 0)
        def _():
            dk_sum[rows, :] = dk
            dv_sum[rows, :] = dv

        @pl.when(head == 1)
        def _():
            total = dk_sum[rows, :] + dk
            dk_ref[rows, :] = turn(total, cos_ref[rows, :], -sin_ref[rows, :]).astype(NARROW)
            dv_ref[rows, :] = (dv_sum[rows, :] + dv).astype(NARROW)

    @pl.when(head == 0)
    def _():
        dq_sum[...] = dq

    @pl.when(head == 1)
    def _():
        dq_sum[HEAD_DIM:, :] = dq[HEAD_DIM:, :]
        total = dq_sum[...].T * scale
        dq_ref[...] = turn(total, cos_q_ref[...], -sin_q_ref[...]).astype(NARROW)


def attention_backward(queries, keys, values, bias, grad, out_t, log_total, tables, own_tables):
    rows, width = queries.shape
    length = keys.shape[0]
    pairs = width // PAIR
    lanes = lambda i, h: (0, i)
    still = lambda i, h: (0, 0)
    own_block = pl.BlockSpec((rows, PAIR), lanes)
    all_block = pl.BlockSpec((length, PAIR), lanes)
    return pl.pallas_call(
        attend_back_kernel,
        grid=(pairs, 2),
        in_specs=[
            own_block,
            all_block,
            all_block,
            pl.BlockSpec((length, PAIR), still),
            own_block,
            pl.BlockSpec((PAIR, rows), lambda i, h: (i, 0)),
            pl.BlockSpec((1, 2, rows), lambda i, h: (i, 0, 0)),
            pl.BlockSpec((length, PAIR), still),
            pl.BlockSpec((length, PAIR), still),
            pl.BlockSpec((rows, PAIR), still),
            pl.BlockSpec((rows, PAIR), still),
        ],
        out_specs=[own_block, all_block, all_block],
        out_shape=[
            jax.ShapeDtypeStruct((rows, width), NARROW),
            jax.ShapeDtypeStruct((length, width), NARROW),
            jax.ShapeDtypeStruct((length, width), NARROW),
        ],
        scratch_shapes=[
            pltpu.VMEM((length, PAIR), WIDE),
            pltpu.VMEM((length, PAIR), WIDE),
            pltpu.VMEM((PAIR, rows), WIDE),
        ],
        compiler_params=params(),
        cost_estimate=pl.CostEstimate(
            flops=10 * rows * length * width,
            bytes_accessed=8 * length * width + 8 * rows * width,
            transcendentals=rows * length * HEADS,
        ),
    )(queries, keys, values, bias, grad, out_t, log_total, *tables, *own_tables)


def project_down(matrix, factor_t):
    high, low = halves(matrix)
    factor_high, factor_low = halves(factor_t)
    both = jnp.concatenate([factor_high, factor_low], axis=0)
    first = jnp.dot(both, high, preferred_element_type=WIDE)
    second = jnp.dot(factor_high, low, preferred_element_type=WIDE)
    return first[:RANK] + first[RANK:] + second


def project_back(matrix, basis_t):
    high, low = halves(matrix)
    basis_high, basis_low = halves(basis_t)
    both = jnp.concatenate([basis_high, basis_low], axis=0)
    first = contract_cols(both, high)
    second = contract_cols(basis_high, low)
    return first[:RANK] + first[RANK:] + second


def expand(back_t, basis_t):
    back_high, back_low = halves(back_t)
    basis_high, basis_low = halves(basis_t)
    left = jnp.concatenate([back_high, back_low, back_high], axis=0)
    right = jnp.concatenate([basis_high, basis_high, basis_low], axis=0)
    return contract_rows(left, right)


def table_kernel(columns, left_ref, tokens_ref, rows_ref, dlogits_ref, error_ref, factor_ref, high_ref, low_ref, p_ref):
    start = pl.program_id(0) * TILE
    place = start + lax.broadcasted_iota(jnp.int32, (TILE, 1), 0)
    hot = (tokens_ref[...] == place).astype(WIDE).astype(NARROW)
    total = jnp.dot(hot, left_ref[...], preferred_element_type=WIDE)
    total = total + contract_rows(dlogits_ref[...], rows_ref[...])
    total = jnp.where(place < columns, total + error_ref[...], 0.0)
    high, low = halves(total)
    high_ref[...] = high
    low_ref[...] = low
    factor_high, factor_low = halves(factor_ref[...])
    both = jnp.concatenate([factor_high, factor_low], axis=0)
    first = contract_cols(both, high)
    p_ref[...] = first[:RANK] + first[RANK:] + contract_cols(factor_high, low)


def table_matrix(left, tokens, rows, dlogits, error, factor_t):
    columns, width = error.shape
    slots = left.shape[0]
    picks = rows.shape[0]
    tiles = -(-columns // TILE)
    still = lambda j: (0, 0)
    down = lambda j: (j, 0)
    along = lambda j: (0, j)
    return pl.pallas_call(
        functools.partial(table_kernel, columns),
        grid=(tiles,),
        in_specs=[
            pl.BlockSpec((slots, width), still),
            pl.BlockSpec((1, slots), still),
            pl.BlockSpec((picks, width), still),
            pl.BlockSpec((picks, TILE), along),
            pl.BlockSpec((TILE, width), down),
            pl.BlockSpec((RANK, width), still),
        ],
        out_specs=[
            pl.BlockSpec((TILE, width), down),
            pl.BlockSpec((TILE, width), down),
            pl.BlockSpec((RANK, TILE), along),
        ],
        out_shape=[
            jax.ShapeDtypeStruct((tiles * TILE, width), NARROW),
            jax.ShapeDtypeStruct((tiles * TILE, width), NARROW),
            jax.ShapeDtypeStruct((RANK, tiles * TILE), WIDE),
        ],
        compiler_params=params(),
        cost_estimate=pl.CostEstimate(
            flops=2 * width * columns * (slots + picks + 24),
            bytes_accessed=8 * width * columns,
            transcendentals=0,
        ),
    )(left, tokens, rows, dlogits, error, factor_t)


def small_kernel(count, *refs):
    grads, errors, factor_ref = refs[:count], refs[count : 2 * count], refs[2 * count]
    m_ref, p_ref = refs[2 * count + 1 :]
    for index in range(count):
        total = grads[index][...] + errors[index][...]
        m_ref[index] = total
        p_ref[index] = project_down(total, factor_ref[index])


def small_matrices(grads, errors, factor_t):
    count, (width, columns) = len(grads), grads[0].shape
    return pl.pallas_call(
        functools.partial(small_kernel, count),
        out_shape=[
            jax.ShapeDtypeStruct((count, width, columns), WIDE),
            jax.ShapeDtypeStruct((count, RANK, columns), WIDE),
        ],
        compiler_params=params(),
        cost_estimate=pl.CostEstimate(
            flops=48 * count * width * columns,
            bytes_accessed=12 * count * width * columns,
            transcendentals=0,
        ),
    )(*grads, *errors, factor_t)


def basis_kernel(spans, p_ref, out_ref):
    index = lax.broadcasted_iota(jnp.int32, (RANK, 1), 0)
    for start, size in spans:
        rows = p_ref[:, pl.ds(start, size)]
        for place in range(RANK):
            row = rows[place : place + 1, :]
            row = row * lax.rsqrt(jnp.sum(row * row, axis=1, keepdims=True))
            inner = jnp.sum(rows * row, axis=1, keepdims=True)
            rows = jnp.where(index == place, row, rows - jnp.where(index > place, inner, 0.0) * row)
        out_ref[:, pl.ds(start, size)] = rows


def bases_of(sums, spans):
    return pl.pallas_call(
        functools.partial(basis_kernel, spans),
        out_shape=jax.ShapeDtypeStruct(sums.shape, WIDE),
        compiler_params=params(),
        cost_estimate=pl.CostEstimate(
            flops=64 * sums.size, bytes_accessed=8 * sums.size, transcendentals=40
        ),
    )(sums)


def small_back_kernel(m_ref, basis_ref, back_ref):
    for index in range(m_ref.shape[0]):
        back_ref[index] = project_back(m_ref[index], basis_ref[index])


def small_backs(matrices, basis):
    count, width, columns = matrices.shape
    return pl.pallas_call(
        small_back_kernel,
        out_shape=jax.ShapeDtypeStruct((count, RANK, width), WIDE),
        compiler_params=params(),
        cost_estimate=pl.CostEstimate(
            flops=48 * count * width * columns,
            bytes_accessed=4 * count * width * columns,
            transcendentals=0,
        ),
    )(matrices, basis)


def table_back_kernel(high_ref, low_ref, basis_ref, back_ref):
    basis_high, basis_low = halves(basis_ref[...])
    both = jnp.concatenate([basis_high, basis_low], axis=0)
    first = jnp.dot(both, high_ref[...], preferred_element_type=WIDE)
    second = jnp.dot(basis_high, low_ref[...], preferred_element_type=WIDE)
    part = first[:RANK] + first[RANK:] + second

    @pl.when(pl.program_id(0) == 0)
    def _():
        back_ref[...] = part

    @pl.when(pl.program_id(0) > 0)
    def _():
        back_ref[...] += part


def table_back(high, low, basis):
    columns, width = high.shape
    down = pl.BlockSpec((TILE, width), lambda j: (j, 0))
    return pl.pallas_call(
        table_back_kernel,
        grid=(columns // TILE,),
        in_specs=[down, down, pl.BlockSpec((RANK, TILE), lambda j: (0, j))],
        out_specs=pl.BlockSpec((RANK, width), lambda j: (0, 0)),
        out_shape=jax.ShapeDtypeStruct((RANK, width), WIDE),
        compiler_params=params(),
        cost_estimate=pl.CostEstimate(
            flops=48 * width * columns, bytes_accessed=4 * width * columns, transcendentals=0
        ),
    )(high, low, basis)


def small_error_kernel(m_ref, back_ref, basis_ref, *out_refs):
    for index, out_ref in enumerate(out_refs):
        out_ref[...] = m_ref[index] - expand(back_ref[index], basis_ref[index])


def small_errors(matrices, backs, basis):
    count, width, columns = matrices.shape
    return pl.pallas_call(
        small_error_kernel,
        out_shape=[jax.ShapeDtypeStruct((width, columns), WIDE)] * count,
        compiler_params=params(),
        cost_estimate=pl.CostEstimate(
            flops=48 * count * width * columns,
            bytes_accessed=8 * count * width * columns,
            transcendentals=0,
        ),
    )(matrices, backs, basis)


def table_error_kernel(high_ref, low_ref, back_ref, basis_ref, out_ref):
    whole = high_ref[...].astype(WIDE) + low_ref[...].astype(WIDE)
    out_ref[...] = whole - expand(basis_ref[...], back_ref[...])


def table_error(high, low, back, basis, columns):
    width = high.shape[1]
    down = pl.BlockSpec((TILE, width), lambda j: (j, 0))
    return pl.pallas_call(
        table_error_kernel,
        grid=(-(-columns // TILE),),
        in_specs=[
            down,
            down,
            pl.BlockSpec((RANK, width), lambda j: (0, 0)),
            pl.BlockSpec((RANK, TILE), lambda j: (0, j)),
        ],
        out_specs=down,
        out_shape=jax.ShapeDtypeStruct((columns, width), WIDE),
        compiler_params=params(),
        cost_estimate=pl.CostEstimate(
            flops=48 * width * columns, bytes_accessed=8 * width * columns, transcendentals=0
        ),
    )(high, low, back, basis)


def normalize_keys(raw_keys):
    wide_keys = raw_keys.astype(WIDE)
    return (
        wide_keys * lax.rsqrt(jnp.sum(wide_keys * wide_keys, axis=-1, keepdims=True) + EPS)
    ).astype(NARROW)


def contrast_terms(
    queries, keys_hat, seq_index, column_ids, doc_ids, queue_docs, false_pairs, positive_rows
):
    scores = contract_cols(queries, keys_hat) / TAU
    seq_docs = lax.dynamic_slice_in_dim(doc_ids, seq_index, 1, 0)
    pairs = lax.dynamic_slice_in_dim(false_pairs, seq_index, 1, 0)
    chosen = lax.dynamic_slice_in_dim(positive_rows, seq_index, 1, 0)
    column_docs = queue_docs
    target = column_ids[None, :] == chosen[:, None]
    blocked = (column_docs[None, :] == seq_docs[:, None]) | jnp.any(
        pairs[:, :, None] == column_ids[None, None, :], axis=1
    )
    blocked = blocked & jnp.logical_not(target)
    masked = jnp.where(blocked, NEGATIVE, scores)
    top = jnp.max(masked, axis=-1)
    total = jnp.sum(jnp.exp(masked - top[:, None]), axis=-1)
    chosen_score = jnp.sum(jnp.where(target, scores, 0.0), axis=-1)
    return (masked, target.astype(WIDE), top, total, chosen_score)


def per_device(
    token_ids,
    seq_lengths,
    mask_slots,
    mask_targets,
    positive_rows,
    doc_ids,
    false_pairs,
    queue_docs,
    queue_embed,
    attend_weight,
    attend_moment,
    gate_up,
    gate_up_moment,
    down_weight,
    down_moment,
    embed_table,
    embed_moment,
    gains,
    gains_moment,
    attend_error,
    gate_up_error,
    down_error,
    embed_error,
    factors,
):
    tensor_count = lax.axis_size("tensor")
    tensor_rank = lax.axis_index("tensor")
    data_count = lax.axis_size("dp")
    data_rank = lax.axis_index("dp")
    groups, seq_len = token_ids.shape
    width = gains.shape[1]
    total_rows = groups * seq_len
    own_rows = total_rows // tensor_count
    slot_count = mask_slots.shape[2]
    seq_total = groups * data_count
    near = jnp.arange(tensor_count) ^ tensor_rank
    row_count = attend_weight.shape[0]

    attend_cols = attend_error.shape[2]
    quarter = lax.dynamic_slice_in_dim(attend_weight, tensor_rank * attend_cols, attend_cols, 1)
    table_b = lax.all_gather(embed_table.astype(NARROW), "dp", axis=0, tiled=True)
    quarter_b = lax.all_gather(quarter.astype(NARROW), "dp", axis=0, tiled=True)
    attend_near = picked_blocks(spread_blocks(quarter_b, "tensor"), near)
    attend_b = jnp.concatenate([attend_near[k] for k in range(tensor_count)], axis=1)
    ff_own = gate_up.shape[2]
    gate_b = lax.all_gather(
        gate_up.astype(NARROW).reshape(row_count, -1), "dp", axis=0, tiled=True
    )
    down_b = lax.all_gather(down_weight.astype(NARROW), "dp", axis=0, tiled=True)
    queue_all = lax.all_gather(queue_embed, "dp", axis=0, tiled=True)

    every_rows = mask_slots + own_rows * jnp.arange(tensor_count)[None, :, None]
    every_len = seq_lengths[:, None, None]
    count = jnp.sum((every_rows < every_len).astype(WIDE))
    my_length = lax.dynamic_index_in_dim(seq_lengths, data_rank, 0, keepdims=False)
    group_valid = lax.dynamic_index_in_dim(
        every_rows < every_len, data_rank, 0, keepdims=False
    )
    own_slots = lax.dynamic_index_in_dim(
        lax.dynamic_index_in_dim(mask_slots, data_rank, 0, keepdims=False),
        tensor_rank,
        0,
        keepdims=False,
    )
    valid_rows = picked_blocks(group_valid, near).reshape(-1).astype(WIDE)
    near_targets = picked_blocks(mask_targets[0], near).reshape(-1)
    near_tokens = picked_blocks(token_ids.reshape(tensor_count, own_rows), near).reshape(-1)
    places = (near[:, None] * own_rows + jnp.arange(own_rows)[None, :]).reshape(-1)
    tables = rotary_tables(places)
    own_tables = tuple(table[:own_rows] for table in tables)
    bias = jnp.broadcast_to(
        jnp.where(places < my_length, 0.0, NEGATIVE).astype(NARROW)[:, None], (total_rows, PAIR)
    )
    keep_own = (places[:own_rows] < my_length)[:, None]

    vocab_own = table_b.shape[1]
    vocab_start = tensor_rank * vocab_own
    shifted = near_tokens - vocab_start
    inside = (shifted >= 0) & (shifted < vocab_own)
    safe_ids = jnp.clip(shifted, 0, vocab_own - 1)
    looked = jnp.take(table_b, safe_ids, axis=1).T
    looked = jnp.where(inside[:, None], looked, jnp.zeros((), NARROW))
    embedded = summed_block(row_blocks(looked, tensor_count), "tensor", NARROW)

    x_zero, norm_zero = jax.vjp(lambda v: layer_norm(v, gains[0]), embedded)
    x_zero_b = x_zero.astype(NARROW)
    x_all_b = jnp.concatenate(spread_blocks(x_zero_b, "tensor"), axis=0)
    scale = HEAD_DIM ** (-0.5)
    queries = project(x_zero_b, attend_b[:, :width], *own_tables, scale)
    keys = project(x_all_b, attend_b[:, width : 2 * width], *tables, 1.0)
    values = jnp.dot(
        x_all_b, attend_b[:, 2 * width : 3 * width], preferred_element_type=WIDE
    ).astype(NARROW)
    attended_t, log_total = attention_forward(queries, keys, values, bias)
    attended_b = attended_t.astype(NARROW)
    branch = contract_rows(attended_b, attend_b[:, 3 * width :])
    pre_one = x_zero + branch
    hidden_in, norm_one = jax.vjp(lambda v: layer_norm(v, gains[1]), pre_one)
    hidden_b = jnp.concatenate(spread_blocks(hidden_in.astype(NARROW), "tensor"), axis=0)
    gate = jnp.dot(hidden_b, gate_b[:, :ff_own], preferred_element_type=WIDE)
    up = jnp.dot(hidden_b, gate_b[:, ff_own:], preferred_element_type=WIDE)
    activated, act_back = jax.vjp(swiglu, gate, up)
    activated_b = activated.astype(NARROW)
    ffn_part = contract_cols(activated_b, down_b)
    ffn_own = summed_block(row_blocks(ffn_part, tensor_count), "tensor", NARROW)
    pre_out = hidden_in + ffn_own
    final, norm_two = jax.vjp(lambda v: layer_norm(v, gains[2]), pre_out)

    pool_part = jnp.sum(jnp.where(keep_own, final, 0.0), axis=0)
    picked = jnp.take(final, own_slots, axis=0).astype(NARROW)
    rows_all = jnp.concatenate(spread_blocks(picked, "tensor"), axis=0)
    logits = jnp.dot(rows_all, table_b, preferred_element_type=WIDE)
    targets = near_targets - vocab_start
    hits = jnp.arange(vocab_own)[None, :] == targets[:, None]
    target_logit = jnp.sum(jnp.where(hits, logits, 0.0), axis=-1)
    top = jnp.max(logits, axis=-1)
    total = jnp.sum(jnp.exp(logits - top[:, None]), axis=-1)
    picks = rows_all.shape[0]
    stats = jnp.stack([top, total, target_logit]).reshape(3, tensor_count, slot_count)
    pooled_sum = pool_part
    for bit in axis_bits("tensor"):
        flat = jnp.concatenate([stats.reshape(-1), pooled_sum])
        other = swap(flat, "tensor", bit)
        theirs = other[: 3 * picks].reshape(3, tensor_count, slot_count)
        theirs = jnp.stack([theirs[:, k ^ bit] for k in range(tensor_count)], axis=1)
        peak = jnp.maximum(stats[0], theirs[0])
        stats = jnp.stack(
            [
                peak,
                stats[1] * jnp.exp(stats[0] - peak) + theirs[1] * jnp.exp(theirs[0] - peak),
                stats[2] + theirs[2],
            ]
        )
        pooled_sum = pooled_sum + other[3 * picks :]
    top_all, total_all, target_all = stats.reshape(3, picks)
    log_all = top_all + jnp.log(total_all)
    row_weight = valid_rows / count
    cross = valid_rows * (log_all - target_all)
    masked_part = jnp.sum(cross[:slot_count])
    dlogits = (
        (jnp.exp(logits - log_all[:, None]) - hits.astype(WIDE)) * row_weight[:, None]
    ).astype(NARROW)
    row_grad = summed_block(
        row_blocks(contract_cols(dlogits, table_b), tensor_count), "tensor", NARROW
    )

    pooled = (pooled_sum / my_length.astype(WIDE))[None]
    embedding, embed_back = jax.vjp(
        lambda v: v * lax.rsqrt(jnp.sum(v * v, axis=-1, keepdims=True) + EPS), pooled
    )
    embedding_b = embedding.astype(NARROW)
    weight_c = LAMBDA / seq_total
    first_rank = jnp.where(tensor_rank == 0, 1.0, 0.0)
    keys_hat = normalize_keys(queue_all)
    masked, target, top_c, total_c, chosen_c = contrast_terms(
        embedding_b,
        keys_hat,
        data_rank,
        jnp.arange(keys_hat.shape[0]),
        doc_ids,
        queue_docs,
        false_pairs,
        positive_rows,
    )
    log_c = top_c + jnp.log(total_c)
    contrast_part = jnp.sum(log_c - chosen_c) * weight_c * first_rank
    dscores = ((jnp.exp(masked - log_c[:, None]) - target) * (weight_c / TAU)).astype(NARROW)
    embed_grad = jnp.dot(dscores, keys_hat, preferred_element_type=WIDE)
    pooled_grad = embed_back(embed_grad)[0] / my_length.astype(WIDE)

    final_grad = jnp.where(keep_own, pooled_grad, 0.0)
    final_grad = final_grad.at[own_slots].add(row_grad)
    pre_grad = norm_two(final_grad)[0]
    gain_two = jnp.sum(final_grad * layer_norm(pre_out, 1.0), axis=0)
    ffn_grad = jnp.concatenate(spread_blocks(pre_grad.astype(NARROW), "tensor"), axis=0)
    act_grad = jnp.dot(ffn_grad, down_b, preferred_element_type=WIDE)
    gate_grad, up_grad = (part.astype(NARROW) for part in act_back(act_grad))
    hidden_part = contract_cols(gate_grad, gate_b[:, :ff_own]) + contract_cols(
        up_grad, gate_b[:, ff_own:]
    )
    hidden_sum = summed_block(row_blocks(hidden_part, tensor_count), "tensor", NARROW)
    hidden_grad = hidden_sum + pre_grad
    down_grad = contract_rows(ffn_grad, activated_b)
    gate_w_grad = contract_rows(hidden_b, gate_grad)
    up_w_grad = contract_rows(hidden_b, up_grad)
    pre_one_grad = norm_one(hidden_grad)[0]
    gain_one = jnp.sum(hidden_grad * layer_norm(pre_one, 1.0), axis=0)
    branch_grad = pre_one_grad.astype(NARROW)
    attended_grad = contract_cols(branch_grad, attend_b[:, 3 * width :]).astype(NARROW)
    dq, dk, dv = attention_backward(
        queries, keys, values, bias, attended_grad, attended_t, log_total, tables, own_tables
    )
    x_part = contract_cols(dk, attend_b[:, width : 2 * width]) + contract_cols(
        dv, attend_b[:, 2 * width : 3 * width]
    )
    x_sum = summed_block(row_blocks(x_part, tensor_count), "tensor", NARROW)
    x_zero_grad = pre_one_grad + contract_cols(dq, attend_b[:, :width]) + x_sum
    embedded_grad = norm_zero(x_zero_grad)[0]
    gain_zero = jnp.sum(x_zero_grad * layer_norm(embedded, 1.0), axis=0)
    emb_all = jnp.concatenate(
        spread_blocks(embedded_grad.astype(NARROW), "tensor"), axis=0
    )
    attend_part = jnp.concatenate(
        [
            contract_rows(x_zero_b, dq),
            contract_rows(x_all_b, dk),
            contract_rows(x_all_b, dv),
            jnp.dot(attended_b, branch_grad, preferred_element_type=WIDE),
        ],
        axis=1,
    )
    attend_blocks = jnp.moveaxis(attend_part.reshape(width, tensor_count, attend_cols), 1, 0)
    attend_blocks = picked_blocks(attend_blocks, near)
    attend_grad = summed_block([attend_blocks[k] for k in range(tensor_count)], "tensor", WIDE)

    factor_t = jnp.swapaxes(factors, 1, 2)
    table_high, table_low, table_p = table_matrix(
        emb_all, shifted[None, :], rows_all, dlogits, embed_error[0].T, factor_t[4]
    )
    small_m, small_p = small_matrices(
        [attend_grad, gate_w_grad, up_w_grad, down_grad],
        [attend_error[0], gate_up_error[0, :, 0], gate_up_error[0, :, 1], down_error[0]],
        factor_t[:4],
    )
    parts = [small_p[k] for k in range(4)] + [table_p]
    spans, start = [], 0
    for part in parts:
        spans.append((start, part.shape[1]))
        start += part.shape[1]
    sums = summed_all(jnp.concatenate(parts, axis=1), "dp")
    bases_t = bases_of(sums, spans)
    small_basis = jnp.stack([bases_t[:, at : at + size] for at, size in spans[:4]])
    table_basis = bases_t[:, spans[4][0] :]
    small_back = small_backs(small_m, small_basis)
    tab_back = table_back(table_high, table_low, table_basis)
    gain_terms = jnp.stack([gain_zero, gain_one, gain_two])
    loss_terms = jnp.stack([masked_part, contrast_part])
    loss_row = jnp.zeros((1, width), WIDE).at[0, :2].set(loss_terms)
    packed = jnp.concatenate(
        [small_back.reshape(-1, width), tab_back, gain_terms, loss_row], axis=0
    )
    packed = summed_all(packed, "dp")
    errors = small_errors(small_m, small_back, small_basis)
    new_table_error = table_error(table_high, table_low, tab_back, table_basis, vocab_own).T
    own_t = packed[: 5 * RANK].reshape(5, RANK, width)
    square = jnp.sum(own_t * own_t)
    tail = packed[5 * RANK :].at[3, 2].set(square)
    shared = jnp.concatenate(
        [own_t[0], tail, jnp.pad(small_basis[0], ((0, 0), (0, width - attend_cols)))], axis=0
    )
    shared = picked_blocks(spread_blocks(shared, "tensor"), near)
    tail_sum = jnp.sum(shared[:, RANK : RANK + 4], axis=0)
    gains_grad = tail_sum[:3]
    loss_sums = tail_sum[3, :2]
    clip_norm = jnp.sqrt(tail_sum[3, 2] + jnp.sum(gains_grad * gains_grad))
    shrink = CLIP / jnp.maximum(clip_norm, CLIP)
    row_start = data_rank * row_count

    def rows_of(factor):
        return lax.dynamic_slice_in_dim(factor, row_start, row_count, factor.ndim - 1)

    reduced_attend = jnp.einsum(
        "tkd,tkn->dtn",
        rows_of(shared[:, :RANK]),
        shared[:, RANK + 4 :, :attend_cols],
        precision=HIGH,
    ).reshape(row_count, -1)
    own_rows_t = rows_of(own_t)

    def reduced(index, basis):
        return dot_in(own_rows_t[index], basis, ((0,), (0,)), precision=HIGH)

    reduced_gate_up = jnp.stack(
        [reduced(1, small_basis[1]), reduced(2, small_basis[2])], axis=1
    )
    reduced_down = reduced(3, small_basis[3])
    reduced_table = reduced(4, table_basis[:, :vocab_own])

    def advance(weight, moment, grad):
        fresh = MOMENTUM * moment + shrink * grad
        return (weight - LRATE * fresh, fresh)

    new_attend, new_attend_moment = advance(attend_weight, attend_moment, reduced_attend)
    new_gate_up, new_gate_up_moment = advance(gate_up, gate_up_moment, reduced_gate_up)
    new_down, new_down_moment = advance(down_weight, down_moment, reduced_down)
    new_table, new_table_moment = advance(embed_table, embed_moment, reduced_table)
    new_gains, new_gains_moment = advance(gains, gains_moment, gains_grad)
    return (
        new_attend,
        new_attend_moment,
        new_gate_up,
        new_gate_up_moment,
        new_down,
        new_down_moment,
        new_table,
        new_table_moment,
        new_gains,
        new_gains_moment,
        errors[0][None],
        jnp.stack([errors[1], errors[2]], axis=1)[None],
        errors[3][None],
        new_table_error[None],
        jnp.swapaxes(own_t, 1, 2),
        clip_norm,
        loss_sums[0],
        count,
        loss_sums[1],
    )


def solution(mesh):
    in_specs = (
        P("dp", None),
        P(),
        P(),
        P("dp", None, None),
        P(),
        P(),
        P(),
        P(),
        P("dp", None),
        P("dp", None),
        P("dp", None),
        P("dp", None, "tensor"),
        P("dp", None, "tensor"),
        P("dp", "tensor"),
        P("dp", "tensor"),
        P("dp", "tensor"),
        P("dp", "tensor"),
        P(),
        P(),
        P("dp", None, "tensor"),
        P("dp", None, None, "tensor"),
        P("dp", None, "tensor"),
        P("dp", None, "tensor"),
        P(None, None, "tensor"),
    )
    out_specs = (
        P("dp", None),
        P("dp", None),
        P("dp", None, "tensor"),
        P("dp", None, "tensor"),
        P("dp", "tensor"),
        P("dp", "tensor"),
        P("dp", "tensor"),
        P("dp", "tensor"),
        P(),
        P(),
        P("dp", None, "tensor"),
        P("dp", None, None, "tensor"),
        P("dp", None, "tensor"),
        P("dp", None, "tensor"),
        P(None, None, "tensor"),
        P(),
        P(),
        P(),
        P(),
    )
    return jax.shard_map(
        per_device, mesh=mesh, in_specs=in_specs, out_specs=out_specs, check_vma=False
    )
```

```python
import functools

import jax
import jax.numpy as jnp
from jax import lax
from jax.experimental import pallas as pl
from jax.experimental.pallas import tpu as pltpu
from jax.sharding import PartitionSpec as P

HEADS = 12
HEAD_DIM = 64
RANK = 8
PAIR = 2 * HEAD_DIM
TILE = 1280
PARTS = 3
CHUNK = 256

EPS = 1e-05
ROPE_BASE = 1000.0
TAU = 0.02
LAMBDA = 1.0
CLIP = 0.02
LRATE = 5000.0
MOMENTUM = 0.9
WIDE = jnp.float32
NARROW = jnp.bfloat16
HIGH = lax.Precision.HIGHEST
NEGATIVE = -1e30
VMEM_BYTES = 56 * 1024 * 1024


def params():
    return pltpu.CompilerParams(vmem_limit_bytes=VMEM_BYTES)


def axis_bits(axis):
    size = lax.axis_size(axis)
    return [1 << place for place in range(size.bit_length() - 1)]


def swap(value, axis, bit):
    size = lax.axis_size(axis)
    return lax.ppermute(value, axis, [(index, index ^ bit) for index in range(size)])


def spread_blocks(value, axis):
    held = {0: value}
    for bit in reversed(axis_bits(axis)):
        for key in sorted(held):
            held[key ^ bit] = swap(held[key], axis, bit)
    return [held[key] for key in range(len(held))]


def summed_block(blocks, axis, kind):
    held = dict(enumerate(blocks))
    for bit in axis_bits(axis):
        for key in sorted((k for k in held if not k & bit), reverse=True):
            if key in held:
                got = swap(held.pop(key ^ bit).astype(kind), axis, bit)
                held[key] = held[key].astype(WIDE) + got.astype(WIDE)
    return held[0]


def summed_pair(blocks, axis):
    held = dict(enumerate(blocks))
    bits = axis_bits(axis)
    for bit in bits[:-1]:
        for key in sorted((k for k in held if not k & bit), reverse=True):
            if key in held:
                got = swap(held.pop(key ^ bit), axis, bit)
                held[key] = (held[key].astype(WIDE) + got.astype(WIDE)).astype(NARROW)
    if not bits:
        return held[0], jnp.zeros_like(held[0])
    return held[0], swap(held[bits[-1]], axis, bits[-1])


def summed_all(value, axis):
    for bit in axis_bits(axis):
        value = value + swap(value, axis, bit)
    return value


def picked_blocks(blocks, order):
    stacked = blocks if isinstance(blocks, jax.Array) else jnp.stack(blocks)
    return jnp.stack(
        [
            lax.dynamic_index_in_dim(stacked, order[k], 0, keepdims=False)
            for k in range(stacked.shape[0])
        ]
    )


def gathered_rows(value, axis):
    size = lax.axis_size(axis)
    if size > 8:
        return lax.all_gather(value, axis, axis=0, tiled=True)
    rank, rows = lax.axis_index(axis), value.shape[0]
    whole = jnp.zeros((size * rows,) + value.shape[1:], value.dtype)
    for key in range(size):
        part = value
        if key:
            part = lax.ppermute(value, axis, [(index, index ^ key) for index in range(size)])
        whole = lax.dynamic_update_slice_in_dim(whole, part, (rank ^ key) * rows, 0)
    return whole


def row_blocks(value, count):
    rows = value.shape[0] // count
    return [value[k * rows : (k + 1) * rows] for k in range(count)]


def layer_norm(values, gain):
    mean = jnp.mean(values, axis=-1, keepdims=True)
    centred = values - mean
    spread = jnp.mean(centred * centred, axis=-1, keepdims=True)
    return centred * lax.rsqrt(spread + EPS) * gain


def swiglu(gate, up):
    return jax.nn.silu(gate) * up


def dot_in(left, right, axes, precision=None):
    return lax.dot_general(
        left, right, (axes, ((), ())), precision=precision, preferred_element_type=WIDE
    )


def contract_rows(left, right):
    return dot_in(left, right, ((0,), (0,)))


def contract_cols(left, right):
    return dot_in(left, right, ((1,), (1,)))


def halves(value):
    high = value.astype(NARROW)
    return high, (value - high.astype(WIDE)).astype(NARROW)


def turn(piece, cosine, sine):
    lane = lax.broadcasted_iota(jnp.int32, piece.shape, 1) % HEAD_DIM
    half = HEAD_DIM // 2
    ahead = pltpu.roll(piece, PAIR - half, 1)
    behind = pltpu.roll(piece, half, 1)
    return piece * cosine + jnp.where(lane < half, -ahead, behind) * sine


def rotary_tables(places):
    half = HEAD_DIM // 2
    column = (jnp.arange(PAIR) % half).astype(WIDE)
    freq = ROPE_BASE ** (-2.0 * column / HEAD_DIM)
    angle = places.astype(WIDE)[:, None] * freq[None, :]
    return (jnp.cos(angle), jnp.sin(angle))


def project_kernel(count, x_ref, *refs):
    weights, (cos_ref, sin_ref), outs = refs[:count], refs[count : count + 2], refs[count + 2 :]
    x, cosine, sine = x_ref[...], cos_ref[...], sin_ref[...]
    for kind, (w_ref, out_ref) in enumerate(zip(weights, outs), 3 - count):
        for at in range(0, out_ref.shape[1], 2 * PAIR):
            flat = jnp.dot(x, w_ref[:, at : at + 2 * PAIR], preferred_element_type=WIDE)
            for start in range(0, 2 * PAIR, PAIR):
                piece = flat[:, start : start + PAIR]
                if kind < 2:
                    piece = turn(piece, cosine, sine)
                piece = piece.astype(NARROW)
                if kind == 0:
                    piece = (piece.astype(WIDE) * HEAD_DIM ** (-0.5)).astype(NARROW)
                out_ref[:, at + start : at + start + PAIR] = piece


def project(count, x, weight, cosine, sine):
    rows, width = x.shape
    still = lambda i: (0, 0)
    block = pl.BlockSpec((rows, width), still)
    lanes = pl.BlockSpec((rows, PAIR), still)
    return pl.pallas_call(
        functools.partial(project_kernel, count),
        grid=(1,),
        in_specs=[block]
        + [weight_block(width, width, kind) for kind in range(3 - count, 3)]
        + [lanes, lanes],
        out_specs=[block] * count,
        out_shape=[jax.ShapeDtypeStruct((rows, width), NARROW)] * count,
        compiler_params=params(),
        cost_estimate=pl.CostEstimate(
            flops=2 * count * rows * width * width,
            bytes_accessed=2 * count * width * (rows + width),
            transcendentals=0,
        ),
    )(x, *[weight] * count, cosine, sine)


def lookup_kernel(row_count, start_ref, ids_ref, table_ref, out_ref, held):
    groups, block = out_ref.shape[1] // row_count, out_ref.shape[0]
    start = start_ref[0]
    for group in range(groups):

        def move(at, carry):
            for place in range(8):
                index = ids_ref[group, start + at * 8 + place]
                held[at, place : place + 1, :] = table_ref[index]
            return carry

        lax.fori_loop(0, block // 8, move, 0, unroll=4)
        rows = held[...].reshape(block, held.shape[2])[:, :row_count]
        out_ref[:, group * row_count : (group + 1) * row_count] = rows.astype(NARROW)


def lookup(ids, table, start, block, row_count):
    groups = ids.shape[0]
    return pl.pallas_call(
        functools.partial(lookup_kernel, row_count),
        in_specs=[
            pl.BlockSpec(memory_space=pltpu.SMEM),
            pl.BlockSpec(memory_space=pltpu.SMEM),
            pl.BlockSpec(memory_space=pltpu.VMEM),
        ],
        out_specs=pl.BlockSpec(memory_space=pltpu.VMEM),
        out_shape=jax.ShapeDtypeStruct((block, groups * row_count), NARROW),
        scratch_shapes=[pltpu.VMEM((block // 8, 8, table.shape[2]), WIDE)],
        compiler_params=params(),
        cost_estimate=pl.CostEstimate(
            flops=groups * block * 4096, bytes_accessed=4 * table.size, transcendentals=0
        ),
    )(start, ids, table)


def norm_parts(values):
    mean = jnp.mean(values, axis=-1, keepdims=True)
    centred = values - mean
    scale = lax.rsqrt(jnp.mean(centred * centred, axis=-1, keepdims=True) + EPS)
    return centred * scale, scale


def norm_back(grad, values, gain):
    unit, scale = norm_parts(values)
    inner = grad * gain
    first = jnp.mean(inner, axis=-1, keepdims=True)
    second = jnp.mean(inner * unit, axis=-1, keepdims=True)
    return (inner - first - unit * second) * scale, jnp.sum(grad * unit, axis=0, keepdims=True)


def whole_call(kernel, outs, flops, *operands):
    return pl.pallas_call(
        kernel,
        out_shape=[jax.ShapeDtypeStruct(shape, kind) for shape, kind in outs],
        compiler_params=params(),
        cost_estimate=pl.CostEstimate(
            flops=flops,
            bytes_accessed=sum(4 * operand.size for operand in operands),
            transcendentals=0,
        ),
    )(*operands)


def norm_kernel(gain_ref, *refs):
    inputs, (out_ref, narrow_ref) = refs[:-2], refs[-2:]
    total = inputs[0][...].astype(WIDE)
    for ref in inputs[1:]:
        total = total + ref[...].astype(WIDE)
    out = norm_parts(total)[0] * gain_ref[...]
    out_ref[...] = out
    narrow_ref[...] = out.astype(NARROW)


def norm_forward(gain, *parts):
    shape = parts[0].shape
    return whole_call(norm_kernel, [(shape, WIDE), (shape, NARROW)], 20 * parts[0].size, gain, *parts)


def merge_kernel(attended_ref, weight_ref, x_ref, gain_ref, narrow_out, pre_ref, out_ref, out_b_ref):
    narrow = attended_ref[...].astype(NARROW)
    narrow_out[...] = narrow
    pre = x_ref[...] + contract_rows(narrow, weight_ref[...])
    pre_ref[...] = pre
    out = norm_parts(pre)[0] * gain_ref[...]
    out_ref[...] = out
    out_b_ref[...] = out.astype(NARROW)


def merge_branch(attended_t, weight, x_zero, gain):
    rows, width = x_zero.shape
    shape = (rows, width)
    return whole_call(
        merge_kernel,
        [((width, rows), NARROW), (shape, WIDE), (shape, WIDE), (shape, NARROW)],
        2 * rows * width * width,
        attended_t,
        weight,
        x_zero,
        gain,
    )


def last_kernel(length_ref, slots_ref, rows_ref, pooled_ref, hidden_ref, local_ref, got_ref, gain_ref, out_ref, narrow_ref, sum_ref):
    total = hidden_ref[...] + local_ref[...].astype(WIDE) + got_ref[...].astype(WIDE)
    spread = rows_ref[...]
    place = lax.broadcasted_iota(jnp.int32, (total.shape[0], slots_ref.shape[1]), 0)
    hot = (place == slots_ref[...]).astype(WIDE).astype(NARROW)
    high, low = halves(spread)
    grad = jnp.dot(hot, high, preferred_element_type=WIDE)
    grad = grad + jnp.dot(hot, low, preferred_element_type=WIDE)
    index = lax.broadcasted_iota(jnp.int32, (total.shape[0], 1), 0)
    grad = grad + jnp.where(index < length_ref[0], pooled_ref[...], 0.0)
    out, gain_grad = norm_back(grad, total, gain_ref[...])
    out_ref[...] = out
    narrow_ref[...] = out.astype(NARROW)
    sum_ref[...] = gain_grad


def last_back(length, slots, row_grad, pooled_grad, hidden_in, local, got, gain):
    shape = hidden_in.shape
    return pl.pallas_call(
        last_kernel,
        in_specs=[pl.BlockSpec(memory_space=pltpu.SMEM)]
        + [pl.BlockSpec(memory_space=pltpu.VMEM)] * 7,
        out_shape=[
            jax.ShapeDtypeStruct(shape, WIDE),
            jax.ShapeDtypeStruct(shape, NARROW),
            jax.ShapeDtypeStruct((1, shape[1]), WIDE),
        ],
        compiler_params=params(),
        cost_estimate=pl.CostEstimate(
            flops=200 * hidden_in.size, bytes_accessed=20 * hidden_in.size, transcendentals=0
        ),
    )(length, slots, row_grad, pooled_grad, hidden_in, local, got, gain)


def branch_back_kernel(grad_ref, local_ref, got_ref, pre_ref, gain_ref, weight_ref, out_ref, narrow_ref, attended_ref, sum_ref):
    grad = grad_ref[...] + local_ref[...].astype(WIDE) + got_ref[...].astype(WIDE)
    out, gain_grad = norm_back(grad, pre_ref[...], gain_ref[...])
    narrow = out.astype(NARROW)
    out_ref[...] = out
    narrow_ref[...] = narrow
    sum_ref[...] = gain_grad
    attended_ref[...] = contract_cols(narrow, weight_ref[...]).astype(NARROW)


def branch_back(pre_grad, local, got, pre_one, gain, weight):
    rows, width = pre_grad.shape
    shape = (rows, width)
    return whole_call(
        branch_back_kernel,
        [(shape, WIDE), (shape, NARROW), (shape, NARROW), ((1, width), WIDE)],
        2 * rows * width * width,
        pre_grad,
        local,
        got,
        pre_one,
        gain,
        weight,
    )


def first_back_kernel(grad_ref, dq_ref, weight_ref, local_ref, got_ref, value_ref, gain_ref, out_ref, sum_ref):
    grad = grad_ref[...] + local_ref[...].astype(WIDE) + got_ref[...].astype(WIDE)
    grad = grad + contract_cols(dq_ref[...], weight_ref[...])
    out, gain_grad = norm_back(grad, value_ref[...].astype(WIDE), gain_ref[...])
    out_ref[...] = out.astype(NARROW)
    sum_ref[...] = gain_grad


def first_back(pre_one_grad, dq, weight, local, got, embedded, gain):
    rows, width = pre_one_grad.shape
    return whole_call(
        first_back_kernel,
        [((rows, width), NARROW), ((1, width), WIDE)],
        2 * rows * width * width,
        pre_one_grad,
        dq,
        weight,
        local,
        got,
        embedded,
        gain,
    )


def ffn_kernel(x_ref, gate_ref, up_ref, down_ref, gate_out, up_out, act_ref, out_ref):
    x = x_ref[...]
    gate = jnp.dot(x, gate_ref[...], preferred_element_type=WIDE)
    up = jnp.dot(x, up_ref[...], preferred_element_type=WIDE)
    gate_out[...] = gate
    up_out[...] = up
    act = (gate / (1.0 + jnp.exp(-gate)) * up).astype(NARROW)
    act_ref[...] = act
    out_ref[...] = contract_cols(act, down_ref[...]).astype(NARROW)


def weight_block(width, hidden, index):
    return pl.BlockSpec((width, hidden), lambda i: (0, index))


def ffn_forward(x, weights):
    rows, width = x.shape
    hidden = weights.shape[1] // 4
    block = min(512, rows)
    tall = lambda i: (i, 0)
    return pl.pallas_call(
        ffn_kernel,
        grid=(rows // block,),
        in_specs=[pl.BlockSpec((block, width), tall)]
        + [weight_block(width, hidden, k) for k in range(1, 4)],
        out_specs=[
            pl.BlockSpec((block, hidden), tall),
            pl.BlockSpec((block, hidden), tall),
            pl.BlockSpec((block, hidden), tall),
            pl.BlockSpec((block, width), tall),
        ],
        out_shape=[
            jax.ShapeDtypeStruct((rows, hidden), WIDE),
            jax.ShapeDtypeStruct((rows, hidden), WIDE),
            jax.ShapeDtypeStruct((rows, hidden), NARROW),
            jax.ShapeDtypeStruct((rows, width), NARROW),
        ],
        compiler_params=params(),
        cost_estimate=pl.CostEstimate(
            flops=6 * rows * width * hidden,
            bytes_accessed=14 * rows * width + 6 * width * hidden,
            transcendentals=rows * hidden,
        ),
    )(x, weights, weights, weights)


def ffn_back_kernel(grad_ref, gate_in, up_in, gate_ref, up_ref, down_ref, dgate_ref, dup_ref, out_ref):
    act_grad = jnp.dot(grad_ref[...], down_ref[...], preferred_element_type=WIDE)
    gate, up = gate_in[...], up_in[...]
    share = 1.0 / (1.0 + jnp.exp(-gate))
    dgate = (act_grad * up * (share * (1.0 + gate * (1.0 - share)))).astype(NARROW)
    dup = (act_grad * (gate * share)).astype(NARROW)
    dgate_ref[...] = dgate
    dup_ref[...] = dup
    out_ref[...] = (
        contract_cols(dgate, gate_ref[...]) + contract_cols(dup, up_ref[...])
    ).astype(NARROW)


def ffn_backward(grad, gate, up, weights):
    rows, width = grad.shape
    hidden = weights.shape[1] // 4
    block = min(512, rows)
    tall = lambda i: (i, 0)
    return pl.pallas_call(
        ffn_back_kernel,
        grid=(rows // block,),
        in_specs=[
            pl.BlockSpec((block, width), tall),
            pl.BlockSpec((block, hidden), tall),
            pl.BlockSpec((block, hidden), tall),
        ]
        + [weight_block(width, hidden, k) for k in range(1, 4)],
        out_specs=[
            pl.BlockSpec((block, hidden), tall),
            pl.BlockSpec((block, hidden), tall),
            pl.BlockSpec((block, width), tall),
        ],
        out_shape=[
            jax.ShapeDtypeStruct((rows, hidden), NARROW),
            jax.ShapeDtypeStruct((rows, hidden), NARROW),
            jax.ShapeDtypeStruct((rows, width), NARROW),
        ],
        compiler_params=params(),
        cost_estimate=pl.CostEstimate(
            flops=6 * rows * width * hidden,
            bytes_accessed=16 * rows * width + 6 * width * hidden,
            transcendentals=rows * hidden,
        ),
    )(grad, gate, up, weights, weights, weights)


def logits_kernel(columns, tile, rows_ref, table_ref, targets_ref, out_ref, stats_ref, top_ref, sum_ref, hit_ref):
    step = pl.program_id(0)

    @pl.when(step == 0)
    def _():
        top_ref[...] = jnp.full(top_ref.shape, NEGATIVE, WIDE)
        sum_ref[...] = jnp.zeros(sum_ref.shape, WIDE)
        hit_ref[...] = jnp.zeros(hit_ref.shape, WIDE)

    logits = jnp.dot(rows_ref[...], table_ref[...], preferred_element_type=WIDE)
    out_ref[...] = logits
    place = step * tile + lax.broadcasted_iota(jnp.int32, (1, tile), 1)
    seen = jnp.where(place < columns, logits, NEGATIVE)
    hits = jnp.where((place == targets_ref[...]) & (place < columns), seen, 0.0)
    pieces = [slice(at, at + 128) for at in range(0, tile, 128)]
    before = top_ref[...]
    top = before
    for piece in pieces:
        top = jnp.maximum(top, seen[:, piece])
    total = sum_ref[...] * jnp.exp(before - top)
    hit = hit_ref[...]
    for piece in pieces:
        total = total + jnp.exp(seen[:, piece] - top)
        hit = hit + hits[:, piece]
    top_ref[...] = top
    sum_ref[...] = total
    hit_ref[...] = hit

    @pl.when(step == pl.num_programs(0) - 1)
    def _():
        peak = jnp.max(top, axis=1, keepdims=True)
        whole = jnp.sum(total * jnp.exp(top - peak), axis=1, keepdims=True)
        found = jnp.sum(hit, axis=1, keepdims=True)
        lane = lax.broadcasted_iota(jnp.int32, (1, 128), 1)
        stats_ref[...] = jnp.where(
            lane == 0, peak, jnp.where(lane == 1, whole, jnp.where(lane == 2, found, 0.0))
        )


def vocab_logits(rows_all, table, targets):
    picks, width = rows_all.shape
    columns = table.shape[1]
    tiles = -(-columns // TILE)
    tile = TILE
    still = lambda j: (0, 0)
    along = lambda j: (0, j)
    return pl.pallas_call(
        functools.partial(logits_kernel, columns, tile),
        grid=(tiles * TILE // tile,),
        in_specs=[
            pl.BlockSpec((picks, width), still),
            pl.BlockSpec((width, tile), along),
            pl.BlockSpec((picks, 1), still),
        ],
        out_specs=[pl.BlockSpec((picks, tile), along), pl.BlockSpec((picks, 128), still)],
        out_shape=[
            jax.ShapeDtypeStruct((picks, tiles * TILE), WIDE),
            jax.ShapeDtypeStruct((picks, 128), WIDE),
        ],
        scratch_shapes=[pltpu.VMEM((picks, 128), WIDE)] * 3,
        compiler_params=params(),
        cost_estimate=pl.CostEstimate(
            flops=2 * picks * width * columns,
            bytes_accessed=2 * width * columns,
            transcendentals=picks * columns,
        ),
    )(rows_all, table, targets)


def combine_kernel(count, slots, bit, mine_ref, other_ref, out_ref):
    lane = lax.broadcasted_iota(jnp.int32, (1, 128), 1)
    for block in range(count):
        mine = mine_ref[block * slots : (block + 1) * slots, :]
        other = other_ref[(block ^ bit) * slots : ((block ^ bit) + 1) * slots, :]
        peak = jnp.maximum(mine[:, :1], other[:, :1])
        total = mine[:, 1:2] * jnp.exp(mine[:, :1] - peak)
        total = total + other[:, 1:2] * jnp.exp(other[:, :1] - peak)
        out_ref[block * slots : (block + 1) * slots, :] = jnp.where(
            lane == 0, peak, jnp.where(lane == 1, total, mine + other)
        )
    rest = count * slots
    out_ref[rest:, :] = mine_ref[rest:, :] + other_ref[rest:, :]


def dlogits_kernel(columns, tile, logits_ref, table_ref, targets_ref, stats_ref, weight_ref, out_ref, grad_ref):
    step = pl.program_id(0)
    log_all = stats_ref[:, :1] + jnp.log(stats_ref[:, 1:2])
    place = step * tile + lax.broadcasted_iota(jnp.int32, (1, tile), 1)
    share = jnp.exp(logits_ref[...] - log_all) - jnp.where(place == targets_ref[...], 1.0, 0.0)
    grad = jnp.where(place < columns, share * weight_ref[...], 0.0).astype(NARROW)
    out_ref[...] = grad
    column = step * tile + lax.broadcasted_iota(jnp.int32, (1, tile), 1)
    table = jnp.where(column < columns, table_ref[...].astype(WIDE), 0.0).astype(NARROW)
    part = contract_cols(grad, table)

    @pl.when(step == 0)
    def _():
        grad_ref[...] = part

    @pl.when(step > 0)
    def _():
        grad_ref[...] += part


def vocab_back(logits, table, targets, stats, weight):
    picks = targets.shape[0]
    width, columns = table.shape
    tile = TILE
    still = lambda j: (0, 0)
    along = lambda j: (0, j)
    return pl.pallas_call(
        functools.partial(dlogits_kernel, columns, tile),
        grid=(logits.shape[1] // tile,),
        in_specs=[
            pl.BlockSpec((picks, tile), along),
            pl.BlockSpec((width, tile), along),
            pl.BlockSpec((picks, 1), still),
            pl.BlockSpec((picks, 128), still),
            pl.BlockSpec((picks, 1), still),
        ],
        out_specs=[pl.BlockSpec((picks, tile), along), pl.BlockSpec((picks, width), still)],
        out_shape=[
            jax.ShapeDtypeStruct(logits.shape, NARROW),
            jax.ShapeDtypeStruct((picks, width), WIDE),
        ],
        compiler_params=params(),
        cost_estimate=pl.CostEstimate(
            flops=2 * picks * width * columns,
            bytes_accessed=2 * width * columns,
            transcendentals=picks * columns,
        ),
    )(logits, table, targets, stats, weight)


def contrast_kernel(weight, length_ref, pooled_ref, keys_ref, blocked_ref, target_ref, grad_ref, part_ref):
    length = length_ref[0].astype(WIDE)
    pooled = pooled_ref[...] / length
    scale = lax.rsqrt(jnp.sum(pooled * pooled, axis=-1, keepdims=True) + EPS)
    narrow = jnp.broadcast_to(pooled * scale, (8, pooled.shape[1])).astype(NARROW)
    keys = keys_ref[...]
    scores = contract_cols(narrow, keys)[:1] / TAU
    target = target_ref[...]
    masked = jnp.where(blocked_ref[...] > 0.0, NEGATIVE, scores)
    top = jnp.max(masked, axis=-1, keepdims=True)
    log_c = top + jnp.log(jnp.sum(jnp.exp(masked - top), axis=-1, keepdims=True))
    chosen = jnp.sum(jnp.where(target > 0.0, scores, 0.0), axis=-1, keepdims=True)
    part_ref[...] = jnp.broadcast_to((log_c - chosen) * weight, part_ref.shape)
    dscores = ((jnp.exp(masked - log_c) - target) * (weight / TAU)).astype(NARROW)
    dscores = jnp.broadcast_to(dscores.astype(WIDE), (8, dscores.shape[1])).astype(NARROW)
    grad = jnp.dot(dscores, keys, preferred_element_type=WIDE)[:1]
    inner = jnp.sum(pooled * grad, axis=-1, keepdims=True)
    grad_ref[...] = (grad - pooled * (inner * scale * scale)) * scale / length


def contrast(weight, length, pooled_sum, keys_hat, blocked, target):
    width = pooled_sum.shape[1]
    return pl.pallas_call(
        functools.partial(contrast_kernel, weight),
        in_specs=[pl.BlockSpec(memory_space=pltpu.SMEM)]
        + [pl.BlockSpec(memory_space=pltpu.VMEM)] * 4,
        out_shape=[
            jax.ShapeDtypeStruct((1, width), WIDE),
            jax.ShapeDtypeStruct((1, 128), WIDE),
        ],
        compiler_params=params(),
        cost_estimate=pl.CostEstimate(
            flops=4 * keys_hat.size, bytes_accessed=2 * keys_hat.size, transcendentals=0
        ),
    )(length, pooled_sum, keys_hat, blocked, target)


def head_lanes(head):
    lane = lax.broadcasted_iota(jnp.int32, (1, PAIR), 1)
    return (lane // HEAD_DIM) == head, lane == HEAD_DIM * (1 - head)


def attend_kernel(count, q_ref, *refs):
    k_refs, v_refs, bias_refs = refs[:count], refs[count : 2 * count], refs[2 * count : 3 * count]
    out_ref, log_ref, s_ref = refs[3 * count :]
    head = pl.program_id(1)
    mine, spare = head_lanes(head)
    step = k_refs[0].shape[0]
    blocks = [pl.ds(k * step, step) for k in range(count)]
    query = jnp.where(spare, 1.0, jnp.where(mine, q_ref[...].astype(WIDE), 0.0)).astype(NARROW)
    top = None
    for rows, k_ref, bias_ref in zip(blocks, k_refs, bias_refs):
        key = jnp.where(spare, bias_ref[...].astype(WIDE), k_ref[...].astype(WIDE))
        scores = contract_cols(key.astype(NARROW), query)
        s_ref[rows, :] = scores
        peak = jnp.max(scores, axis=0, keepdims=True)
        top = peak if top is None else jnp.maximum(top, peak)
    total = None
    for rows in blocks:
        powers = jnp.exp(s_ref[rows, :] - top)
        s_ref[rows, :] = powers
        part = jnp.sum(powers, axis=0, keepdims=True)
        total = part if total is None else total + part
    share = 1.0 / total
    result = None
    for rows, v_ref in zip(blocks, v_refs):
        probs = (s_ref[rows, :] * share).astype(NARROW)
        part = contract_rows(v_ref[...], probs)
        result = part if result is None else result + part
    log_ref[0, pl.ds(head, 1), :] = top + jnp.log(total)

    @pl.when(head == 0)
    def _():
        out_ref[...] = result

    @pl.when(head == 1)
    def _():
        out_ref[HEAD_DIM:, :] = result[HEAD_DIM:, :]


def attention_forward(queries, keys, values, biases):
    rows, width = queries.shape
    count = len(keys)
    length = rows * count
    pairs = width // PAIR
    lanes = pl.BlockSpec((rows, PAIR), lambda i, h: (0, i))
    still = pl.BlockSpec((rows, PAIR), lambda i, h: (0, 0))
    return pl.pallas_call(
        functools.partial(attend_kernel, count),
        grid=(pairs, 2),
        in_specs=[lanes] * (1 + 2 * count) + [still] * count,
        out_specs=[
            pl.BlockSpec((PAIR, rows), lambda i, h: (i, 0)),
            pl.BlockSpec((1, 2, rows), lambda i, h: (i, 0, 0)),
        ],
        out_shape=[
            jax.ShapeDtypeStruct((width, rows), WIDE),
            jax.ShapeDtypeStruct((pairs, 2, rows), WIDE),
        ],
        scratch_shapes=[pltpu.VMEM((length, rows), WIDE)],
        compiler_params=params(),
        cost_estimate=pl.CostEstimate(
            flops=4 * rows * length * width,
            bytes_accessed=4 * length * width + 8 * rows * width,
            transcendentals=rows * length * HEADS,
        ),
    )(queries, *keys, *values, *biases)


def attend_back_kernel(count, q_ref, grad_ref, out_ref, log_ref, *refs):
    groups = [refs[k * count : (k + 1) * count] for k in range(5)]
    k_refs, v_refs, bias_refs, cos_refs, sin_refs = groups
    rest = refs[5 * count :]
    dq_ref, dk_refs, dv_refs = rest[0], rest[1 : 1 + count], rest[1 + count : 1 + 2 * count]
    dk_sum, dv_sum, dq_sum = rest[1 + 2 * count :]
    head = pl.program_id(1)
    mine, spare = head_lanes(head)
    step, scale = k_refs[0].shape[0], HEAD_DIM ** (-0.5)
    own = jnp.where(mine, q_ref[...].astype(WIDE), 0.0)
    query = own.astype(NARROW)
    asked = jnp.where(spare, 1.0, own).astype(NARROW)
    grad_wide = jnp.where(mine, grad_ref[...].astype(WIDE), 0.0)
    grad = grad_wide.astype(NARROW)
    delta = jnp.sum(grad_wide.T * out_ref[...], axis=0, keepdims=True)
    log_total = log_ref[0, pl.ds(head, 1), :]
    dq = None
    for k in range(count):
        rows = pl.ds(k * step, step)
        key_block = k_refs[k][...]
        key = jnp.where(spare, bias_refs[k][...].astype(WIDE), key_block.astype(WIDE))
        scores = contract_cols(key.astype(NARROW), asked)
        probs = jnp.exp(scores - log_total)
        dprobs = contract_cols(v_refs[k][...], grad)
        dv = jnp.dot(probs.astype(NARROW), grad, preferred_element_type=WIDE)
        dscores = (probs * (dprobs - delta)).astype(NARROW)
        dk = jnp.dot(dscores, query, preferred_element_type=WIDE)
        part = contract_rows(key_block, dscores)
        dq = part if dq is None else dq + part

        @pl.when(head == 0)
        def _():
            dk_sum[rows, :] = dk
            dv_sum[rows, :] = dv

        @pl.when(head == 1)
        def _():
            total = dk_sum[rows, :] + dk
            dk_refs[k][...] = turn(total, cos_refs[k][...], -sin_refs[k][...]).astype(NARROW)
            dv_refs[k][...] = (dv_sum[rows, :] + dv).astype(NARROW)

    @pl.when(head == 0)
    def _():
        dq_sum[...] = dq

    @pl.when(head == 1)
    def _():
        dq_sum[HEAD_DIM:, :] = dq[HEAD_DIM:, :]
        total = dq_sum[...].T * scale
        dq_ref[...] = turn(total, cos_refs[0][...], -sin_refs[0][...]).astype(NARROW)


def attention_backward(queries, keys, values, biases, grad, out_t, log_total, cosines, sines):
    rows, width = queries.shape
    count = len(keys)
    length = rows * count
    pairs = width // PAIR
    lanes = pl.BlockSpec((rows, PAIR), lambda i, h: (0, i))
    still = pl.BlockSpec((rows, PAIR), lambda i, h: (0, 0))
    found = pl.pallas_call(
        functools.partial(attend_back_kernel, count),
        grid=(pairs, 2),
        in_specs=[
            lanes,
            lanes,
            pl.BlockSpec((PAIR, rows), lambda i, h: (i, 0)),
            pl.BlockSpec((1, 2, rows), lambda i, h: (i, 0, 0)),
        ]
        + [lanes] * (2 * count)
        + [still] * (3 * count),
        out_specs=[lanes] * (1 + 2 * count),
        out_shape=[jax.ShapeDtypeStruct((rows, width), NARROW)] * (1 + 2 * count),
        scratch_shapes=[
            pltpu.VMEM((length, PAIR), WIDE),
            pltpu.VMEM((length, PAIR), WIDE),
            pltpu.VMEM((PAIR, rows), WIDE),
        ],
        compiler_params=params(),
        cost_estimate=pl.CostEstimate(
            flops=10 * rows * length * width,
            bytes_accessed=8 * length * width + 8 * rows * width,
            transcendentals=rows * length * HEADS,
        ),
    )(queries, grad, out_t, log_total, *keys, *values, *biases, *cosines, *sines)
    return found[0], found[1 : 1 + count], found[1 + count :]


def project_down(matrix, factor_t):
    high, low = halves(matrix)
    factor_high, factor_low = halves(factor_t)
    both = jnp.concatenate([factor_high, factor_low], axis=0)
    first = jnp.dot(both, high, preferred_element_type=WIDE)
    second = jnp.dot(factor_high, low, preferred_element_type=WIDE)
    return first[:RANK] + first[RANK:] + second


def project_back(matrix, basis_t):
    high, low = halves(matrix)
    basis_high, basis_low = halves(basis_t)
    both = jnp.concatenate([basis_high, basis_low], axis=0)
    first = contract_cols(both, high)
    second = contract_cols(basis_high, low)
    return first[:RANK] + first[RANK:] + second


def expand(back_t, basis_t):
    back_high, back_low = halves(back_t)
    basis_high, basis_low = halves(basis_t)
    left = jnp.concatenate([back_high, back_low, back_high], axis=0)
    right = jnp.concatenate([basis_high, basis_high, basis_low], axis=0)
    return contract_rows(left, right)


def table_kernel(columns, first, starts_ref, left_ref, tokens_ref, rows_ref, dlogits_ref, error_ref, factor_ref, high_ref, low_ref, p_ref, sum_ref):
    tile = first + pl.program_id(0)
    place = tile * TILE + lax.broadcasted_iota(jnp.int32, (TILE, 1), 0)
    sum_ref[...] = error_ref[...] + contract_rows(dlogits_ref[...], rows_ref[...])

    def visit(chunk, carry):
        at = pl.ds(pl.multiple_of(chunk * CHUNK, CHUNK), CHUNK)
        hot = jnp.where(tokens_ref[:, at] == place, 1.0, 0.0).astype(NARROW)
        sum_ref[...] += jnp.dot(hot, left_ref[at, :], preferred_element_type=WIDE)
        return carry

    lax.fori_loop(
        starts_ref[tile] // CHUNK, (starts_ref[tile + 1] + CHUNK - 1) // CHUNK, visit, 0
    )
    total = jnp.where(place < columns, sum_ref[...], 0.0)
    high, low = halves(total)
    high_ref[...] = high
    low_ref[...] = low
    factor_high, factor_low = halves(factor_ref[...])
    both = jnp.concatenate([factor_high, factor_low], axis=0)
    found = contract_cols(high, both).T
    rest = contract_cols(low, both).T
    p_ref[...] = found[:RANK] + found[RANK:] + rest[:RANK]


def table_matrix(bounds, starts, left, tokens, rows, dlogits, error, factor_t):
    columns, width = error.shape
    slots = left.shape[0]
    picks = rows.shape[0]
    first, tiles = bounds[0], bounds[1] - bounds[0]
    still = lambda j: (0, 0)
    down = lambda j: (j, 0)
    return pl.pallas_call(
        functools.partial(table_kernel, columns, first),
        grid=(tiles,),
        in_specs=[
            pl.BlockSpec(memory_space=pltpu.SMEM),
            pl.BlockSpec((slots, width), still),
            pl.BlockSpec((1, slots), still),
            pl.BlockSpec((picks, width), still),
            pl.BlockSpec((picks, TILE), lambda j: (0, first + j)),
            pl.BlockSpec((TILE, width), lambda j: (first + j, 0)),
            pl.BlockSpec((RANK, width), still),
        ],
        out_specs=[
            pl.BlockSpec((TILE, width), down),
            pl.BlockSpec((TILE, width), down),
            pl.BlockSpec((RANK, TILE), lambda j: (0, j)),
        ],
        out_shape=[
            jax.ShapeDtypeStruct((tiles * TILE, width), NARROW),
            jax.ShapeDtypeStruct((tiles * TILE, width), NARROW),
            jax.ShapeDtypeStruct((RANK, tiles * TILE), WIDE),
        ],
        scratch_shapes=[pltpu.VMEM((TILE, width), WIDE)],
        compiler_params=params(),
        cost_estimate=pl.CostEstimate(
            flops=2 * width * tiles * TILE * (slots // 4 + picks + 24),
            bytes_accessed=8 * width * tiles * TILE,
            transcendentals=0,
        ),
    )(starts, left, tokens, rows, dlogits, error, factor_t)


def partial_kernel(*refs):
    count = (len(refs) - 1) // 2
    for index in range(count):
        refs[-1][index] = project_down(refs[index][...], refs[count + index][...])


def partial_projections(matrices, factors_t):
    count, (width, columns) = len(matrices), matrices[0].shape
    return whole_call(
        partial_kernel,
        [((count, RANK, columns), WIDE)],
        48 * count * width * columns,
        *matrices,
        *factors_t,
    )[0]


def small_kernel(count, *refs):
    grads, errors, factor_ref = refs[:count], refs[count : 2 * count], refs[2 * count]
    m_ref, p_ref = refs[2 * count + 1 :]
    for index in range(count):
        total = grads[index][...] + errors[index][...]
        m_ref[index] = total
        p_ref[index] = project_down(total, factor_ref[index])


def small_matrices(grads, errors, factor_t):
    count, (width, columns) = len(grads), grads[0].shape
    return pl.pallas_call(
        functools.partial(small_kernel, count),
        out_shape=[
            jax.ShapeDtypeStruct((count, width, columns), WIDE),
            jax.ShapeDtypeStruct((count, RANK, columns), WIDE),
        ],
        compiler_params=params(),
        cost_estimate=pl.CostEstimate(
            flops=48 * count * width * columns,
            bytes_accessed=12 * count * width * columns,
            transcendentals=0,
        ),
    )(*grads, *errors, factor_t)


def basis_kernel(spans, p_ref, out_ref):
    index = lax.broadcasted_iota(jnp.int32, (RANK, 1), 0)
    for start, size in spans:
        rows = p_ref[:, pl.ds(start, size)]
        for place in range(RANK):
            row = rows[place : place + 1, :]
            row = row * lax.rsqrt(jnp.sum(row * row, axis=1, keepdims=True))
            inner = jnp.sum(rows * row, axis=1, keepdims=True)
            rows = jnp.where(index == place, row, rows - jnp.where(index > place, inner, 0.0) * row)
        out_ref[:, pl.ds(start, size)] = rows


def bases_of(sums, spans):
    return pl.pallas_call(
        functools.partial(basis_kernel, spans),
        out_shape=jax.ShapeDtypeStruct(sums.shape, WIDE),
        compiler_params=params(),
        cost_estimate=pl.CostEstimate(
            flops=64 * sums.size, bytes_accessed=8 * sums.size, transcendentals=40
        ),
    )(sums)


def small_back_kernel(m_ref, basis_ref, back_ref):
    for index in range(m_ref.shape[0]):
        back_ref[index] = project_back(m_ref[index], basis_ref[index])


def small_backs(matrices, basis):
    count, width, columns = matrices.shape
    return pl.pallas_call(
        small_back_kernel,
        out_shape=jax.ShapeDtypeStruct((count, RANK, width), WIDE),
        compiler_params=params(),
        cost_estimate=pl.CostEstimate(
            flops=48 * count * width * columns,
            bytes_accessed=4 * count * width * columns,
            transcendentals=0,
        ),
    )(matrices, basis)


def table_specs(parts, width):
    bounds, first = [], 0
    for part in parts:
        bounds.append((first, first + part.shape[0] // TILE))
        first = bounds[-1][1]
    specs = [
        pl.BlockSpec(
            (TILE, width), lambda j, low=low, high=high: (jnp.clip(j, low, high - 1) - low, 0)
        )
        for low, high in bounds
    ]
    return bounds, specs


def table_back_kernel(bounds, *refs):
    highs, lows = refs[: len(bounds)], refs[len(bounds) : 2 * len(bounds)]
    basis_ref, back_ref = refs[2 * len(bounds) :]
    step = pl.program_id(0)
    basis_high, basis_low = halves(basis_ref[...])
    both = jnp.concatenate([basis_high, basis_low], axis=0)

    @pl.when(step == 0)
    def _():
        back_ref[...] = jnp.zeros(back_ref.shape, WIDE)

    for (low, high), high_ref, low_ref in zip(bounds, highs, lows):

        @pl.when((step >= low) & (step < high))
        def _():
            first = jnp.dot(both, high_ref[...], preferred_element_type=WIDE)
            second = jnp.dot(basis_high, low_ref[...], preferred_element_type=WIDE)
            back_ref[...] += first[:RANK] + first[RANK:] + second


def table_back(highs, lows, basis):
    width = highs[0].shape[1]
    columns = basis.shape[1]
    bounds, specs = table_specs(highs, width)
    return pl.pallas_call(
        functools.partial(table_back_kernel, bounds),
        grid=(columns // TILE,),
        in_specs=specs + specs + [pl.BlockSpec((RANK, TILE), lambda j: (0, j))],
        out_specs=pl.BlockSpec((RANK, width), lambda j: (0, 0)),
        out_shape=jax.ShapeDtypeStruct((RANK, width), WIDE),
        compiler_params=params(),
        cost_estimate=pl.CostEstimate(
            flops=48 * width * columns, bytes_accessed=4 * width * columns, transcendentals=0
        ),
    )(*highs, *lows, basis)


def small_error_kernel(m_ref, back_ref, basis_ref, *out_refs):
    for index, out_ref in enumerate(out_refs):
        out_ref[...] = m_ref[index] - expand(back_ref[index], basis_ref[index])


def small_errors(matrices, backs, basis):
    count, width, columns = matrices.shape
    return pl.pallas_call(
        small_error_kernel,
        out_shape=[jax.ShapeDtypeStruct((width, columns), WIDE)] * count,
        compiler_params=params(),
        cost_estimate=pl.CostEstimate(
            flops=48 * count * width * columns,
            bytes_accessed=8 * count * width * columns,
            transcendentals=0,
        ),
    )(matrices, backs, basis)


def table_error_kernel(bounds, *refs):
    highs, lows = refs[: len(bounds)], refs[len(bounds) : 2 * len(bounds)]
    back_ref, basis_ref, out_ref = refs[2 * len(bounds) :]
    step = pl.program_id(0)
    for (low, high), high_ref, low_ref in zip(bounds, highs, lows):

        @pl.when((step >= low) & (step < high))
        def _():
            whole = high_ref[...].astype(WIDE) + low_ref[...].astype(WIDE)
            out_ref[...] = whole - expand(basis_ref[...], back_ref[...])


def table_error(highs, lows, back, basis, columns):
    width = highs[0].shape[1]
    bounds, specs = table_specs(highs, width)
    return pl.pallas_call(
        functools.partial(table_error_kernel, bounds),
        grid=(basis.shape[1] // TILE,),
        in_specs=specs
        + specs
        + [
            pl.BlockSpec((RANK, width), lambda j: (0, 0)),
            pl.BlockSpec((RANK, TILE), lambda j: (0, j)),
        ],
        out_specs=pl.BlockSpec((TILE, width), lambda j: (j, 0)),
        out_shape=jax.ShapeDtypeStruct((columns, width), WIDE),
        compiler_params=params(),
        cost_estimate=pl.CostEstimate(
            flops=48 * width * columns, bytes_accessed=8 * width * columns, transcendentals=0
        ),
    )(*highs, *lows, back, basis)


def normalize_keys(raw_keys):
    wide_keys = raw_keys.astype(WIDE)
    return (
        wide_keys * lax.rsqrt(jnp.sum(wide_keys * wide_keys, axis=-1, keepdims=True) + EPS)
    ).astype(NARROW)


def per_device(
    token_ids,
    seq_lengths,
    mask_slots,
    mask_targets,
    positive_rows,
    doc_ids,
    false_pairs,
    queue_docs,
    queue_embed,
    attend_weight,
    attend_moment,
    gate_up,
    gate_up_moment,
    down_weight,
    down_moment,
    embed_table,
    embed_moment,
    gains,
    gains_moment,
    attend_error,
    gate_up_error,
    down_error,
    embed_error,
    factors,
):
    tensor_count = lax.axis_size("tensor")
    tensor_rank = lax.axis_index("tensor")
    data_count = lax.axis_size("dp")
    data_rank = lax.axis_index("dp")
    groups, seq_len = token_ids.shape
    width = gains.shape[1]
    total_rows = groups * seq_len
    own_rows = total_rows // tensor_count
    slot_count = mask_slots.shape[2]
    seq_total = groups * data_count
    near = jnp.arange(tensor_count) ^ tensor_rank
    row_count = attend_weight.shape[0]

    tokens_all = lax.all_to_all(
        jnp.broadcast_to(token_ids, (data_count, seq_len)), "dp", 0, 0, tiled=True
    )
    vocab_own = embed_table.shape[1]
    vocab_start = tensor_rank * vocab_own
    ids = tokens_all - vocab_start
    ids = jnp.where((ids >= 0) & (ids < vocab_own), ids, vocab_own)
    fill = -(-row_count // 128) * 128 - row_count
    table_local = embed_table.astype(NARROW)
    table_rows = jnp.pad(table_local.astype(WIDE).T, ((0, 1), (0, fill)))[:, None]
    looked = {}
    for key in reversed(range(tensor_count)):
        start = ((tensor_rank ^ key) * own_rows).reshape(1)
        looked[key] = lookup(ids, table_rows, start, own_rows, row_count)
    mine = summed_block([looked[key] for key in range(tensor_count)], "tensor", NARROW)
    side = (seq_lengths, mask_slots, mask_targets, positive_rows, doc_ids, false_pairs)
    side = side + (queue_docs, factors, gate_up_error, down_error, attend_error, data_rank)
    side, near_ids, near, _ = lax.optimization_barrier((side, token_ids, near, looked[0]))
    seq_lengths, mask_slots, mask_targets, positive_rows, doc_ids, false_pairs = side[:6]
    queue_docs, factors, gate_up_error, down_error, attend_error, data_rank = side[6:]
    pieces = mine.astype(NARROW).T.reshape(data_count, row_count, own_rows)
    embedded = lax.all_to_all(pieces, "dp", 0, 0).reshape(width, own_rows).T

    attend_cols = attend_error.shape[2]
    quarter = lax.dynamic_slice_in_dim(attend_weight, tensor_rank * attend_cols, attend_cols, 1)
    joined = jnp.concatenate(
        [quarter, gate_up[:, 0], gate_up[:, 1], down_weight], axis=1
    ).astype(NARROW)
    joined_b = lax.all_gather(joined, "dp", axis=0, tiled=True)
    quarter_b, ffn_b = joined_b[:, :attend_cols], joined_b
    attend_near = picked_blocks(spread_blocks(quarter_b, "tensor"), near)
    attend_b = jnp.concatenate([attend_near[k] for k in range(tensor_count)], axis=1)
    table_local, _ = lax.optimization_barrier((table_local, looked[tensor_count - 1]))
    table_b = lax.all_gather(table_local, "dp", axis=0, tiled=True)

    every_rows = mask_slots + own_rows * jnp.arange(tensor_count)[None, :, None]
    every_len = seq_lengths[:, None, None]
    count = jnp.sum((every_rows < every_len).astype(WIDE))
    my_length = lax.dynamic_index_in_dim(seq_lengths, data_rank, 0, keepdims=False)
    group_valid = lax.dynamic_index_in_dim(every_rows < every_len, data_rank, 0, keepdims=False)
    own_slots = lax.dynamic_slice(
        mask_slots, (data_rank, tensor_rank, 0), (1, 1, slot_count)
    ).reshape(1, slot_count)
    own_length = (my_length - tensor_rank * own_rows).reshape(1)
    valid_rows = picked_blocks(group_valid, near).reshape(-1, 1).astype(WIDE)
    row_weight = valid_rows / count
    targets = picked_blocks(mask_targets[0], near).reshape(-1, 1) - vocab_start
    near_tokens = picked_blocks(near_ids.reshape(tensor_count, own_rows), near).reshape(1, -1)
    shifted = near_tokens - vocab_start
    tiles = -(-vocab_own // TILE)
    index = jnp.arange(total_rows)
    before = (shifted < shifted.T) | ((shifted == shifted.T) & (index[None, :] < index[:, None]))
    ranks = jnp.sum(before.astype(jnp.int32), axis=1)
    ordered = ranks[None, :] == index[:, None]
    sorted_ids = jnp.sum(jnp.where(ordered, shifted, 0), axis=1)[None, :]
    starts = jnp.sum(
        (shifted < jnp.minimum(jnp.arange(tiles + 1) * TILE, vocab_own)[:, None]).astype(jnp.int32),
        axis=1,
    )
    places = near[:, None] * own_rows + jnp.arange(own_rows)[None, :]
    cosine, sine = rotary_tables(places.reshape(-1))
    cosines, sines = row_blocks(cosine, tensor_count), row_blocks(sine, tensor_count)
    bias = jnp.where(places < my_length, 0.0, NEGATIVE).astype(NARROW)
    biases = [jnp.broadcast_to(bias[k][:, None], (own_rows, PAIR)) for k in range(tensor_count)]
    columns = jnp.arange(queue_docs.shape[0])
    pick = lambda array: lax.dynamic_slice_in_dim(array, data_rank, 1, 0)
    target_c = columns[None, :] == pick(positive_rows)[:, None]
    blocked = (queue_docs[None, :] == pick(doc_ids)[:, None]) | jnp.any(
        pick(false_pairs)[:, :, None] == columns[None, None, :], axis=1
    )
    blocked = (blocked & jnp.logical_not(target_c)).astype(WIDE)
    target_c = target_c.astype(WIDE)

    x_zero, x_zero_b = norm_forward(gains[:1], embedded)
    x_blocks = spread_blocks(x_zero_b, "tensor")
    queries, first_key, first_value = project(3, x_zero_b, attend_b, cosines[0], sines[0])
    keys, values = [first_key], [first_value]
    for k in range(1, tensor_count):
        key, value = project(2, x_blocks[k], attend_b, cosines[k], sines[k])
        keys.append(key)
        values.append(value)
    attended_t, log_total = attention_forward(queries, keys, values, biases)
    queue_local, _ = lax.optimization_barrier((queue_embed, log_total))
    queue_all = lax.all_gather(queue_local, "dp", axis=0, tiled=True)
    keys_hat = normalize_keys(queue_all)
    weight_out = attend_b[:, 3 * width :]
    attended_b, pre_one, hidden_in, hidden_in_b = merge_branch(
        attended_t, weight_out, x_zero, gains[1:2]
    )
    hidden_blocks = spread_blocks(hidden_in_b, "tensor")
    half = max(1, tensor_count // 2)
    hidden_parts = [
        jnp.concatenate(hidden_blocks[at : at + half], axis=0)
        for at in range(0, tensor_count, half)
    ]
    states = []
    for part in hidden_parts:
        if states:
            part, _ = lax.optimization_barrier((part, states[-1][3]))
        states.append(ffn_forward(part, ffn_b))
    ffn_blocks = [block for state in states for block in row_blocks(state[3], half)]
    ffn_mine, ffn_got = summed_pair(ffn_blocks, "tensor")
    final, _ = norm_forward(gains[2:], hidden_in, ffn_mine, ffn_got)

    factor_t = jnp.swapaxes(factors, 1, 2)
    factor_near = spread_blocks(factor_t[0], "tensor")
    error_p = partial_projections([attend_error[0]], [factor_t[0]])[0]
    ff_own = down_weight.shape[1]

    keep_own = (places[0] < my_length)[:, None]
    pool_part = jnp.sum(jnp.where(keep_own, final, 0.0), axis=0)
    picked = jnp.take(final, own_slots[0], axis=0).astype(NARROW)
    rows_all = jnp.concatenate(spread_blocks(picked, "tensor"), axis=0)
    logits, stats = vocab_logits(rows_all, table_b, targets)
    picks = rows_all.shape[0]
    pool_rows = jnp.pad(pool_part.reshape(-1, 128), ((0, 8 - width // 128), (0, 0)))
    stats = jnp.concatenate([stats, pool_rows], axis=0)
    for bit in axis_bits("tensor"):
        other = swap(stats, "tensor", bit)
        stats = whole_call(
            functools.partial(combine_kernel, tensor_count, slot_count, bit),
            [(stats.shape, WIDE)],
            20 * stats.size,
            stats,
            other,
        )[0]
    pooled_sum = stats[picks : picks + width // 128].reshape(1, width)
    own_stats = stats[:slot_count]
    cross = own_stats[:, 0] + jnp.log(own_stats[:, 1]) - own_stats[:, 2]
    masked_part = jnp.sum(valid_rows[:slot_count, 0] * cross)
    dlogits, row_part = vocab_back(logits, table_b, targets, stats[:picks], row_weight)
    row_grad = summed_block(row_blocks(row_part, tensor_count), "tensor", NARROW)

    weight_c = LAMBDA / seq_total
    first_rank = jnp.where(tensor_rank == 0, 1.0, 0.0)
    pooled_grad, contrast_row = contrast(
        weight_c, my_length.reshape(1), pooled_sum, keys_hat, blocked, target_c
    )
    contrast_part = contrast_row[0, 0] * first_rank

    pre_grad, pre_grad_b, gain_two = last_back(
        own_length, own_slots, row_grad, pooled_grad, hidden_in, ffn_mine, ffn_got, gains[2:]
    )
    grad_blocks = spread_blocks(pre_grad_b, "tensor")
    grad_parts = [
        jnp.concatenate(grad_blocks[at : at + half], axis=0) for at in range(0, tensor_count, half)
    ]
    backs = [
        ffn_backward(part, state[0], state[1], ffn_b) for part, state in zip(grad_parts, states)
    ]
    hidden_sums = [block for back in backs for block in row_blocks(back[2], half)]
    hidden_mine, hidden_got = summed_pair(hidden_sums, "tensor")
    down_grad = sum(contract_rows(part, state[2]) for part, state in zip(grad_parts, states))
    gate_w_grad = sum(contract_rows(part, back[0]) for part, back in zip(hidden_parts, backs))
    up_w_grad = sum(contract_rows(part, back[1]) for part, back in zip(hidden_parts, backs))
    pre_one_grad, branch_grad, attended_grad, gain_one = branch_back(
        pre_grad, hidden_mine, hidden_got, pre_one, gains[1:2], weight_out
    )
    dq, dk, dv = attention_backward(
        queries, keys, values, biases, attended_grad, attended_t, log_total, cosines, sines
    )
    weight_k, weight_v = attend_b[:, width : 2 * width], attend_b[:, 2 * width : 3 * width]
    x_parts = [
        (contract_cols(dk[k], weight_k) + contract_cols(dv[k], weight_v)).astype(NARROW)
        for k in range(tensor_count)
    ]
    x_mine, x_got = summed_pair(x_parts, "tensor")
    embedded_grad, gain_zero = first_back(
        pre_one_grad, dq, attend_b[:, :width], x_mine, x_got, embedded, gains[:1]
    )
    emb_all = jnp.concatenate(spread_blocks(embedded_grad, "tensor"), axis=0)
    emb_all = jnp.dot(ordered.astype(NARROW), emb_all)
    attend_part = jnp.concatenate(
        [
            contract_rows(x_zero_b, dq),
            sum(contract_rows(x_blocks[k], dk[k]) for k in range(tensor_count)),
            sum(contract_rows(x_blocks[k], dv[k]) for k in range(tensor_count)),
            jnp.dot(attended_b, branch_grad, preferred_element_type=WIDE),
        ],
        axis=1,
    )
    attend_blocks = jnp.moveaxis(attend_part.reshape(width, tensor_count, attend_cols), 1, 0)
    attend_blocks = picked_blocks(attend_blocks, near)
    attend_p = partial_projections(
        [attend_blocks[k] for k in range(tensor_count)], factor_near
    )
    attend_p = summed_block([attend_p[k] for k in range(tensor_count)], "tensor", WIDE)
    attend_p = attend_p + error_p
    attend_held = dict(enumerate(attend_blocks[k] for k in range(tensor_count)))
    bits = axis_bits("tensor")
    for bit in bits[:-1]:
        for key in sorted((k for k in attend_held if not k & bit), reverse=True):
            attend_held[key] = attend_held[key] + swap(attend_held.pop(key ^ bit), "tensor", bit)
    emb_all, attend_held[bits[-1]] = lax.optimization_barrier((emb_all, attend_held[bits[-1]]))
    attend_grad = attend_held[0] + swap(attend_held[bits[-1]], "tensor", bits[-1])

    other_m, other_p = small_matrices(
        [gate_w_grad, up_w_grad, down_grad],
        [gate_up_error[0, :, 0], gate_up_error[0, :, 1], down_error[0]],
        factor_t[1:4],
    )
    other_sum = summed_all(jnp.concatenate([other_p[k] for k in range(3)], axis=1), "dp")
    cuts = [tiles * part // PARTS for part in range(PARTS + 1)]
    table_parts, table_sums = [], []
    for bounds in zip(cuts, cuts[1:]):
        found = table_matrix(
            bounds, starts, emb_all, sorted_ids, rows_all, dlogits, embed_error[0].T, factor_t[4]
        )
        table_parts.append(found)
        piece = found[2]
        if bounds[1] == tiles:
            piece = jnp.concatenate([piece, attend_p], axis=1)
        table_sums.append(summed_all(piece, "dp"))
    highs, lows = [part[0] for part in table_parts], [part[1] for part in table_parts]
    parts = [table_sums[-1][:, -attend_cols:], other_sum] + table_sums[:-1]
    parts.append(table_sums[-1][:, :-attend_cols])
    sums = jnp.concatenate(parts, axis=1)
    first_m = (attend_grad + attend_error[0])[None]
    spans, start = [], 0
    for size in (attend_cols, ff_own, ff_own, ff_own, tiles * TILE):
        spans.append((start, size))
        start += size
    bases_t = bases_of(sums, spans)
    small_basis = jnp.stack([bases_t[:, at : at + size] for at, size in spans[:4]])
    table_basis = bases_t[:, spans[4][0] :]
    other_back = small_backs(other_m, small_basis[1:])
    tab_back = table_back(highs, lows, table_basis)
    gain_terms = jnp.concatenate([gain_zero, gain_one, gain_two], axis=0)
    loss_terms = jnp.stack([masked_part, contrast_part])
    loss_row = jnp.zeros((1, width), WIDE).at[0, :2].set(loss_terms)
    packed = jnp.concatenate(
        [other_back.reshape(-1, width), tab_back, gain_terms, loss_row], axis=0
    )
    packed = summed_all(packed, "dp")
    first_back_t = small_backs(first_m, small_basis[:1])
    first_sum = summed_all(first_back_t[0], "dp")
    errors = small_errors(first_m, first_back_t, small_basis[:1]) + small_errors(
        other_m, other_back, small_basis[1:]
    )
    new_table_error = table_error(highs, lows, tab_back, table_basis, vocab_own).T
    own_t = jnp.concatenate([first_sum, packed[: 4 * RANK]], axis=0).reshape(5, RANK, width)
    square = jnp.sum(own_t * own_t)
    tail = packed[4 * RANK :].at[3, 2].set(square)
    shared = jnp.concatenate(
        [own_t[0], tail, jnp.pad(small_basis[0], ((0, 0), (0, width - attend_cols)))], axis=0
    )
    shared = picked_blocks(spread_blocks(shared, "tensor"), near)
    tail_sum = jnp.sum(shared[:, RANK : RANK + 4], axis=0)
    gains_grad = tail_sum[:3]
    loss_sums = tail_sum[3, :2]
    clip_norm = jnp.sqrt(tail_sum[3, 2] + jnp.sum(gains_grad * gains_grad))
    shrink = CLIP / jnp.maximum(clip_norm, CLIP)
    row_start = data_rank * row_count

    def rows_of(factor):
        return lax.dynamic_slice_in_dim(factor, row_start, row_count, factor.ndim - 1)

    reduced_attend = jnp.einsum(
        "tkd,tkn->dtn",
        rows_of(shared[:, :RANK]),
        shared[:, RANK + 4 :, :attend_cols],
        precision=HIGH,
    ).reshape(row_count, -1)
    own_rows_t = rows_of(own_t)

    def reduced(index, basis):
        return dot_in(own_rows_t[index], basis, ((0,), (0,)), precision=HIGH)

    reduced_gate_up = jnp.stack(
        [reduced(1, small_basis[1]), reduced(2, small_basis[2])], axis=1
    )
    reduced_down = reduced(3, small_basis[3])
    reduced_table = reduced(4, table_basis[:, :vocab_own])

    def advance(weight, moment, grad):
        fresh = MOMENTUM * moment + shrink * grad
        return (weight - LRATE * fresh, fresh)

    new_attend, new_attend_moment = advance(attend_weight, attend_moment, reduced_attend)
    new_gate_up, new_gate_up_moment = advance(gate_up, gate_up_moment, reduced_gate_up)
    new_down, new_down_moment = advance(down_weight, down_moment, reduced_down)
    new_table, new_table_moment = advance(embed_table, embed_moment, reduced_table)
    new_gains, new_gains_moment = advance(gains, gains_moment, gains_grad)
    return (
        new_attend,
        new_attend_moment,
        new_gate_up,
        new_gate_up_moment,
        new_down,
        new_down_moment,
        new_table,
        new_table_moment,
        new_gains,
        new_gains_moment,
        errors[0][None],
        jnp.stack([errors[1], errors[2]], axis=1)[None],
        errors[3][None],
        new_table_error[None],
        jnp.swapaxes(own_t, 1, 2),
        clip_norm,
        loss_sums[0],
        count,
        loss_sums[1],
    )


def solution(mesh):
    in_specs = (
        P("dp", None),
        P(),
        P(),
        P("dp", None, None),
        P(),
        P(),
        P(),
        P(),
        P("dp", None),
        P("dp", None),
        P("dp", None),
        P("dp", None, "tensor"),
        P("dp", None, "tensor"),
        P("dp", "tensor"),
        P("dp", "tensor"),
        P("dp", "tensor"),
        P("dp", "tensor"),
        P(),
        P(),
        P("dp", None, "tensor"),
        P("dp", None, None, "tensor"),
        P("dp", None, "tensor"),
        P("dp", None, "tensor"),
        P(None, None, "tensor"),
    )
    out_specs = (
        P("dp", None),
        P("dp", None),
        P("dp", None, "tensor"),
        P("dp", None, "tensor"),
        P("dp", "tensor"),
        P("dp", "tensor"),
        P("dp", "tensor"),
        P("dp", "tensor"),
        P(),
        P(),
        P("dp", None, "tensor"),
        P("dp", None, None, "tensor"),
        P("dp", None, "tensor"),
        P("dp", None, "tensor"),
        P(None, None, "tensor"),
        P(),
        P(),
        P(),
        P(),
    )
    return jax.shard_map(
        per_device, mesh=mesh, in_specs=in_specs, out_specs=out_specs, check_vma=False
    )
```

```python
import functools
import math

import jax
import jax.numpy as jnp
from jax import lax
from jax.experimental import pallas as pl
from jax.experimental.pallas import tpu as pltpu
from jax.sharding import PartitionSpec as P

HEADS = 12
HEAD_DIM = 64
RANK = 8
PAIR = 2 * HEAD_DIM
TILE = 640
WIDE_TILE = 1280
CHUNK = 256

EPS = 1e-05
ROPE_BASE = 1000.0
TAU = 0.02
LAMBDA = 1.0
CLIP = 0.02
LRATE = 5000.0
MOMENTUM = 0.9
WIDE = jnp.float32
NARROW = jnp.bfloat16
HIGH = lax.Precision.HIGHEST
NEGATIVE = -1e30


def params(mebibytes):
    return pltpu.CompilerParams(vmem_limit_bytes=mebibytes * 1024 * 1024)


def axis_bits(axis):
    size = lax.axis_size(axis)
    return [1 << place for place in range(size.bit_length() - 1)]


def swap(value, axis, bit):
    size = lax.axis_size(axis)
    return lax.ppermute(value, axis, [(index, index ^ bit) for index in range(size)])


def spread_blocks(value, axis):
    held = {0: value}
    for bit in reversed(axis_bits(axis)):
        for key in sorted(held):
            held[key ^ bit] = swap(held[key], axis, bit)
    return [held[key] for key in range(len(held))]


def summed_block(blocks, axis, kind):
    held = dict(enumerate(blocks))
    for bit in axis_bits(axis):
        for key in sorted((k for k in held if not k & bit), reverse=True):
            if key in held:
                got = swap(held.pop(key ^ bit).astype(kind), axis, bit)
                held[key] = held[key].astype(WIDE) + got.astype(WIDE)
    return held[0]


def summed_pair(blocks, axis):
    held = dict(enumerate(blocks))
    bits = axis_bits(axis)
    for bit in bits[:-1]:
        for key in sorted((k for k in held if not k & bit), reverse=True):
            if key in held:
                got = swap(held.pop(key ^ bit), axis, bit)
                held[key] = (held[key].astype(WIDE) + got.astype(WIDE)).astype(NARROW)
    if not bits:
        return held[0], jnp.zeros_like(held[0])
    return held[0], swap(held[bits[-1]], axis, bits[-1])


def summed_all(value, axis):
    for bit in axis_bits(axis):
        value = value + swap(value, axis, bit)
    return value


def picked_blocks(blocks, order):
    stacked = blocks if isinstance(blocks, jax.Array) else jnp.stack(blocks)
    return jnp.stack(
        [
            lax.dynamic_index_in_dim(stacked, order[k], 0, keepdims=False)
            for k in range(stacked.shape[0])
        ]
    )


def gathered_rows(value, axis):
    size = lax.axis_size(axis)
    if size > 8:
        return lax.all_gather(value, axis, axis=0, tiled=True)
    rank, rows = lax.axis_index(axis), value.shape[0]
    whole = jnp.zeros((size * rows,) + value.shape[1:], value.dtype)
    for key in range(size):
        part = value
        if key:
            part = lax.ppermute(value, axis, [(index, index ^ key) for index in range(size)])
        whole = lax.dynamic_update_slice_in_dim(whole, part, (rank ^ key) * rows, 0)
    return whole


def row_blocks(value, count):
    rows = value.shape[0] // count
    return [value[k * rows : (k + 1) * rows] for k in range(count)]


def layer_norm(values, gain):
    mean = jnp.mean(values, axis=-1, keepdims=True)
    centred = values - mean
    spread = jnp.mean(centred * centred, axis=-1, keepdims=True)
    return centred * lax.rsqrt(spread + EPS) * gain


def swiglu(gate, up):
    return jax.nn.silu(gate) * up


def dot_in(left, right, axes, precision=None):
    return lax.dot_general(
        left, right, (axes, ((), ())), precision=precision, preferred_element_type=WIDE
    )


def contract_rows(left, right):
    return dot_in(left, right, ((0,), (0,)))


def contract_cols(left, right):
    return dot_in(left, right, ((1,), (1,)))


def halves(value):
    high = value.astype(NARROW)
    return high, (value - high.astype(WIDE)).astype(NARROW)


def turn(piece, cosine, sine):
    lane = lax.broadcasted_iota(jnp.int32, piece.shape, 1) % HEAD_DIM
    half = HEAD_DIM // 2
    ahead = pltpu.roll(piece, PAIR - half, 1)
    behind = pltpu.roll(piece, half, 1)
    return piece * cosine + jnp.where(lane < half, -ahead, behind) * sine


def rotary_tables(places):
    half = HEAD_DIM // 2
    column = (jnp.arange(PAIR) % half).astype(WIDE)
    freq = ROPE_BASE ** (-2.0 * column / HEAD_DIM)
    angle = places.astype(WIDE)[:, None] * freq[None, :]
    return (jnp.cos(angle), jnp.sin(angle))


def project_kernel(count, x_ref, *refs):
    weights, (cos_ref, sin_ref), outs = refs[:count], refs[count : count + 2], refs[count + 2 :]
    x, cosine, sine = x_ref[...], cos_ref[...], sin_ref[...]
    for kind, (w_ref, out_ref) in enumerate(zip(weights, outs), 3 - count):
        for at in range(0, out_ref.shape[1], 2 * PAIR):
            flat = jnp.dot(x, w_ref[:, at : at + 2 * PAIR], preferred_element_type=WIDE)
            for start in range(0, 2 * PAIR, PAIR):
                piece = flat[:, start : start + PAIR]
                if kind < 2:
                    piece = turn(piece, cosine, sine)
                piece = piece.astype(NARROW)
                if kind == 0:
                    piece = (piece.astype(WIDE) * HEAD_DIM ** (-0.5)).astype(NARROW)
                out_ref[:, at + start : at + start + PAIR] = piece


def project(count, x, weight, cosine, sine):
    rows, width = x.shape
    still = lambda i: (0, 0)
    block = pl.BlockSpec((rows, width), still)
    lanes = pl.BlockSpec((rows, PAIR), still)
    return pl.pallas_call(
        functools.partial(project_kernel, count),
        grid=(1,),
        in_specs=[block]
        + [weight_block(width, width, kind) for kind in range(3 - count, 3)]
        + [lanes, lanes],
        out_specs=[block] * count,
        out_shape=[jax.ShapeDtypeStruct((rows, width), NARROW)] * count,
        compiler_params=params(20),
        cost_estimate=pl.CostEstimate(
            flops=2 * count * rows * width * width,
            bytes_accessed=2 * count * width * (rows + width),
            transcendentals=0,
        ),
    )(x, *[weight] * count, cosine, sine)


def turn_table_kernel(table_ref, out_ref):
    rows, columns = table_ref.shape
    empty = jnp.zeros((columns, out_ref.shape[1] - rows), WIDE)
    for at in range(0, columns, 128):
        size = min(128, columns - at)
        piece = table_ref[:, at : at + size].astype(NARROW).astype(WIDE).T
        if rows < out_ref.shape[1]:
            piece = jnp.concatenate([piece, empty[:size]], axis=1)
        out_ref[at : at + size, :] = piece
    out_ref[columns:, :] = jnp.zeros((out_ref.shape[0] - columns, out_ref.shape[1]), WIDE)


def turned_table(table):
    rows, columns = table.shape
    lanes = -(-rows // 128) * 128
    return whole_call(
        turn_table_kernel, [((columns // 8 * 8 + 8, lanes), WIDE)], 8 * table.size, table
    )[0]


def lookup_kernel(row_count, start_ref, ids_ref, table_ref, out_ref, held):
    groups, block = out_ref.shape[1] // row_count, out_ref.shape[0]
    start = start_ref[0]
    for group in range(groups):

        def move(at, carry):
            base = start + (group * block + at * 8)
            for place in range(8):
                index = ids_ref[base + place]
                held[at, place : place + 1, :] = table_ref[pl.ds(index, 1), :]
            return carry

        lax.fori_loop(0, block // 8, move, 0, unroll=8)
        rows = held[...].reshape(block, held.shape[2])[:, :row_count]
        out_ref[:, group * row_count : (group + 1) * row_count] = rows.astype(NARROW)


def lookup(ids, table, start, groups, block, row_count):
    return pl.pallas_call(
        functools.partial(lookup_kernel, row_count),
        in_specs=[
            pl.BlockSpec(memory_space=pltpu.SMEM),
            pl.BlockSpec(memory_space=pltpu.SMEM),
            pl.BlockSpec(memory_space=pltpu.VMEM),
        ],
        out_specs=pl.BlockSpec(memory_space=pltpu.VMEM),
        out_shape=jax.ShapeDtypeStruct((block, groups * row_count), NARROW),
        scratch_shapes=[pltpu.VMEM((block // 8, 8, table.shape[1]), WIDE)],
        compiler_params=params(10),
        cost_estimate=pl.CostEstimate(
            flops=groups * block * 4096, bytes_accessed=4 * table.size, transcendentals=0
        ),
    )(start, ids, table)


def norm_parts(values):
    mean = jnp.mean(values, axis=-1, keepdims=True)
    centred = values - mean
    scale = lax.rsqrt(jnp.mean(centred * centred, axis=-1, keepdims=True) + EPS)
    return centred * scale, scale


def norm_back(grad, values, gain):
    unit, scale = norm_parts(values)
    inner = grad * gain
    first = jnp.mean(inner, axis=-1, keepdims=True)
    second = jnp.mean(inner * unit, axis=-1, keepdims=True)
    return (inner - first - unit * second) * scale, jnp.sum(grad * unit, axis=0, keepdims=True)


def whole_call(kernel, outs, flops, *operands):
    moved = sum(operand.size * operand.dtype.itemsize for operand in operands)
    moved += sum(math.prod(shape) * jnp.dtype(kind).itemsize for shape, kind in outs)
    budget = 8 + moved * 2 // (1 << 20)
    return pl.pallas_call(
        kernel,
        out_shape=[jax.ShapeDtypeStruct(shape, kind) for shape, kind in outs],
        compiler_params=params(budget),
        cost_estimate=pl.CostEstimate(
            flops=flops,
            bytes_accessed=sum(4 * operand.size for operand in operands),
            transcendentals=0,
        ),
    )(*operands)


def norm_kernel(gain_ref, *refs):
    inputs, (out_ref, narrow_ref) = refs[:-2], refs[-2:]
    total = inputs[0][...].astype(WIDE)
    for ref in inputs[1:]:
        total = total + ref[...].astype(WIDE)
    out = norm_parts(total)[0] * gain_ref[...]
    out_ref[...] = out
    narrow_ref[...] = out.astype(NARROW)


def norm_forward(gain, *parts):
    shape = parts[0].shape
    return whole_call(norm_kernel, [(shape, WIDE), (shape, NARROW)], 20 * parts[0].size, gain, *parts)


def merge_kernel(attended_ref, weight_ref, x_ref, gain_ref, narrow_out, pre_ref, out_ref, out_b_ref):
    narrow = attended_ref[...].astype(NARROW)
    narrow_out[...] = narrow
    pre = x_ref[...] + contract_rows(narrow, weight_ref[...])
    pre_ref[...] = pre
    out = norm_parts(pre)[0] * gain_ref[...]
    out_ref[...] = out
    out_b_ref[...] = out.astype(NARROW)


def merge_branch(attended_t, weight, x_zero, gain):
    rows, width = x_zero.shape
    shape = (rows, width)
    return whole_call(
        merge_kernel,
        [((width, rows), NARROW), (shape, WIDE), (shape, WIDE), (shape, NARROW)],
        2 * rows * width * width,
        attended_t,
        weight,
        x_zero,
        gain,
    )


def last_kernel(length_ref, slots_ref, rows_ref, pooled_ref, hidden_ref, local_ref, got_ref, gain_ref, out_ref, narrow_ref, sum_ref):
    total = hidden_ref[...] + local_ref[...].astype(WIDE) + got_ref[...].astype(WIDE)
    spread = rows_ref[...]
    place = lax.broadcasted_iota(jnp.int32, (total.shape[0], slots_ref.shape[1]), 0)
    hot = (place == slots_ref[...]).astype(WIDE).astype(NARROW)
    high, low = halves(spread)
    grad = jnp.dot(hot, high, preferred_element_type=WIDE)
    grad = grad + jnp.dot(hot, low, preferred_element_type=WIDE)
    index = lax.broadcasted_iota(jnp.int32, (total.shape[0], 1), 0)
    grad = grad + jnp.where(index < length_ref[0], pooled_ref[...], 0.0)
    out, gain_grad = norm_back(grad, total, gain_ref[...])
    out_ref[...] = out
    narrow_ref[...] = out.astype(NARROW)
    sum_ref[...] = gain_grad


def last_back(length, slots, row_grad, pooled_grad, hidden_in, local, got, gain):
    shape = hidden_in.shape
    return pl.pallas_call(
        last_kernel,
        in_specs=[pl.BlockSpec(memory_space=pltpu.SMEM)]
        + [pl.BlockSpec(memory_space=pltpu.VMEM)] * 7,
        out_shape=[
            jax.ShapeDtypeStruct(shape, WIDE),
            jax.ShapeDtypeStruct(shape, NARROW),
            jax.ShapeDtypeStruct((1, shape[1]), WIDE),
        ],
        compiler_params=params(24),
        cost_estimate=pl.CostEstimate(
            flops=200 * hidden_in.size, bytes_accessed=20 * hidden_in.size, transcendentals=0
        ),
    )(length, slots, row_grad, pooled_grad, hidden_in, local, got, gain)


def branch_back_kernel(grad_ref, local_ref, got_ref, pre_ref, gain_ref, weight_ref, out_ref, narrow_ref, attended_ref, sum_ref):
    grad = grad_ref[...] + local_ref[...].astype(WIDE) + got_ref[...].astype(WIDE)
    out, gain_grad = norm_back(grad, pre_ref[...], gain_ref[...])
    narrow = out.astype(NARROW)
    out_ref[...] = out
    narrow_ref[...] = narrow
    sum_ref[...] = gain_grad
    attended_ref[...] = contract_cols(narrow, weight_ref[...]).astype(NARROW)


def branch_back(pre_grad, local, got, pre_one, gain, weight):
    rows, width = pre_grad.shape
    shape = (rows, width)
    return whole_call(
        branch_back_kernel,
        [(shape, WIDE), (shape, NARROW), (shape, NARROW), ((1, width), WIDE)],
        2 * rows * width * width,
        pre_grad,
        local,
        got,
        pre_one,
        gain,
        weight,
    )


def first_back_kernel(grad_ref, dq_ref, weight_ref, local_ref, got_ref, value_ref, gain_ref, out_ref, sum_ref):
    grad = grad_ref[...] + local_ref[...].astype(WIDE) + got_ref[...].astype(WIDE)
    grad = grad + contract_cols(dq_ref[...], weight_ref[...])
    out, gain_grad = norm_back(grad, value_ref[...].astype(WIDE), gain_ref[...])
    out_ref[...] = out.astype(NARROW)
    sum_ref[...] = gain_grad


def first_back(pre_one_grad, dq, weight, local, got, embedded, gain):
    rows, width = pre_one_grad.shape
    return whole_call(
        first_back_kernel,
        [((rows, width), NARROW), ((1, width), WIDE)],
        2 * rows * width * width,
        pre_one_grad,
        dq,
        weight,
        local,
        got,
        embedded,
        gain,
    )


def ffn_step(x_ref, weights, gate_out, up_out, act_ref, x_out, out_ref):
    gate_ref, up_ref, down_ref = weights
    x = x_ref[...]
    gate = jnp.dot(x, gate_ref[...], preferred_element_type=WIDE)
    up = jnp.dot(x, up_ref[...], preferred_element_type=WIDE)
    gate_out[...] = gate
    up_out[...] = up
    act = (gate / (1.0 + jnp.exp(-gate)) * up).astype(NARROW)
    act_ref[...] = act
    x_out[...] = x
    out_ref[...] = contract_cols(act, down_ref[...]).astype(NARROW)


def ffn_kernel(first_ref, second_ref, *refs):
    weights, kept, outs = refs[:3], refs[3:7], refs[7:]
    for step, x_ref in enumerate((first_ref, second_ref)):

        @pl.when(pl.program_id(0) == step)
        def _():
            ffn_step(x_ref, weights, *kept, outs[step])


def weight_block(width, hidden, index):
    return pl.BlockSpec((width, hidden), lambda i: (0, index))


def ffn_forward(first, second, weights, hidden):
    rows, width = first.shape
    whole = pl.BlockSpec((rows, width), lambda i: (0, 0))
    tall = lambda i: (i, 0)
    return pl.pallas_call(
        ffn_kernel,
        grid=(2,),
        in_specs=[whole, whole] + [weight_block(width, hidden, k) for k in range(1, 4)],
        out_specs=[pl.BlockSpec((rows, hidden), tall)] * 3
        + [pl.BlockSpec((rows, width), tall), whole, whole],
        out_shape=[
            jax.ShapeDtypeStruct((2 * rows, hidden), WIDE),
            jax.ShapeDtypeStruct((2 * rows, hidden), WIDE),
            jax.ShapeDtypeStruct((2 * rows, hidden), NARROW),
            jax.ShapeDtypeStruct((2 * rows, width), NARROW),
            jax.ShapeDtypeStruct((rows, width), NARROW),
            jax.ShapeDtypeStruct((rows, width), NARROW),
        ],
        compiler_params=params(32),
        cost_estimate=pl.CostEstimate(
            flops=12 * rows * width * hidden,
            bytes_accessed=28 * rows * width + 6 * width * hidden,
            transcendentals=2 * rows * hidden,
        ),
    )(first, second, weights, weights, weights)


def ffn_back_step(grad_ref, gate_in, up_in, weights, dgate_ref, dup_ref, grad_out, out_ref):
    gate_ref, up_ref, down_ref = weights
    grad = grad_ref[...]
    grad_out[...] = grad
    act_grad = jnp.dot(grad, down_ref[...], preferred_element_type=WIDE)
    gate, up = gate_in[...], up_in[...]
    share = 1.0 / (1.0 + jnp.exp(-gate))
    dgate = (act_grad * up * (share * (1.0 + gate * (1.0 - share)))).astype(NARROW)
    dup = (act_grad * (gate * share)).astype(NARROW)
    dgate_ref[...] = dgate
    dup_ref[...] = dup
    out_ref[...] = (
        contract_cols(dgate, gate_ref[...]) + contract_cols(dup, up_ref[...])
    ).astype(NARROW)


def ffn_back_kernel(first_ref, second_ref, gate_in, up_in, *refs):
    weights, kept, outs = refs[:3], refs[3:6], refs[6:]
    for step, grad_ref in enumerate((first_ref, second_ref)):

        @pl.when(pl.program_id(0) == step)
        def _():
            ffn_back_step(grad_ref, gate_in, up_in, weights, *kept, outs[step])


def ffn_backward(first, second, gate, up, weights):
    rows, width = first.shape
    hidden = gate.shape[1]
    whole = pl.BlockSpec((rows, width), lambda i: (0, 0))
    tall = lambda i: (i, 0)
    return pl.pallas_call(
        ffn_back_kernel,
        grid=(2,),
        in_specs=[whole, whole]
        + [pl.BlockSpec((rows, hidden), tall)] * 2
        + [weight_block(width, hidden, k) for k in range(1, 4)],
        out_specs=[pl.BlockSpec((rows, hidden), tall)] * 2
        + [pl.BlockSpec((rows, width), tall), whole, whole],
        out_shape=[
            jax.ShapeDtypeStruct((2 * rows, hidden), NARROW),
            jax.ShapeDtypeStruct((2 * rows, hidden), NARROW),
            jax.ShapeDtypeStruct((2 * rows, width), NARROW),
            jax.ShapeDtypeStruct((rows, width), NARROW),
            jax.ShapeDtypeStruct((rows, width), NARROW),
        ],
        compiler_params=params(34),
        cost_estimate=pl.CostEstimate(
            flops=12 * rows * width * hidden,
            bytes_accessed=32 * rows * width + 6 * width * hidden,
            transcendentals=2 * rows * hidden,
        ),
    )(first, second, gate, up, weights, weights, weights)


def input_kernel(first_k, first_v, second_k, second_v, key_ref, value_ref, *outs):
    for dk_ref, dv_ref, out_ref in zip((first_k, second_k), (first_v, second_v), outs):
        total = contract_cols(dk_ref[...], key_ref[...])
        total = total + contract_cols(dv_ref[...], value_ref[...])
        out_ref[...] = total.astype(NARROW)


def input_grads(first_k, first_v, second_k, second_v, weights):
    rows, width = first_k.shape
    whole = pl.BlockSpec((rows, width), lambda i: (0, 0))
    return pl.pallas_call(
        input_kernel,
        grid=(1,),
        in_specs=[whole] * 4 + [weight_block(width, width, k) for k in (1, 2)],
        out_specs=[whole] * 2,
        out_shape=[jax.ShapeDtypeStruct((rows, width), NARROW)] * 2,
        compiler_params=params(24),
        cost_estimate=pl.CostEstimate(
            flops=8 * rows * width * width,
            bytes_accessed=12 * rows * width + 4 * width * width,
            transcendentals=0,
        ),
    )(first_k, first_v, second_k, second_v, weights, weights)


def paired(value, work):
    near_bit, *far_bits = axis_bits("tensor")
    held = {0: value}
    for bit in reversed(far_bits):
        for key in sorted(held):
            held[key ^ bit] = swap(held[key], "tensor", bit)
    results, sums = [], {}
    for key in sorted(held):
        block = held[key]
        if results:
            block, _ = lax.optimization_barrier((block, results[-1][-1]))
        results.append(work(len(results), block, swap(block, "tensor", near_bit)))
        sums[key] = near_sum(*results[-1][-2:])
    return results, sums


def near_sum(own, other):
    got = swap(other, "tensor", axis_bits("tensor")[0])
    return (own.astype(WIDE) + got.astype(WIDE)).astype(NARROW)


def far_sum(sums):
    sums = dict(sums)
    near_bit, *far_bits = axis_bits("tensor")
    for bit in far_bits[:-1]:
        for key in sorted(k for k in sums if not k & bit):
            got = swap(sums.pop(key ^ bit), "tensor", bit)
            sums[key] = (sums[key].astype(WIDE) + got.astype(WIDE)).astype(NARROW)
    return sums[0], sums[far_bits[-1]], swap(sums[far_bits[-1]], "tensor", far_bits[-1])


def logits_kernel(columns, tile, rows_ref, table_ref, targets_ref, out_ref, stats_ref, top_ref, sum_ref, hit_ref):
    step = pl.program_id(0)

    @pl.when(step == 0)
    def _():
        top_ref[...] = jnp.full(top_ref.shape, NEGATIVE, WIDE)
        sum_ref[...] = jnp.zeros(sum_ref.shape, WIDE)
        hit_ref[...] = jnp.zeros(hit_ref.shape, WIDE)

    logits = jnp.dot(rows_ref[...], table_ref[...], preferred_element_type=WIDE)
    out_ref[...] = logits
    place = step * tile + lax.broadcasted_iota(jnp.int32, (1, tile), 1)
    seen = jnp.where(place < columns, logits, NEGATIVE)
    hits = jnp.where((place == targets_ref[...]) & (place < columns), seen, 0.0)
    pieces = [slice(at, at + 128) for at in range(0, tile, 128)]
    before = top_ref[...]
    top = before
    for piece in pieces:
        top = jnp.maximum(top, seen[:, piece])
    total = sum_ref[...] * jnp.exp(before - top)
    hit = hit_ref[...]
    for piece in pieces:
        total = total + jnp.exp(seen[:, piece] - top)
        hit = hit + hits[:, piece]
    top_ref[...] = top
    sum_ref[...] = total
    hit_ref[...] = hit

    @pl.when(step == pl.num_programs(0) - 1)
    def _():
        peak = jnp.max(top, axis=1, keepdims=True)
        whole = jnp.sum(total * jnp.exp(top - peak), axis=1, keepdims=True)
        found = jnp.sum(hit, axis=1, keepdims=True)
        lane = lax.broadcasted_iota(jnp.int32, (1, 128), 1)
        stats_ref[...] = jnp.where(
            lane == 0, peak, jnp.where(lane == 1, whole, jnp.where(lane == 2, found, 0.0))
        )


def vocab_logits(rows_all, table, targets):
    picks, width = rows_all.shape
    columns = table.shape[1]
    tiles = -(-columns // TILE)
    tile = WIDE_TILE
    still = lambda j: (0, 0)
    along = lambda j: (0, j)
    return pl.pallas_call(
        functools.partial(logits_kernel, columns, tile),
        grid=(tiles * TILE // tile,),
        in_specs=[
            pl.BlockSpec((picks, width), still),
            pl.BlockSpec((width, tile), along),
            pl.BlockSpec((picks, 1), still),
        ],
        out_specs=[pl.BlockSpec((picks, tile), along), pl.BlockSpec((picks, 128), still)],
        out_shape=[
            jax.ShapeDtypeStruct((picks, tiles * TILE), WIDE),
            jax.ShapeDtypeStruct((picks, 128), WIDE),
        ],
        scratch_shapes=[pltpu.VMEM((picks, 128), WIDE)] * 3,
        compiler_params=params(14),
        cost_estimate=pl.CostEstimate(
            flops=2 * picks * width * columns,
            bytes_accessed=2 * width * columns,
            transcendentals=picks * columns,
        ),
    )(rows_all, table, targets)


def combine_kernel(count, slots, bit, mine_ref, other_ref, out_ref):
    lane = lax.broadcasted_iota(jnp.int32, (1, 128), 1)
    for block in range(count):
        mine = mine_ref[block * slots : (block + 1) * slots, :]
        other = other_ref[(block ^ bit) * slots : ((block ^ bit) + 1) * slots, :]
        peak = jnp.maximum(mine[:, :1], other[:, :1])
        total = mine[:, 1:2] * jnp.exp(mine[:, :1] - peak)
        total = total + other[:, 1:2] * jnp.exp(other[:, :1] - peak)
        out_ref[block * slots : (block + 1) * slots, :] = jnp.where(
            lane == 0, peak, jnp.where(lane == 1, total, mine + other)
        )
    rest = count * slots
    out_ref[rest:, :] = mine_ref[rest:, :] + other_ref[rest:, :]


def dlogits_kernel(columns, tile, logits_ref, table_ref, targets_ref, stats_ref, weight_ref, out_ref, grad_ref):
    step = pl.program_id(0)
    log_all = stats_ref[:, :1] + jnp.log(stats_ref[:, 1:2])
    place = step * tile + lax.broadcasted_iota(jnp.int32, (1, tile), 1)
    share = jnp.exp(logits_ref[...] - log_all) - jnp.where(place == targets_ref[...], 1.0, 0.0)
    grad = jnp.where(place < columns, share * weight_ref[...], 0.0).astype(NARROW)
    out_ref[...] = grad
    column = step * tile + lax.broadcasted_iota(jnp.int32, (1, tile), 1)
    table = jnp.where(column < columns, table_ref[...].astype(WIDE), 0.0).astype(NARROW)
    part = contract_cols(grad, table)

    @pl.when(step == 0)
    def _():
        grad_ref[...] = part

    @pl.when(step > 0)
    def _():
        grad_ref[...] += part


def vocab_back(logits, table, targets, stats, weight):
    picks = targets.shape[0]
    width, columns = table.shape
    tile = WIDE_TILE
    still = lambda j: (0, 0)
    along = lambda j: (0, j)
    return pl.pallas_call(
        functools.partial(dlogits_kernel, columns, tile),
        grid=(logits.shape[1] // tile,),
        in_specs=[
            pl.BlockSpec((picks, tile), along),
            pl.BlockSpec((width, tile), along),
            pl.BlockSpec((picks, 1), still),
            pl.BlockSpec((picks, 128), still),
            pl.BlockSpec((picks, 1), still),
        ],
        out_specs=[pl.BlockSpec((picks, tile), along), pl.BlockSpec((picks, width), still)],
        out_shape=[
            jax.ShapeDtypeStruct(logits.shape, NARROW),
            jax.ShapeDtypeStruct((picks, width), WIDE),
        ],
        compiler_params=params(14),
        cost_estimate=pl.CostEstimate(
            flops=2 * picks * width * columns,
            bytes_accessed=2 * width * columns,
            transcendentals=picks * columns,
        ),
    )(logits, table, targets, stats, weight)


def contrast_kernel(weight, length_ref, pooled_ref, keys_ref, blocked_ref, target_ref, grad_ref, part_ref):
    length = length_ref[0].astype(WIDE)
    pooled = pooled_ref[...] / length
    scale = lax.rsqrt(jnp.sum(pooled * pooled, axis=-1, keepdims=True) + EPS)
    narrow = jnp.broadcast_to(pooled * scale, (8, pooled.shape[1])).astype(NARROW)
    keys = keys_ref[...]
    scores = contract_cols(narrow, keys)[:1] / TAU
    target = target_ref[...]
    masked = jnp.where(blocked_ref[...] > 0.0, NEGATIVE, scores)
    top = jnp.max(masked, axis=-1, keepdims=True)
    log_c = top + jnp.log(jnp.sum(jnp.exp(masked - top), axis=-1, keepdims=True))
    chosen = jnp.sum(jnp.where(target > 0.0, scores, 0.0), axis=-1, keepdims=True)
    part_ref[...] = jnp.broadcast_to((log_c - chosen) * weight, part_ref.shape)
    dscores = ((jnp.exp(masked - log_c) - target) * (weight / TAU)).astype(NARROW)
    dscores = jnp.broadcast_to(dscores.astype(WIDE), (8, dscores.shape[1])).astype(NARROW)
    grad = jnp.dot(dscores, keys, preferred_element_type=WIDE)[:1]
    inner = jnp.sum(pooled * grad, axis=-1, keepdims=True)
    grad_ref[...] = (grad - pooled * (inner * scale * scale)) * scale / length


def contrast(weight, length, pooled_sum, keys_hat, blocked, target):
    width = pooled_sum.shape[1]
    return pl.pallas_call(
        functools.partial(contrast_kernel, weight),
        in_specs=[pl.BlockSpec(memory_space=pltpu.SMEM)]
        + [pl.BlockSpec(memory_space=pltpu.VMEM)] * 4,
        out_shape=[
            jax.ShapeDtypeStruct((1, width), WIDE),
            jax.ShapeDtypeStruct((1, 128), WIDE),
        ],
        compiler_params=params(8),
        cost_estimate=pl.CostEstimate(
            flops=4 * keys_hat.size, bytes_accessed=2 * keys_hat.size, transcendentals=0
        ),
    )(length, pooled_sum, keys_hat, blocked, target)


def head_lanes(head):
    lane = lax.broadcasted_iota(jnp.int32, (1, PAIR), 1)
    return (lane // HEAD_DIM) == head, lane == HEAD_DIM * (1 - head)


def attend_kernel(count, q_ref, *refs):
    k_refs, v_refs, bias_refs = refs[:count], refs[count : 2 * count], refs[2 * count : 3 * count]
    out_ref, log_ref, s_ref = refs[3 * count :]
    head = pl.program_id(1)
    mine, spare = head_lanes(head)
    step = k_refs[0].shape[0]
    blocks = [pl.ds(k * step, step) for k in range(count)]
    query = jnp.where(spare, 1.0, jnp.where(mine, q_ref[...].astype(WIDE), 0.0)).astype(NARROW)
    top = None
    for rows, k_ref, bias_ref in zip(blocks, k_refs, bias_refs):
        key = jnp.where(spare, bias_ref[...].astype(WIDE), k_ref[...].astype(WIDE))
        scores = contract_cols(key.astype(NARROW), query)
        s_ref[rows, :] = scores
        peak = jnp.max(scores, axis=0, keepdims=True)
        top = peak if top is None else jnp.maximum(top, peak)
    total = None
    for rows in blocks:
        powers = jnp.exp(s_ref[rows, :] - top)
        s_ref[rows, :] = powers
        part = jnp.sum(powers, axis=0, keepdims=True)
        total = part if total is None else total + part
    share = 1.0 / total
    result = None
    for rows, v_ref in zip(blocks, v_refs):
        probs = (s_ref[rows, :] * share).astype(NARROW)
        part = contract_rows(v_ref[...], probs)
        result = part if result is None else result + part
    log_ref[0, pl.ds(head, 1), :] = top + jnp.log(total)

    @pl.when(head == 0)
    def _():
        out_ref[...] = result

    @pl.when(head == 1)
    def _():
        out_ref[HEAD_DIM:, :] = result[HEAD_DIM:, :]


def attention_forward(queries, keys, values, biases):
    rows, width = queries.shape
    count = len(keys)
    length = rows * count
    pairs = width // PAIR
    lanes = pl.BlockSpec((rows, PAIR), lambda i, h: (0, i))
    still = pl.BlockSpec((rows, PAIR), lambda i, h: (0, 0))
    return pl.pallas_call(
        functools.partial(attend_kernel, count),
        grid=(pairs, 2),
        in_specs=[lanes] * (1 + 2 * count) + [still] * count,
        out_specs=[
            pl.BlockSpec((PAIR, rows), lambda i, h: (i, 0)),
            pl.BlockSpec((1, 2, rows), lambda i, h: (i, 0, 0)),
        ],
        out_shape=[
            jax.ShapeDtypeStruct((width, rows), WIDE),
            jax.ShapeDtypeStruct((pairs, 2, rows), WIDE),
        ],
        scratch_shapes=[pltpu.VMEM((length, rows), WIDE)],
        compiler_params=params(22),
        cost_estimate=pl.CostEstimate(
            flops=4 * rows * length * width,
            bytes_accessed=4 * length * width + 8 * rows * width,
            transcendentals=rows * length * HEADS,
        ),
    )(queries, *keys, *values, *biases)


def attend_back_kernel(count, q_ref, grad_ref, out_ref, log_ref, *refs):
    groups = [refs[k * count : (k + 1) * count] for k in range(5)]
    k_refs, v_refs, bias_refs, cos_refs, sin_refs = groups
    rest = refs[5 * count :]
    dq_ref, dk_refs, dv_refs = rest[0], rest[1 : 1 + count], rest[1 + count : 1 + 2 * count]
    dk_sum, dv_sum, dq_sum = rest[1 + 2 * count :]
    head = pl.program_id(1)
    mine, spare = head_lanes(head)
    step, scale = k_refs[0].shape[0], HEAD_DIM ** (-0.5)
    own = jnp.where(mine, q_ref[...].astype(WIDE), 0.0)
    query = own.astype(NARROW)
    asked = jnp.where(spare, 1.0, own).astype(NARROW)
    grad_wide = jnp.where(mine, grad_ref[...].astype(WIDE), 0.0)
    grad = grad_wide.astype(NARROW)
    delta = jnp.sum(grad_wide.T * out_ref[...], axis=0, keepdims=True)
    log_total = log_ref[0, pl.ds(head, 1), :]
    dq = None
    for k in range(count):
        rows = pl.ds(k * step, step)
        key_block = k_refs[k][...]
        key = jnp.where(spare, bias_refs[k][...].astype(WIDE), key_block.astype(WIDE))
        scores = contract_cols(key.astype(NARROW), asked)
        probs = jnp.exp(scores - log_total)
        dprobs = contract_cols(v_refs[k][...], grad)
        dv = jnp.dot(probs.astype(NARROW), grad, preferred_element_type=WIDE)
        dscores = (probs * (dprobs - delta)).astype(NARROW)
        dk = jnp.dot(dscores, query, preferred_element_type=WIDE)
        part = contract_rows(key_block, dscores)
        dq = part if dq is None else dq + part

        @pl.when(head == 0)
        def _():
            dk_sum[rows, :] = dk
            dv_sum[rows, :] = dv

        @pl.when(head == 1)
        def _():
            total = dk_sum[rows, :] + dk
            dk_refs[k][...] = turn(total, cos_refs[k][...], -sin_refs[k][...]).astype(NARROW)
            dv_refs[k][...] = (dv_sum[rows, :] + dv).astype(NARROW)

    @pl.when(head == 0)
    def _():
        dq_sum[...] = dq

    @pl.when(head == 1)
    def _():
        dq_sum[HEAD_DIM:, :] = dq[HEAD_DIM:, :]
        total = dq_sum[...].T * scale
        dq_ref[...] = turn(total, cos_refs[0][...], -sin_refs[0][...]).astype(NARROW)


def attention_backward(queries, keys, values, biases, grad, out_t, log_total, cosines, sines):
    rows, width = queries.shape
    count = len(keys)
    length = rows * count
    pairs = width // PAIR
    lanes = pl.BlockSpec((rows, PAIR), lambda i, h: (0, i))
    still = pl.BlockSpec((rows, PAIR), lambda i, h: (0, 0))
    found = pl.pallas_call(
        functools.partial(attend_back_kernel, count),
        grid=(pairs, 2),
        in_specs=[
            lanes,
            lanes,
            pl.BlockSpec((PAIR, rows), lambda i, h: (i, 0)),
            pl.BlockSpec((1, 2, rows), lambda i, h: (i, 0, 0)),
        ]
        + [lanes] * (2 * count)
        + [still] * (3 * count),
        out_specs=[lanes] * (1 + 2 * count),
        out_shape=[jax.ShapeDtypeStruct((rows, width), NARROW)] * (1 + 2 * count),
        scratch_shapes=[
            pltpu.VMEM((length, PAIR), WIDE),
            pltpu.VMEM((length, PAIR), WIDE),
            pltpu.VMEM((PAIR, rows), WIDE),
        ],
        compiler_params=params(24),
        cost_estimate=pl.CostEstimate(
            flops=10 * rows * length * width,
            bytes_accessed=8 * length * width + 8 * rows * width,
            transcendentals=rows * length * HEADS,
        ),
    )(queries, grad, out_t, log_total, *keys, *values, *biases, *cosines, *sines)
    return found[0], found[1 : 1 + count], found[1 + count :]


def project_down(matrix, factor_t):
    high, low = halves(matrix)
    factor_high, factor_low = halves(factor_t)
    both = jnp.concatenate([factor_high, factor_low], axis=0)
    first = jnp.dot(both, high, preferred_element_type=WIDE)
    second = jnp.dot(factor_high, low, preferred_element_type=WIDE)
    return first[:RANK] + first[RANK:] + second


def project_back(matrix, basis_t):
    high, low = halves(matrix)
    basis_high, basis_low = halves(basis_t)
    both = jnp.concatenate([basis_high, basis_low], axis=0)
    first = contract_cols(both, high)
    second = contract_cols(basis_high, low)
    return first[:RANK] + first[RANK:] + second


def expand(back_t, basis_t):
    back_high, back_low = halves(back_t)
    basis_high, basis_low = halves(basis_t)
    left = jnp.concatenate([back_high, back_low, back_high], axis=0)
    right = jnp.concatenate([basis_high, basis_high, basis_low], axis=0)
    return contract_rows(left, right)


def table_kernel(columns, first, starts_ref, left_ref, tokens_ref, rows_ref, dlogits_ref, error_ref, factor_ref, high_ref, low_ref, p_ref, sum_ref):
    tile = first + pl.program_id(0)
    place = tile * TILE + lax.broadcasted_iota(jnp.int32, (TILE, 1), 0)
    sum_ref[...] = error_ref[...] + contract_rows(dlogits_ref[...], rows_ref[...])

    def visit(chunk, carry):
        at = pl.ds(pl.multiple_of(chunk * CHUNK, CHUNK), CHUNK)
        hot = jnp.where(tokens_ref[:, at] == place, 1.0, 0.0).astype(NARROW)
        sum_ref[...] += jnp.dot(hot, left_ref[at, :], preferred_element_type=WIDE)
        return carry

    lax.fori_loop(
        starts_ref[tile] // CHUNK, (starts_ref[tile + 1] + CHUNK - 1) // CHUNK, visit, 0
    )
    total = jnp.where(place < columns, sum_ref[...], 0.0)
    high, low = halves(total)
    high_ref[...] = high
    low_ref[...] = low
    factor_high, factor_low = halves(factor_ref[...])
    both = jnp.concatenate([factor_high, factor_low], axis=0)
    found = contract_cols(high, both).T
    rest = contract_cols(low, both).T
    p_ref[...] = found[:RANK] + found[RANK:] + rest[:RANK]


def table_matrix(bounds, starts, left, tokens, rows, dlogits, error, factor_t):
    columns, width = error.shape
    slots = left.shape[0]
    picks = rows.shape[0]
    first, tiles = bounds[0], bounds[1] - bounds[0]
    still = lambda j: (0, 0)
    down = lambda j: (j, 0)
    return pl.pallas_call(
        functools.partial(table_kernel, columns, first),
        grid=(tiles,),
        in_specs=[
            pl.BlockSpec(memory_space=pltpu.SMEM),
            pl.BlockSpec((slots, width), still),
            pl.BlockSpec((1, slots), still),
            pl.BlockSpec((picks, width), still),
            pl.BlockSpec((picks, TILE), lambda j: (0, first + j)),
            pl.BlockSpec((TILE, width), lambda j: (first + j, 0)),
            pl.BlockSpec((RANK, width), still),
        ],
        out_specs=[
            pl.BlockSpec((TILE, width), down),
            pl.BlockSpec((TILE, width), down),
            pl.BlockSpec((RANK, TILE), lambda j: (0, j)),
        ],
        out_shape=[
            jax.ShapeDtypeStruct((tiles * TILE, width), NARROW),
            jax.ShapeDtypeStruct((tiles * TILE, width), NARROW),
            jax.ShapeDtypeStruct((RANK, tiles * TILE), WIDE),
        ],
        scratch_shapes=[pltpu.VMEM((TILE, width), WIDE)],
        compiler_params=params(32),
        cost_estimate=pl.CostEstimate(
            flops=2 * width * tiles * TILE * (slots // 4 + picks + 24),
            bytes_accessed=8 * width * tiles * TILE,
            transcendentals=0,
        ),
    )(starts, left, tokens, rows, dlogits, error, factor_t)


def partial_kernel(*refs):
    count = (len(refs) - 1) // 2
    for index in range(count):
        refs[-1][index] = project_down(refs[index][...], refs[count + index][...])


def partial_projections(matrices, factors_t):
    count, (width, columns) = len(matrices), matrices[0].shape
    return whole_call(
        partial_kernel,
        [((count, RANK, columns), WIDE)],
        48 * count * width * columns,
        *matrices,
        *factors_t,
    )[0]


def small_kernel(count, *refs):
    grads, errors, factor_ref = refs[:count], refs[count : 2 * count], refs[2 * count]
    m_ref, p_ref = refs[2 * count + 1 :]
    for index in range(count):
        total = grads[index][...] + errors[index][...]
        m_ref[index] = total
        p_ref[index] = project_down(total, factor_ref[index])


def small_matrices(grads, errors, factor_t):
    count, (width, columns) = len(grads), grads[0].shape
    return pl.pallas_call(
        functools.partial(small_kernel, count),
        out_shape=[
            jax.ShapeDtypeStruct((count, width, columns), WIDE),
            jax.ShapeDtypeStruct((count, RANK, columns), WIDE),
        ],
        compiler_params=params(36),
        cost_estimate=pl.CostEstimate(
            flops=48 * count * width * columns,
            bytes_accessed=12 * count * width * columns,
            transcendentals=0,
        ),
    )(*grads, *errors, factor_t)


def basis_kernel(spans, p_ref, out_ref):
    index = lax.broadcasted_iota(jnp.int32, (RANK, 1), 0)
    for start, size in spans:
        rows = p_ref[:, pl.ds(start, size)]
        for place in range(RANK):
            row = rows[place : place + 1, :]
            row = row * lax.rsqrt(jnp.sum(row * row, axis=1, keepdims=True))
            inner = jnp.sum(rows * row, axis=1, keepdims=True)
            rows = jnp.where(index == place, row, rows - jnp.where(index > place, inner, 0.0) * row)
        out_ref[:, pl.ds(start, size)] = rows


def bases_of(sums, spans):
    return pl.pallas_call(
        functools.partial(basis_kernel, spans),
        out_shape=jax.ShapeDtypeStruct(sums.shape, WIDE),
        compiler_params=params(8),
        cost_estimate=pl.CostEstimate(
            flops=64 * sums.size, bytes_accessed=8 * sums.size, transcendentals=40
        ),
    )(sums)


def small_back_kernel(m_ref, basis_ref, back_ref):
    for index in range(m_ref.shape[0]):
        back_ref[index] = project_back(m_ref[index], basis_ref[index])


def small_backs(matrices, basis):
    count, width, columns = matrices.shape
    return pl.pallas_call(
        small_back_kernel,
        out_shape=jax.ShapeDtypeStruct((count, RANK, width), WIDE),
        compiler_params=params(24),
        cost_estimate=pl.CostEstimate(
            flops=48 * count * width * columns,
            bytes_accessed=4 * count * width * columns,
            transcendentals=0,
        ),
    )(matrices, basis)


def table_specs(parts, width):
    bounds, first = [], 0
    for part in parts:
        bounds.append((first, first + part.shape[0] // TILE))
        first = bounds[-1][1]
    specs = [
        pl.BlockSpec(
            (TILE, width), lambda j, low=low, high=high: (jnp.clip(j, low, high - 1) - low, 0)
        )
        for low, high in bounds
    ]
    return bounds, specs


def table_back_kernel(bounds, *refs):
    highs, lows = refs[: len(bounds)], refs[len(bounds) : 2 * len(bounds)]
    basis_ref, back_ref = refs[2 * len(bounds) :]
    step = pl.program_id(0)
    basis_high, basis_low = halves(basis_ref[...])
    both = jnp.concatenate([basis_high, basis_low], axis=0)

    @pl.when(step == 0)
    def _():
        back_ref[...] = jnp.zeros(back_ref.shape, WIDE)

    for (low, high), high_ref, low_ref in zip(bounds, highs, lows):

        @pl.when((step >= low) & (step < high))
        def _():
            first = jnp.dot(both, high_ref[...], preferred_element_type=WIDE)
            second = jnp.dot(basis_high, low_ref[...], preferred_element_type=WIDE)
            back_ref[...] += first[:RANK] + first[RANK:] + second


def table_back(highs, lows, basis):
    width = highs[0].shape[1]
    columns = basis.shape[1]
    bounds, specs = table_specs(highs, width)
    return pl.pallas_call(
        functools.partial(table_back_kernel, bounds),
        grid=(columns // TILE,),
        in_specs=specs + specs + [pl.BlockSpec((RANK, TILE), lambda j: (0, j))],
        out_specs=pl.BlockSpec((RANK, width), lambda j: (0, 0)),
        out_shape=jax.ShapeDtypeStruct((RANK, width), WIDE),
        compiler_params=params(18),
        cost_estimate=pl.CostEstimate(
            flops=48 * width * columns, bytes_accessed=4 * width * columns, transcendentals=0
        ),
    )(*highs, *lows, basis)


def small_error_kernel(m_ref, back_ref, basis_ref, *out_refs):
    for index, out_ref in enumerate(out_refs):
        out_ref[...] = m_ref[index] - expand(back_ref[index], basis_ref[index])


def small_errors(matrices, backs, basis):
    count, width, columns = matrices.shape
    return pl.pallas_call(
        small_error_kernel,
        out_shape=[jax.ShapeDtypeStruct((width, columns), WIDE)] * count,
        compiler_params=params(32),
        cost_estimate=pl.CostEstimate(
            flops=48 * count * width * columns,
            bytes_accessed=8 * count * width * columns,
            transcendentals=0,
        ),
    )(matrices, backs, basis)


def table_error_kernel(bounds, *refs):
    highs, lows = refs[: len(bounds)], refs[len(bounds) : 2 * len(bounds)]
    back_ref, basis_ref, out_ref = refs[2 * len(bounds) :]
    step = pl.program_id(0)
    for (low, high), high_ref, low_ref in zip(bounds, highs, lows):

        @pl.when((step >= low) & (step < high))
        def _():
            whole = high_ref[...].astype(WIDE) + low_ref[...].astype(WIDE)
            out_ref[...] = whole - expand(basis_ref[...], back_ref[...])


def table_error(highs, lows, back, basis, columns):
    width = highs[0].shape[1]
    bounds, specs = table_specs(highs, width)
    return pl.pallas_call(
        functools.partial(table_error_kernel, bounds),
        grid=(basis.shape[1] // TILE,),
        in_specs=specs
        + specs
        + [
            pl.BlockSpec((RANK, width), lambda j: (0, 0)),
            pl.BlockSpec((RANK, TILE), lambda j: (0, j)),
        ],
        out_specs=pl.BlockSpec((TILE, width), lambda j: (j, 0)),
        out_shape=jax.ShapeDtypeStruct((columns, width), WIDE),
        compiler_params=params(24),
        cost_estimate=pl.CostEstimate(
            flops=48 * width * columns, bytes_accessed=8 * width * columns, transcendentals=0
        ),
    )(*highs, *lows, back, basis)


def normalize_keys(raw_keys):
    wide_keys = raw_keys.astype(WIDE)
    return (
        wide_keys * lax.rsqrt(jnp.sum(wide_keys * wide_keys, axis=-1, keepdims=True) + EPS)
    ).astype(NARROW)


def per_device(
    token_ids,
    seq_lengths,
    mask_slots,
    mask_targets,
    positive_rows,
    doc_ids,
    false_pairs,
    queue_docs,
    queue_embed,
    attend_weight,
    attend_moment,
    gate_up,
    gate_up_moment,
    down_weight,
    down_moment,
    embed_table,
    embed_moment,
    gains,
    gains_moment,
    attend_error,
    gate_up_error,
    down_error,
    embed_error,
    factors,
):
    tensor_count = lax.axis_size("tensor")
    tensor_rank = lax.axis_index("tensor")
    data_count = lax.axis_size("dp")
    data_rank = lax.axis_index("dp")
    groups, seq_len = token_ids.shape
    width = gains.shape[1]
    total_rows = groups * seq_len
    own_rows = total_rows // tensor_count
    slot_count = mask_slots.shape[2]
    seq_total = groups * data_count
    near = jnp.arange(tensor_count) ^ tensor_rank
    row_count = attend_weight.shape[0]

    tokens_all = lax.all_to_all(
        jnp.broadcast_to(token_ids, (data_count, seq_len)), "dp", 0, 0, tiled=True
    )
    vocab_own = embed_table.shape[1]
    vocab_start = tensor_rank * vocab_own
    ids = tokens_all - vocab_start
    ids = jnp.where((ids >= 0) & (ids < vocab_own), ids, vocab_own)
    table_local = embed_table.astype(NARROW)
    table_rows = turned_table(embed_table)
    ids = jnp.swapaxes(ids.reshape(data_count, tensor_count, own_rows), 0, 1).reshape(-1)
    looked, looked_sums = {}, {}
    for key in reversed(range(tensor_count)):
        start = ((tensor_rank ^ key) * (data_count * own_rows)).reshape(1)
        looked[key] = lookup(ids, table_rows, start, data_count, own_rows, row_count)
        if key == 1:
            for base in range(2, tensor_count, 2):
                looked_sums[base] = near_sum(looked[base], looked[base + 1])
            ids, looked_sums, looked[1] = lax.optimization_barrier((ids, looked_sums, looked[1]))
        elif key:
            ids, looked[key] = lax.optimization_barrier((ids, looked[key]))
    looked_sums[0] = near_sum(looked[0], looked[1])
    mine, _, got = far_sum(looked_sums)
    pieces = (mine + got).T.reshape(data_count, row_count, own_rows)
    none, pieces = lax.optimization_barrier((jnp.minimum(data_rank, 0), pieces))
    gate_error = lax.dynamic_slice_in_dim(gate_up_error[0], none, 1, 1)[:, 0]
    up_error = lax.dynamic_slice_in_dim(gate_up_error[0], none + 1, 1, 1)[:, 0]
    embedded = lax.all_to_all(pieces, "dp", 0, 0).reshape(width, own_rows).T

    attend_cols = attend_error.shape[2]
    quarter = lax.dynamic_slice_in_dim(attend_weight, tensor_rank * attend_cols, attend_cols, 1)
    queue_rows = queue_embed.shape[0] // tensor_count
    queue_own = lax.dynamic_slice_in_dim(queue_embed, tensor_rank * queue_rows, queue_rows, 0)
    joined = jnp.concatenate([quarter, gate_up[:, 0], gate_up[:, 1], down_weight], axis=1)
    joined = jnp.concatenate(
        [joined.astype(NARROW), queue_own.reshape(row_count, -1)], axis=1
    )
    joined_b = lax.all_gather(joined, "dp", axis=0, tiled=True)
    table_local, _ = lax.optimization_barrier((table_local, looked[tensor_count - 1]))
    table_b = lax.all_gather(table_local, "dp", axis=0, tiled=True)

    x_zero, x_zero_b = norm_forward(gains[:1], embedded)
    side = (seq_lengths, mask_slots, mask_targets, positive_rows, doc_ids, false_pairs)
    side = side + (queue_docs, factors, data_rank, token_ids, near)
    errors = (gate_error, up_error)
    x_zero_b, joined_b, side, errors = lax.optimization_barrier((x_zero_b, joined_b, side, errors))
    gate_error, up_error = errors
    seq_lengths, mask_slots, mask_targets, positive_rows, doc_ids, false_pairs = side[:6]
    queue_docs, factors, data_rank, near_ids, near = side[6:]
    x_blocks = spread_blocks(x_zero_b, "tensor")
    quarter_b, queue_near = joined_b[:, :attend_cols], joined_b[:, 4 * attend_cols :]
    attend_near = picked_blocks(spread_blocks(quarter_b, "tensor"), near)
    attend_b = jnp.concatenate([attend_near[k] for k in range(tensor_count)], axis=1)
    queue_near = normalize_keys(queue_near.reshape(data_count * queue_rows, width))

    every_rows = mask_slots + own_rows * jnp.arange(tensor_count)[None, :, None]
    every_len = seq_lengths[:, None, None]
    count = jnp.sum((every_rows < every_len).astype(WIDE))
    my_length = lax.dynamic_index_in_dim(seq_lengths, data_rank, 0, keepdims=False)
    group_valid = lax.dynamic_index_in_dim(every_rows < every_len, data_rank, 0, keepdims=False)
    own_slots = lax.dynamic_slice(
        mask_slots, (data_rank, tensor_rank, 0), (1, 1, slot_count)
    ).reshape(1, slot_count)
    own_length = (my_length - tensor_rank * own_rows).reshape(1)
    valid_rows = picked_blocks(group_valid, near).reshape(-1, 1).astype(WIDE)
    row_weight = valid_rows / count
    targets = picked_blocks(mask_targets[0], near).reshape(-1, 1) - vocab_start
    near_tokens = picked_blocks(near_ids.reshape(tensor_count, own_rows), near).reshape(1, -1)
    shifted = near_tokens - vocab_start
    tiles = -(-vocab_own // TILE)
    index = jnp.arange(total_rows)
    before = (shifted < shifted.T) | ((shifted == shifted.T) & (index[None, :] < index[:, None]))
    ranks = jnp.sum(before.astype(jnp.int32), axis=1)
    ordered = ranks[None, :] == index[:, None]
    sorted_ids = jnp.sum(jnp.where(ordered, shifted, 0), axis=1)[None, :]
    starts = jnp.sum(
        (shifted < jnp.minimum(jnp.arange(tiles + 1) * TILE, vocab_own)[:, None]).astype(jnp.int32),
        axis=1,
    )
    places = near[:, None] * own_rows + jnp.arange(own_rows)[None, :]
    keep_own = (places[0] < my_length)[:, None]
    cosine, sine = rotary_tables(places.reshape(-1))
    cosines, sines = row_blocks(cosine, tensor_count), row_blocks(sine, tensor_count)
    bias = jnp.where(places < my_length, 0.0, NEGATIVE).astype(NARROW)
    biases = [jnp.broadcast_to(bias[k][:, None], (own_rows, PAIR)) for k in range(tensor_count)]
    columns = jnp.arange(queue_docs.shape[0]).reshape(data_count, tensor_count, queue_rows)
    columns = picked_blocks(jnp.swapaxes(columns, 0, 1), near).reshape(-1)
    queue_docs = queue_docs.reshape(data_count, tensor_count, queue_rows)
    queue_docs = picked_blocks(jnp.swapaxes(queue_docs, 0, 1), near).reshape(-1)
    pick = lambda array: lax.dynamic_slice_in_dim(array, data_rank, 1, 0)
    target_c = columns[None, :] == pick(positive_rows)[:, None]
    blocked = (queue_docs[None, :] == pick(doc_ids)[:, None]) | jnp.any(
        pick(false_pairs)[:, :, None] == columns[None, None, :], axis=1
    )
    blocked = (blocked & jnp.logical_not(target_c)).astype(WIDE)
    target_c = target_c.astype(WIDE)

    factor_t = jnp.swapaxes(factors, 1, 2)
    factor_near = spread_blocks(factor_t[0], "tensor")
    error_p = partial_projections([attend_error[0]], [factor_t[0]])[0]

    queries, first_key, first_value = project(3, x_zero_b, attend_b, cosines[0], sines[0])
    keys, values = [first_key], [first_value]
    for k in range(1, tensor_count):
        key, value = project(2, x_blocks[k], attend_b, cosines[k], sines[k])
        keys.append(key)
        values.append(value)
    attended_t, log_total = attention_forward(queries, keys, values, biases)
    queue_near, _ = lax.optimization_barrier((queue_near, log_total))
    keys_hat = jnp.concatenate(spread_blocks(queue_near, "tensor"), axis=0)
    weight_out = attend_b[:, 3 * width :]
    attended_b, pre_one, hidden_in, hidden_in_b = merge_branch(
        attended_t, weight_out, x_zero, gains[1:2]
    )
    states, ffn_sums = paired(
        hidden_in_b, lambda index, first, second: ffn_forward(first, second, joined_b, attend_cols)
    )
    ffn_mine, _, ffn_got = far_sum(ffn_sums)
    final, _ = norm_forward(gains[2:], hidden_in, ffn_mine, ffn_got)

    ff_own = down_weight.shape[1]

    pool_part = jnp.sum(jnp.where(keep_own, final, 0.0), axis=0)
    picked = jnp.take(final, own_slots[0], axis=0).astype(NARROW)
    rows_all = jnp.concatenate(spread_blocks(picked, "tensor"), axis=0)
    logits, stats = vocab_logits(rows_all, table_b, targets)
    picks = rows_all.shape[0]
    pool_rows = jnp.pad(pool_part.reshape(-1, 128), ((0, 8 - width // 128), (0, 0)))
    stats = jnp.concatenate([stats, pool_rows], axis=0)
    for bit in axis_bits("tensor"):
        other = swap(stats, "tensor", bit)
        stats = whole_call(
            functools.partial(combine_kernel, tensor_count, slot_count, bit),
            [(stats.shape, WIDE)],
            20 * stats.size,
            stats,
            other,
        )[0]
    pooled_sum = stats[picks : picks + width // 128].reshape(1, width)
    own_stats = stats[:slot_count]
    cross = own_stats[:, 0] + jnp.log(own_stats[:, 1]) - own_stats[:, 2]
    masked_part = jnp.sum(valid_rows[:slot_count, 0] * cross)
    dlogits, row_part = vocab_back(logits, table_b, targets, stats[:picks], row_weight)
    row_grad = summed_block(row_blocks(row_part, tensor_count), "tensor", NARROW)

    weight_c = LAMBDA / seq_total
    first_rank = jnp.where(tensor_rank == 0, 1.0, 0.0)
    pooled_grad, contrast_row = contrast(
        weight_c, my_length.reshape(1), pooled_sum, keys_hat, blocked, target_c
    )
    contrast_part = contrast_row[0, 0] * first_rank

    pre_grad, pre_grad_b, gain_two = last_back(
        own_length, own_slots, row_grad, pooled_grad, hidden_in, ffn_mine, ffn_got, gains[2:]
    )
    backs, hidden_sums = paired(
        pre_grad_b,
        lambda index, first, second: ffn_backward(first, second, *states[index][:2], joined_b),
    )
    hidden_mine, hidden_sent, hidden_got = far_sum(hidden_sums)
    late = [(back[2], state[2], state[3], back[0], back[1]) for back, state in zip(backs, states)]
    late, _ = lax.optimization_barrier((late, hidden_sent))
    down_grad = sum(contract_rows(part[0], part[1]) for part in late)
    gate_w_grad = sum(contract_rows(part[2], part[3]) for part in late)
    up_w_grad = sum(contract_rows(part[2], part[4]) for part in late)
    pre_one_grad, branch_grad, attended_grad, gain_one = branch_back(
        pre_grad, hidden_mine, hidden_got, pre_one, gains[1:2], weight_out
    )
    dq, dk, dv = attention_backward(
        queries, keys, values, biases, attended_grad, attended_t, log_total, cosines, sines
    )
    x_sums = {}
    for key in reversed(range(0, tensor_count, 2)):
        operands = (dk[key], dv[key], dk[key + 1], dv[key + 1])
        if x_sums:
            operands, _ = lax.optimization_barrier((operands, x_sums[key + 2]))
        x_sums[key] = near_sum(*input_grads(*operands, attend_b))
    x_mine, x_sent, x_got = far_sum(x_sums)
    late = (dq, dk, dv, branch_grad)
    late, _, x_mine = lax.optimization_barrier((late, x_sent, x_mine))
    dq_late, dk, dv, branch_grad = late
    embedded_grad, gain_zero = first_back(
        pre_one_grad, dq, attend_b[:, :width], x_mine, x_got, embedded, gains[:1]
    )
    emb_all = jnp.concatenate(spread_blocks(embedded_grad, "tensor"), axis=0)
    emb_all = jnp.dot(ordered.astype(NARROW), emb_all)
    attend_part = jnp.concatenate(
        [
            contract_rows(x_zero_b, dq_late),
            sum(contract_rows(x_blocks[k], dk[k]) for k in range(tensor_count)),
            sum(contract_rows(x_blocks[k], dv[k]) for k in range(tensor_count)),
            jnp.dot(attended_b, branch_grad, preferred_element_type=WIDE),
        ],
        axis=1,
    )
    attend_blocks = [
        lax.dynamic_slice_in_dim(attend_part, near[k] * attend_cols, attend_cols, 1)
        for k in range(tensor_count)
    ]
    attend_p = partial_projections(
        [attend_blocks[k] for k in range(tensor_count)], factor_near
    )
    attend_p = summed_block([attend_p[k] for k in range(tensor_count)], "tensor", WIDE)
    attend_p = attend_p + error_p
    attend_held = dict(enumerate(attend_blocks[k] for k in range(tensor_count)))
    bits = axis_bits("tensor")
    for bit in bits[:-1]:
        for key in sorted((k for k in attend_held if not k & bit), reverse=True):
            attend_held[key] = attend_held[key] + swap(attend_held.pop(key ^ bit), "tensor", bit)
    emb_all, attend_held[bits[-1]] = lax.optimization_barrier((emb_all, attend_held[bits[-1]]))
    attend_got = swap(attend_held[bits[-1]], "tensor", bits[-1])

    other_m, other_p = small_matrices(
        [gate_w_grad, up_w_grad, down_grad],
        [gate_error, up_error, down_error[0]],
        factor_t[1:4],
    )
    other_sum = summed_all(jnp.concatenate([other_p[k] for k in range(3)], axis=1), "dp")
    cuts = sorted({0, (tiles + 1) // 2, tiles - 1, tiles})
    table_parts, table_sums = [], []
    for bounds in zip(cuts, cuts[1:]):
        found = table_matrix(
            bounds, starts, emb_all, sorted_ids, rows_all, dlogits, embed_error[0].T, factor_t[4]
        )
        table_parts.append(found)
        piece = found[2]
        if bounds[1] == tiles:
            piece = jnp.concatenate([piece, attend_p], axis=1)
        table_sums.append(summed_all(piece, "dp"))
    highs, lows = [part[0] for part in table_parts], [part[1] for part in table_parts]
    parts = [table_sums[-1][:, -attend_cols:], other_sum] + table_sums[:-1]
    parts.append(table_sums[-1][:, :-attend_cols])
    sums = jnp.concatenate(parts, axis=1)
    attend_got, _ = lax.optimization_barrier((attend_got, sums))
    first_m = (attend_held[0] + attend_got + attend_error[0])[None]
    spans, start = [], 0
    for size in (attend_cols, ff_own, ff_own, ff_own, tiles * TILE):
        spans.append((start, size))
        start += size
    bases_t = bases_of(sums, spans)
    small_basis = jnp.stack([bases_t[:, at : at + size] for at, size in spans[:4]])
    table_basis = bases_t[:, spans[4][0] :]
    other_back = small_backs(other_m, small_basis[1:])
    tab_back = table_back(highs, lows, table_basis)
    gain_terms = jnp.concatenate([gain_zero, gain_one, gain_two], axis=0)
    loss_terms = jnp.stack([masked_part, contrast_part])
    loss_row = jnp.zeros((1, width), WIDE).at[0, :2].set(loss_terms)
    packed = jnp.concatenate(
        [other_back.reshape(-1, width), tab_back, gain_terms, loss_row], axis=0
    )
    packed = summed_all(packed, "dp")
    first_back_t = small_backs(first_m, small_basis[:1])
    first_sum = summed_all(first_back_t[0], "dp")
    errors = small_errors(first_m, first_back_t, small_basis[:1]) + small_errors(
        other_m, other_back, small_basis[1:]
    )
    new_table_error = table_error(highs, lows, tab_back, table_basis, vocab_own).T
    own_t = jnp.concatenate([first_sum, packed[: 4 * RANK]], axis=0).reshape(5, RANK, width)
    square = jnp.sum(own_t * own_t)
    tail = packed[4 * RANK :].at[3, 2].set(square)
    shared = jnp.concatenate(
        [own_t[0], tail, jnp.pad(small_basis[0], ((0, 0), (0, width - attend_cols)))], axis=0
    )
    shared = picked_blocks(spread_blocks(shared, "tensor"), near)
    tail_sum = jnp.sum(shared[:, RANK : RANK + 4], axis=0)
    gains_grad = tail_sum[:3]
    loss_sums = tail_sum[3, :2]
    clip_norm = jnp.sqrt(tail_sum[3, 2] + jnp.sum(gains_grad * gains_grad))
    shrink = CLIP / jnp.maximum(clip_norm, CLIP)
    row_start = data_rank * row_count

    def rows_of(factor):
        return lax.dynamic_slice_in_dim(factor, row_start, row_count, factor.ndim - 1)

    reduced_attend = jnp.einsum(
        "tkd,tkn->dtn",
        rows_of(shared[:, :RANK]),
        shared[:, RANK + 4 :, :attend_cols],
        precision=HIGH,
    ).reshape(row_count, -1)
    own_rows_t = rows_of(own_t)

    def reduced(index, basis):
        return dot_in(own_rows_t[index], basis, ((0,), (0,)), precision=HIGH)

    reduced_gate_up = jnp.stack(
        [reduced(1, small_basis[1]), reduced(2, small_basis[2])], axis=1
    )
    reduced_down = reduced(3, small_basis[3])
    reduced_table = reduced(4, table_basis[:, :vocab_own])

    def advance(weight, moment, grad):
        fresh = MOMENTUM * moment + shrink * grad
        return (weight - LRATE * fresh, fresh)

    new_attend, new_attend_moment = advance(attend_weight, attend_moment, reduced_attend)
    new_gate_up, new_gate_up_moment = advance(gate_up, gate_up_moment, reduced_gate_up)
    new_down, new_down_moment = advance(down_weight, down_moment, reduced_down)
    new_table, new_table_moment = advance(embed_table, embed_moment, reduced_table)
    new_gains, new_gains_moment = advance(gains, gains_moment, gains_grad)
    return (
        new_attend,
        new_attend_moment,
        new_gate_up,
        new_gate_up_moment,
        new_down,
        new_down_moment,
        new_table,
        new_table_moment,
        new_gains,
        new_gains_moment,
        errors[0][None],
        jnp.stack([errors[1], errors[2]], axis=1)[None],
        errors[3][None],
        new_table_error[None],
        jnp.swapaxes(own_t, 1, 2),
        clip_norm,
        loss_sums[0],
        count,
        loss_sums[1],
    )


def solution(mesh):
    in_specs = (
        P("dp", None),
        P(),
        P(),
        P("dp", None, None),
        P(),
        P(),
        P(),
        P(),
        P("dp", None),
        P("dp", None),
        P("dp", None),
        P("dp", None, "tensor"),
        P("dp", None, "tensor"),
        P("dp", "tensor"),
        P("dp", "tensor"),
        P("dp", "tensor"),
        P("dp", "tensor"),
        P(),
        P(),
        P("dp", None, "tensor"),
        P("dp", None, None, "tensor"),
        P("dp", None, "tensor"),
        P("dp", None, "tensor"),
        P(None, None, "tensor"),
    )
    out_specs = (
        P("dp", None),
        P("dp", None),
        P("dp", None, "tensor"),
        P("dp", None, "tensor"),
        P("dp", "tensor"),
        P("dp", "tensor"),
        P("dp", "tensor"),
        P("dp", "tensor"),
        P(),
        P(),
        P("dp", None, "tensor"),
        P("dp", None, None, "tensor"),
        P("dp", None, "tensor"),
        P("dp", None, "tensor"),
        P(None, None, "tensor"),
        P(),
        P(),
        P(),
        P(),
    )
    return jax.shard_map(
        per_device, mesh=mesh, in_specs=in_specs, out_specs=out_specs, check_vma=False
    )
```

```python
import functools
import math

import jax
import jax.numpy as jnp
from jax import lax
from jax.experimental import pallas as pl
from jax.experimental.pallas import tpu as pltpu
from jax.sharding import PartitionSpec as P

HEADS = 12
HEAD_DIM = 64
RANK = 8
PAIR = 2 * HEAD_DIM
TILE = 640
WIDE_TILE = 1280
CHUNK = 256

EPS = 1e-05
ROPE_BASE = 1000.0
TAU = 0.02
LAMBDA = 1.0
CLIP = 0.02
LRATE = 5000.0
MOMENTUM = 0.9
WIDE = jnp.float32
NARROW = jnp.bfloat16
HIGH = lax.Precision.HIGHEST
NEGATIVE = -1e30


def params(mebibytes):
    return pltpu.CompilerParams(vmem_limit_bytes=mebibytes * 1024 * 1024)


def axis_bits(axis):
    size = lax.axis_size(axis)
    return [1 << place for place in range(size.bit_length() - 1)]


def swap(value, axis, bit):
    size = lax.axis_size(axis)
    return lax.ppermute(value, axis, [(index, index ^ bit) for index in range(size)])


def spread_blocks(value, axis):
    held = {0: value}
    for bit in reversed(axis_bits(axis)):
        for key in sorted(held):
            held[key ^ bit] = swap(held[key], axis, bit)
    return [held[key] for key in range(len(held))]


def summed_block(blocks, axis, kind):
    held = dict(enumerate(blocks))
    for bit in axis_bits(axis):
        for key in sorted((k for k in held if not k & bit), reverse=True):
            if key in held:
                got = swap(held.pop(key ^ bit).astype(kind), axis, bit)
                held[key] = held[key].astype(WIDE) + got.astype(WIDE)
    return held[0]


def summed_pair(blocks, axis):
    held = dict(enumerate(blocks))
    bits = axis_bits(axis)
    for bit in bits[:-1]:
        for key in sorted((k for k in held if not k & bit), reverse=True):
            if key in held:
                got = swap(held.pop(key ^ bit), axis, bit)
                held[key] = (held[key].astype(WIDE) + got.astype(WIDE)).astype(NARROW)
    if not bits:
        return held[0], jnp.zeros_like(held[0])
    return held[0], swap(held[bits[-1]], axis, bits[-1])


def summed_all(value, axis):
    for bit in axis_bits(axis):
        value = value + swap(value, axis, bit)
    return value


def picked_blocks(blocks, order):
    stacked = blocks if isinstance(blocks, jax.Array) else jnp.stack(blocks)
    return jnp.stack(
        [
            lax.dynamic_index_in_dim(stacked, order[k], 0, keepdims=False)
            for k in range(stacked.shape[0])
        ]
    )


def gathered_rows(value, axis):
    size = lax.axis_size(axis)
    if size > 8:
        return lax.all_gather(value, axis, axis=0, tiled=True)
    rank, rows = lax.axis_index(axis), value.shape[0]
    whole = jnp.zeros((size * rows,) + value.shape[1:], value.dtype)
    for key in range(size):
        part = value
        if key:
            part = lax.ppermute(value, axis, [(index, index ^ key) for index in range(size)])
        whole = lax.dynamic_update_slice_in_dim(whole, part, (rank ^ key) * rows, 0)
    return whole


def row_blocks(value, count):
    rows = value.shape[0] // count
    return [value[k * rows : (k + 1) * rows] for k in range(count)]


def layer_norm(values, gain):
    mean = jnp.mean(values, axis=-1, keepdims=True)
    centred = values - mean
    spread = jnp.mean(centred * centred, axis=-1, keepdims=True)
    return centred * lax.rsqrt(spread + EPS) * gain


def swiglu(gate, up):
    return jax.nn.silu(gate) * up


def dot_in(left, right, axes, precision=None):
    return lax.dot_general(
        left, right, (axes, ((), ())), precision=precision, preferred_element_type=WIDE
    )


def contract_rows(left, right):
    return dot_in(left, right, ((0,), (0,)))


def contract_cols(left, right):
    return dot_in(left, right, ((1,), (1,)))


def halves(value):
    high = value.astype(NARROW)
    return high, (value - high.astype(WIDE)).astype(NARROW)


def turn(piece, cosine, sine):
    lane = lax.broadcasted_iota(jnp.int32, piece.shape, 1) % HEAD_DIM
    half = HEAD_DIM // 2
    ahead = pltpu.roll(piece, PAIR - half, 1)
    behind = pltpu.roll(piece, half, 1)
    return piece * cosine + jnp.where(lane < half, -ahead, behind) * sine


def rotary_tables(places):
    half = HEAD_DIM // 2
    column = (jnp.arange(PAIR) % half).astype(WIDE)
    freq = ROPE_BASE ** (-2.0 * column / HEAD_DIM)
    angle = places.astype(WIDE)[:, None] * freq[None, :]
    return (jnp.cos(angle), jnp.sin(angle))


def project_kernel(count, x_ref, *refs):
    weights, (cos_ref, sin_ref), outs = refs[:count], refs[count : count + 2], refs[count + 2 :]
    x, cosine, sine = x_ref[...], cos_ref[...], sin_ref[...]
    for kind, (w_ref, out_ref) in enumerate(zip(weights, outs), 3 - count):
        for at in range(0, out_ref.shape[1], 2 * PAIR):
            flat = jnp.dot(x, w_ref[:, at : at + 2 * PAIR], preferred_element_type=WIDE)
            for start in range(0, 2 * PAIR, PAIR):
                piece = flat[:, start : start + PAIR]
                if kind < 2:
                    piece = turn(piece, cosine, sine)
                piece = piece.astype(NARROW)
                if kind == 0:
                    piece = (piece.astype(WIDE) * HEAD_DIM ** (-0.5)).astype(NARROW)
                out_ref[:, at + start : at + start + PAIR] = piece


def project(count, x, weight, cosine, sine):
    rows, width = x.shape
    still = lambda i: (0, 0)
    block = pl.BlockSpec((rows, width), still)
    lanes = pl.BlockSpec((rows, PAIR), still)
    return pl.pallas_call(
        functools.partial(project_kernel, count),
        grid=(1,),
        in_specs=[block]
        + [weight_block(width, width, kind) for kind in range(3 - count, 3)]
        + [lanes, lanes],
        out_specs=[block] * count,
        out_shape=[jax.ShapeDtypeStruct((rows, width), NARROW)] * count,
        compiler_params=params(20),
        cost_estimate=pl.CostEstimate(
            flops=2 * count * rows * width * width,
            bytes_accessed=2 * count * width * (rows + width),
            transcendentals=0,
        ),
    )(x, *[weight] * count, cosine, sine)


def turn_table_kernel(table_ref, out_ref):
    rows, columns = table_ref.shape
    empty = jnp.zeros((columns, out_ref.shape[1] - rows), WIDE)
    for at in range(0, columns, 128):
        size = min(128, columns - at)
        piece = table_ref[:, at : at + size].astype(NARROW).astype(WIDE).T
        if rows < out_ref.shape[1]:
            piece = jnp.concatenate([piece, empty[:size]], axis=1)
        out_ref[at : at + size, :] = piece
    out_ref[columns:, :] = jnp.zeros((out_ref.shape[0] - columns, out_ref.shape[1]), WIDE)


def turned_table(table):
    rows, columns = table.shape
    lanes = -(-rows // 128) * 128
    return whole_call(
        turn_table_kernel, [((columns // 8 * 8 + 8, lanes), WIDE)], 8 * table.size, table
    )[0]


def lookup_kernel(row_count, start_ref, ids_ref, table_ref, out_ref, held):
    groups, block = out_ref.shape[1] // row_count, out_ref.shape[0]
    start = start_ref[0]
    for group in range(groups):

        def move(at, carry):
            base = start + (group * block + at * 8)
            for place in range(8):
                index = ids_ref[base + place]
                held[at, place : place + 1, :] = table_ref[pl.ds(index, 1), :]
            return carry

        lax.fori_loop(0, block // 8, move, 0, unroll=8)
        rows = held[...].reshape(block, held.shape[2])[:, :row_count]
        out_ref[:, group * row_count : (group + 1) * row_count] = rows.astype(NARROW)


def lookup(ids, table, start, groups, block, row_count):
    return pl.pallas_call(
        functools.partial(lookup_kernel, row_count),
        in_specs=[
            pl.BlockSpec(memory_space=pltpu.SMEM),
            pl.BlockSpec(memory_space=pltpu.SMEM),
            pl.BlockSpec(memory_space=pltpu.VMEM),
        ],
        out_specs=pl.BlockSpec(memory_space=pltpu.VMEM),
        out_shape=jax.ShapeDtypeStruct((block, groups * row_count), NARROW),
        scratch_shapes=[pltpu.VMEM((block // 8, 8, table.shape[1]), WIDE)],
        compiler_params=params(10),
        cost_estimate=pl.CostEstimate(
            flops=groups * block * 4096, bytes_accessed=4 * table.size, transcendentals=0
        ),
    )(start, ids, table)


def norm_parts(values):
    mean = jnp.mean(values, axis=-1, keepdims=True)
    centred = values - mean
    scale = lax.rsqrt(jnp.mean(centred * centred, axis=-1, keepdims=True) + EPS)
    return centred * scale, scale


def norm_back(grad, values, gain):
    unit, scale = norm_parts(values)
    inner = grad * gain
    first = jnp.mean(inner, axis=-1, keepdims=True)
    second = jnp.mean(inner * unit, axis=-1, keepdims=True)
    return (inner - first - unit * second) * scale, jnp.sum(grad * unit, axis=0, keepdims=True)


def whole_call(kernel, outs, flops, *operands):
    moved = sum(operand.size * operand.dtype.itemsize for operand in operands)
    moved += sum(math.prod(shape) * jnp.dtype(kind).itemsize for shape, kind in outs)
    budget = 8 + moved * 2 // (1 << 20)
    return pl.pallas_call(
        kernel,
        out_shape=[jax.ShapeDtypeStruct(shape, kind) for shape, kind in outs],
        compiler_params=params(budget),
        cost_estimate=pl.CostEstimate(
            flops=flops,
            bytes_accessed=sum(4 * operand.size for operand in operands),
            transcendentals=0,
        ),
    )(*operands)


def norm_kernel(gain_ref, *refs):
    inputs, (out_ref, narrow_ref) = refs[:-2], refs[-2:]
    total = inputs[0][...].astype(WIDE)
    for ref in inputs[1:]:
        total = total + ref[...].astype(WIDE)
    out = norm_parts(total)[0] * gain_ref[...]
    out_ref[...] = out
    narrow_ref[...] = out.astype(NARROW)


def norm_forward(gain, *parts):
    shape = parts[0].shape
    return whole_call(norm_kernel, [(shape, WIDE), (shape, NARROW)], 20 * parts[0].size, gain, *parts)


def merge_kernel(attended_ref, weight_ref, x_ref, gain_ref, narrow_out, pre_ref, out_ref, out_b_ref):
    narrow = attended_ref[...].astype(NARROW)
    narrow_out[...] = narrow
    pre = x_ref[...] + contract_rows(narrow, weight_ref[...])
    pre_ref[...] = pre
    out = norm_parts(pre)[0] * gain_ref[...]
    out_ref[...] = out
    out_b_ref[...] = out.astype(NARROW)


def merge_branch(attended_t, weight, x_zero, gain):
    rows, width = x_zero.shape
    shape = (rows, width)
    return whole_call(
        merge_kernel,
        [((width, rows), NARROW), (shape, WIDE), (shape, WIDE), (shape, NARROW)],
        2 * rows * width * width,
        attended_t,
        weight,
        x_zero,
        gain,
    )


def last_kernel(length_ref, slots_ref, rows_ref, pooled_ref, hidden_ref, local_ref, got_ref, gain_ref, out_ref, narrow_ref, sum_ref):
    total = hidden_ref[...] + local_ref[...].astype(WIDE) + got_ref[...].astype(WIDE)
    spread = rows_ref[...]
    place = lax.broadcasted_iota(jnp.int32, (total.shape[0], slots_ref.shape[1]), 0)
    hot = (place == slots_ref[...]).astype(WIDE).astype(NARROW)
    high, low = halves(spread)
    grad = jnp.dot(hot, high, preferred_element_type=WIDE)
    grad = grad + jnp.dot(hot, low, preferred_element_type=WIDE)
    index = lax.broadcasted_iota(jnp.int32, (total.shape[0], 1), 0)
    grad = grad + jnp.where(index < length_ref[0], pooled_ref[...], 0.0)
    out, gain_grad = norm_back(grad, total, gain_ref[...])
    out_ref[...] = out
    narrow_ref[...] = out.astype(NARROW)
    sum_ref[...] = gain_grad


def last_back(length, slots, row_grad, pooled_grad, hidden_in, local, got, gain):
    shape = hidden_in.shape
    return pl.pallas_call(
        last_kernel,
        in_specs=[pl.BlockSpec(memory_space=pltpu.SMEM)]
        + [pl.BlockSpec(memory_space=pltpu.VMEM)] * 7,
        out_shape=[
            jax.ShapeDtypeStruct(shape, WIDE),
            jax.ShapeDtypeStruct(shape, NARROW),
            jax.ShapeDtypeStruct((1, shape[1]), WIDE),
        ],
        compiler_params=params(24),
        cost_estimate=pl.CostEstimate(
            flops=200 * hidden_in.size, bytes_accessed=20 * hidden_in.size, transcendentals=0
        ),
    )(length, slots, row_grad, pooled_grad, hidden_in, local, got, gain)


def branch_back_kernel(grad_ref, local_ref, got_ref, pre_ref, gain_ref, weight_ref, out_ref, narrow_ref, attended_ref, sum_ref):
    grad = grad_ref[...] + local_ref[...].astype(WIDE) + got_ref[...].astype(WIDE)
    out, gain_grad = norm_back(grad, pre_ref[...], gain_ref[...])
    narrow = out.astype(NARROW)
    out_ref[...] = out
    narrow_ref[...] = narrow
    sum_ref[...] = gain_grad
    attended_ref[...] = contract_cols(narrow, weight_ref[...]).astype(NARROW)


def branch_back(pre_grad, local, got, pre_one, gain, weight):
    rows, width = pre_grad.shape
    shape = (rows, width)
    return whole_call(
        branch_back_kernel,
        [(shape, WIDE), (shape, NARROW), (shape, NARROW), ((1, width), WIDE)],
        2 * rows * width * width,
        pre_grad,
        local,
        got,
        pre_one,
        gain,
        weight,
    )


def first_back_kernel(grad_ref, dq_ref, weight_ref, local_ref, got_ref, value_ref, gain_ref, out_ref, sum_ref):
    grad = grad_ref[...] + local_ref[...].astype(WIDE) + got_ref[...].astype(WIDE)
    grad = grad + contract_cols(dq_ref[...], weight_ref[...])
    out, gain_grad = norm_back(grad, value_ref[...].astype(WIDE), gain_ref[...])
    out_ref[...] = out.astype(NARROW)
    sum_ref[...] = gain_grad


def first_back(pre_one_grad, dq, weight, local, got, embedded, gain):
    rows, width = pre_one_grad.shape
    return whole_call(
        first_back_kernel,
        [((rows, width), NARROW), ((1, width), WIDE)],
        2 * rows * width * width,
        pre_one_grad,
        dq,
        weight,
        local,
        got,
        embedded,
        gain,
    )


def ffn_step(x_ref, weights, gate_out, up_out, act_ref, x_out, out_ref):
    gate_ref, up_ref, down_ref = weights
    x = x_ref[...]
    gate = jnp.dot(x, gate_ref[...], preferred_element_type=WIDE)
    up = jnp.dot(x, up_ref[...], preferred_element_type=WIDE)
    gate_out[...] = gate
    up_out[...] = up
    act = (gate / (1.0 + jnp.exp(-gate)) * up).astype(NARROW)
    act_ref[...] = act
    x_out[...] = x
    out_ref[...] = contract_cols(act, down_ref[...]).astype(NARROW)


def ffn_kernel(first_ref, second_ref, *refs):
    weights, kept, outs = refs[:3], refs[3:7], refs[7:]
    for step, x_ref in enumerate((first_ref, second_ref)):

        @pl.when(pl.program_id(0) == step)
        def _():
            ffn_step(x_ref, weights, *kept, outs[step])


def weight_block(width, hidden, index):
    return pl.BlockSpec((width, hidden), lambda i: (0, index))


def ffn_forward(first, second, weights, hidden):
    rows, width = first.shape
    whole = pl.BlockSpec((rows, width), lambda i: (0, 0))
    tall = lambda i: (i, 0)
    return pl.pallas_call(
        ffn_kernel,
        grid=(2,),
        in_specs=[whole, whole] + [weight_block(width, hidden, k) for k in range(1, 4)],
        out_specs=[pl.BlockSpec((rows, hidden), tall)] * 3
        + [pl.BlockSpec((rows, width), tall), whole, whole],
        out_shape=[
            jax.ShapeDtypeStruct((2 * rows, hidden), WIDE),
            jax.ShapeDtypeStruct((2 * rows, hidden), WIDE),
            jax.ShapeDtypeStruct((2 * rows, hidden), NARROW),
            jax.ShapeDtypeStruct((2 * rows, width), NARROW),
            jax.ShapeDtypeStruct((rows, width), NARROW),
            jax.ShapeDtypeStruct((rows, width), NARROW),
        ],
        compiler_params=params(32),
        cost_estimate=pl.CostEstimate(
            flops=12 * rows * width * hidden,
            bytes_accessed=28 * rows * width + 6 * width * hidden,
            transcendentals=2 * rows * hidden,
        ),
    )(first, second, weights, weights, weights)


def ffn_back_step(grad_ref, gate_in, up_in, weights, dgate_ref, dup_ref, grad_out, out_ref):
    gate_ref, up_ref, down_ref = weights
    grad = grad_ref[...]
    grad_out[...] = grad
    act_grad = jnp.dot(grad, down_ref[...], preferred_element_type=WIDE)
    gate, up = gate_in[...], up_in[...]
    share = 1.0 / (1.0 + jnp.exp(-gate))
    dgate = (act_grad * up * (share * (1.0 + gate * (1.0 - share)))).astype(NARROW)
    dup = (act_grad * (gate * share)).astype(NARROW)
    dgate_ref[...] = dgate
    dup_ref[...] = dup
    out_ref[...] = (
        contract_cols(dgate, gate_ref[...]) + contract_cols(dup, up_ref[...])
    ).astype(NARROW)


def ffn_back_kernel(first_ref, second_ref, gate_in, up_in, *refs):
    weights, kept, outs = refs[:3], refs[3:6], refs[6:]
    for step, grad_ref in enumerate((first_ref, second_ref)):

        @pl.when(pl.program_id(0) == step)
        def _():
            ffn_back_step(grad_ref, gate_in, up_in, weights, *kept, outs[step])


def ffn_backward(first, second, gate, up, weights):
    rows, width = first.shape
    hidden = gate.shape[1]
    whole = pl.BlockSpec((rows, width), lambda i: (0, 0))
    tall = lambda i: (i, 0)
    return pl.pallas_call(
        ffn_back_kernel,
        grid=(2,),
        in_specs=[whole, whole]
        + [pl.BlockSpec((rows, hidden), tall)] * 2
        + [weight_block(width, hidden, k) for k in range(1, 4)],
        out_specs=[pl.BlockSpec((rows, hidden), tall)] * 2
        + [pl.BlockSpec((rows, width), tall), whole, whole],
        out_shape=[
            jax.ShapeDtypeStruct((2 * rows, hidden), NARROW),
            jax.ShapeDtypeStruct((2 * rows, hidden), NARROW),
            jax.ShapeDtypeStruct((2 * rows, width), NARROW),
            jax.ShapeDtypeStruct((rows, width), NARROW),
            jax.ShapeDtypeStruct((rows, width), NARROW),
        ],
        compiler_params=params(34),
        cost_estimate=pl.CostEstimate(
            flops=12 * rows * width * hidden,
            bytes_accessed=32 * rows * width + 6 * width * hidden,
            transcendentals=2 * rows * hidden,
        ),
    )(first, second, gate, up, weights, weights, weights)


def input_kernel(first_k, first_v, second_k, second_v, key_ref, value_ref, *outs):
    for dk_ref, dv_ref, out_ref in zip((first_k, second_k), (first_v, second_v), outs):
        total = contract_cols(dk_ref[...], key_ref[...])
        total = total + contract_cols(dv_ref[...], value_ref[...])
        out_ref[...] = total.astype(NARROW)


def input_grads(first_k, first_v, second_k, second_v, weights):
    rows, width = first_k.shape
    whole = pl.BlockSpec((rows, width), lambda i: (0, 0))
    return pl.pallas_call(
        input_kernel,
        grid=(1,),
        in_specs=[whole] * 4 + [weight_block(width, width, k) for k in (1, 2)],
        out_specs=[whole] * 2,
        out_shape=[jax.ShapeDtypeStruct((rows, width), NARROW)] * 2,
        compiler_params=params(24),
        cost_estimate=pl.CostEstimate(
            flops=8 * rows * width * width,
            bytes_accessed=12 * rows * width + 4 * width * width,
            transcendentals=0,
        ),
    )(first_k, first_v, second_k, second_v, weights, weights)


def paired(value, work):
    near_bit, *far_bits = axis_bits("tensor")
    held = {0: value}
    for bit in reversed(far_bits):
        for key in sorted(held):
            held[key ^ bit] = swap(held[key], "tensor", bit)
    results, sums = [], {}
    for key in sorted(held):
        block = held[key]
        if results:
            block, _ = lax.optimization_barrier((block, results[-1][-1]))
        results.append(work(len(results), block, swap(block, "tensor", near_bit)))
        sums[key] = near_sum(*results[-1][-2:])
    return results, sums


def near_sum(own, other):
    got = swap(other, "tensor", axis_bits("tensor")[0])
    return (own.astype(WIDE) + got.astype(WIDE)).astype(NARROW)


def far_sum(sums):
    sums = dict(sums)
    near_bit, *far_bits = axis_bits("tensor")
    for bit in far_bits[:-1]:
        for key in sorted(k for k in sums if not k & bit):
            got = swap(sums.pop(key ^ bit), "tensor", bit)
            sums[key] = (sums[key].astype(WIDE) + got.astype(WIDE)).astype(NARROW)
    return sums[0], sums[far_bits[-1]], swap(sums[far_bits[-1]], "tensor", far_bits[-1])


def logits_kernel(columns, tile, rows_ref, table_ref, targets_ref, out_ref, stats_ref, top_ref, sum_ref, hit_ref):
    step = pl.program_id(0)

    @pl.when(step == 0)
    def _():
        top_ref[...] = jnp.full(top_ref.shape, NEGATIVE, WIDE)
        sum_ref[...] = jnp.zeros(sum_ref.shape, WIDE)
        hit_ref[...] = jnp.zeros(hit_ref.shape, WIDE)

    logits = jnp.dot(rows_ref[...], table_ref[...], preferred_element_type=WIDE)
    out_ref[...] = logits
    place = step * tile + lax.broadcasted_iota(jnp.int32, (1, tile), 1)
    seen = jnp.where(place < columns, logits, NEGATIVE)
    hits = jnp.where((place == targets_ref[...]) & (place < columns), seen, 0.0)
    pieces = [slice(at, at + 128) for at in range(0, tile, 128)]
    before = top_ref[...]
    top = before
    for piece in pieces:
        top = jnp.maximum(top, seen[:, piece])
    total = sum_ref[...] * jnp.exp(before - top)
    hit = hit_ref[...]
    for piece in pieces:
        total = total + jnp.exp(seen[:, piece] - top)
        hit = hit + hits[:, piece]
    top_ref[...] = top
    sum_ref[...] = total
    hit_ref[...] = hit

    @pl.when(step == pl.num_programs(0) - 1)
    def _():
        peak = jnp.max(top, axis=1, keepdims=True)
        whole = jnp.sum(total * jnp.exp(top - peak), axis=1, keepdims=True)
        found = jnp.sum(hit, axis=1, keepdims=True)
        lane = lax.broadcasted_iota(jnp.int32, (1, 128), 1)
        stats_ref[...] = jnp.where(
            lane == 0, peak, jnp.where(lane == 1, whole, jnp.where(lane == 2, found, 0.0))
        )


def vocab_logits(rows_all, table, targets):
    picks, width = rows_all.shape
    columns = table.shape[1]
    tiles = -(-columns // TILE)
    tile = WIDE_TILE
    still = lambda j: (0, 0)
    along = lambda j: (0, j)
    return pl.pallas_call(
        functools.partial(logits_kernel, columns, tile),
        grid=(tiles * TILE // tile,),
        in_specs=[
            pl.BlockSpec((picks, width), still),
            pl.BlockSpec((width, tile), along),
            pl.BlockSpec((picks, 1), still),
        ],
        out_specs=[pl.BlockSpec((picks, tile), along), pl.BlockSpec((picks, 128), still)],
        out_shape=[
            jax.ShapeDtypeStruct((picks, tiles * TILE), WIDE),
            jax.ShapeDtypeStruct((picks, 128), WIDE),
        ],
        scratch_shapes=[pltpu.VMEM((picks, 128), WIDE)] * 3,
        compiler_params=params(56),
        cost_estimate=pl.CostEstimate(
            flops=2 * picks * width * columns,
            bytes_accessed=2 * width * columns,
            transcendentals=picks * columns,
        ),
    )(rows_all, table, targets)


def combine_kernel(count, slots, bit, mine_ref, other_ref, out_ref):
    lane = lax.broadcasted_iota(jnp.int32, (1, 128), 1)
    for block in range(count):
        mine = mine_ref[block * slots : (block + 1) * slots, :]
        other = other_ref[(block ^ bit) * slots : ((block ^ bit) + 1) * slots, :]
        peak = jnp.maximum(mine[:, :1], other[:, :1])
        total = mine[:, 1:2] * jnp.exp(mine[:, :1] - peak)
        total = total + other[:, 1:2] * jnp.exp(other[:, :1] - peak)
        out_ref[block * slots : (block + 1) * slots, :] = jnp.where(
            lane == 0, peak, jnp.where(lane == 1, total, mine + other)
        )
    rest = count * slots
    out_ref[rest:, :] = mine_ref[rest:, :] + other_ref[rest:, :]


def dlogits_kernel(columns, tile, logits_ref, table_ref, targets_ref, stats_ref, weight_ref, out_ref, grad_ref):
    step = pl.program_id(0)
    log_all = stats_ref[:, :1] + jnp.log(stats_ref[:, 1:2])
    place = step * tile + lax.broadcasted_iota(jnp.int32, (1, tile), 1)
    share = jnp.exp(logits_ref[...] - log_all) - jnp.where(place == targets_ref[...], 1.0, 0.0)
    grad = jnp.where(place < columns, share * weight_ref[...], 0.0).astype(NARROW)
    out_ref[...] = grad
    column = step * tile + lax.broadcasted_iota(jnp.int32, (1, tile), 1)
    table = jnp.where(column < columns, table_ref[...].astype(WIDE), 0.0).astype(NARROW)
    part = contract_cols(grad, table)

    @pl.when(step == 0)
    def _():
        grad_ref[...] = part

    @pl.when(step > 0)
    def _():
        grad_ref[...] += part


def vocab_back(logits, table, targets, stats, weight):
    picks = targets.shape[0]
    width, columns = table.shape
    tile = WIDE_TILE
    still = lambda j: (0, 0)
    along = lambda j: (0, j)
    return pl.pallas_call(
        functools.partial(dlogits_kernel, columns, tile),
        grid=(logits.shape[1] // tile,),
        in_specs=[
            pl.BlockSpec((picks, tile), along),
            pl.BlockSpec((width, tile), along),
            pl.BlockSpec((picks, 1), still),
            pl.BlockSpec((picks, 128), still),
            pl.BlockSpec((picks, 1), still),
        ],
        out_specs=[pl.BlockSpec((picks, tile), along), pl.BlockSpec((picks, width), still)],
        out_shape=[
            jax.ShapeDtypeStruct(logits.shape, NARROW),
            jax.ShapeDtypeStruct((picks, width), WIDE),
        ],
        compiler_params=params(56),
        cost_estimate=pl.CostEstimate(
            flops=2 * picks * width * columns,
            bytes_accessed=2 * width * columns,
            transcendentals=picks * columns,
        ),
    )(logits, table, targets, stats, weight)


def contrast_kernel(weight, length_ref, pooled_ref, keys_ref, blocked_ref, target_ref, grad_ref, part_ref):
    length = length_ref[0].astype(WIDE)
    pooled = pooled_ref[...] / length
    scale = lax.rsqrt(jnp.sum(pooled * pooled, axis=-1, keepdims=True) + EPS)
    narrow = jnp.broadcast_to(pooled * scale, (8, pooled.shape[1])).astype(NARROW)
    keys = keys_ref[...]
    scores = contract_cols(narrow, keys)[:1] / TAU
    target = target_ref[...]
    masked = jnp.where(blocked_ref[...] > 0.0, NEGATIVE, scores)
    top = jnp.max(masked, axis=-1, keepdims=True)
    log_c = top + jnp.log(jnp.sum(jnp.exp(masked - top), axis=-1, keepdims=True))
    chosen = jnp.sum(jnp.where(target > 0.0, scores, 0.0), axis=-1, keepdims=True)
    part_ref[...] = jnp.broadcast_to((log_c - chosen) * weight, part_ref.shape)
    dscores = ((jnp.exp(masked - log_c) - target) * (weight / TAU)).astype(NARROW)
    dscores = jnp.broadcast_to(dscores.astype(WIDE), (8, dscores.shape[1])).astype(NARROW)
    grad = jnp.dot(dscores, keys, preferred_element_type=WIDE)[:1]
    inner = jnp.sum(pooled * grad, axis=-1, keepdims=True)
    grad_ref[...] = (grad - pooled * (inner * scale * scale)) * scale / length


def contrast(weight, length, pooled_sum, keys_hat, blocked, target):
    width = pooled_sum.shape[1]
    return pl.pallas_call(
        functools.partial(contrast_kernel, weight),
        in_specs=[pl.BlockSpec(memory_space=pltpu.SMEM)]
        + [pl.BlockSpec(memory_space=pltpu.VMEM)] * 4,
        out_shape=[
            jax.ShapeDtypeStruct((1, width), WIDE),
            jax.ShapeDtypeStruct((1, 128), WIDE),
        ],
        compiler_params=params(8),
        cost_estimate=pl.CostEstimate(
            flops=4 * keys_hat.size, bytes_accessed=2 * keys_hat.size, transcendentals=0
        ),
    )(length, pooled_sum, keys_hat, blocked, target)


def head_lanes(head):
    lane = lax.broadcasted_iota(jnp.int32, (1, PAIR), 1)
    return (lane // HEAD_DIM) == head, lane == HEAD_DIM * (1 - head)


def attend_kernel(count, q_ref, *refs):
    k_refs, v_refs, bias_refs = refs[:count], refs[count : 2 * count], refs[2 * count : 3 * count]
    out_ref, log_ref, s_ref = refs[3 * count :]
    head = pl.program_id(1)
    mine, spare = head_lanes(head)
    step = k_refs[0].shape[0]
    blocks = [pl.ds(k * step, step) for k in range(count)]
    query = jnp.where(spare, 1.0, jnp.where(mine, q_ref[...].astype(WIDE), 0.0)).astype(NARROW)
    top = None
    for rows, k_ref, bias_ref in zip(blocks, k_refs, bias_refs):
        key = jnp.where(spare, bias_ref[...].astype(WIDE), k_ref[...].astype(WIDE))
        scores = contract_cols(key.astype(NARROW), query)
        s_ref[rows, :] = scores
        peak = jnp.max(scores, axis=0, keepdims=True)
        top = peak if top is None else jnp.maximum(top, peak)
    total = None
    for rows in blocks:
        powers = jnp.exp(s_ref[rows, :] - top)
        s_ref[rows, :] = powers
        part = jnp.sum(powers, axis=0, keepdims=True)
        total = part if total is None else total + part
    share = 1.0 / total
    result = None
    for rows, v_ref in zip(blocks, v_refs):
        probs = (s_ref[rows, :] * share).astype(NARROW)
        part = contract_rows(v_ref[...], probs)
        result = part if result is None else result + part
    log_ref[0, pl.ds(head, 1), :] = top + jnp.log(total)

    @pl.when(head == 0)
    def _():
        out_ref[...] = result

    @pl.when(head == 1)
    def _():
        out_ref[HEAD_DIM:, :] = result[HEAD_DIM:, :]


def attention_forward(queries, keys, values, biases):
    rows, width = queries.shape
    count = len(keys)
    length = rows * count
    pairs = width // PAIR
    lanes = pl.BlockSpec((rows, PAIR), lambda i, h: (0, i))
    still = pl.BlockSpec((rows, PAIR), lambda i, h: (0, 0))
    return pl.pallas_call(
        functools.partial(attend_kernel, count),
        grid=(pairs, 2),
        in_specs=[lanes] * (1 + 2 * count) + [still] * count,
        out_specs=[
            pl.BlockSpec((PAIR, rows), lambda i, h: (i, 0)),
            pl.BlockSpec((1, 2, rows), lambda i, h: (i, 0, 0)),
        ],
        out_shape=[
            jax.ShapeDtypeStruct((width, rows), WIDE),
            jax.ShapeDtypeStruct((pairs, 2, rows), WIDE),
        ],
        scratch_shapes=[pltpu.VMEM((length, rows), WIDE)],
        compiler_params=params(22),
        cost_estimate=pl.CostEstimate(
            flops=4 * rows * length * width,
            bytes_accessed=4 * length * width + 8 * rows * width,
            transcendentals=rows * length * HEADS,
        ),
    )(queries, *keys, *values, *biases)


def attend_back_kernel(count, q_ref, grad_ref, out_ref, log_ref, *refs):
    groups = [refs[k * count : (k + 1) * count] for k in range(5)]
    k_refs, v_refs, bias_refs, cos_refs, sin_refs = groups
    rest = refs[5 * count :]
    dq_ref, dk_refs, dv_refs = rest[0], rest[1 : 1 + count], rest[1 + count : 1 + 2 * count]
    dk_sum, dv_sum, dq_sum = rest[1 + 2 * count :]
    head = pl.program_id(1)
    mine, spare = head_lanes(head)
    step, scale = k_refs[0].shape[0], HEAD_DIM ** (-0.5)
    own = jnp.where(mine, q_ref[...].astype(WIDE), 0.0)
    query = own.astype(NARROW)
    asked = jnp.where(spare, 1.0, own).astype(NARROW)
    grad_wide = jnp.where(mine, grad_ref[...].astype(WIDE), 0.0)
    grad = grad_wide.astype(NARROW)
    delta = jnp.sum(grad_wide.T * out_ref[...], axis=0, keepdims=True)
    log_total = log_ref[0, pl.ds(head, 1), :]
    dq = None
    for k in range(count):
        rows = pl.ds(k * step, step)
        key_block = k_refs[k][...]
        key = jnp.where(spare, bias_refs[k][...].astype(WIDE), key_block.astype(WIDE))
        scores = contract_cols(key.astype(NARROW), asked)
        probs = jnp.exp(scores - log_total)
        dprobs = contract_cols(v_refs[k][...], grad)
        dv = jnp.dot(probs.astype(NARROW), grad, preferred_element_type=WIDE)
        dscores = (probs * (dprobs - delta)).astype(NARROW)
        dk = jnp.dot(dscores, query, preferred_element_type=WIDE)
        part = contract_rows(key_block, dscores)
        dq = part if dq is None else dq + part

        @pl.when(head == 0)
        def _():
            dk_sum[rows, :] = dk
            dv_sum[rows, :] = dv

        @pl.when(head == 1)
        def _():
            total = dk_sum[rows, :] + dk
            dk_refs[k][...] = turn(total, cos_refs[k][...], -sin_refs[k][...]).astype(NARROW)
            dv_refs[k][...] = (dv_sum[rows, :] + dv).astype(NARROW)

    @pl.when(head == 0)
    def _():
        dq_sum[...] = dq

    @pl.when(head == 1)
    def _():
        dq_sum[HEAD_DIM:, :] = dq[HEAD_DIM:, :]
        total = dq_sum[...].T * scale
        dq_ref[...] = turn(total, cos_refs[0][...], -sin_refs[0][...]).astype(NARROW)


def attention_backward(queries, keys, values, biases, grad, out_t, log_total, cosines, sines):
    rows, width = queries.shape
    count = len(keys)
    length = rows * count
    pairs = width // PAIR
    lanes = pl.BlockSpec((rows, PAIR), lambda i, h: (0, i))
    still = pl.BlockSpec((rows, PAIR), lambda i, h: (0, 0))
    found = pl.pallas_call(
        functools.partial(attend_back_kernel, count),
        grid=(pairs, 2),
        in_specs=[
            lanes,
            lanes,
            pl.BlockSpec((PAIR, rows), lambda i, h: (i, 0)),
            pl.BlockSpec((1, 2, rows), lambda i, h: (i, 0, 0)),
        ]
        + [lanes] * (2 * count)
        + [still] * (3 * count),
        out_specs=[lanes] * (1 + 2 * count),
        out_shape=[jax.ShapeDtypeStruct((rows, width), NARROW)] * (1 + 2 * count),
        scratch_shapes=[
            pltpu.VMEM((length, PAIR), WIDE),
            pltpu.VMEM((length, PAIR), WIDE),
            pltpu.VMEM((PAIR, rows), WIDE),
        ],
        compiler_params=params(56),
        cost_estimate=pl.CostEstimate(
            flops=10 * rows * length * width,
            bytes_accessed=8 * length * width + 8 * rows * width,
            transcendentals=rows * length * HEADS,
        ),
    )(queries, grad, out_t, log_total, *keys, *values, *biases, *cosines, *sines)
    return found[0], found[1 : 1 + count], found[1 + count :]


def project_down(matrix, factor_t):
    high, low = halves(matrix)
    factor_high, factor_low = halves(factor_t)
    both = jnp.concatenate([factor_high, factor_low], axis=0)
    first = jnp.dot(both, high, preferred_element_type=WIDE)
    second = jnp.dot(factor_high, low, preferred_element_type=WIDE)
    return first[:RANK] + first[RANK:] + second


def project_back(matrix, basis_t):
    high, low = halves(matrix)
    basis_high, basis_low = halves(basis_t)
    both = jnp.concatenate([basis_high, basis_low], axis=0)
    first = contract_cols(both, high)
    second = contract_cols(basis_high, low)
    return first[:RANK] + first[RANK:] + second


def expand(back_t, basis_t):
    back_high, back_low = halves(back_t)
    basis_high, basis_low = halves(basis_t)
    left = jnp.concatenate([back_high, back_low, back_high], axis=0)
    right = jnp.concatenate([basis_high, basis_high, basis_low], axis=0)
    return contract_rows(left, right)


def table_kernel(columns, first, starts_ref, left_ref, tokens_ref, rows_ref, dlogits_ref, error_ref, factor_ref, high_ref, low_ref, p_ref, sum_ref):
    tile = first + pl.program_id(0)
    place = tile * TILE + lax.broadcasted_iota(jnp.int32, (TILE, 1), 0)
    sum_ref[...] = error_ref[...] + contract_rows(dlogits_ref[...], rows_ref[...])

    def visit(chunk, carry):
        at = pl.ds(pl.multiple_of(chunk * CHUNK, CHUNK), CHUNK)
        hot = jnp.where(tokens_ref[:, at] == place, 1.0, 0.0).astype(NARROW)
        sum_ref[...] += jnp.dot(hot, left_ref[at, :], preferred_element_type=WIDE)
        return carry

    lax.fori_loop(
        starts_ref[tile] // CHUNK, (starts_ref[tile + 1] + CHUNK - 1) // CHUNK, visit, 0
    )
    total = jnp.where(place < columns, sum_ref[...], 0.0)
    high, low = halves(total)
    high_ref[...] = high
    low_ref[...] = low
    factor_high, factor_low = halves(factor_ref[...])
    both = jnp.concatenate([factor_high, factor_low], axis=0)
    found = contract_cols(high, both).T
    rest = contract_cols(low, both).T
    p_ref[...] = found[:RANK] + found[RANK:] + rest[:RANK]


def table_matrix(bounds, starts, left, tokens, rows, dlogits, error, factor_t):
    columns, width = error.shape
    slots = left.shape[0]
    picks = rows.shape[0]
    first, tiles = bounds[0], bounds[1] - bounds[0]
    still = lambda j: (0, 0)
    down = lambda j: (j, 0)
    return pl.pallas_call(
        functools.partial(table_kernel, columns, first),
        grid=(tiles,),
        in_specs=[
            pl.BlockSpec(memory_space=pltpu.SMEM),
            pl.BlockSpec((slots, width), still),
            pl.BlockSpec((1, slots), still),
            pl.BlockSpec((picks, width), still),
            pl.BlockSpec((picks, TILE), lambda j: (0, first + j)),
            pl.BlockSpec((TILE, width), lambda j: (first + j, 0)),
            pl.BlockSpec((RANK, width), still),
        ],
        out_specs=[
            pl.BlockSpec((TILE, width), down),
            pl.BlockSpec((TILE, width), down),
            pl.BlockSpec((RANK, TILE), lambda j: (0, j)),
        ],
        out_shape=[
            jax.ShapeDtypeStruct((tiles * TILE, width), NARROW),
            jax.ShapeDtypeStruct((tiles * TILE, width), NARROW),
            jax.ShapeDtypeStruct((RANK, tiles * TILE), WIDE),
        ],
        scratch_shapes=[pltpu.VMEM((TILE, width), WIDE)],
        compiler_params=params(32),
        cost_estimate=pl.CostEstimate(
            flops=2 * width * tiles * TILE * (slots // 4 + picks + 24),
            bytes_accessed=8 * width * tiles * TILE,
            transcendentals=0,
        ),
    )(starts, left, tokens, rows, dlogits, error, factor_t)


def partial_kernel(*refs):
    count = (len(refs) - 1) // 2
    for index in range(count):
        refs[-1][index] = project_down(refs[index][...], refs[count + index][...])


def partial_projections(matrices, factors_t):
    count, (width, columns) = len(matrices), matrices[0].shape
    return whole_call(
        partial_kernel,
        [((count, RANK, columns), WIDE)],
        48 * count * width * columns,
        *matrices,
        *factors_t,
    )[0]


def small_kernel(count, *refs):
    grads, errors, factor_ref = refs[:count], refs[count : 2 * count], refs[2 * count]
    m_ref, p_ref = refs[2 * count + 1 :]
    for index in range(count):
        total = grads[index][...] + errors[index][...]
        m_ref[index] = total
        p_ref[index] = project_down(total, factor_ref[index])


def small_matrices(grads, errors, factor_t):
    count, (width, columns) = len(grads), grads[0].shape
    block = columns // 3
    tall = pl.BlockSpec((width, block), lambda j: (0, j))
    return pl.pallas_call(
        functools.partial(small_kernel, count),
        grid=(3,),
        in_specs=[tall] * (2 * count)
        + [pl.BlockSpec((count, RANK, width), lambda j: (0, 0, 0))],
        out_specs=[
            pl.BlockSpec((count, width, block), lambda j: (0, 0, j)),
            pl.BlockSpec((count, RANK, block), lambda j: (0, 0, j)),
        ],
        out_shape=[
            jax.ShapeDtypeStruct((count, width, columns), WIDE),
            jax.ShapeDtypeStruct((count, RANK, columns), WIDE),
        ],
        compiler_params=params(56),
        cost_estimate=pl.CostEstimate(
            flops=48 * count * width * columns,
            bytes_accessed=12 * count * width * columns,
            transcendentals=0,
        ),
    )(*grads, *errors, factor_t)


def basis_kernel(spans, p_ref, out_ref):
    index = lax.broadcasted_iota(jnp.int32, (RANK, 1), 0)
    for start, size in spans:
        rows = p_ref[:, pl.ds(start, size)]
        for place in range(RANK):
            row = rows[place : place + 1, :]
            row = row * lax.rsqrt(jnp.sum(row * row, axis=1, keepdims=True))
            inner = jnp.sum(rows * row, axis=1, keepdims=True)
            rows = jnp.where(index == place, row, rows - jnp.where(index > place, inner, 0.0) * row)
        out_ref[:, pl.ds(start, size)] = rows


def bases_of(sums, spans):
    return pl.pallas_call(
        functools.partial(basis_kernel, spans),
        out_shape=jax.ShapeDtypeStruct(sums.shape, WIDE),
        compiler_params=params(8),
        cost_estimate=pl.CostEstimate(
            flops=64 * sums.size, bytes_accessed=8 * sums.size, transcendentals=40
        ),
    )(sums)


def small_back_kernel(m_ref, basis_ref, back_ref):
    for index in range(m_ref.shape[0]):
        back_ref[index] = project_back(m_ref[index], basis_ref[index])


def small_backs(matrices, basis):
    count, width, columns = matrices.shape
    return pl.pallas_call(
        small_back_kernel,
        out_shape=jax.ShapeDtypeStruct((count, RANK, width), WIDE),
        compiler_params=params(24),
        cost_estimate=pl.CostEstimate(
            flops=48 * count * width * columns,
            bytes_accessed=4 * count * width * columns,
            transcendentals=0,
        ),
    )(matrices, basis)


def table_specs(parts, width):
    bounds, first = [], 0
    for part in parts:
        bounds.append((first, first + part.shape[0] // TILE))
        first = bounds[-1][1]
    specs = [
        pl.BlockSpec(
            (TILE, width), lambda j, low=low, high=high: (jnp.clip(j, low, high - 1) - low, 0)
        )
        for low, high in bounds
    ]
    return bounds, specs


def table_back_kernel(bounds, *refs):
    highs, lows = refs[: len(bounds)], refs[len(bounds) : 2 * len(bounds)]
    basis_ref, back_ref = refs[2 * len(bounds) :]
    step = pl.program_id(0)
    basis_high, basis_low = halves(basis_ref[...])
    both = jnp.concatenate([basis_high, basis_low], axis=0)

    @pl.when(step == 0)
    def _():
        back_ref[...] = jnp.zeros(back_ref.shape, WIDE)

    for (low, high), high_ref, low_ref in zip(bounds, highs, lows):

        @pl.when((step >= low) & (step < high))
        def _():
            first = jnp.dot(both, high_ref[...], preferred_element_type=WIDE)
            second = jnp.dot(basis_high, low_ref[...], preferred_element_type=WIDE)
            back_ref[...] += first[:RANK] + first[RANK:] + second


def table_back(highs, lows, basis):
    width = highs[0].shape[1]
    columns = basis.shape[1]
    bounds, specs = table_specs(highs, width)
    return pl.pallas_call(
        functools.partial(table_back_kernel, bounds),
        grid=(columns // TILE,),
        in_specs=specs + specs + [pl.BlockSpec((RANK, TILE), lambda j: (0, j))],
        out_specs=pl.BlockSpec((RANK, width), lambda j: (0, 0)),
        out_shape=jax.ShapeDtypeStruct((RANK, width), WIDE),
        compiler_params=params(18),
        cost_estimate=pl.CostEstimate(
            flops=48 * width * columns, bytes_accessed=4 * width * columns, transcendentals=0
        ),
    )(*highs, *lows, basis)


def small_error_kernel(m_ref, back_ref, basis_ref, *out_refs):
    count = m_ref.shape[0]
    for index in range(count):
        error = m_ref[index] - expand(back_ref[index], basis_ref[index])
        if count > 1 and index < 2:
            out_refs[0][:, index, :] = error
        else:
            out_refs[-1][...] = error


def small_errors(matrices, backs, basis):
    count, width, columns = matrices.shape
    return pl.pallas_call(
        small_error_kernel,
        out_shape=[jax.ShapeDtypeStruct((width, 2, columns), WIDE)] * (count - 1 > 0)
        + [jax.ShapeDtypeStruct((width, columns), WIDE)],
        compiler_params=params(32),
        cost_estimate=pl.CostEstimate(
            flops=48 * count * width * columns,
            bytes_accessed=8 * count * width * columns,
            transcendentals=0,
        ),
    )(matrices, backs, basis)


def table_error_kernel(bounds, *refs):
    highs, lows = refs[: len(bounds)], refs[len(bounds) : 2 * len(bounds)]
    back_ref, basis_ref, out_ref = refs[2 * len(bounds) :]
    step = pl.program_id(0)
    for (low, high), high_ref, low_ref in zip(bounds, highs, lows):

        @pl.when((step >= low) & (step < high))
        def _():
            whole = high_ref[...].astype(WIDE) + low_ref[...].astype(WIDE)
            out_ref[...] = whole - expand(basis_ref[...], back_ref[...])


def table_error(highs, lows, back, basis, columns):
    width = highs[0].shape[1]
    bounds, specs = table_specs(highs, width)
    return pl.pallas_call(
        functools.partial(table_error_kernel, bounds),
        grid=(basis.shape[1] // TILE,),
        in_specs=specs
        + specs
        + [
            pl.BlockSpec((RANK, width), lambda j: (0, 0)),
            pl.BlockSpec((RANK, TILE), lambda j: (0, j)),
        ],
        out_specs=pl.BlockSpec((TILE, width), lambda j: (j, 0)),
        out_shape=jax.ShapeDtypeStruct((columns, width), WIDE),
        compiler_params=params(24),
        cost_estimate=pl.CostEstimate(
            flops=48 * width * columns, bytes_accessed=8 * width * columns, transcendentals=0
        ),
    )(*highs, *lows, back, basis)


def normalize_keys(raw_keys):
    wide_keys = raw_keys.astype(WIDE)
    return (
        wide_keys * lax.rsqrt(jnp.sum(wide_keys * wide_keys, axis=-1, keepdims=True) + EPS)
    ).astype(NARROW)


def per_device(
    token_ids,
    seq_lengths,
    mask_slots,
    mask_targets,
    positive_rows,
    doc_ids,
    false_pairs,
    queue_docs,
    queue_embed,
    attend_weight,
    attend_moment,
    gate_up,
    gate_up_moment,
    down_weight,
    down_moment,
    embed_table,
    embed_moment,
    gains,
    gains_moment,
    attend_error,
    gate_up_error,
    down_error,
    embed_error,
    factors,
):
    tensor_count = lax.axis_size("tensor")
    tensor_rank = lax.axis_index("tensor")
    data_count = lax.axis_size("dp")
    data_rank = lax.axis_index("dp")
    groups, seq_len = token_ids.shape
    width = gains.shape[1]
    total_rows = groups * seq_len
    own_rows = total_rows // tensor_count
    slot_count = mask_slots.shape[2]
    seq_total = groups * data_count
    near = jnp.arange(tensor_count) ^ tensor_rank
    row_count = attend_weight.shape[0]

    tokens_all = lax.all_to_all(
        jnp.broadcast_to(token_ids, (data_count, seq_len)), "dp", 0, 0, tiled=True
    )
    vocab_own = embed_table.shape[1]
    vocab_start = tensor_rank * vocab_own
    ids = tokens_all - vocab_start
    ids = jnp.where((ids >= 0) & (ids < vocab_own), ids, vocab_own)
    table_local = embed_table.astype(NARROW)
    table_rows = turned_table(embed_table)
    ids = jnp.swapaxes(ids.reshape(data_count, tensor_count, own_rows), 0, 1).reshape(-1)
    looked, looked_sums = {}, {}
    for key in reversed(range(tensor_count)):
        start = ((tensor_rank ^ key) * (data_count * own_rows)).reshape(1)
        looked[key] = lookup(ids, table_rows, start, data_count, own_rows, row_count)
        if key == 1:
            for base in range(2, tensor_count, 2):
                looked_sums[base] = near_sum(looked[base], looked[base + 1])
            ids, looked_sums, looked[1] = lax.optimization_barrier((ids, looked_sums, looked[1]))
        elif key:
            ids, looked[key] = lax.optimization_barrier((ids, looked[key]))
    looked_sums[0] = near_sum(looked[0], looked[1])
    mine, _, got = far_sum(looked_sums)
    pieces = (mine + got).T.reshape(data_count, row_count, own_rows)
    soon = (jnp.minimum(data_rank, 0), token_ids, near)
    (none, near_ids, near_soon), pieces = lax.optimization_barrier((soon, pieces))
    near_tokens = picked_blocks(near_ids.reshape(tensor_count, own_rows), near_soon).reshape(1, -1)
    shifted = near_tokens - vocab_start
    tiles = -(-vocab_own // TILE)
    index = jnp.arange(total_rows)
    before = (shifted < shifted.T) | ((shifted == shifted.T) & (index[None, :] < index[:, None]))
    ranks = jnp.sum(before.astype(jnp.int32), axis=1)
    ordered = ranks[None, :] == index[:, None]
    sorted_ids = jnp.sum(jnp.where(ordered, shifted, 0), axis=1)[None, :]
    starts = jnp.sum(
        (shifted < jnp.minimum(jnp.arange(tiles + 1) * TILE, vocab_own)[:, None]).astype(jnp.int32),
        axis=1,
    )
    gate_error = lax.dynamic_slice_in_dim(gate_up_error[0], none, 1, 1)[:, 0]
    up_error = lax.dynamic_slice_in_dim(gate_up_error[0], none + 1, 1, 1)[:, 0]
    embedded = lax.all_to_all(pieces, "dp", 0, 0).reshape(width, own_rows).T

    attend_cols = attend_error.shape[2]
    quarter = lax.dynamic_slice_in_dim(attend_weight, tensor_rank * attend_cols, attend_cols, 1)
    queue_rows = queue_embed.shape[0] // tensor_count
    queue_own = lax.dynamic_slice_in_dim(queue_embed, tensor_rank * queue_rows, queue_rows, 0)
    joined = jnp.concatenate([quarter, gate_up[:, 0], gate_up[:, 1], down_weight], axis=1)
    joined = jnp.concatenate(
        [joined.astype(NARROW), queue_own.reshape(row_count, -1)], axis=1
    )
    joined_b = lax.all_gather(joined, "dp", axis=0, tiled=True)
    table_local, _ = lax.optimization_barrier((table_local, looked[tensor_count - 1]))
    table_b = lax.all_gather(table_local, "dp", axis=0, tiled=True)

    x_zero, x_zero_b = norm_forward(gains[:1], embedded)
    side = (seq_lengths, mask_slots, mask_targets, positive_rows, doc_ids, false_pairs)
    side = side + (queue_docs, factors, data_rank, near)
    errors = (gate_error, up_error, ranks, sorted_ids, starts)
    x_zero_b, joined_b, side, errors = lax.optimization_barrier((x_zero_b, joined_b, side, errors))
    gate_error, up_error, ranks, sorted_ids, starts = errors
    ordered = ranks[None, :] == index[:, None]
    seq_lengths, mask_slots, mask_targets, positive_rows, doc_ids, false_pairs = side[:6]
    queue_docs, factors, data_rank, near = side[6:]
    x_blocks = spread_blocks(x_zero_b, "tensor")
    quarter_b, queue_near = joined_b[:, :attend_cols], joined_b[:, 4 * attend_cols :]
    attend_near = picked_blocks(spread_blocks(quarter_b, "tensor"), near)
    attend_b = jnp.concatenate([attend_near[k] for k in range(tensor_count)], axis=1)
    queue_near = normalize_keys(queue_near.reshape(data_count * queue_rows, width))

    every_rows = mask_slots + own_rows * jnp.arange(tensor_count)[None, :, None]
    every_len = seq_lengths[:, None, None]
    count = jnp.sum((every_rows < every_len).astype(WIDE))
    my_length = lax.dynamic_index_in_dim(seq_lengths, data_rank, 0, keepdims=False)
    group_valid = lax.dynamic_index_in_dim(every_rows < every_len, data_rank, 0, keepdims=False)
    own_slots = lax.dynamic_slice(
        mask_slots, (data_rank, tensor_rank, 0), (1, 1, slot_count)
    ).reshape(1, slot_count)
    own_length = (my_length - tensor_rank * own_rows).reshape(1)
    valid_rows = picked_blocks(group_valid, near).reshape(-1, 1).astype(WIDE)
    row_weight = valid_rows / count
    targets = picked_blocks(mask_targets[0], near).reshape(-1, 1) - vocab_start
    places = near[:, None] * own_rows + jnp.arange(own_rows)[None, :]
    keep_own = (places[0] < my_length)[:, None]
    cosine, sine = rotary_tables(places.reshape(-1))
    cosines, sines = row_blocks(cosine, tensor_count), row_blocks(sine, tensor_count)
    bias = jnp.where(places < my_length, 0.0, NEGATIVE).astype(NARROW)
    biases = [jnp.broadcast_to(bias[k][:, None], (own_rows, PAIR)) for k in range(tensor_count)]
    columns = jnp.arange(queue_docs.shape[0]).reshape(data_count, tensor_count, queue_rows)
    columns = picked_blocks(jnp.swapaxes(columns, 0, 1), near).reshape(-1)
    queue_docs = queue_docs.reshape(data_count, tensor_count, queue_rows)
    queue_docs = picked_blocks(jnp.swapaxes(queue_docs, 0, 1), near).reshape(-1)
    pick = lambda array: lax.dynamic_slice_in_dim(array, data_rank, 1, 0)
    target_c = columns[None, :] == pick(positive_rows)[:, None]
    blocked = (queue_docs[None, :] == pick(doc_ids)[:, None]) | jnp.any(
        pick(false_pairs)[:, :, None] == columns[None, None, :], axis=1
    )
    blocked = (blocked & jnp.logical_not(target_c)).astype(WIDE)
    target_c = target_c.astype(WIDE)

    factor_t = jnp.swapaxes(factors, 1, 2)
    factor_near = spread_blocks(factor_t[0], "tensor")
    error_p = partial_projections([attend_error[0]], [factor_t[0]])[0]

    queries, first_key, first_value = project(3, x_zero_b, attend_b, cosines[0], sines[0])
    keys, values = [first_key], [first_value]
    for k in range(1, tensor_count):
        key, value = project(2, x_blocks[k], attend_b, cosines[k], sines[k])
        keys.append(key)
        values.append(value)
    attended_t, log_total = attention_forward(queries, keys, values, biases)
    queue_near, _ = lax.optimization_barrier((queue_near, log_total))
    keys_hat = jnp.concatenate(spread_blocks(queue_near, "tensor"), axis=0)
    weight_out = attend_b[:, 3 * width :]
    attended_b, pre_one, hidden_in, hidden_in_b = merge_branch(
        attended_t, weight_out, x_zero, gains[1:2]
    )
    states, ffn_sums = paired(
        hidden_in_b, lambda index, first, second: ffn_forward(first, second, joined_b, attend_cols)
    )
    ffn_mine, _, ffn_got = far_sum(ffn_sums)
    final, _ = norm_forward(gains[2:], hidden_in, ffn_mine, ffn_got)

    ff_own = down_weight.shape[1]

    pool_part = jnp.sum(jnp.where(keep_own, final, 0.0), axis=0)
    picked = jnp.take(final, own_slots[0], axis=0).astype(NARROW)
    rows_all = jnp.concatenate(spread_blocks(picked, "tensor"), axis=0)
    logits, stats = vocab_logits(rows_all, table_b, targets)
    picks = rows_all.shape[0]
    pool_rows = jnp.pad(pool_part.reshape(-1, 128), ((0, 8 - width // 128), (0, 0)))
    stats = jnp.concatenate([stats, pool_rows], axis=0)
    for bit in axis_bits("tensor"):
        other = swap(stats, "tensor", bit)
        stats = whole_call(
            functools.partial(combine_kernel, tensor_count, slot_count, bit),
            [(stats.shape, WIDE)],
            20 * stats.size,
            stats,
            other,
        )[0]
    pooled_sum = stats[picks : picks + width // 128].reshape(1, width)
    own_stats = stats[:slot_count]
    cross = own_stats[:, 0] + jnp.log(own_stats[:, 1]) - own_stats[:, 2]
    masked_part = jnp.sum(valid_rows[:slot_count, 0] * cross)
    dlogits, row_part = vocab_back(logits, table_b, targets, stats[:picks], row_weight)
    row_grad = summed_block(row_blocks(row_part, tensor_count), "tensor", NARROW)

    weight_c = LAMBDA / seq_total
    first_rank = jnp.where(tensor_rank == 0, 1.0, 0.0)
    pooled_grad, contrast_row = contrast(
        weight_c, my_length.reshape(1), pooled_sum, keys_hat, blocked, target_c
    )
    contrast_part = contrast_row[0, 0] * first_rank

    pre_grad, pre_grad_b, gain_two = last_back(
        own_length, own_slots, row_grad, pooled_grad, hidden_in, ffn_mine, ffn_got, gains[2:]
    )
    backs, hidden_sums = paired(
        pre_grad_b,
        lambda index, first, second: ffn_backward(first, second, *states[index][:2], joined_b),
    )
    hidden_mine, hidden_sent, hidden_got = far_sum(hidden_sums)
    late = [(back[2], state[2], state[3], back[0], back[1]) for back, state in zip(backs, states)]
    late, _ = lax.optimization_barrier((late, hidden_sent))
    down_grad = sum(contract_rows(part[0], part[1]) for part in late)
    gate_w_grad = sum(contract_rows(part[2], part[3]) for part in late)
    up_w_grad = sum(contract_rows(part[2], part[4]) for part in late)
    ffn_grads = (down_grad, gate_w_grad, up_w_grad)
    ffn_grads, hidden_mine = lax.optimization_barrier((ffn_grads, hidden_mine))
    down_grad, gate_w_grad, up_w_grad = ffn_grads
    pre_one_grad, branch_grad, attended_grad, gain_one = branch_back(
        pre_grad, hidden_mine, hidden_got, pre_one, gains[1:2], weight_out
    )
    dq, dk, dv = attention_backward(
        queries, keys, values, biases, attended_grad, attended_t, log_total, cosines, sines
    )
    x_sums = {}
    for key in reversed(range(0, tensor_count, 2)):
        operands = (dk[key], dv[key], dk[key + 1], dv[key + 1])
        if x_sums:
            operands, _ = lax.optimization_barrier((operands, x_sums[key + 2]))
        x_sums[key] = near_sum(*input_grads(*operands, attend_b))
    x_mine, x_sent, x_got = far_sum(x_sums)
    late = (dq, dk, dv, branch_grad)
    late, _, x_mine = lax.optimization_barrier((late, x_sent, x_mine))
    dq_late, dk, dv, branch_grad = late
    attend_part = jnp.concatenate(
        [
            contract_rows(x_zero_b, dq_late),
            sum(contract_rows(x_blocks[k], dk[k]) for k in range(tensor_count)),
            sum(contract_rows(x_blocks[k], dv[k]) for k in range(tensor_count)),
            jnp.dot(attended_b, branch_grad, preferred_element_type=WIDE),
        ],
        axis=1,
    )
    attend_part, x_mine = lax.optimization_barrier((attend_part, x_mine))
    embedded_grad, gain_zero = first_back(
        pre_one_grad, dq, attend_b[:, :width], x_mine, x_got, embedded, gains[:1]
    )
    other_m, other_p = small_matrices(
        [gate_w_grad, up_w_grad, down_grad],
        [gate_error, up_error, down_error[0]],
        factor_t[1:4],
    )
    near_bit, *far_bits = axis_bits("tensor")
    held = {0: embedded_grad}
    for bit in reversed(far_bits):
        for key in sorted(held):
            held[key ^ bit] = swap(held[key], "tensor", bit)
    emb_blocks = dict(held)
    emb_blocks[1] = swap(held[0], "tensor", near_bit)
    rest = {key: held[key] for key in held if key}
    rest, other_p = lax.optimization_barrier((rest, other_p))
    for key in rest:
        emb_blocks[key] = rest[key]
        emb_blocks[key + 1] = swap(rest[key], "tensor", near_bit)
    emb_all = jnp.concatenate([emb_blocks[key] for key in range(tensor_count)], axis=0)
    emb_all = jnp.dot(ordered.astype(NARROW), emb_all)
    attend_blocks = [
        lax.dynamic_slice_in_dim(attend_part, near[k] * attend_cols, attend_cols, 1)
        for k in range(tensor_count)
    ]
    attend_p = partial_projections(
        [attend_blocks[k] for k in range(tensor_count)], factor_near
    )
    attend_p = summed_block([attend_p[k] for k in range(tensor_count)], "tensor", WIDE)
    attend_p = attend_p + error_p
    attend_held = dict(enumerate(attend_blocks[k] for k in range(tensor_count)))
    bits = axis_bits("tensor")
    for bit in bits[:-1]:
        for key in sorted((k for k in attend_held if not k & bit), reverse=True):
            attend_held[key] = attend_held[key] + swap(attend_held.pop(key ^ bit), "tensor", bit)
    emb_all, attend_held[bits[-1]] = lax.optimization_barrier((emb_all, attend_held[bits[-1]]))
    attend_got = [
        swap(piece, "tensor", bits[-1]) for piece in row_blocks(attend_held[bits[-1]], 2)
    ]

    other_sum = summed_all(jnp.concatenate([other_p[k] for k in range(3)], axis=1), "dp")
    cuts = sorted({0, tiles * 5 // 12, tiles * 9 // 12, tiles})
    table_parts, table_sums = [], []
    for bounds in zip(cuts, cuts[1:]):
        if table_parts:
            emb_all, table_parts[-1][2] = lax.optimization_barrier((emb_all, table_parts[-1][2]))
        if bounds[1] == tiles:
            emb_all, attend_got[0] = lax.optimization_barrier((emb_all, attend_got[0]))
        found = table_matrix(
            bounds, starts, emb_all, sorted_ids, rows_all, dlogits, embed_error[0].T, factor_t[4]
        )
        table_parts.append(list(found))
    for bounds, found in zip(zip(cuts, cuts[1:]), table_parts):
        piece = found[2]
        if bounds[1] == tiles:
            piece = jnp.concatenate([piece, attend_p], axis=1)
        table_sums.append(summed_all(piece, "dp"))
    highs, lows = [part[0] for part in table_parts], [part[1] for part in table_parts]
    parts = [table_sums[-1][:, -attend_cols:], other_sum] + table_sums[:-1]
    parts.append(table_sums[-1][:, :-attend_cols])
    sums = jnp.concatenate(parts, axis=1)
    attend_got[1], _ = lax.optimization_barrier((attend_got[1], sums))
    attend_got = jnp.concatenate(attend_got, axis=0)
    first_m = (attend_held[0] + attend_got + attend_error[0])[None]
    spans, start = [], 0
    for size in (attend_cols, ff_own, ff_own, ff_own, tiles * TILE):
        spans.append((start, size))
        start += size
    bases_t = bases_of(sums, spans)
    small_basis = jnp.stack([bases_t[:, at : at + size] for at, size in spans[:4]])
    table_basis = bases_t[:, spans[4][0] :]
    other_back = small_backs(other_m, small_basis[1:])
    tab_back = table_back(highs, lows, table_basis)
    gain_terms = jnp.concatenate([gain_zero, gain_one, gain_two], axis=0)
    loss_terms = jnp.stack([masked_part, contrast_part])
    loss_row = jnp.zeros((1, width), WIDE).at[0, :2].set(loss_terms)
    packed = jnp.concatenate(
        [other_back.reshape(-1, width), tab_back, gain_terms, loss_row], axis=0
    )
    packed = summed_all(packed, "dp")
    first_back_t = small_backs(first_m, small_basis[:1])
    first_sum = summed_all(first_back_t[0], "dp")
    errors = small_errors(first_m, first_back_t, small_basis[:1]) + small_errors(
        other_m, other_back, small_basis[1:]
    )
    new_table_error = table_error(highs, lows, tab_back, table_basis, vocab_own).T
    own_t = jnp.concatenate([first_sum, packed[: 4 * RANK]], axis=0).reshape(5, RANK, width)
    square = jnp.sum(own_t * own_t)
    tail = packed[4 * RANK :].at[3, 2].set(square)
    shared = jnp.concatenate(
        [own_t[0], tail, jnp.pad(small_basis[0], ((0, 0), (0, width - attend_cols)))], axis=0
    )
    shared = picked_blocks(spread_blocks(shared, "tensor"), near)
    tail_sum = jnp.sum(shared[:, RANK : RANK + 4], axis=0)
    gains_grad = tail_sum[:3]
    loss_sums = tail_sum[3, :2]
    clip_norm = jnp.sqrt(tail_sum[3, 2] + jnp.sum(gains_grad * gains_grad))
    shrink = CLIP / jnp.maximum(clip_norm, CLIP)
    row_start = data_rank * row_count

    def rows_of(factor):
        return lax.dynamic_slice_in_dim(factor, row_start, row_count, factor.ndim - 1)

    reduced_attend = jnp.einsum(
        "tkd,tkn->dtn",
        rows_of(shared[:, :RANK]),
        shared[:, RANK + 4 :, :attend_cols],
        precision=HIGH,
    ).reshape(row_count, -1)
    own_rows_t = rows_of(own_t)

    def reduced(index, basis):
        return dot_in(own_rows_t[index], basis, ((0,), (0,)), precision=HIGH)

    reduced_gate_up = jnp.stack(
        [reduced(1, small_basis[1]), reduced(2, small_basis[2])], axis=1
    )
    reduced_down = reduced(3, small_basis[3])
    reduced_table = reduced(4, table_basis[:, :vocab_own])

    def advance(weight, moment, grad):
        fresh = MOMENTUM * moment + shrink * grad
        return (weight - LRATE * fresh, fresh)

    new_attend, new_attend_moment = advance(attend_weight, attend_moment, reduced_attend)
    new_gate_up, new_gate_up_moment = advance(gate_up, gate_up_moment, reduced_gate_up)
    new_down, new_down_moment = advance(down_weight, down_moment, reduced_down)
    new_table, new_table_moment = advance(embed_table, embed_moment, reduced_table)
    new_gains, new_gains_moment = advance(gains, gains_moment, gains_grad)
    return (
        new_attend,
        new_attend_moment,
        new_gate_up,
        new_gate_up_moment,
        new_down,
        new_down_moment,
        new_table,
        new_table_moment,
        new_gains,
        new_gains_moment,
        errors[0][None],
        errors[1][None],
        errors[2][None],
        new_table_error[None],
        jnp.swapaxes(own_t, 1, 2),
        clip_norm,
        loss_sums[0],
        count,
        loss_sums[1],
    )


def solution(mesh):
    in_specs = (
        P("dp", None),
        P(),
        P(),
        P("dp", None, None),
        P(),
        P(),
        P(),
        P(),
        P("dp", None),
        P("dp", None),
        P("dp", None),
        P("dp", None, "tensor"),
        P("dp", None, "tensor"),
        P("dp", "tensor"),
        P("dp", "tensor"),
        P("dp", "tensor"),
        P("dp", "tensor"),
        P(),
        P(),
        P("dp", None, "tensor"),
        P("dp", None, None, "tensor"),
        P("dp", None, "tensor"),
        P("dp", None, "tensor"),
        P(None, None, "tensor"),
    )
    out_specs = (
        P("dp", None),
        P("dp", None),
        P("dp", None, "tensor"),
        P("dp", None, "tensor"),
        P("dp", "tensor"),
        P("dp", "tensor"),
        P("dp", "tensor"),
        P("dp", "tensor"),
        P(),
        P(),
        P("dp", None, "tensor"),
        P("dp", None, None, "tensor"),
        P("dp", None, "tensor"),
        P("dp", None, "tensor"),
        P(None, None, "tensor"),
        P(),
        P(),
        P(),
        P(),
    )
    return jax.shard_map(
        per_device, mesh=mesh, in_specs=in_specs, out_specs=out_specs, check_vma=False
    )
```

```python
import functools
import math

import jax
import jax.numpy as jnp
from jax import lax
from jax.experimental import pallas as pl
from jax.experimental.pallas import tpu as pltpu
from jax.sharding import PartitionSpec as P

HEADS = 12
HEAD_DIM = 64
RANK = 8
PAIR = 2 * HEAD_DIM
TILE = 640
WIDE_TILE = 1280
CHUNK = 256

EPS = 1e-05
ROPE_BASE = 1000.0
TAU = 0.02
LAMBDA = 1.0
CLIP = 0.02
LRATE = 5000.0
MOMENTUM = 0.9
WIDE = jnp.float32
NARROW = jnp.bfloat16
HIGH = lax.Precision.HIGHEST
NEGATIVE = -1e30


def params(mebibytes):
    return pltpu.CompilerParams(vmem_limit_bytes=mebibytes * 1024 * 1024)


def axis_bits(axis):
    size = lax.axis_size(axis)
    return [1 << place for place in range(size.bit_length() - 1)]


def swap(value, axis, bit):
    size = lax.axis_size(axis)
    return lax.ppermute(value, axis, [(index, index ^ bit) for index in range(size)])


def spread_blocks(value, axis):
    held = {0: value}
    for bit in reversed(axis_bits(axis)):
        for key in sorted(held):
            held[key ^ bit] = swap(held[key], axis, bit)
    return [held[key] for key in range(len(held))]


def summed_block(blocks, axis, kind):
    held = dict(enumerate(blocks))
    for bit in axis_bits(axis):
        for key in sorted((k for k in held if not k & bit), reverse=True):
            if key in held:
                got = swap(held.pop(key ^ bit).astype(kind), axis, bit)
                held[key] = held[key].astype(WIDE) + got.astype(WIDE)
    return held[0]


def summed_pair(blocks, axis):
    held = dict(enumerate(blocks))
    bits = axis_bits(axis)
    for bit in bits[:-1]:
        for key in sorted((k for k in held if not k & bit), reverse=True):
            if key in held:
                got = swap(held.pop(key ^ bit), axis, bit)
                held[key] = (held[key].astype(WIDE) + got.astype(WIDE)).astype(NARROW)
    if not bits:
        return held[0], jnp.zeros_like(held[0])
    return held[0], swap(held[bits[-1]], axis, bits[-1])


def summed_all(value, axis):
    for bit in axis_bits(axis):
        value = value + swap(value, axis, bit)
    return value


def picked_blocks(blocks, order):
    stacked = blocks if isinstance(blocks, jax.Array) else jnp.stack(blocks)
    return jnp.stack(
        [
            lax.dynamic_index_in_dim(stacked, order[k], 0, keepdims=False)
            for k in range(stacked.shape[0])
        ]
    )


def gathered_rows(value, axis):
    size = lax.axis_size(axis)
    if size > 8:
        return lax.all_gather(value, axis, axis=0, tiled=True)
    rank, rows = lax.axis_index(axis), value.shape[0]
    whole = jnp.zeros((size * rows,) + value.shape[1:], value.dtype)
    for key in range(size):
        part = value
        if key:
            part = lax.ppermute(value, axis, [(index, index ^ key) for index in range(size)])
        whole = lax.dynamic_update_slice_in_dim(whole, part, (rank ^ key) * rows, 0)
    return whole


def row_blocks(value, count):
    rows = value.shape[0] // count
    return [value[k * rows : (k + 1) * rows] for k in range(count)]


def layer_norm(values, gain):
    mean = jnp.mean(values, axis=-1, keepdims=True)
    centred = values - mean
    spread = jnp.mean(centred * centred, axis=-1, keepdims=True)
    return centred * lax.rsqrt(spread + EPS) * gain


def swiglu(gate, up):
    return jax.nn.silu(gate) * up


def dot_in(left, right, axes, precision=None):
    return lax.dot_general(
        left, right, (axes, ((), ())), precision=precision, preferred_element_type=WIDE
    )


def contract_rows(left, right):
    return dot_in(left, right, ((0,), (0,)))


def contract_cols(left, right):
    return dot_in(left, right, ((1,), (1,)))


def halves(value):
    high = value.astype(NARROW)
    return high, (value - high.astype(WIDE)).astype(NARROW)


def turn(piece, cosine, sine):
    lane = lax.broadcasted_iota(jnp.int32, piece.shape, 1) % HEAD_DIM
    half = HEAD_DIM // 2
    ahead = pltpu.roll(piece, PAIR - half, 1)
    behind = pltpu.roll(piece, half, 1)
    return piece * cosine + jnp.where(lane < half, -ahead, behind) * sine


def rotary_tables(places):
    half = HEAD_DIM // 2
    column = (jnp.arange(PAIR) % half).astype(WIDE)
    freq = ROPE_BASE ** (-2.0 * column / HEAD_DIM)
    angle = places.astype(WIDE)[:, None] * freq[None, :]
    return (jnp.cos(angle), jnp.sin(angle))


def project_kernel(count, x_ref, *refs):
    weights, (cos_ref, sin_ref), outs = refs[:count], refs[count : count + 2], refs[count + 2 :]
    x, cosine, sine = x_ref[...], cos_ref[...], sin_ref[...]
    for kind, (w_ref, out_ref) in enumerate(zip(weights, outs), 3 - count):
        for at in range(0, out_ref.shape[1], 2 * PAIR):
            flat = jnp.dot(x, w_ref[:, at : at + 2 * PAIR], preferred_element_type=WIDE)
            for start in range(0, 2 * PAIR, PAIR):
                piece = flat[:, start : start + PAIR]
                if kind < 2:
                    piece = turn(piece, cosine, sine)
                piece = piece.astype(NARROW)
                if kind == 0:
                    piece = (piece.astype(WIDE) * HEAD_DIM ** (-0.5)).astype(NARROW)
                out_ref[:, at + start : at + start + PAIR] = piece


def project(count, x, weight, cosine, sine):
    rows, width = x.shape
    still = lambda i: (0, 0)
    block = pl.BlockSpec((rows, width), still)
    lanes = pl.BlockSpec((rows, PAIR), still)
    return pl.pallas_call(
        functools.partial(project_kernel, count),
        grid=(1,),
        in_specs=[block]
        + [weight_block(width, width, kind) for kind in range(3 - count, 3)]
        + [lanes, lanes],
        out_specs=[block] * count,
        out_shape=[jax.ShapeDtypeStruct((rows, width), NARROW)] * count,
        compiler_params=params(20),
        cost_estimate=pl.CostEstimate(
            flops=2 * count * rows * width * width,
            bytes_accessed=2 * count * width * (rows + width),
            transcendentals=0,
        ),
    )(x, *[weight] * count, cosine, sine)


def turn_table_kernel(table_ref, out_ref):
    rows, columns = table_ref.shape
    empty = jnp.zeros((columns, out_ref.shape[1] - rows), WIDE)
    for at in range(0, columns, 128):
        size = min(128, columns - at)
        piece = table_ref[:, at : at + size].astype(NARROW).astype(WIDE).T
        if rows < out_ref.shape[1]:
            piece = jnp.concatenate([piece, empty[:size]], axis=1)
        out_ref[at : at + size, :] = piece
    out_ref[columns:, :] = jnp.zeros((out_ref.shape[0] - columns, out_ref.shape[1]), WIDE)


def turned_table(table):
    rows, columns = table.shape
    lanes = -(-rows // 128) * 128
    return whole_call(
        turn_table_kernel, [((columns // 8 * 8 + 8, lanes), WIDE)], 8 * table.size, table
    )[0]


def lookup_kernel(row_count, start_ref, ids_ref, table_ref, out_ref, held):
    groups, block = out_ref.shape[1] // row_count, out_ref.shape[0]
    start = start_ref[0]
    for group in range(groups):

        def move(at, carry):
            base = start + (group * block + at * 8)
            for place in range(8):
                index = ids_ref[base + place]
                held[at, place : place + 1, :] = table_ref[pl.ds(index, 1), :]
            return carry

        lax.fori_loop(0, block // 8, move, 0, unroll=8)
        rows = held[...].reshape(block, held.shape[2])[:, :row_count]
        out_ref[:, group * row_count : (group + 1) * row_count] = rows.astype(NARROW)


def lookup(ids, table, start, groups, block, row_count):
    return pl.pallas_call(
        functools.partial(lookup_kernel, row_count),
        in_specs=[
            pl.BlockSpec(memory_space=pltpu.SMEM),
            pl.BlockSpec(memory_space=pltpu.SMEM),
            pl.BlockSpec(memory_space=pltpu.VMEM),
        ],
        out_specs=pl.BlockSpec(memory_space=pltpu.VMEM),
        out_shape=jax.ShapeDtypeStruct((block, groups * row_count), NARROW),
        scratch_shapes=[pltpu.VMEM((block // 8, 8, table.shape[1]), WIDE)],
        compiler_params=params(10),
        cost_estimate=pl.CostEstimate(
            flops=groups * block * 4096, bytes_accessed=4 * table.size, transcendentals=0
        ),
    )(start, ids, table)


def norm_parts(values):
    mean = jnp.mean(values, axis=-1, keepdims=True)
    centred = values - mean
    scale = lax.rsqrt(jnp.mean(centred * centred, axis=-1, keepdims=True) + EPS)
    return centred * scale, scale


def norm_back(grad, values, gain):
    unit, scale = norm_parts(values)
    inner = grad * gain
    first = jnp.mean(inner, axis=-1, keepdims=True)
    second = jnp.mean(inner * unit, axis=-1, keepdims=True)
    return (inner - first - unit * second) * scale, jnp.sum(grad * unit, axis=0, keepdims=True)


def whole_call(kernel, outs, flops, *operands):
    moved = sum(operand.size * operand.dtype.itemsize for operand in operands)
    moved += sum(math.prod(shape) * jnp.dtype(kind).itemsize for shape, kind in outs)
    budget = 8 + moved * 2 // (1 << 20)
    return pl.pallas_call(
        kernel,
        out_shape=[jax.ShapeDtypeStruct(shape, kind) for shape, kind in outs],
        compiler_params=params(budget),
        cost_estimate=pl.CostEstimate(
            flops=flops,
            bytes_accessed=sum(4 * operand.size for operand in operands),
            transcendentals=0,
        ),
    )(*operands)


def norm_kernel(gain_ref, *refs):
    inputs, (out_ref, narrow_ref) = refs[:-2], refs[-2:]
    total = inputs[0][...].astype(WIDE)
    for ref in inputs[1:]:
        total = total + ref[...].astype(WIDE)
    out = norm_parts(total)[0] * gain_ref[...]
    out_ref[...] = out
    narrow_ref[...] = out.astype(NARROW)


def norm_forward(gain, *parts):
    shape = parts[0].shape
    return whole_call(norm_kernel, [(shape, WIDE), (shape, NARROW)], 20 * parts[0].size, gain, *parts)


def merge_kernel(attended_ref, weight_ref, x_ref, gain_ref, narrow_out, pre_ref, out_ref, out_b_ref):
    narrow = attended_ref[...].astype(NARROW)
    narrow_out[...] = narrow
    pre = x_ref[...] + contract_rows(narrow, weight_ref[...])
    pre_ref[...] = pre
    out = norm_parts(pre)[0] * gain_ref[...]
    out_ref[...] = out
    out_b_ref[...] = out.astype(NARROW)


def merge_branch(attended_t, weight, x_zero, gain):
    rows, width = x_zero.shape
    shape = (rows, width)
    return whole_call(
        merge_kernel,
        [((width, rows), NARROW), (shape, WIDE), (shape, WIDE), (shape, NARROW)],
        2 * rows * width * width,
        attended_t,
        weight,
        x_zero,
        gain,
    )


def last_kernel(length_ref, slots_ref, rows_ref, pooled_ref, hidden_ref, local_ref, got_ref, gain_ref, out_ref, narrow_ref, sum_ref):
    total = hidden_ref[...] + local_ref[...].astype(WIDE) + got_ref[...].astype(WIDE)
    spread = rows_ref[...]
    place = lax.broadcasted_iota(jnp.int32, (total.shape[0], slots_ref.shape[1]), 0)
    hot = (place == slots_ref[...]).astype(WIDE).astype(NARROW)
    high, low = halves(spread)
    grad = jnp.dot(hot, high, preferred_element_type=WIDE)
    grad = grad + jnp.dot(hot, low, preferred_element_type=WIDE)
    index = lax.broadcasted_iota(jnp.int32, (total.shape[0], 1), 0)
    grad = grad + jnp.where(index < length_ref[0], pooled_ref[...], 0.0)
    out, gain_grad = norm_back(grad, total, gain_ref[...])
    out_ref[...] = out
    narrow_ref[...] = out.astype(NARROW)
    sum_ref[...] = gain_grad


def last_back(length, slots, row_grad, pooled_grad, hidden_in, local, got, gain):
    shape = hidden_in.shape
    return pl.pallas_call(
        last_kernel,
        in_specs=[pl.BlockSpec(memory_space=pltpu.SMEM)]
        + [pl.BlockSpec(memory_space=pltpu.VMEM)] * 7,
        out_shape=[
            jax.ShapeDtypeStruct(shape, WIDE),
            jax.ShapeDtypeStruct(shape, NARROW),
            jax.ShapeDtypeStruct((1, shape[1]), WIDE),
        ],
        compiler_params=params(24),
        cost_estimate=pl.CostEstimate(
            flops=200 * hidden_in.size, bytes_accessed=20 * hidden_in.size, transcendentals=0
        ),
    )(length, slots, row_grad, pooled_grad, hidden_in, local, got, gain)


def branch_back_kernel(grad_ref, local_ref, got_ref, pre_ref, gain_ref, weight_ref, out_ref, narrow_ref, attended_ref, sum_ref):
    grad = grad_ref[...] + local_ref[...].astype(WIDE) + got_ref[...].astype(WIDE)
    out, gain_grad = norm_back(grad, pre_ref[...], gain_ref[...])
    narrow = out.astype(NARROW)
    out_ref[...] = out
    narrow_ref[...] = narrow
    sum_ref[...] = gain_grad
    attended_ref[...] = contract_cols(narrow, weight_ref[...]).astype(NARROW)


def branch_back(pre_grad, local, got, pre_one, gain, weight):
    rows, width = pre_grad.shape
    shape = (rows, width)
    return whole_call(
        branch_back_kernel,
        [(shape, WIDE), (shape, NARROW), (shape, NARROW), ((1, width), WIDE)],
        2 * rows * width * width,
        pre_grad,
        local,
        got,
        pre_one,
        gain,
        weight,
    )


def first_back_kernel(grad_ref, dq_ref, weight_ref, local_ref, got_ref, value_ref, gain_ref, out_ref, sum_ref):
    grad = grad_ref[...] + local_ref[...].astype(WIDE) + got_ref[...].astype(WIDE)
    grad = grad + contract_cols(dq_ref[...], weight_ref[...])
    out, gain_grad = norm_back(grad, value_ref[...].astype(WIDE), gain_ref[...])
    out_ref[...] = out.astype(NARROW)
    sum_ref[...] = gain_grad


def first_back(pre_one_grad, dq, weight, local, got, embedded, gain):
    rows, width = pre_one_grad.shape
    return whole_call(
        first_back_kernel,
        [((rows, width), NARROW), ((1, width), WIDE)],
        2 * rows * width * width,
        pre_one_grad,
        dq,
        weight,
        local,
        got,
        embedded,
        gain,
    )


def ffn_step(x_ref, weights, gate_out, up_out, act_ref, x_out, out_ref):
    gate_ref, up_ref, down_ref = weights
    x = x_ref[...]
    gate = jnp.dot(x, gate_ref[...], preferred_element_type=WIDE)
    up = jnp.dot(x, up_ref[...], preferred_element_type=WIDE)
    gate_out[...] = gate
    up_out[...] = up
    act = (gate / (1.0 + jnp.exp(-gate)) * up).astype(NARROW)
    act_ref[...] = act
    x_out[...] = x
    out_ref[...] = contract_cols(act, down_ref[...]).astype(NARROW)


def ffn_kernel(first_ref, second_ref, *refs):
    weights, kept, outs = refs[:3], refs[3:7], refs[7:]
    for step, x_ref in enumerate((first_ref, second_ref)):

        @pl.when(pl.program_id(0) == step)
        def _():
            ffn_step(x_ref, weights, *kept, outs[step])


def weight_block(width, hidden, index):
    return pl.BlockSpec((width, hidden), lambda i: (0, index))


def ffn_forward(first, second, weights, hidden):
    rows, width = first.shape
    whole = pl.BlockSpec((rows, width), lambda i: (0, 0))
    tall = lambda i: (i, 0)
    return pl.pallas_call(
        ffn_kernel,
        grid=(2,),
        in_specs=[whole, whole] + [weight_block(width, hidden, k) for k in range(1, 4)],
        out_specs=[pl.BlockSpec((rows, hidden), tall)] * 3
        + [pl.BlockSpec((rows, width), tall), whole, whole],
        out_shape=[
            jax.ShapeDtypeStruct((2 * rows, hidden), WIDE),
            jax.ShapeDtypeStruct((2 * rows, hidden), WIDE),
            jax.ShapeDtypeStruct((2 * rows, hidden), NARROW),
            jax.ShapeDtypeStruct((2 * rows, width), NARROW),
            jax.ShapeDtypeStruct((rows, width), NARROW),
            jax.ShapeDtypeStruct((rows, width), NARROW),
        ],
        compiler_params=params(32),
        cost_estimate=pl.CostEstimate(
            flops=12 * rows * width * hidden,
            bytes_accessed=28 * rows * width + 6 * width * hidden,
            transcendentals=2 * rows * hidden,
        ),
    )(first, second, weights, weights, weights)


def ffn_back_step(grad_ref, gate_in, up_in, weights, dgate_ref, dup_ref, grad_out, out_ref):
    gate_ref, up_ref, down_ref = weights
    grad = grad_ref[...]
    grad_out[...] = grad
    act_grad = jnp.dot(grad, down_ref[...], preferred_element_type=WIDE)
    gate, up = gate_in[...], up_in[...]
    share = 1.0 / (1.0 + jnp.exp(-gate))
    dgate = (act_grad * up * (share * (1.0 + gate * (1.0 - share)))).astype(NARROW)
    dup = (act_grad * (gate * share)).astype(NARROW)
    dgate_ref[...] = dgate
    dup_ref[...] = dup
    out_ref[...] = (
        contract_cols(dgate, gate_ref[...]) + contract_cols(dup, up_ref[...])
    ).astype(NARROW)


def ffn_back_kernel(first_ref, second_ref, gate_in, up_in, *refs):
    weights, kept, outs = refs[:3], refs[3:6], refs[6:]
    for step, grad_ref in enumerate((first_ref, second_ref)):

        @pl.when(pl.program_id(0) == step)
        def _():
            ffn_back_step(grad_ref, gate_in, up_in, weights, *kept, outs[step])


def ffn_backward(first, second, gate, up, weights):
    rows, width = first.shape
    hidden = gate.shape[1]
    whole = pl.BlockSpec((rows, width), lambda i: (0, 0))
    tall = lambda i: (i, 0)
    return pl.pallas_call(
        ffn_back_kernel,
        grid=(2,),
        in_specs=[whole, whole]
        + [pl.BlockSpec((rows, hidden), tall)] * 2
        + [weight_block(width, hidden, k) for k in range(1, 4)],
        out_specs=[pl.BlockSpec((rows, hidden), tall)] * 2
        + [pl.BlockSpec((rows, width), tall), whole, whole],
        out_shape=[
            jax.ShapeDtypeStruct((2 * rows, hidden), NARROW),
            jax.ShapeDtypeStruct((2 * rows, hidden), NARROW),
            jax.ShapeDtypeStruct((2 * rows, width), NARROW),
            jax.ShapeDtypeStruct((rows, width), NARROW),
            jax.ShapeDtypeStruct((rows, width), NARROW),
        ],
        compiler_params=params(34),
        cost_estimate=pl.CostEstimate(
            flops=12 * rows * width * hidden,
            bytes_accessed=32 * rows * width + 6 * width * hidden,
            transcendentals=2 * rows * hidden,
        ),
    )(first, second, gate, up, weights, weights, weights)


def input_kernel(first_k, first_v, second_k, second_v, key_ref, value_ref, *outs):
    for dk_ref, dv_ref, out_ref in zip((first_k, second_k), (first_v, second_v), outs):
        total = contract_cols(dk_ref[...], key_ref[...])
        total = total + contract_cols(dv_ref[...], value_ref[...])
        out_ref[...] = total.astype(NARROW)


def input_grads(first_k, first_v, second_k, second_v, weights):
    rows, width = first_k.shape
    whole = pl.BlockSpec((rows, width), lambda i: (0, 0))
    return pl.pallas_call(
        input_kernel,
        grid=(1,),
        in_specs=[whole] * 4 + [weight_block(width, width, k) for k in (1, 2)],
        out_specs=[whole] * 2,
        out_shape=[jax.ShapeDtypeStruct((rows, width), NARROW)] * 2,
        compiler_params=params(24),
        cost_estimate=pl.CostEstimate(
            flops=8 * rows * width * width,
            bytes_accessed=12 * rows * width + 4 * width * width,
            transcendentals=0,
        ),
    )(first_k, first_v, second_k, second_v, weights, weights)


def paired(value, work):
    near_bit, *far_bits = axis_bits("tensor")
    held = {0: value}
    for bit in reversed(far_bits):
        for key in sorted(held):
            held[key ^ bit] = swap(held[key], "tensor", bit)
    results, sums = [], {}
    for key in sorted(held):
        block = held[key]
        if results:
            block, _ = lax.optimization_barrier((block, results[-1][-1]))
        results.append(work(len(results), block, swap(block, "tensor", near_bit)))
        sums[key] = near_sum(*results[-1][-2:])
    return results, sums


def near_sum(own, other):
    got = swap(other, "tensor", axis_bits("tensor")[0])
    return (own.astype(WIDE) + got.astype(WIDE)).astype(NARROW)


def far_sum(sums):
    sums = dict(sums)
    near_bit, *far_bits = axis_bits("tensor")
    for bit in far_bits[:-1]:
        for key in sorted(k for k in sums if not k & bit):
            got = swap(sums.pop(key ^ bit), "tensor", bit)
            sums[key] = (sums[key].astype(WIDE) + got.astype(WIDE)).astype(NARROW)
    return sums[0], sums[far_bits[-1]], swap(sums[far_bits[-1]], "tensor", far_bits[-1])


def logits_kernel(columns, tile, rows_ref, table_ref, targets_ref, out_ref, stats_ref, top_ref, sum_ref, hit_ref):
    step = pl.program_id(0)

    @pl.when(step == 0)
    def _():
        top_ref[...] = jnp.full(top_ref.shape, NEGATIVE, WIDE)
        sum_ref[...] = jnp.zeros(sum_ref.shape, WIDE)
        hit_ref[...] = jnp.zeros(hit_ref.shape, WIDE)

    logits = jnp.dot(rows_ref[...], table_ref[...], preferred_element_type=WIDE)
    out_ref[...] = logits
    place = step * tile + lax.broadcasted_iota(jnp.int32, (1, tile), 1)
    seen = jnp.where(place < columns, logits, NEGATIVE)
    hits = jnp.where((place == targets_ref[...]) & (place < columns), seen, 0.0)
    pieces = [slice(at, at + 128) for at in range(0, tile, 128)]
    before = top_ref[...]
    top = before
    for piece in pieces:
        top = jnp.maximum(top, seen[:, piece])
    total = sum_ref[...] * jnp.exp(before - top)
    hit = hit_ref[...]
    for piece in pieces:
        total = total + jnp.exp(seen[:, piece] - top)
        hit = hit + hits[:, piece]
    top_ref[...] = top
    sum_ref[...] = total
    hit_ref[...] = hit

    @pl.when(step == pl.num_programs(0) - 1)
    def _():
        peak = jnp.max(top, axis=1, keepdims=True)
        whole = jnp.sum(total * jnp.exp(top - peak), axis=1, keepdims=True)
        found = jnp.sum(hit, axis=1, keepdims=True)
        lane = lax.broadcasted_iota(jnp.int32, (1, 128), 1)
        stats_ref[...] = jnp.where(
            lane == 0, peak, jnp.where(lane == 1, whole, jnp.where(lane == 2, found, 0.0))
        )


def vocab_logits(rows_all, table, targets):
    picks, width = rows_all.shape
    columns = table.shape[1]
    tiles = -(-columns // TILE)
    tile = WIDE_TILE
    still = lambda j: (0, 0)
    along = lambda j: (0, j)
    return pl.pallas_call(
        functools.partial(logits_kernel, columns, tile),
        grid=(tiles * TILE // tile,),
        in_specs=[
            pl.BlockSpec((picks, width), still),
            pl.BlockSpec((width, tile), along),
            pl.BlockSpec((picks, 1), still),
        ],
        out_specs=[pl.BlockSpec((picks, tile), along), pl.BlockSpec((picks, 128), still)],
        out_shape=[
            jax.ShapeDtypeStruct((picks, tiles * TILE), WIDE),
            jax.ShapeDtypeStruct((picks, 128), WIDE),
        ],
        scratch_shapes=[pltpu.VMEM((picks, 128), WIDE)] * 3,
        compiler_params=params(56),
        cost_estimate=pl.CostEstimate(
            flops=2 * picks * width * columns,
            bytes_accessed=2 * width * columns,
            transcendentals=picks * columns,
        ),
    )(rows_all, table, targets)


def combine_kernel(count, slots, bit, mine_ref, other_ref, out_ref):
    lane = lax.broadcasted_iota(jnp.int32, (1, 128), 1)
    for block in range(count):
        mine = mine_ref[block * slots : (block + 1) * slots, :]
        other = other_ref[(block ^ bit) * slots : ((block ^ bit) + 1) * slots, :]
        peak = jnp.maximum(mine[:, :1], other[:, :1])
        total = mine[:, 1:2] * jnp.exp(mine[:, :1] - peak)
        total = total + other[:, 1:2] * jnp.exp(other[:, :1] - peak)
        out_ref[block * slots : (block + 1) * slots, :] = jnp.where(
            lane == 0, peak, jnp.where(lane == 1, total, mine + other)
        )
    rest = count * slots
    out_ref[rest:, :] = mine_ref[rest:, :] + other_ref[rest:, :]


def dlogits_kernel(columns, tile, logits_ref, table_ref, targets_ref, stats_ref, weight_ref, out_ref, grad_ref):
    step = pl.program_id(0)
    log_all = stats_ref[:, :1] + jnp.log(stats_ref[:, 1:2])
    place = step * tile + lax.broadcasted_iota(jnp.int32, (1, tile), 1)
    share = jnp.exp(logits_ref[...] - log_all) - jnp.where(place == targets_ref[...], 1.0, 0.0)
    grad = jnp.where(place < columns, share * weight_ref[...], 0.0).astype(NARROW)
    out_ref[...] = grad
    column = step * tile + lax.broadcasted_iota(jnp.int32, (1, tile), 1)
    table = jnp.where(column < columns, table_ref[...].astype(WIDE), 0.0).astype(NARROW)
    part = contract_cols(grad, table)

    @pl.when(step == 0)
    def _():
        grad_ref[...] = part

    @pl.when(step > 0)
    def _():
        grad_ref[...] += part


def vocab_back(logits, table, targets, stats, weight):
    picks = targets.shape[0]
    width, columns = table.shape
    tile = WIDE_TILE
    still = lambda j: (0, 0)
    along = lambda j: (0, j)
    return pl.pallas_call(
        functools.partial(dlogits_kernel, columns, tile),
        grid=(logits.shape[1] // tile,),
        in_specs=[
            pl.BlockSpec((picks, tile), along),
            pl.BlockSpec((width, tile), along),
            pl.BlockSpec((picks, 1), still),
            pl.BlockSpec((picks, 128), still),
            pl.BlockSpec((picks, 1), still),
        ],
        out_specs=[pl.BlockSpec((picks, tile), along), pl.BlockSpec((picks, width), still)],
        out_shape=[
            jax.ShapeDtypeStruct(logits.shape, NARROW),
            jax.ShapeDtypeStruct((picks, width), WIDE),
        ],
        compiler_params=params(56),
        cost_estimate=pl.CostEstimate(
            flops=2 * picks * width * columns,
            bytes_accessed=2 * width * columns,
            transcendentals=picks * columns,
        ),
    )(logits, table, targets, stats, weight)


def contrast_kernel(weight, length_ref, pooled_ref, keys_ref, blocked_ref, target_ref, grad_ref, part_ref):
    length = length_ref[0].astype(WIDE)
    pooled = pooled_ref[...] / length
    scale = lax.rsqrt(jnp.sum(pooled * pooled, axis=-1, keepdims=True) + EPS)
    narrow = jnp.broadcast_to(pooled * scale, (8, pooled.shape[1])).astype(NARROW)
    keys = keys_ref[...]
    scores = contract_cols(narrow, keys)[:1] / TAU
    target = target_ref[...]
    masked = jnp.where(blocked_ref[...] > 0.0, NEGATIVE, scores)
    top = jnp.max(masked, axis=-1, keepdims=True)
    log_c = top + jnp.log(jnp.sum(jnp.exp(masked - top), axis=-1, keepdims=True))
    chosen = jnp.sum(jnp.where(target > 0.0, scores, 0.0), axis=-1, keepdims=True)
    part_ref[...] = jnp.broadcast_to((log_c - chosen) * weight, part_ref.shape)
    dscores = ((jnp.exp(masked - log_c) - target) * (weight / TAU)).astype(NARROW)
    dscores = jnp.broadcast_to(dscores.astype(WIDE), (8, dscores.shape[1])).astype(NARROW)
    grad = jnp.dot(dscores, keys, preferred_element_type=WIDE)[:1]
    inner = jnp.sum(pooled * grad, axis=-1, keepdims=True)
    grad_ref[...] = (grad - pooled * (inner * scale * scale)) * scale / length


def contrast(weight, length, pooled_sum, keys_hat, blocked, target):
    width = pooled_sum.shape[1]
    return pl.pallas_call(
        functools.partial(contrast_kernel, weight),
        in_specs=[pl.BlockSpec(memory_space=pltpu.SMEM)]
        + [pl.BlockSpec(memory_space=pltpu.VMEM)] * 4,
        out_shape=[
            jax.ShapeDtypeStruct((1, width), WIDE),
            jax.ShapeDtypeStruct((1, 128), WIDE),
        ],
        compiler_params=params(8),
        cost_estimate=pl.CostEstimate(
            flops=4 * keys_hat.size, bytes_accessed=2 * keys_hat.size, transcendentals=0
        ),
    )(length, pooled_sum, keys_hat, blocked, target)


def head_lanes(head):
    lane = lax.broadcasted_iota(jnp.int32, (1, PAIR), 1)
    return (lane // HEAD_DIM) == head, lane == HEAD_DIM * (1 - head)


def attend_kernel(count, q_ref, *refs):
    k_refs, v_refs, bias_refs = refs[:count], refs[count : 2 * count], refs[2 * count : 3 * count]
    out_ref, log_ref, s_ref = refs[3 * count :]
    head = pl.program_id(1)
    mine, spare = head_lanes(head)
    step = k_refs[0].shape[0]
    blocks = [pl.ds(k * step, step) for k in range(count)]
    query = jnp.where(spare, 1.0, jnp.where(mine, q_ref[...].astype(WIDE), 0.0)).astype(NARROW)
    top = None
    for rows, k_ref, bias_ref in zip(blocks, k_refs, bias_refs):
        key = jnp.where(spare, bias_ref[...].astype(WIDE), k_ref[...].astype(WIDE))
        scores = contract_cols(key.astype(NARROW), query)
        s_ref[rows, :] = scores
        peak = jnp.max(scores, axis=0, keepdims=True)
        top = peak if top is None else jnp.maximum(top, peak)
    total = None
    for rows in blocks:
        powers = jnp.exp(s_ref[rows, :] - top)
        s_ref[rows, :] = powers
        part = jnp.sum(powers, axis=0, keepdims=True)
        total = part if total is None else total + part
    share = 1.0 / total
    result = None
    for rows, v_ref in zip(blocks, v_refs):
        probs = (s_ref[rows, :] * share).astype(NARROW)
        part = contract_rows(v_ref[...], probs)
        result = part if result is None else result + part
    log_ref[0, pl.ds(head, 1), :] = top + jnp.log(total)

    @pl.when(head == 0)
    def _():
        out_ref[...] = result

    @pl.when(head == 1)
    def _():
        out_ref[HEAD_DIM:, :] = result[HEAD_DIM:, :]


def attention_forward(queries, keys, values, biases):
    rows, width = queries.shape
    count = len(keys)
    length = rows * count
    pairs = width // PAIR
    lanes = pl.BlockSpec((rows, PAIR), lambda i, h: (0, i))
    still = pl.BlockSpec((rows, PAIR), lambda i, h: (0, 0))
    return pl.pallas_call(
        functools.partial(attend_kernel, count),
        grid=(pairs, 2),
        in_specs=[lanes] * (1 + 2 * count) + [still] * count,
        out_specs=[
            pl.BlockSpec((PAIR, rows), lambda i, h: (i, 0)),
            pl.BlockSpec((1, 2, rows), lambda i, h: (i, 0, 0)),
        ],
        out_shape=[
            jax.ShapeDtypeStruct((width, rows), WIDE),
            jax.ShapeDtypeStruct((pairs, 2, rows), WIDE),
        ],
        scratch_shapes=[pltpu.VMEM((length, rows), WIDE)],
        compiler_params=params(22),
        cost_estimate=pl.CostEstimate(
            flops=4 * rows * length * width,
            bytes_accessed=4 * length * width + 8 * rows * width,
            transcendentals=rows * length * HEADS,
        ),
    )(queries, *keys, *values, *biases)


def attend_back_kernel(count, q_ref, grad_ref, out_ref, log_ref, *refs):
    groups = [refs[k * count : (k + 1) * count] for k in range(5)]
    k_refs, v_refs, bias_refs, cos_refs, sin_refs = groups
    rest = refs[5 * count :]
    dq_ref, dk_refs, dv_refs = rest[0], rest[1 : 1 + count], rest[1 + count : 1 + 2 * count]
    dk_sum, dv_sum, dq_sum, key_all, value_all = rest[1 + 2 * count :]
    head = pl.program_id(1)
    mine, spare = head_lanes(head)
    step, scale = k_refs[0].shape[0], HEAD_DIM ** (-0.5)
    own = jnp.where(mine, q_ref[...].astype(WIDE), 0.0)
    query = own.astype(NARROW)
    asked = jnp.where(spare, 1.0, own).astype(NARROW)
    grad_wide = jnp.where(mine, grad_ref[...].astype(WIDE), 0.0)
    grad = grad_wide.astype(NARROW)
    delta = jnp.sum(grad_wide.T * out_ref[...], axis=0, keepdims=True)
    log_total = log_ref[0, pl.ds(head, 1), :]
    for k in range(count):
        rows = pl.ds(k * step, step)
        key = jnp.where(spare, bias_refs[k][...].astype(WIDE), k_refs[k][...].astype(WIDE))
        key_all[rows, :] = key.astype(NARROW)
        value_all[rows, :] = v_refs[k][...]
    keys = key_all[...]
    probs = jnp.exp(contract_cols(keys, asked) - log_total)
    dprobs = contract_cols(value_all[...], grad)
    dv = jnp.dot(probs.astype(NARROW), grad, preferred_element_type=WIDE)
    dscores = (probs * (dprobs - delta)).astype(NARROW)
    dk = jnp.dot(dscores, query, preferred_element_type=WIDE)
    dq = contract_rows(keys, dscores)

    @pl.when(head == 0)
    def _():
        dk_sum[...] = dk
        dv_sum[...] = dv

    @pl.when(head == 1)
    def _():
        key_grad, value_grad = dk_sum[...] + dk, dv_sum[...] + dv
        for k in range(count):
            rows = slice(k * step, (k + 1) * step)
            piece = turn(key_grad[rows], cos_refs[k][...], -sin_refs[k][...])
            dk_refs[k][...] = piece.astype(NARROW)
            dv_refs[k][...] = value_grad[rows].astype(NARROW)

    @pl.when(head == 0)
    def _():
        dq_sum[...] = dq

    @pl.when(head == 1)
    def _():
        dq_sum[HEAD_DIM:, :] = dq[HEAD_DIM:, :]
        total = dq_sum[...].T * scale
        dq_ref[...] = turn(total, cos_refs[0][...], -sin_refs[0][...]).astype(NARROW)


def attention_backward(queries, keys, values, biases, grad, out_t, log_total, cosines, sines):
    rows, width = queries.shape
    count = len(keys)
    length = rows * count
    pairs = width // PAIR
    lanes = pl.BlockSpec((rows, PAIR), lambda i, h: (0, i))
    still = pl.BlockSpec((rows, PAIR), lambda i, h: (0, 0))
    found = pl.pallas_call(
        functools.partial(attend_back_kernel, count),
        grid=(pairs, 2),
        in_specs=[
            lanes,
            lanes,
            pl.BlockSpec((PAIR, rows), lambda i, h: (i, 0)),
            pl.BlockSpec((1, 2, rows), lambda i, h: (i, 0, 0)),
        ]
        + [lanes] * (2 * count)
        + [still] * (3 * count),
        out_specs=[lanes] * (1 + 2 * count),
        out_shape=[jax.ShapeDtypeStruct((rows, width), NARROW)] * (1 + 2 * count),
        scratch_shapes=[
            pltpu.VMEM((length, PAIR), WIDE),
            pltpu.VMEM((length, PAIR), WIDE),
            pltpu.VMEM((PAIR, rows), WIDE),
            pltpu.VMEM((length, PAIR), NARROW),
            pltpu.VMEM((length, PAIR), NARROW),
        ],
        compiler_params=params(56),
        cost_estimate=pl.CostEstimate(
            flops=10 * rows * length * width,
            bytes_accessed=8 * length * width + 8 * rows * width,
            transcendentals=rows * length * HEADS,
        ),
    )(queries, grad, out_t, log_total, *keys, *values, *biases, *cosines, *sines)
    return found[0], found[1 : 1 + count], found[1 + count :]


def project_down(matrix, factor_t):
    high, low = halves(matrix)
    factor_high, factor_low = halves(factor_t)
    both = jnp.concatenate([factor_high, factor_low], axis=0)
    first = jnp.dot(both, high, preferred_element_type=WIDE)
    second = jnp.dot(factor_high, low, preferred_element_type=WIDE)
    return first[:RANK] + first[RANK:] + second


def project_back(matrix, basis_t):
    high, low = halves(matrix)
    basis_high, basis_low = halves(basis_t)
    both = jnp.concatenate([basis_high, basis_low], axis=0)
    first = contract_cols(both, high)
    second = contract_cols(basis_high, low)
    return first[:RANK] + first[RANK:] + second


def expand(back_t, basis_t):
    back_high, back_low = halves(back_t)
    basis_high, basis_low = halves(basis_t)
    left = jnp.concatenate([back_high, back_low, back_high], axis=0)
    right = jnp.concatenate([basis_high, basis_high, basis_low], axis=0)
    return contract_rows(left, right)


def table_kernel(columns, first, starts_ref, left_ref, tokens_ref, rows_ref, dlogits_ref, error_ref, factor_ref, high_ref, low_ref, p_ref, sum_ref):
    tile = first + pl.program_id(0)
    place = tile * TILE + lax.broadcasted_iota(jnp.int32, (TILE, 1), 0)
    sum_ref[...] = error_ref[...] + contract_rows(dlogits_ref[...], rows_ref[...])

    def visit(chunk, carry):
        at = pl.ds(pl.multiple_of(chunk * CHUNK, CHUNK), CHUNK)
        hot = jnp.where(tokens_ref[:, at] == place, 1.0, 0.0).astype(NARROW)
        sum_ref[...] += jnp.dot(hot, left_ref[at, :], preferred_element_type=WIDE)
        return carry

    lax.fori_loop(
        starts_ref[tile] // CHUNK, (starts_ref[tile + 1] + CHUNK - 1) // CHUNK, visit, 0
    )
    total = jnp.where(place < columns, sum_ref[...], 0.0)
    high, low = halves(total)
    high_ref[...] = high
    low_ref[...] = low
    factor_high, factor_low = halves(factor_ref[...])
    both = jnp.concatenate([factor_high, factor_low], axis=0)
    found = contract_cols(high, both).T
    rest = contract_cols(low, both).T
    p_ref[...] = found[:RANK] + found[RANK:] + rest[:RANK]


def table_matrix(bounds, starts, left, tokens, rows, dlogits, error, factor_t):
    columns, width = error.shape
    slots = left.shape[0]
    picks = rows.shape[0]
    first, tiles = bounds[0], bounds[1] - bounds[0]
    still = lambda j: (0, 0)
    down = lambda j: (j, 0)
    return pl.pallas_call(
        functools.partial(table_kernel, columns, first),
        grid=(tiles,),
        in_specs=[
            pl.BlockSpec(memory_space=pltpu.SMEM),
            pl.BlockSpec((slots, width), still),
            pl.BlockSpec((1, slots), still),
            pl.BlockSpec((picks, width), still),
            pl.BlockSpec((picks, TILE), lambda j: (0, first + j)),
            pl.BlockSpec((TILE, width), lambda j: (first + j, 0)),
            pl.BlockSpec((RANK, width), still),
        ],
        out_specs=[
            pl.BlockSpec((TILE, width), down),
            pl.BlockSpec((TILE, width), down),
            pl.BlockSpec((RANK, TILE), lambda j: (0, j)),
        ],
        out_shape=[
            jax.ShapeDtypeStruct((tiles * TILE, width), NARROW),
            jax.ShapeDtypeStruct((tiles * TILE, width), NARROW),
            jax.ShapeDtypeStruct((RANK, tiles * TILE), WIDE),
        ],
        scratch_shapes=[pltpu.VMEM((TILE, width), WIDE)],
        compiler_params=params(32),
        cost_estimate=pl.CostEstimate(
            flops=2 * width * tiles * TILE * (slots // 4 + picks + 24),
            bytes_accessed=8 * width * tiles * TILE,
            transcendentals=0,
        ),
    )(starts, left, tokens, rows, dlogits, error, factor_t)


def partial_kernel(*refs):
    count = (len(refs) - 1) // 2
    for index in range(count):
        refs[-1][index] = project_down(refs[index][...], refs[count + index][...])


def partial_projections(matrices, factors_t):
    count, (width, columns) = len(matrices), matrices[0].shape
    return whole_call(
        partial_kernel,
        [((count, RANK, columns), WIDE)],
        48 * count * width * columns,
        *matrices,
        *factors_t,
    )[0]


def small_kernel(count, *refs):
    grads, errors, factor_ref = refs[:count], refs[count : 2 * count], refs[2 * count]
    m_ref, p_ref = refs[2 * count + 1 :]
    for index in range(count):
        total = grads[index][...] + errors[index][...]
        m_ref[index] = total
        p_ref[index] = project_down(total, factor_ref[index])


def small_matrices(grads, errors, factor_t):
    count, (width, columns) = len(grads), grads[0].shape
    block = columns // 3
    tall = pl.BlockSpec((width, block), lambda j: (0, j))
    return pl.pallas_call(
        functools.partial(small_kernel, count),
        grid=(3,),
        in_specs=[tall] * (2 * count)
        + [pl.BlockSpec((count, RANK, width), lambda j: (0, 0, 0))],
        out_specs=[
            pl.BlockSpec((count, width, block), lambda j: (0, 0, j)),
            pl.BlockSpec((count, RANK, block), lambda j: (0, 0, j)),
        ],
        out_shape=[
            jax.ShapeDtypeStruct((count, width, columns), WIDE),
            jax.ShapeDtypeStruct((count, RANK, columns), WIDE),
        ],
        compiler_params=params(56),
        cost_estimate=pl.CostEstimate(
            flops=48 * count * width * columns,
            bytes_accessed=12 * count * width * columns,
            transcendentals=0,
        ),
    )(*grads, *errors, factor_t)


def basis_kernel(spans, p_ref, out_ref):
    index = lax.broadcasted_iota(jnp.int32, (RANK, 1), 0)
    for start, size in spans:
        rows = p_ref[:, pl.ds(start, size)]
        for place in range(RANK):
            row = rows[place : place + 1, :]
            row = row * lax.rsqrt(jnp.sum(row * row, axis=1, keepdims=True))
            inner = jnp.sum(rows * row, axis=1, keepdims=True)
            rows = jnp.where(index == place, row, rows - jnp.where(index > place, inner, 0.0) * row)
        out_ref[:, pl.ds(start, size)] = rows


def bases_of(sums, spans):
    return pl.pallas_call(
        functools.partial(basis_kernel, spans),
        out_shape=jax.ShapeDtypeStruct(sums.shape, WIDE),
        compiler_params=params(8),
        cost_estimate=pl.CostEstimate(
            flops=64 * sums.size, bytes_accessed=8 * sums.size, transcendentals=40
        ),
    )(sums)


def small_back_kernel(m_ref, basis_ref, back_ref):
    for index in range(m_ref.shape[0]):
        back_ref[index] = project_back(m_ref[index], basis_ref[index])


def small_backs(matrices, basis):
    count, width, columns = matrices.shape
    return pl.pallas_call(
        small_back_kernel,
        out_shape=jax.ShapeDtypeStruct((count, RANK, width), WIDE),
        compiler_params=params(24),
        cost_estimate=pl.CostEstimate(
            flops=48 * count * width * columns,
            bytes_accessed=4 * count * width * columns,
            transcendentals=0,
        ),
    )(matrices, basis)


def table_specs(parts, width):
    bounds, first = [], 0
    for part in parts:
        bounds.append((first, first + part.shape[0] // TILE))
        first = bounds[-1][1]
    specs = [
        pl.BlockSpec(
            (TILE, width), lambda j, low=low, high=high: (jnp.clip(j, low, high - 1) - low, 0)
        )
        for low, high in bounds
    ]
    return bounds, specs


def table_back_kernel(bounds, *refs):
    highs, lows = refs[: len(bounds)], refs[len(bounds) : 2 * len(bounds)]
    basis_ref, back_ref = refs[2 * len(bounds) :]
    step = pl.program_id(0)
    basis_high, basis_low = halves(basis_ref[...])
    both = jnp.concatenate([basis_high, basis_low], axis=0)

    @pl.when(step == 0)
    def _():
        back_ref[...] = jnp.zeros(back_ref.shape, WIDE)

    for (low, high), high_ref, low_ref in zip(bounds, highs, lows):

        @pl.when((step >= low) & (step < high))
        def _():
            first = jnp.dot(both, high_ref[...], preferred_element_type=WIDE)
            second = jnp.dot(basis_high, low_ref[...], preferred_element_type=WIDE)
            back_ref[...] += first[:RANK] + first[RANK:] + second


def table_back(highs, lows, basis):
    width = highs[0].shape[1]
    columns = basis.shape[1]
    bounds, specs = table_specs(highs, width)
    return pl.pallas_call(
        functools.partial(table_back_kernel, bounds),
        grid=(columns // TILE,),
        in_specs=specs + specs + [pl.BlockSpec((RANK, TILE), lambda j: (0, j))],
        out_specs=pl.BlockSpec((RANK, width), lambda j: (0, 0)),
        out_shape=jax.ShapeDtypeStruct((RANK, width), WIDE),
        compiler_params=params(18),
        cost_estimate=pl.CostEstimate(
            flops=48 * width * columns, bytes_accessed=4 * width * columns, transcendentals=0
        ),
    )(*highs, *lows, basis)


def small_error_kernel(m_ref, back_ref, basis_ref, *out_refs):
    count = m_ref.shape[0]
    for index in range(count):
        error = m_ref[index] - expand(back_ref[index], basis_ref[index])
        if count > 1 and index < 2:
            out_refs[0][:, index, :] = error
        else:
            out_refs[-1][...] = error


def small_errors(matrices, backs, basis):
    count, width, columns = matrices.shape
    return pl.pallas_call(
        small_error_kernel,
        out_shape=[jax.ShapeDtypeStruct((width, 2, columns), WIDE)] * (count - 1 > 0)
        + [jax.ShapeDtypeStruct((width, columns), WIDE)],
        compiler_params=params(32),
        cost_estimate=pl.CostEstimate(
            flops=48 * count * width * columns,
            bytes_accessed=8 * count * width * columns,
            transcendentals=0,
        ),
    )(matrices, backs, basis)


def table_error_kernel(bounds, *refs):
    highs, lows = refs[: len(bounds)], refs[len(bounds) : 2 * len(bounds)]
    back_ref, basis_ref, out_ref = refs[2 * len(bounds) :]
    step = pl.program_id(0)
    for (low, high), high_ref, low_ref in zip(bounds, highs, lows):

        @pl.when((step >= low) & (step < high))
        def _():
            whole = high_ref[...].astype(WIDE) + low_ref[...].astype(WIDE)
            out_ref[...] = whole - expand(basis_ref[...], back_ref[...])


def table_error(highs, lows, back, basis, columns):
    width = highs[0].shape[1]
    bounds, specs = table_specs(highs, width)
    return pl.pallas_call(
        functools.partial(table_error_kernel, bounds),
        grid=(basis.shape[1] // TILE,),
        in_specs=specs
        + specs
        + [
            pl.BlockSpec((RANK, width), lambda j: (0, 0)),
            pl.BlockSpec((RANK, TILE), lambda j: (0, j)),
        ],
        out_specs=pl.BlockSpec((TILE, width), lambda j: (j, 0)),
        out_shape=jax.ShapeDtypeStruct((columns, width), WIDE),
        compiler_params=params(24),
        cost_estimate=pl.CostEstimate(
            flops=48 * width * columns, bytes_accessed=8 * width * columns, transcendentals=0
        ),
    )(*highs, *lows, back, basis)


def normalize_keys(raw_keys):
    wide_keys = raw_keys.astype(WIDE)
    return (
        wide_keys * lax.rsqrt(jnp.sum(wide_keys * wide_keys, axis=-1, keepdims=True) + EPS)
    ).astype(NARROW)


def per_device(
    token_ids,
    seq_lengths,
    mask_slots,
    mask_targets,
    positive_rows,
    doc_ids,
    false_pairs,
    queue_docs,
    queue_embed,
    attend_weight,
    attend_moment,
    gate_up,
    gate_up_moment,
    down_weight,
    down_moment,
    embed_table,
    embed_moment,
    gains,
    gains_moment,
    attend_error,
    gate_up_error,
    down_error,
    embed_error,
    factors,
):
    tensor_count = lax.axis_size("tensor")
    tensor_rank = lax.axis_index("tensor")
    data_count = lax.axis_size("dp")
    data_rank = lax.axis_index("dp")
    groups, seq_len = token_ids.shape
    width = gains.shape[1]
    total_rows = groups * seq_len
    own_rows = total_rows // tensor_count
    slot_count = mask_slots.shape[2]
    seq_total = groups * data_count
    near = jnp.arange(tensor_count) ^ tensor_rank
    row_count = attend_weight.shape[0]

    tokens_all = lax.all_to_all(
        jnp.broadcast_to(token_ids, (data_count, seq_len)), "dp", 0, 0, tiled=True
    )
    vocab_own = embed_table.shape[1]
    vocab_start = tensor_rank * vocab_own
    ids = tokens_all - vocab_start
    ids = jnp.where((ids >= 0) & (ids < vocab_own), ids, vocab_own)
    table_local = embed_table.astype(NARROW)
    table_rows = turned_table(embed_table)
    ids = jnp.swapaxes(ids.reshape(data_count, tensor_count, own_rows), 0, 1).reshape(-1)
    looked, looked_sums = {}, {}
    for key in reversed(range(tensor_count)):
        start = ((tensor_rank ^ key) * (data_count * own_rows)).reshape(1)
        looked[key] = lookup(ids, table_rows, start, data_count, own_rows, row_count)
        if key == 1:
            for base in range(2, tensor_count, 2):
                looked_sums[base] = near_sum(looked[base], looked[base + 1])
            ids, looked_sums, looked[1] = lax.optimization_barrier((ids, looked_sums, looked[1]))
        elif key:
            ids, looked[key] = lax.optimization_barrier((ids, looked[key]))
    looked_sums[0] = near_sum(looked[0], looked[1])
    mine, _, got = far_sum(looked_sums)
    pieces = (mine + got).T.reshape(data_count, row_count, own_rows)
    soon = (jnp.minimum(data_rank, 0), token_ids, near)
    (none, near_ids, near_soon), pieces = lax.optimization_barrier((soon, pieces))
    near_tokens = picked_blocks(near_ids.reshape(tensor_count, own_rows), near_soon).reshape(1, -1)
    shifted = near_tokens - vocab_start
    tiles = -(-vocab_own // TILE)
    index = jnp.arange(total_rows)
    before = (shifted < shifted.T) | ((shifted == shifted.T) & (index[None, :] < index[:, None]))
    ranks = jnp.sum(before.astype(jnp.int32), axis=1)
    ordered = ranks[None, :] == index[:, None]
    sorted_ids = jnp.sum(jnp.where(ordered, shifted, 0), axis=1)[None, :]
    starts = jnp.sum(
        (shifted < jnp.minimum(jnp.arange(tiles + 1) * TILE, vocab_own)[:, None]).astype(jnp.int32),
        axis=1,
    )
    gate_error = lax.dynamic_slice_in_dim(gate_up_error[0], none, 1, 1)[:, 0]
    up_error = lax.dynamic_slice_in_dim(gate_up_error[0], none + 1, 1, 1)[:, 0]
    embedded = lax.all_to_all(pieces, "dp", 0, 0).reshape(width, own_rows).T

    attend_cols = attend_error.shape[2]
    quarter = lax.dynamic_slice_in_dim(attend_weight, tensor_rank * attend_cols, attend_cols, 1)
    queue_rows = queue_embed.shape[0] // tensor_count
    queue_own = lax.dynamic_slice_in_dim(queue_embed, tensor_rank * queue_rows, queue_rows, 0)
    joined = jnp.concatenate([quarter, gate_up[:, 0], gate_up[:, 1], down_weight], axis=1)
    joined = jnp.concatenate(
        [joined.astype(NARROW), queue_own.reshape(row_count, -1)], axis=1
    )
    joined_b = lax.all_gather(joined, "dp", axis=0, tiled=True)
    table_local, _ = lax.optimization_barrier((table_local, looked[tensor_count - 1]))
    table_b = lax.all_gather(table_local, "dp", axis=0, tiled=True)

    x_zero, x_zero_b = norm_forward(gains[:1], embedded)
    side = (seq_lengths, mask_slots, mask_targets, positive_rows, doc_ids, false_pairs)
    side = side + (queue_docs, factors, data_rank, near)
    errors = (gate_error, up_error, ranks, sorted_ids, starts)
    x_zero_b, joined_b, side, errors = lax.optimization_barrier((x_zero_b, joined_b, side, errors))
    gate_error, up_error, ranks, sorted_ids, starts = errors
    ordered = ranks[None, :] == index[:, None]
    seq_lengths, mask_slots, mask_targets, positive_rows, doc_ids, false_pairs = side[:6]
    queue_docs, factors, data_rank, near = side[6:]
    x_blocks = spread_blocks(x_zero_b, "tensor")
    quarter_b, queue_near = joined_b[:, :attend_cols], joined_b[:, 4 * attend_cols :]
    attend_near = picked_blocks(spread_blocks(quarter_b, "tensor"), near)
    attend_b = jnp.concatenate([attend_near[k] for k in range(tensor_count)], axis=1)
    queue_near = normalize_keys(queue_near.reshape(data_count * queue_rows, width))

    every_rows = mask_slots + own_rows * jnp.arange(tensor_count)[None, :, None]
    every_len = seq_lengths[:, None, None]
    count = jnp.sum((every_rows < every_len).astype(WIDE))
    my_length = lax.dynamic_index_in_dim(seq_lengths, data_rank, 0, keepdims=False)
    group_valid = lax.dynamic_index_in_dim(every_rows < every_len, data_rank, 0, keepdims=False)
    own_slots = lax.dynamic_slice(
        mask_slots, (data_rank, tensor_rank, 0), (1, 1, slot_count)
    ).reshape(1, slot_count)
    own_length = (my_length - tensor_rank * own_rows).reshape(1)
    valid_rows = picked_blocks(group_valid, near).reshape(-1, 1).astype(WIDE)
    row_weight = valid_rows / count
    targets = picked_blocks(mask_targets[0], near).reshape(-1, 1) - vocab_start
    places = near[:, None] * own_rows + jnp.arange(own_rows)[None, :]
    keep_own = (places[0] < my_length)[:, None]
    cosine, sine = rotary_tables(places.reshape(-1))
    cosines, sines = row_blocks(cosine, tensor_count), row_blocks(sine, tensor_count)
    bias = jnp.where(places < my_length, 0.0, NEGATIVE).astype(NARROW)
    biases = [jnp.broadcast_to(bias[k][:, None], (own_rows, PAIR)) for k in range(tensor_count)]
    columns = jnp.arange(queue_docs.shape[0]).reshape(data_count, tensor_count, queue_rows)
    columns = picked_blocks(jnp.swapaxes(columns, 0, 1), near).reshape(-1)
    queue_docs = queue_docs.reshape(data_count, tensor_count, queue_rows)
    queue_docs = picked_blocks(jnp.swapaxes(queue_docs, 0, 1), near).reshape(-1)
    pick = lambda array: lax.dynamic_slice_in_dim(array, data_rank, 1, 0)
    target_c = columns[None, :] == pick(positive_rows)[:, None]
    blocked = (queue_docs[None, :] == pick(doc_ids)[:, None]) | jnp.any(
        pick(false_pairs)[:, :, None] == columns[None, None, :], axis=1
    )
    blocked = (blocked & jnp.logical_not(target_c)).astype(WIDE)
    target_c = target_c.astype(WIDE)

    factor_t = jnp.swapaxes(factors, 1, 2)
    factor_near = spread_blocks(factor_t[0], "tensor")
    error_p = partial_projections([attend_error[0]], [factor_t[0]])[0]

    queries, first_key, first_value = project(3, x_zero_b, attend_b, cosines[0], sines[0])
    keys, values = [first_key], [first_value]
    for k in range(1, tensor_count):
        key, value = project(2, x_blocks[k], attend_b, cosines[k], sines[k])
        keys.append(key)
        values.append(value)
    attended_t, log_total = attention_forward(queries, keys, values, biases)
    queue_near, _ = lax.optimization_barrier((queue_near, log_total))
    keys_hat = jnp.concatenate(spread_blocks(queue_near, "tensor"), axis=0)
    weight_out = attend_b[:, 3 * width :]
    attended_b, pre_one, hidden_in, hidden_in_b = merge_branch(
        attended_t, weight_out, x_zero, gains[1:2]
    )
    states, ffn_sums = paired(
        hidden_in_b, lambda index, first, second: ffn_forward(first, second, joined_b, attend_cols)
    )
    ffn_mine, _, ffn_got = far_sum(ffn_sums)
    final, _ = norm_forward(gains[2:], hidden_in, ffn_mine, ffn_got)

    ff_own = down_weight.shape[1]

    pool_part = jnp.sum(jnp.where(keep_own, final, 0.0), axis=0)
    picked = jnp.take(final, own_slots[0], axis=0).astype(NARROW)
    rows_all = jnp.concatenate(spread_blocks(picked, "tensor"), axis=0)
    logits, stats = vocab_logits(rows_all, table_b, targets)
    picks = rows_all.shape[0]
    pool_rows = jnp.pad(pool_part.reshape(-1, 128), ((0, 8 - width // 128), (0, 0)))
    stats = jnp.concatenate([stats, pool_rows], axis=0)
    for bit in axis_bits("tensor"):
        other = swap(stats, "tensor", bit)
        stats = whole_call(
            functools.partial(combine_kernel, tensor_count, slot_count, bit),
            [(stats.shape, WIDE)],
            20 * stats.size,
            stats,
            other,
        )[0]
    pooled_sum = stats[picks : picks + width // 128].reshape(1, width)
    own_stats = stats[:slot_count]
    cross = own_stats[:, 0] + jnp.log(own_stats[:, 1]) - own_stats[:, 2]
    masked_part = jnp.sum(valid_rows[:slot_count, 0] * cross)
    dlogits, row_part = vocab_back(logits, table_b, targets, stats[:picks], row_weight)
    row_grad = summed_block(row_blocks(row_part, tensor_count), "tensor", NARROW)

    weight_c = LAMBDA / seq_total
    first_rank = jnp.where(tensor_rank == 0, 1.0, 0.0)
    pooled_grad, contrast_row = contrast(
        weight_c, my_length.reshape(1), pooled_sum, keys_hat, blocked, target_c
    )
    contrast_part = contrast_row[0, 0] * first_rank

    pre_grad, pre_grad_b, gain_two = last_back(
        own_length, own_slots, row_grad, pooled_grad, hidden_in, ffn_mine, ffn_got, gains[2:]
    )
    backs, hidden_sums = paired(
        pre_grad_b,
        lambda index, first, second: ffn_backward(first, second, *states[index][:2], joined_b),
    )
    hidden_mine, hidden_sent, hidden_got = far_sum(hidden_sums)
    late = [(back[2], state[2], state[3], back[0], back[1]) for back, state in zip(backs, states)]
    late, _ = lax.optimization_barrier((late, hidden_sent))
    down_grad = sum(contract_rows(part[0], part[1]) for part in late)
    gate_w_grad = sum(contract_rows(part[2], part[3]) for part in late)
    up_w_grad = sum(contract_rows(part[2], part[4]) for part in late)
    ffn_grads = (down_grad, gate_w_grad, up_w_grad)
    ffn_grads, hidden_mine = lax.optimization_barrier((ffn_grads, hidden_mine))
    down_grad, gate_w_grad, up_w_grad = ffn_grads
    pre_one_grad, branch_grad, attended_grad, gain_one = branch_back(
        pre_grad, hidden_mine, hidden_got, pre_one, gains[1:2], weight_out
    )
    dq, dk, dv = attention_backward(
        queries, keys, values, biases, attended_grad, attended_t, log_total, cosines, sines
    )
    x_sums = {}
    for key in reversed(range(0, tensor_count, 2)):
        operands = (dk[key], dv[key], dk[key + 1], dv[key + 1])
        if x_sums:
            operands, _ = lax.optimization_barrier((operands, x_sums[key + 2]))
        x_sums[key] = near_sum(*input_grads(*operands, attend_b))
    x_mine, x_sent, x_got = far_sum(x_sums)
    late = (dq, dk, dv, branch_grad)
    late, _, x_mine = lax.optimization_barrier((late, x_sent, x_mine))
    dq_late, dk, dv, branch_grad = late
    attend_part = jnp.concatenate(
        [
            contract_rows(x_zero_b, dq_late),
            sum(contract_rows(x_blocks[k], dk[k]) for k in range(tensor_count)),
            sum(contract_rows(x_blocks[k], dv[k]) for k in range(tensor_count)),
            jnp.dot(attended_b, branch_grad, preferred_element_type=WIDE),
        ],
        axis=1,
    )
    attend_part, x_mine = lax.optimization_barrier((attend_part, x_mine))
    embedded_grad, gain_zero = first_back(
        pre_one_grad, dq, attend_b[:, :width], x_mine, x_got, embedded, gains[:1]
    )
    other_m, other_p = small_matrices(
        [gate_w_grad, up_w_grad, down_grad],
        [gate_error, up_error, down_error[0]],
        factor_t[1:4],
    )
    near_bit, *far_bits = axis_bits("tensor")
    held = {0: embedded_grad}
    for bit in reversed(far_bits):
        for key in sorted(held):
            held[key ^ bit] = swap(held[key], "tensor", bit)
    emb_blocks = dict(held)
    emb_blocks[1] = swap(held[0], "tensor", near_bit)
    rest = {key: held[key] for key in held if key}
    rest, other_p = lax.optimization_barrier((rest, other_p))
    for key in rest:
        emb_blocks[key] = rest[key]
        emb_blocks[key + 1] = swap(rest[key], "tensor", near_bit)
    emb_all = jnp.concatenate([emb_blocks[key] for key in range(tensor_count)], axis=0)
    emb_all = jnp.dot(ordered.astype(NARROW), emb_all)
    attend_blocks = [
        lax.dynamic_slice_in_dim(attend_part, near[k] * attend_cols, attend_cols, 1)
        for k in range(tensor_count)
    ]
    attend_p = partial_projections(
        [attend_blocks[k] for k in range(tensor_count)], factor_near
    )
    attend_p = summed_block([attend_p[k] for k in range(tensor_count)], "tensor", WIDE)
    attend_p = attend_p + error_p
    attend_held = dict(enumerate(attend_blocks[k] for k in range(tensor_count)))
    bits = axis_bits("tensor")
    for bit in bits[:-1]:
        for key in sorted((k for k in attend_held if not k & bit), reverse=True):
            attend_held[key] = attend_held[key] + swap(attend_held.pop(key ^ bit), "tensor", bit)
    emb_all, attend_held[bits[-1]] = lax.optimization_barrier((emb_all, attend_held[bits[-1]]))
    attend_got = [
        swap(piece, "tensor", bits[-1]) for piece in row_blocks(attend_held[bits[-1]], 2)
    ]

    other_sum = summed_all(jnp.concatenate([other_p[k] for k in range(3)], axis=1), "dp")
    cuts = sorted({0, tiles * 5 // 12, tiles * 9 // 12, tiles})
    table_parts, table_sums = [], []
    for bounds in zip(cuts, cuts[1:]):
        if table_parts:
            emb_all, table_parts[-1][2] = lax.optimization_barrier((emb_all, table_parts[-1][2]))
        if bounds[1] == tiles:
            emb_all, attend_got[0] = lax.optimization_barrier((emb_all, attend_got[0]))
        found = table_matrix(
            bounds, starts, emb_all, sorted_ids, rows_all, dlogits, embed_error[0].T, factor_t[4]
        )
        table_parts.append(list(found))
    for bounds, found in zip(zip(cuts, cuts[1:]), table_parts):
        piece = found[2]
        if bounds[1] == tiles:
            piece = jnp.concatenate([piece, attend_p], axis=1)
        table_sums.append(summed_all(piece, "dp"))
    highs, lows = [part[0] for part in table_parts], [part[1] for part in table_parts]
    parts = [table_sums[-1][:, -attend_cols:], other_sum] + table_sums[:-1]
    parts.append(table_sums[-1][:, :-attend_cols])
    sums = jnp.concatenate(parts, axis=1)
    attend_got[1], _ = lax.optimization_barrier((attend_got[1], sums))
    attend_got = jnp.concatenate(attend_got, axis=0)
    first_m = (attend_held[0] + attend_got + attend_error[0])[None]
    spans, start = [], 0
    for size in (attend_cols, ff_own, ff_own, ff_own, tiles * TILE):
        spans.append((start, size))
        start += size
    bases_t = bases_of(sums, spans)
    small_basis = jnp.stack([bases_t[:, at : at + size] for at, size in spans[:4]])
    table_basis = bases_t[:, spans[4][0] :]
    other_back = small_backs(other_m, small_basis[1:])
    tab_back = table_back(highs, lows, table_basis)
    gain_terms = jnp.concatenate([gain_zero, gain_one, gain_two], axis=0)
    loss_terms = jnp.stack([masked_part, contrast_part])
    loss_row = jnp.zeros((1, width), WIDE).at[0, :2].set(loss_terms)
    packed = jnp.concatenate(
        [other_back.reshape(-1, width), tab_back, gain_terms, loss_row], axis=0
    )
    packed = summed_all(packed, "dp")
    first_back_t = small_backs(first_m, small_basis[:1])
    first_sum = summed_all(first_back_t[0], "dp")
    errors = small_errors(first_m, first_back_t, small_basis[:1]) + small_errors(
        other_m, other_back, small_basis[1:]
    )
    new_table_error = table_error(highs, lows, tab_back, table_basis, vocab_own).T
    own_t = jnp.concatenate([first_sum, packed[: 4 * RANK]], axis=0).reshape(5, RANK, width)
    square = jnp.sum(own_t * own_t)
    tail = packed[4 * RANK :].at[3, 2].set(square)
    shared = jnp.concatenate(
        [own_t[0], tail, jnp.pad(small_basis[0], ((0, 0), (0, width - attend_cols)))], axis=0
    )
    shared = picked_blocks(spread_blocks(shared, "tensor"), near)
    tail_sum = jnp.sum(shared[:, RANK : RANK + 4], axis=0)
    gains_grad = tail_sum[:3]
    loss_sums = tail_sum[3, :2]
    clip_norm = jnp.sqrt(tail_sum[3, 2] + jnp.sum(gains_grad * gains_grad))
    shrink = CLIP / jnp.maximum(clip_norm, CLIP)
    row_start = data_rank * row_count

    def rows_of(factor):
        return lax.dynamic_slice_in_dim(factor, row_start, row_count, factor.ndim - 1)

    reduced_attend = jnp.einsum(
        "tkd,tkn->dtn",
        rows_of(shared[:, :RANK]),
        shared[:, RANK + 4 :, :attend_cols],
        precision=HIGH,
    ).reshape(row_count, -1)
    own_rows_t = rows_of(own_t)

    def reduced(index, basis):
        return dot_in(own_rows_t[index], basis, ((0,), (0,)), precision=HIGH)

    reduced_gate_up = jnp.stack(
        [reduced(1, small_basis[1]), reduced(2, small_basis[2])], axis=1
    )
    reduced_down = reduced(3, small_basis[3])
    reduced_table = reduced(4, table_basis[:, :vocab_own])

    def advance(weight, moment, grad):
        fresh = MOMENTUM * moment + shrink * grad
        return (weight - LRATE * fresh, fresh)

    new_attend, new_attend_moment = advance(attend_weight, attend_moment, reduced_attend)
    new_gate_up, new_gate_up_moment = advance(gate_up, gate_up_moment, reduced_gate_up)
    new_down, new_down_moment = advance(down_weight, down_moment, reduced_down)
    new_table, new_table_moment = advance(embed_table, embed_moment, reduced_table)
    new_gains, new_gains_moment = advance(gains, gains_moment, gains_grad)
    return (
        new_attend,
        new_attend_moment,
        new_gate_up,
        new_gate_up_moment,
        new_down,
        new_down_moment,
        new_table,
        new_table_moment,
        new_gains,
        new_gains_moment,
        errors[0][None],
        errors[1][None],
        errors[2][None],
        new_table_error[None],
        jnp.swapaxes(own_t, 1, 2),
        clip_norm,
        loss_sums[0],
        count,
        loss_sums[1],
    )


def solution(mesh):
    in_specs = (
        P("dp", None),
        P(),
        P(),
        P("dp", None, None),
        P(),
        P(),
        P(),
        P(),
        P("dp", None),
        P("dp", None),
        P("dp", None),
        P("dp", None, "tensor"),
        P("dp", None, "tensor"),
        P("dp", "tensor"),
        P("dp", "tensor"),
        P("dp", "tensor"),
        P("dp", "tensor"),
        P(),
        P(),
        P("dp", None, "tensor"),
        P("dp", None, None, "tensor"),
        P("dp", None, "tensor"),
        P("dp", None, "tensor"),
        P(None, None, "tensor"),
    )
    out_specs = (
        P("dp", None),
        P("dp", None),
        P("dp", None, "tensor"),
        P("dp", None, "tensor"),
        P("dp", "tensor"),
        P("dp", "tensor"),
        P("dp", "tensor"),
        P("dp", "tensor"),
        P(),
        P(),
        P("dp", None, "tensor"),
        P("dp", None, None, "tensor"),
        P("dp", None, "tensor"),
        P("dp", None, "tensor"),
        P(None, None, "tensor"),
        P(),
        P(),
        P(),
        P(),
    )
    return jax.shard_map(
        per_device, mesh=mesh, in_specs=in_specs, out_specs=out_specs, check_vma=False
    )
```

```python
import functools
import math

import jax
import jax.numpy as jnp
from jax import lax
from jax.experimental import pallas as pl
from jax.experimental.pallas import tpu as pltpu
from jax.sharding import PartitionSpec as P

HEADS = 12
HEAD_DIM = 64
RANK = 8
PAIR = 2 * HEAD_DIM
TILE = 640
WIDE_TILE = 1280
CHUNK = 256

EPS = 1e-05
ROPE_BASE = 1000.0
TAU = 0.02
LAMBDA = 1.0
CLIP = 0.02
LRATE = 5000.0
MOMENTUM = 0.9
WIDE = jnp.float32
NARROW = jnp.bfloat16
HIGH = lax.Precision.HIGHEST
NEGATIVE = -1e30


def params(mebibytes):
    return pltpu.CompilerParams(vmem_limit_bytes=mebibytes * 1024 * 1024)


def axis_bits(axis):
    size = lax.axis_size(axis)
    return [1 << place for place in range(size.bit_length() - 1)]


def swap(value, axis, bit):
    size = lax.axis_size(axis)
    return lax.ppermute(value, axis, [(index, index ^ bit) for index in range(size)])


def spread_blocks(value, axis):
    held = {0: value}
    for bit in reversed(axis_bits(axis)):
        for key in sorted(held):
            held[key ^ bit] = swap(held[key], axis, bit)
    return [held[key] for key in range(len(held))]


def summed_block(blocks, axis, kind):
    held = dict(enumerate(blocks))
    for bit in axis_bits(axis):
        for key in sorted((k for k in held if not k & bit), reverse=True):
            if key in held:
                got = swap(held.pop(key ^ bit).astype(kind), axis, bit)
                held[key] = held[key].astype(WIDE) + got.astype(WIDE)
    return held[0]


def summed_pair(blocks, axis):
    held = dict(enumerate(blocks))
    bits = axis_bits(axis)
    for bit in bits[:-1]:
        for key in sorted((k for k in held if not k & bit), reverse=True):
            if key in held:
                got = swap(held.pop(key ^ bit), axis, bit)
                held[key] = (held[key].astype(WIDE) + got.astype(WIDE)).astype(NARROW)
    if not bits:
        return held[0], jnp.zeros_like(held[0])
    return held[0], swap(held[bits[-1]], axis, bits[-1])


def summed_all(value, axis):
    for bit in axis_bits(axis):
        value = value + swap(value, axis, bit)
    return value


def picked_blocks(blocks, order):
    stacked = blocks if isinstance(blocks, jax.Array) else jnp.stack(blocks)
    return jnp.stack(
        [
            lax.dynamic_index_in_dim(stacked, order[k], 0, keepdims=False)
            for k in range(stacked.shape[0])
        ]
    )


def gathered_rows(value, axis):
    size = lax.axis_size(axis)
    if size > 8:
        return lax.all_gather(value, axis, axis=0, tiled=True)
    rank, rows = lax.axis_index(axis), value.shape[0]
    whole = jnp.zeros((size * rows,) + value.shape[1:], value.dtype)
    for key in range(size):
        part = value
        if key:
            part = lax.ppermute(value, axis, [(index, index ^ key) for index in range(size)])
        whole = lax.dynamic_update_slice_in_dim(whole, part, (rank ^ key) * rows, 0)
    return whole


def row_blocks(value, count):
    rows = value.shape[0] // count
    return [value[k * rows : (k + 1) * rows] for k in range(count)]


def layer_norm(values, gain):
    mean = jnp.mean(values, axis=-1, keepdims=True)
    centred = values - mean
    spread = jnp.mean(centred * centred, axis=-1, keepdims=True)
    return centred * lax.rsqrt(spread + EPS) * gain


def swiglu(gate, up):
    return jax.nn.silu(gate) * up


def dot_in(left, right, axes, precision=None):
    return lax.dot_general(
        left, right, (axes, ((), ())), precision=precision, preferred_element_type=WIDE
    )


def contract_rows(left, right):
    return dot_in(left, right, ((0,), (0,)))


def contract_cols(left, right):
    return dot_in(left, right, ((1,), (1,)))


def halves(value):
    high = value.astype(NARROW)
    return high, (value - high.astype(WIDE)).astype(NARROW)


def turn(piece, cosine, sine):
    lane = lax.broadcasted_iota(jnp.int32, piece.shape, 1) % HEAD_DIM
    half = HEAD_DIM // 2
    ahead = pltpu.roll(piece, PAIR - half, 1)
    behind = pltpu.roll(piece, half, 1)
    return piece * cosine + jnp.where(lane < half, -ahead, behind) * sine


def rotary_tables(places):
    half = HEAD_DIM // 2
    column = (jnp.arange(PAIR) % half).astype(WIDE)
    freq = ROPE_BASE ** (-2.0 * column / HEAD_DIM)
    angle = places.astype(WIDE)[:, None] * freq[None, :]
    return (jnp.cos(angle), jnp.sin(angle))


def project_kernel(count, x_ref, *refs):
    weights, (cos_ref, sin_ref), outs = refs[:count], refs[count : count + 2], refs[count + 2 :]
    x, cosine, sine = x_ref[...], cos_ref[...], sin_ref[...]
    for kind, (w_ref, out_ref) in enumerate(zip(weights, outs), 3 - count):
        for at in range(0, out_ref.shape[1], 2 * PAIR):
            flat = jnp.dot(x, w_ref[:, at : at + 2 * PAIR], preferred_element_type=WIDE)
            for start in range(0, 2 * PAIR, PAIR):
                piece = flat[:, start : start + PAIR]
                if kind < 2:
                    piece = turn(piece, cosine, sine)
                piece = piece.astype(NARROW)
                if kind == 0:
                    piece = (piece.astype(WIDE) * HEAD_DIM ** (-0.5)).astype(NARROW)
                out_ref[:, at + start : at + start + PAIR] = piece


def project(count, x, weight, cosine, sine):
    rows, width = x.shape
    still = lambda i: (0, 0)
    block = pl.BlockSpec((rows, width), still)
    lanes = pl.BlockSpec((rows, PAIR), still)
    return pl.pallas_call(
        functools.partial(project_kernel, count),
        grid=(1,),
        in_specs=[block]
        + [weight_block(width, width, kind) for kind in range(3 - count, 3)]
        + [lanes, lanes],
        out_specs=[block] * count,
        out_shape=[jax.ShapeDtypeStruct((rows, width), NARROW)] * count,
        compiler_params=params(20),
        cost_estimate=pl.CostEstimate(
            flops=2 * count * rows * width * width,
            bytes_accessed=2 * count * width * (rows + width),
            transcendentals=0,
        ),
    )(x, *[weight] * count, cosine, sine)


def turn_table_kernel(table_ref, out_ref):
    rows, columns = table_ref.shape
    empty = jnp.zeros((columns, out_ref.shape[1] - rows), WIDE)
    for at in range(0, columns, 128):
        size = min(128, columns - at)
        piece = table_ref[:, at : at + size].astype(NARROW).astype(WIDE).T
        if rows < out_ref.shape[1]:
            piece = jnp.concatenate([piece, empty[:size]], axis=1)
        out_ref[at : at + size, :] = piece
    out_ref[columns:, :] = jnp.zeros((out_ref.shape[0] - columns, out_ref.shape[1]), WIDE)


def turned_table(table):
    rows, columns = table.shape
    lanes = -(-rows // 128) * 128
    return whole_call(
        turn_table_kernel, [((columns // 8 * 8 + 8, lanes), WIDE)], 8 * table.size, table
    )[0]


def pack_kernel(rank_ref, attend_ref, gate_ref, down_ref, queue_ref, out_ref):
    at = 0
    for part in (attend_ref[...], gate_ref[:, 0, :], gate_ref[:, 1, :], down_ref[...]):
        out_ref[:, at : at + part.shape[1]] = part.astype(NARROW)
        at += part.shape[1]
    out_ref[:, at:] = queue_ref[...]


def packed_weights(rank, attend, gate_up, down, queue, columns):
    rows, hidden = down.shape
    span = queue.shape[1]
    still = lambda i, rank_ref: (0, 0)
    total = columns + 3 * hidden + span
    return pl.pallas_call(
        pack_kernel,
        grid_spec=pltpu.PrefetchScalarGridSpec(
            num_scalar_prefetch=1,
            grid=(1,),
            in_specs=[
                pl.BlockSpec((rows, columns), lambda i, rank_ref: (0, rank_ref[0])),
                pl.BlockSpec((rows, 2, hidden), lambda i, rank_ref: (0, 0, 0)),
                pl.BlockSpec((rows, hidden), still),
                pl.BlockSpec((rows, span), still),
            ],
            out_specs=pl.BlockSpec((rows, total), still),
        ),
        out_shape=jax.ShapeDtypeStruct((rows, total), NARROW),
        compiler_params=params(12),
        cost_estimate=pl.CostEstimate(
            flops=rows * total, bytes_accessed=6 * rows * total, transcendentals=0
        ),
    )(rank, attend, gate_up, down, queue)


def lookup_kernel(row_count, start_ref, ids_ref, table_ref, out_ref, held):
    groups, block = out_ref.shape[1] // row_count, out_ref.shape[0]
    start = start_ref[0]
    for group in range(groups):

        def move(at, carry):
            base = start + (group * block + at * 8)
            for place in range(8):
                index = ids_ref[base + place]
                held[at, place : place + 1, :] = table_ref[pl.ds(index, 1), :]
            return carry

        lax.fori_loop(0, block // 8, move, 0, unroll=8)
        rows = held[...].reshape(block, held.shape[2])[:, :row_count]
        out_ref[:, group * row_count : (group + 1) * row_count] = rows.astype(NARROW)


def lookup(ids, table, start, groups, block, row_count):
    return pl.pallas_call(
        functools.partial(lookup_kernel, row_count),
        in_specs=[
            pl.BlockSpec(memory_space=pltpu.SMEM),
            pl.BlockSpec(memory_space=pltpu.SMEM),
            pl.BlockSpec(memory_space=pltpu.VMEM),
        ],
        out_specs=pl.BlockSpec(memory_space=pltpu.VMEM),
        out_shape=jax.ShapeDtypeStruct((block, groups * row_count), NARROW),
        scratch_shapes=[pltpu.VMEM((block // 8, 8, table.shape[1]), WIDE)],
        compiler_params=params(10),
        cost_estimate=pl.CostEstimate(
            flops=groups * block * 4096, bytes_accessed=4 * table.size, transcendentals=0
        ),
    )(start, ids, table)


def norm_parts(values):
    mean = jnp.mean(values, axis=-1, keepdims=True)
    centred = values - mean
    scale = lax.rsqrt(jnp.mean(centred * centred, axis=-1, keepdims=True) + EPS)
    return centred * scale, scale


def norm_back(grad, values, gain):
    unit, scale = norm_parts(values)
    inner = grad * gain
    first = jnp.mean(inner, axis=-1, keepdims=True)
    second = jnp.mean(inner * unit, axis=-1, keepdims=True)
    return (inner - first - unit * second) * scale, jnp.sum(grad * unit, axis=0, keepdims=True)


def whole_call(kernel, outs, flops, *operands):
    moved = sum(operand.size * operand.dtype.itemsize for operand in operands)
    moved += sum(math.prod(shape) * jnp.dtype(kind).itemsize for shape, kind in outs)
    budget = 8 + moved * 2 // (1 << 20)
    return pl.pallas_call(
        kernel,
        out_shape=[jax.ShapeDtypeStruct(shape, kind) for shape, kind in outs],
        compiler_params=params(budget),
        cost_estimate=pl.CostEstimate(
            flops=flops,
            bytes_accessed=sum(4 * operand.size for operand in operands),
            transcendentals=0,
        ),
    )(*operands)


def norm_kernel(gain_ref, *refs):
    inputs, (out_ref, narrow_ref) = refs[:-2], refs[-2:]
    total = inputs[0][...].astype(WIDE)
    for ref in inputs[1:]:
        total = total + ref[...].astype(WIDE)
    out = norm_parts(total)[0] * gain_ref[...]
    out_ref[...] = out
    narrow_ref[...] = out.astype(NARROW)


def norm_forward(gain, *parts):
    shape = parts[0].shape
    return whole_call(norm_kernel, [(shape, WIDE), (shape, NARROW)], 20 * parts[0].size, gain, *parts)


def merge_kernel(attended_ref, weight_ref, x_ref, gain_ref, narrow_out, pre_ref, out_ref, out_b_ref):
    narrow = attended_ref[...].astype(NARROW)
    narrow_out[...] = narrow
    pre = x_ref[...] + contract_rows(narrow, weight_ref[...])
    pre_ref[...] = pre
    out = norm_parts(pre)[0] * gain_ref[...]
    out_ref[...] = out
    out_b_ref[...] = out.astype(NARROW)


def merge_branch(attended_t, weight, x_zero, gain):
    rows, width = x_zero.shape
    shape = (rows, width)
    return whole_call(
        merge_kernel,
        [((width, rows), NARROW), (shape, WIDE), (shape, WIDE), (shape, NARROW)],
        2 * rows * width * width,
        attended_t,
        weight,
        x_zero,
        gain,
    )


def last_kernel(length_ref, slots_ref, rows_ref, pooled_ref, hidden_ref, local_ref, got_ref, gain_ref, out_ref, narrow_ref, sum_ref):
    total = hidden_ref[...] + local_ref[...].astype(WIDE) + got_ref[...].astype(WIDE)
    spread = rows_ref[...]
    place = lax.broadcasted_iota(jnp.int32, (total.shape[0], slots_ref.shape[1]), 0)
    hot = (place == slots_ref[...]).astype(WIDE).astype(NARROW)
    high, low = halves(spread)
    grad = jnp.dot(hot, high, preferred_element_type=WIDE)
    grad = grad + jnp.dot(hot, low, preferred_element_type=WIDE)
    index = lax.broadcasted_iota(jnp.int32, (total.shape[0], 1), 0)
    grad = grad + jnp.where(index < length_ref[0], pooled_ref[...], 0.0)
    out, gain_grad = norm_back(grad, total, gain_ref[...])
    out_ref[...] = out
    narrow_ref[...] = out.astype(NARROW)
    sum_ref[...] = gain_grad


def last_back(length, slots, row_grad, pooled_grad, hidden_in, local, got, gain):
    shape = hidden_in.shape
    return pl.pallas_call(
        last_kernel,
        in_specs=[pl.BlockSpec(memory_space=pltpu.SMEM)]
        + [pl.BlockSpec(memory_space=pltpu.VMEM)] * 7,
        out_shape=[
            jax.ShapeDtypeStruct(shape, WIDE),
            jax.ShapeDtypeStruct(shape, NARROW),
            jax.ShapeDtypeStruct((1, shape[1]), WIDE),
        ],
        compiler_params=params(24),
        cost_estimate=pl.CostEstimate(
            flops=200 * hidden_in.size, bytes_accessed=20 * hidden_in.size, transcendentals=0
        ),
    )(length, slots, row_grad, pooled_grad, hidden_in, local, got, gain)


def branch_back_kernel(grad_ref, local_ref, got_ref, pre_ref, gain_ref, weight_ref, out_ref, narrow_ref, attended_ref, sum_ref):
    grad = grad_ref[...] + local_ref[...].astype(WIDE) + got_ref[...].astype(WIDE)
    out, gain_grad = norm_back(grad, pre_ref[...], gain_ref[...])
    narrow = out.astype(NARROW)
    out_ref[...] = out
    narrow_ref[...] = narrow
    sum_ref[...] = gain_grad
    attended_ref[...] = contract_cols(narrow, weight_ref[...]).astype(NARROW)


def branch_back(pre_grad, local, got, pre_one, gain, weight):
    rows, width = pre_grad.shape
    shape = (rows, width)
    return whole_call(
        branch_back_kernel,
        [(shape, WIDE), (shape, NARROW), (shape, NARROW), ((1, width), WIDE)],
        2 * rows * width * width,
        pre_grad,
        local,
        got,
        pre_one,
        gain,
        weight,
    )


def first_back_kernel(grad_ref, dq_ref, weight_ref, local_ref, got_ref, value_ref, gain_ref, out_ref, sum_ref):
    grad = grad_ref[...] + local_ref[...].astype(WIDE) + got_ref[...].astype(WIDE)
    grad = grad + contract_cols(dq_ref[...], weight_ref[...])
    out, gain_grad = norm_back(grad, value_ref[...].astype(WIDE), gain_ref[...])
    out_ref[...] = out.astype(NARROW)
    sum_ref[...] = gain_grad


def first_back(pre_one_grad, dq, weight, local, got, embedded, gain):
    rows, width = pre_one_grad.shape
    return whole_call(
        first_back_kernel,
        [((rows, width), NARROW), ((1, width), WIDE)],
        2 * rows * width * width,
        pre_one_grad,
        dq,
        weight,
        local,
        got,
        embedded,
        gain,
    )


def ffn_step(x_ref, weights, gate_out, up_out, act_ref, x_out, out_ref):
    gate_ref, up_ref, down_ref = weights
    x = x_ref[...]
    gate = jnp.dot(x, gate_ref[...], preferred_element_type=WIDE)
    up = jnp.dot(x, up_ref[...], preferred_element_type=WIDE)
    gate_out[...] = gate
    up_out[...] = up
    act = (gate / (1.0 + jnp.exp(-gate)) * up).astype(NARROW)
    act_ref[...] = act
    x_out[...] = x
    out_ref[...] = contract_cols(act, down_ref[...]).astype(NARROW)


def ffn_kernel(first_ref, second_ref, *refs):
    weights, kept, outs = refs[:3], refs[3:7], refs[7:]
    for step, x_ref in enumerate((first_ref, second_ref)):

        @pl.when(pl.program_id(0) == step)
        def _():
            ffn_step(x_ref, weights, *kept, outs[step])


def weight_block(width, hidden, index):
    return pl.BlockSpec((width, hidden), lambda i: (0, index))


def ffn_forward(first, second, weights, hidden):
    rows, width = first.shape
    whole = pl.BlockSpec((rows, width), lambda i: (0, 0))
    tall = lambda i: (i, 0)
    return pl.pallas_call(
        ffn_kernel,
        grid=(2,),
        in_specs=[whole, whole] + [weight_block(width, hidden, k) for k in range(1, 4)],
        out_specs=[pl.BlockSpec((rows, hidden), tall)] * 3
        + [pl.BlockSpec((rows, width), tall), whole, whole],
        out_shape=[
            jax.ShapeDtypeStruct((2 * rows, hidden), WIDE),
            jax.ShapeDtypeStruct((2 * rows, hidden), WIDE),
            jax.ShapeDtypeStruct((2 * rows, hidden), NARROW),
            jax.ShapeDtypeStruct((2 * rows, width), NARROW),
            jax.ShapeDtypeStruct((rows, width), NARROW),
            jax.ShapeDtypeStruct((rows, width), NARROW),
        ],
        compiler_params=params(32),
        cost_estimate=pl.CostEstimate(
            flops=12 * rows * width * hidden,
            bytes_accessed=28 * rows * width + 6 * width * hidden,
            transcendentals=2 * rows * hidden,
        ),
    )(first, second, weights, weights, weights)


def ffn_back_step(grad_ref, gate_in, up_in, weights, dgate_ref, dup_ref, grad_out, out_ref):
    gate_ref, up_ref, down_ref = weights
    grad = grad_ref[...]
    grad_out[...] = grad
    act_grad = jnp.dot(grad, down_ref[...], preferred_element_type=WIDE)
    gate, up = gate_in[...], up_in[...]
    share = 1.0 / (1.0 + jnp.exp(-gate))
    dgate = (act_grad * up * (share * (1.0 + gate * (1.0 - share)))).astype(NARROW)
    dup = (act_grad * (gate * share)).astype(NARROW)
    dgate_ref[...] = dgate
    dup_ref[...] = dup
    out_ref[...] = (
        contract_cols(dgate, gate_ref[...]) + contract_cols(dup, up_ref[...])
    ).astype(NARROW)


def ffn_back_kernel(first_ref, second_ref, gate_in, up_in, *refs):
    weights, kept, outs = refs[:3], refs[3:6], refs[6:]
    for step, grad_ref in enumerate((first_ref, second_ref)):

        @pl.when(pl.program_id(0) == step)
        def _():
            ffn_back_step(grad_ref, gate_in, up_in, weights, *kept, outs[step])


def ffn_backward(first, second, gate, up, weights):
    rows, width = first.shape
    hidden = gate.shape[1]
    whole = pl.BlockSpec((rows, width), lambda i: (0, 0))
    tall = lambda i: (i, 0)
    return pl.pallas_call(
        ffn_back_kernel,
        grid=(2,),
        in_specs=[whole, whole]
        + [pl.BlockSpec((rows, hidden), tall)] * 2
        + [weight_block(width, hidden, k) for k in range(1, 4)],
        out_specs=[pl.BlockSpec((rows, hidden), tall)] * 2
        + [pl.BlockSpec((rows, width), tall), whole, whole],
        out_shape=[
            jax.ShapeDtypeStruct((2 * rows, hidden), NARROW),
            jax.ShapeDtypeStruct((2 * rows, hidden), NARROW),
            jax.ShapeDtypeStruct((2 * rows, width), NARROW),
            jax.ShapeDtypeStruct((rows, width), NARROW),
            jax.ShapeDtypeStruct((rows, width), NARROW),
        ],
        compiler_params=params(34),
        cost_estimate=pl.CostEstimate(
            flops=12 * rows * width * hidden,
            bytes_accessed=32 * rows * width + 6 * width * hidden,
            transcendentals=2 * rows * hidden,
        ),
    )(first, second, gate, up, weights, weights, weights)


def input_kernel(first_k, first_v, second_k, second_v, key_ref, value_ref, *outs):
    for dk_ref, dv_ref, out_ref in zip((first_k, second_k), (first_v, second_v), outs):
        total = contract_cols(dk_ref[...], key_ref[...])
        total = total + contract_cols(dv_ref[...], value_ref[...])
        out_ref[...] = total.astype(NARROW)


def input_grads(first_k, first_v, second_k, second_v, weights):
    rows, width = first_k.shape
    whole = pl.BlockSpec((rows, width), lambda i: (0, 0))
    return pl.pallas_call(
        input_kernel,
        grid=(1,),
        in_specs=[whole] * 4 + [weight_block(width, width, k) for k in (1, 2)],
        out_specs=[whole] * 2,
        out_shape=[jax.ShapeDtypeStruct((rows, width), NARROW)] * 2,
        compiler_params=params(24),
        cost_estimate=pl.CostEstimate(
            flops=8 * rows * width * width,
            bytes_accessed=12 * rows * width + 4 * width * width,
            transcendentals=0,
        ),
    )(first_k, first_v, second_k, second_v, weights, weights)


def paired(value, work):
    near_bit, *far_bits = axis_bits("tensor")
    held = {0: value}
    for bit in reversed(far_bits):
        for key in sorted(held):
            held[key ^ bit] = swap(held[key], "tensor", bit)
    results, sums = [], {}
    for key in sorted(held):
        block = held[key]
        if results:
            block, _ = lax.optimization_barrier((block, results[-1][-1]))
        results.append(work(len(results), block, swap(block, "tensor", near_bit)))
        sums[key] = near_sum(*results[-1][-2:])
    return results, sums


def near_sum(own, other):
    got = swap(other, "tensor", axis_bits("tensor")[0])
    return (own.astype(WIDE) + got.astype(WIDE)).astype(NARROW)


def far_sum(sums):
    sums = dict(sums)
    near_bit, *far_bits = axis_bits("tensor")
    for bit in far_bits[:-1]:
        for key in sorted(k for k in sums if not k & bit):
            got = swap(sums.pop(key ^ bit), "tensor", bit)
            sums[key] = (sums[key].astype(WIDE) + got.astype(WIDE)).astype(NARROW)
    return sums[0], sums[far_bits[-1]], swap(sums[far_bits[-1]], "tensor", far_bits[-1])


def logits_kernel(columns, tile, rows_ref, table_ref, targets_ref, out_ref, stats_ref, top_ref, sum_ref, hit_ref):
    step = pl.program_id(0)

    @pl.when(step == 0)
    def _():
        top_ref[...] = jnp.full(top_ref.shape, NEGATIVE, WIDE)
        sum_ref[...] = jnp.zeros(sum_ref.shape, WIDE)
        hit_ref[...] = jnp.zeros(hit_ref.shape, WIDE)

    logits = jnp.dot(rows_ref[...], table_ref[...], preferred_element_type=WIDE)
    out_ref[...] = logits
    place = step * tile + lax.broadcasted_iota(jnp.int32, (1, tile), 1)
    seen = jnp.where(place < columns, logits, NEGATIVE)
    hits = jnp.where((place == targets_ref[...]) & (place < columns), seen, 0.0)
    pieces = [slice(at, at + 128) for at in range(0, tile, 128)]
    before = top_ref[...]
    top = before
    for piece in pieces:
        top = jnp.maximum(top, seen[:, piece])
    total = sum_ref[...] * jnp.exp(before - top)
    hit = hit_ref[...]
    for piece in pieces:
        total = total + jnp.exp(seen[:, piece] - top)
        hit = hit + hits[:, piece]
    top_ref[...] = top
    sum_ref[...] = total
    hit_ref[...] = hit

    @pl.when(step == pl.num_programs(0) - 1)
    def _():
        peak = jnp.max(top, axis=1, keepdims=True)
        whole = jnp.sum(total * jnp.exp(top - peak), axis=1, keepdims=True)
        found = jnp.sum(hit, axis=1, keepdims=True)
        lane = lax.broadcasted_iota(jnp.int32, (1, 128), 1)
        stats_ref[...] = jnp.where(
            lane == 0, peak, jnp.where(lane == 1, whole, jnp.where(lane == 2, found, 0.0))
        )


def vocab_logits(rows_all, table, targets):
    picks, width = rows_all.shape
    columns = table.shape[1]
    tiles = -(-columns // TILE)
    tile = WIDE_TILE
    still = lambda j: (0, 0)
    along = lambda j: (0, j)
    return pl.pallas_call(
        functools.partial(logits_kernel, columns, tile),
        grid=(tiles * TILE // tile,),
        in_specs=[
            pl.BlockSpec((picks, width), still),
            pl.BlockSpec((width, tile), along),
            pl.BlockSpec((picks, 1), still),
        ],
        out_specs=[pl.BlockSpec((picks, tile), along), pl.BlockSpec((picks, 128), still)],
        out_shape=[
            jax.ShapeDtypeStruct((picks, tiles * TILE), WIDE),
            jax.ShapeDtypeStruct((picks, 128), WIDE),
        ],
        scratch_shapes=[pltpu.VMEM((picks, 128), WIDE)] * 3,
        compiler_params=params(56),
        cost_estimate=pl.CostEstimate(
            flops=2 * picks * width * columns,
            bytes_accessed=2 * width * columns,
            transcendentals=picks * columns,
        ),
    )(rows_all, table, targets)


def combine_kernel(count, slots, bit, mine_ref, other_ref, out_ref):
    lane = lax.broadcasted_iota(jnp.int32, (1, 128), 1)
    for block in range(count):
        mine = mine_ref[block * slots : (block + 1) * slots, :]
        other = other_ref[(block ^ bit) * slots : ((block ^ bit) + 1) * slots, :]
        peak = jnp.maximum(mine[:, :1], other[:, :1])
        total = mine[:, 1:2] * jnp.exp(mine[:, :1] - peak)
        total = total + other[:, 1:2] * jnp.exp(other[:, :1] - peak)
        out_ref[block * slots : (block + 1) * slots, :] = jnp.where(
            lane == 0, peak, jnp.where(lane == 1, total, mine + other)
        )
    rest = count * slots
    out_ref[rest:, :] = mine_ref[rest:, :] + other_ref[rest:, :]


def dlogits_kernel(columns, tile, logits_ref, table_ref, targets_ref, stats_ref, weight_ref, out_ref, grad_ref):
    step = pl.program_id(0)
    log_all = stats_ref[:, :1] + jnp.log(stats_ref[:, 1:2])
    place = step * tile + lax.broadcasted_iota(jnp.int32, (1, tile), 1)
    share = jnp.exp(logits_ref[...] - log_all) - jnp.where(place == targets_ref[...], 1.0, 0.0)
    grad = jnp.where(place < columns, share * weight_ref[...], 0.0).astype(NARROW)
    out_ref[...] = grad
    column = step * tile + lax.broadcasted_iota(jnp.int32, (1, tile), 1)
    table = jnp.where(column < columns, table_ref[...].astype(WIDE), 0.0).astype(NARROW)
    part = contract_cols(grad, table)

    @pl.when(step == 0)
    def _():
        grad_ref[...] = part

    @pl.when(step > 0)
    def _():
        grad_ref[...] += part


def vocab_back(logits, table, targets, stats, weight):
    picks = targets.shape[0]
    width, columns = table.shape
    tile = WIDE_TILE
    still = lambda j: (0, 0)
    along = lambda j: (0, j)
    return pl.pallas_call(
        functools.partial(dlogits_kernel, columns, tile),
        grid=(logits.shape[1] // tile,),
        in_specs=[
            pl.BlockSpec((picks, tile), along),
            pl.BlockSpec((width, tile), along),
            pl.BlockSpec((picks, 1), still),
            pl.BlockSpec((picks, 128), still),
            pl.BlockSpec((picks, 1), still),
        ],
        out_specs=[pl.BlockSpec((picks, tile), along), pl.BlockSpec((picks, width), still)],
        out_shape=[
            jax.ShapeDtypeStruct(logits.shape, NARROW),
            jax.ShapeDtypeStruct((picks, width), WIDE),
        ],
        compiler_params=params(56),
        cost_estimate=pl.CostEstimate(
            flops=2 * picks * width * columns,
            bytes_accessed=2 * width * columns,
            transcendentals=picks * columns,
        ),
    )(logits, table, targets, stats, weight)


def contrast_kernel(weight, length_ref, pooled_ref, keys_ref, blocked_ref, target_ref, grad_ref, part_ref):
    length = length_ref[0].astype(WIDE)
    pooled = pooled_ref[...] / length
    scale = lax.rsqrt(jnp.sum(pooled * pooled, axis=-1, keepdims=True) + EPS)
    narrow = jnp.broadcast_to(pooled * scale, (8, pooled.shape[1])).astype(NARROW)
    keys = keys_ref[...]
    scores = contract_cols(narrow, keys)[:1] / TAU
    target = target_ref[...]
    masked = jnp.where(blocked_ref[...] > 0.0, NEGATIVE, scores)
    top = jnp.max(masked, axis=-1, keepdims=True)
    log_c = top + jnp.log(jnp.sum(jnp.exp(masked - top), axis=-1, keepdims=True))
    chosen = jnp.sum(jnp.where(target > 0.0, scores, 0.0), axis=-1, keepdims=True)
    part_ref[...] = jnp.broadcast_to((log_c - chosen) * weight, part_ref.shape)
    dscores = ((jnp.exp(masked - log_c) - target) * (weight / TAU)).astype(NARROW)
    dscores = jnp.broadcast_to(dscores.astype(WIDE), (8, dscores.shape[1])).astype(NARROW)
    grad = jnp.dot(dscores, keys, preferred_element_type=WIDE)[:1]
    inner = jnp.sum(pooled * grad, axis=-1, keepdims=True)
    grad_ref[...] = (grad - pooled * (inner * scale * scale)) * scale / length


def contrast(weight, length, pooled_sum, keys_hat, blocked, target):
    width = pooled_sum.shape[1]
    return pl.pallas_call(
        functools.partial(contrast_kernel, weight),
        in_specs=[pl.BlockSpec(memory_space=pltpu.SMEM)]
        + [pl.BlockSpec(memory_space=pltpu.VMEM)] * 4,
        out_shape=[
            jax.ShapeDtypeStruct((1, width), WIDE),
            jax.ShapeDtypeStruct((1, 128), WIDE),
        ],
        compiler_params=params(8),
        cost_estimate=pl.CostEstimate(
            flops=4 * keys_hat.size, bytes_accessed=2 * keys_hat.size, transcendentals=0
        ),
    )(length, pooled_sum, keys_hat, blocked, target)


def head_lanes(head):
    lane = lax.broadcasted_iota(jnp.int32, (1, PAIR), 1)
    return (lane // HEAD_DIM) == head, lane == HEAD_DIM * (1 - head)


def attend_kernel(count, q_ref, *refs):
    k_refs, v_refs, bias_refs = refs[:count], refs[count : 2 * count], refs[2 * count : 3 * count]
    out_ref, log_ref, s_ref = refs[3 * count :]
    head = pl.program_id(1)
    mine, spare = head_lanes(head)
    step = k_refs[0].shape[0]
    blocks = [pl.ds(k * step, step) for k in range(count)]
    query = jnp.where(spare, 1.0, jnp.where(mine, q_ref[...].astype(WIDE), 0.0)).astype(NARROW)
    top = None
    for rows, k_ref, bias_ref in zip(blocks, k_refs, bias_refs):
        key = jnp.where(spare, bias_ref[...].astype(WIDE), k_ref[...].astype(WIDE))
        scores = contract_cols(key.astype(NARROW), query)
        s_ref[rows, :] = scores
        peak = jnp.max(scores, axis=0, keepdims=True)
        top = peak if top is None else jnp.maximum(top, peak)
    total = None
    for rows in blocks:
        powers = jnp.exp(s_ref[rows, :] - top)
        s_ref[rows, :] = powers
        part = jnp.sum(powers, axis=0, keepdims=True)
        total = part if total is None else total + part
    share = 1.0 / total
    result = None
    for rows, v_ref in zip(blocks, v_refs):
        probs = (s_ref[rows, :] * share).astype(NARROW)
        part = contract_rows(v_ref[...], probs)
        result = part if result is None else result + part
    log_ref[0, pl.ds(head, 1), :] = top + jnp.log(total)

    @pl.when(head == 0)
    def _():
        out_ref[...] = result

    @pl.when(head == 1)
    def _():
        out_ref[HEAD_DIM:, :] = result[HEAD_DIM:, :]


def attention_forward(queries, keys, values, biases):
    rows, width = queries.shape
    count = len(keys)
    length = rows * count
    pairs = width // PAIR
    lanes = pl.BlockSpec((rows, PAIR), lambda i, h: (0, i))
    still = pl.BlockSpec((rows, PAIR), lambda i, h: (0, 0))
    return pl.pallas_call(
        functools.partial(attend_kernel, count),
        grid=(pairs, 2),
        in_specs=[lanes] * (1 + 2 * count) + [still] * count,
        out_specs=[
            pl.BlockSpec((PAIR, rows), lambda i, h: (i, 0)),
            pl.BlockSpec((1, 2, rows), lambda i, h: (i, 0, 0)),
        ],
        out_shape=[
            jax.ShapeDtypeStruct((width, rows), WIDE),
            jax.ShapeDtypeStruct((pairs, 2, rows), WIDE),
        ],
        scratch_shapes=[pltpu.VMEM((length, rows), WIDE)],
        compiler_params=params(22),
        cost_estimate=pl.CostEstimate(
            flops=4 * rows * length * width,
            bytes_accessed=4 * length * width + 8 * rows * width,
            transcendentals=rows * length * HEADS,
        ),
    )(queries, *keys, *values, *biases)


def attend_back_kernel(count, q_ref, grad_ref, out_ref, log_ref, *refs):
    groups = [refs[k * count : (k + 1) * count] for k in range(5)]
    k_refs, v_refs, bias_refs, cos_refs, sin_refs = groups
    rest = refs[5 * count :]
    dq_ref, dk_refs, dv_refs = rest[0], rest[1 : 1 + count], rest[1 + count : 1 + 2 * count]
    dk_sum, dv_sum, dq_sum, key_all, value_all = rest[1 + 2 * count :]
    head = pl.program_id(1)
    mine, spare = head_lanes(head)
    step, scale = k_refs[0].shape[0], HEAD_DIM ** (-0.5)
    own = jnp.where(mine, q_ref[...].astype(WIDE), 0.0)
    query = own.astype(NARROW)
    asked = jnp.where(spare, 1.0, own).astype(NARROW)
    grad_wide = jnp.where(mine, grad_ref[...].astype(WIDE), 0.0)
    grad = grad_wide.astype(NARROW)
    delta = jnp.sum(grad_wide.T * out_ref[...], axis=0, keepdims=True)
    log_total = log_ref[0, pl.ds(head, 1), :]
    for k in range(count):
        rows = pl.ds(k * step, step)
        key = jnp.where(spare, bias_refs[k][...].astype(WIDE), k_refs[k][...].astype(WIDE))
        key_all[rows, :] = key.astype(NARROW)
        value_all[rows, :] = v_refs[k][...]
    keys = key_all[...]
    probs = jnp.exp(contract_cols(keys, asked) - log_total)
    dprobs = contract_cols(value_all[...], grad)
    dv = jnp.dot(probs.astype(NARROW), grad, preferred_element_type=WIDE)
    dscores = (probs * (dprobs - delta)).astype(NARROW)
    dk = jnp.dot(dscores, query, preferred_element_type=WIDE)
    dq = contract_rows(keys, dscores)

    @pl.when(head == 0)
    def _():
        dk_sum[...] = dk
        dv_sum[...] = dv

    @pl.when(head == 1)
    def _():
        key_grad, value_grad = dk_sum[...] + dk, dv_sum[...] + dv
        for k in range(count):
            rows = slice(k * step, (k + 1) * step)
            piece = turn(key_grad[rows], cos_refs[k][...], -sin_refs[k][...])
            dk_refs[k][...] = piece.astype(NARROW)
            dv_refs[k][...] = value_grad[rows].astype(NARROW)

    @pl.when(head == 0)
    def _():
        dq_sum[...] = dq

    @pl.when(head == 1)
    def _():
        dq_sum[HEAD_DIM:, :] = dq[HEAD_DIM:, :]
        total = dq_sum[...].T * scale
        dq_ref[...] = turn(total, cos_refs[0][...], -sin_refs[0][...]).astype(NARROW)


def attention_backward(queries, keys, values, biases, grad, out_t, log_total, cosines, sines):
    rows, width = queries.shape
    count = len(keys)
    length = rows * count
    pairs = width // PAIR
    lanes = pl.BlockSpec((rows, PAIR), lambda i, h: (0, i))
    still = pl.BlockSpec((rows, PAIR), lambda i, h: (0, 0))
    found = pl.pallas_call(
        functools.partial(attend_back_kernel, count),
        grid=(pairs, 2),
        in_specs=[
            lanes,
            lanes,
            pl.BlockSpec((PAIR, rows), lambda i, h: (i, 0)),
            pl.BlockSpec((1, 2, rows), lambda i, h: (i, 0, 0)),
        ]
        + [lanes] * (2 * count)
        + [still] * (3 * count),
        out_specs=[lanes] * (1 + 2 * count),
        out_shape=[jax.ShapeDtypeStruct((rows, width), NARROW)] * (1 + 2 * count),
        scratch_shapes=[
            pltpu.VMEM((length, PAIR), WIDE),
            pltpu.VMEM((length, PAIR), WIDE),
            pltpu.VMEM((PAIR, rows), WIDE),
            pltpu.VMEM((length, PAIR), NARROW),
            pltpu.VMEM((length, PAIR), NARROW),
        ],
        compiler_params=params(56),
        cost_estimate=pl.CostEstimate(
            flops=10 * rows * length * width,
            bytes_accessed=8 * length * width + 8 * rows * width,
            transcendentals=rows * length * HEADS,
        ),
    )(queries, grad, out_t, log_total, *keys, *values, *biases, *cosines, *sines)
    return found[0], found[1 : 1 + count], found[1 + count :]


def project_down(matrix, factor_t):
    high, low = halves(matrix)
    factor_high, factor_low = halves(factor_t)
    both = jnp.concatenate([factor_high, factor_low], axis=0)
    first = jnp.dot(both, high, preferred_element_type=WIDE)
    second = jnp.dot(factor_high, low, preferred_element_type=WIDE)
    return first[:RANK] + first[RANK:] + second


def project_back(matrix, basis_t):
    high, low = halves(matrix)
    basis_high, basis_low = halves(basis_t)
    both = jnp.concatenate([basis_high, basis_low], axis=0)
    first = contract_cols(both, high)
    second = contract_cols(basis_high, low)
    return first[:RANK] + first[RANK:] + second


def expand(back_t, basis_t):
    back_high, back_low = halves(back_t)
    basis_high, basis_low = halves(basis_t)
    left = jnp.concatenate([back_high, back_low, back_high], axis=0)
    right = jnp.concatenate([basis_high, basis_high, basis_low], axis=0)
    return contract_rows(left, right)


def table_kernel(columns, first, starts_ref, left_ref, tokens_ref, rows_ref, dlogits_ref, error_ref, factor_ref, high_ref, low_ref, p_ref, sum_ref):
    tile = first + pl.program_id(0)
    place = tile * TILE + lax.broadcasted_iota(jnp.int32, (TILE, 1), 0)
    sum_ref[...] = error_ref[...] + contract_rows(dlogits_ref[...], rows_ref[...])

    def visit(chunk, carry):
        at = pl.ds(pl.multiple_of(chunk * CHUNK, CHUNK), CHUNK)
        hot = jnp.where(tokens_ref[:, at] == place, 1.0, 0.0).astype(NARROW)
        sum_ref[...] += jnp.dot(hot, left_ref[at, :], preferred_element_type=WIDE)
        return carry

    lax.fori_loop(
        starts_ref[tile] // CHUNK, (starts_ref[tile + 1] + CHUNK - 1) // CHUNK, visit, 0
    )
    total = jnp.where(place < columns, sum_ref[...], 0.0)
    high, low = halves(total)
    high_ref[...] = high
    low_ref[...] = low
    factor_high, factor_low = halves(factor_ref[...])
    both = jnp.concatenate([factor_high, factor_low], axis=0)
    found = contract_cols(high, both).T
    rest = contract_cols(low, both).T
    p_ref[...] = found[:RANK] + found[RANK:] + rest[:RANK]


def table_matrix(bounds, starts, left, tokens, rows, dlogits, error, factor_t):
    columns, width = error.shape
    slots = left.shape[0]
    picks = rows.shape[0]
    first, tiles = bounds[0], bounds[1] - bounds[0]
    still = lambda j: (0, 0)
    down = lambda j: (j, 0)
    return pl.pallas_call(
        functools.partial(table_kernel, columns, first),
        grid=(tiles,),
        in_specs=[
            pl.BlockSpec(memory_space=pltpu.SMEM),
            pl.BlockSpec((slots, width), still),
            pl.BlockSpec((1, slots), still),
            pl.BlockSpec((picks, width), still),
            pl.BlockSpec((picks, TILE), lambda j: (0, first + j)),
            pl.BlockSpec((TILE, width), lambda j: (first + j, 0)),
            pl.BlockSpec((RANK, width), still),
        ],
        out_specs=[
            pl.BlockSpec((TILE, width), down),
            pl.BlockSpec((TILE, width), down),
            pl.BlockSpec((RANK, TILE), lambda j: (0, j)),
        ],
        out_shape=[
            jax.ShapeDtypeStruct((tiles * TILE, width), NARROW),
            jax.ShapeDtypeStruct((tiles * TILE, width), NARROW),
            jax.ShapeDtypeStruct((RANK, tiles * TILE), WIDE),
        ],
        scratch_shapes=[pltpu.VMEM((TILE, width), WIDE)],
        compiler_params=params(32),
        cost_estimate=pl.CostEstimate(
            flops=2 * width * tiles * TILE * (slots // 4 + picks + 24),
            bytes_accessed=8 * width * tiles * TILE,
            transcendentals=0,
        ),
    )(starts, left, tokens, rows, dlogits, error, factor_t)


def partial_kernel(*refs):
    count = (len(refs) - 1) // 2
    for index in range(count):
        refs[-1][index] = project_down(refs[index][...], refs[count + index][...])


def partial_projections(matrices, factors_t):
    count, (width, columns) = len(matrices), matrices[0].shape
    return whole_call(
        partial_kernel,
        [((count, RANK, columns), WIDE)],
        48 * count * width * columns,
        *matrices,
        *factors_t,
    )[0]


def small_kernel(count, *refs):
    grads, errors, factor_ref = refs[:count], refs[count : 2 * count], refs[2 * count]
    m_ref, p_ref = refs[2 * count + 1 :]
    for index in range(count):
        total = grads[index][...] + errors[index][...]
        m_ref[index] = total
        p_ref[index] = project_down(total, factor_ref[index])


def small_matrices(grads, errors, factor_t):
    count, (width, columns) = len(grads), grads[0].shape
    block = columns // 3
    tall = pl.BlockSpec((width, block), lambda j: (0, j))
    return pl.pallas_call(
        functools.partial(small_kernel, count),
        grid=(3,),
        in_specs=[tall] * (2 * count)
        + [pl.BlockSpec((count, RANK, width), lambda j: (0, 0, 0))],
        out_specs=[
            pl.BlockSpec((count, width, block), lambda j: (0, 0, j)),
            pl.BlockSpec((count, RANK, block), lambda j: (0, 0, j)),
        ],
        out_shape=[
            jax.ShapeDtypeStruct((count, width, columns), WIDE),
            jax.ShapeDtypeStruct((count, RANK, columns), WIDE),
        ],
        compiler_params=params(56),
        cost_estimate=pl.CostEstimate(
            flops=48 * count * width * columns,
            bytes_accessed=12 * count * width * columns,
            transcendentals=0,
        ),
    )(*grads, *errors, factor_t)


def basis_kernel(spans, p_ref, out_ref):
    index = lax.broadcasted_iota(jnp.int32, (RANK, 1), 0)
    for start, size in spans:
        rows = p_ref[:, pl.ds(start, size)]
        for place in range(RANK):
            row = rows[place : place + 1, :]
            row = row * lax.rsqrt(jnp.sum(row * row, axis=1, keepdims=True))
            inner = jnp.sum(rows * row, axis=1, keepdims=True)
            rows = jnp.where(index == place, row, rows - jnp.where(index > place, inner, 0.0) * row)
        out_ref[:, pl.ds(start, size)] = rows


def bases_of(sums, spans):
    return pl.pallas_call(
        functools.partial(basis_kernel, spans),
        out_shape=jax.ShapeDtypeStruct(sums.shape, WIDE),
        compiler_params=params(8),
        cost_estimate=pl.CostEstimate(
            flops=64 * sums.size, bytes_accessed=8 * sums.size, transcendentals=40
        ),
    )(sums)


def small_back_kernel(m_ref, basis_ref, back_ref):
    for index in range(m_ref.shape[0]):
        back_ref[index] = project_back(m_ref[index], basis_ref[index])


def small_backs(matrices, basis):
    count, width, columns = matrices.shape
    return pl.pallas_call(
        small_back_kernel,
        out_shape=jax.ShapeDtypeStruct((count, RANK, width), WIDE),
        compiler_params=params(24),
        cost_estimate=pl.CostEstimate(
            flops=48 * count * width * columns,
            bytes_accessed=4 * count * width * columns,
            transcendentals=0,
        ),
    )(matrices, basis)


def table_specs(parts, width):
    bounds, first = [], 0
    for part in parts:
        bounds.append((first, first + part.shape[0] // TILE))
        first = bounds[-1][1]
    specs = [
        pl.BlockSpec(
            (TILE, width), lambda j, low=low, high=high: (jnp.clip(j, low, high - 1) - low, 0)
        )
        for low, high in bounds
    ]
    return bounds, specs


def table_back_kernel(bounds, *refs):
    highs, lows = refs[: len(bounds)], refs[len(bounds) : 2 * len(bounds)]
    basis_ref, back_ref = refs[2 * len(bounds) :]
    step = pl.program_id(0)
    basis_high, basis_low = halves(basis_ref[...])
    both = jnp.concatenate([basis_high, basis_low], axis=0)

    @pl.when(step == 0)
    def _():
        back_ref[...] = jnp.zeros(back_ref.shape, WIDE)

    for (low, high), high_ref, low_ref in zip(bounds, highs, lows):

        @pl.when((step >= low) & (step < high))
        def _():
            first = jnp.dot(both, high_ref[...], preferred_element_type=WIDE)
            second = jnp.dot(basis_high, low_ref[...], preferred_element_type=WIDE)
            back_ref[...] += first[:RANK] + first[RANK:] + second


def table_back(highs, lows, basis):
    width = highs[0].shape[1]
    columns = basis.shape[1]
    bounds, specs = table_specs(highs, width)
    return pl.pallas_call(
        functools.partial(table_back_kernel, bounds),
        grid=(columns // TILE,),
        in_specs=specs + specs + [pl.BlockSpec((RANK, TILE), lambda j: (0, j))],
        out_specs=pl.BlockSpec((RANK, width), lambda j: (0, 0)),
        out_shape=jax.ShapeDtypeStruct((RANK, width), WIDE),
        compiler_params=params(18),
        cost_estimate=pl.CostEstimate(
            flops=48 * width * columns, bytes_accessed=4 * width * columns, transcendentals=0
        ),
    )(*highs, *lows, basis)


def small_error_kernel(m_ref, back_ref, basis_ref, *out_refs):
    count = m_ref.shape[0]
    for index in range(count):
        error = m_ref[index] - expand(back_ref[index], basis_ref[index])
        if count > 1 and index < 2:
            out_refs[0][:, index, :] = error
        else:
            out_refs[-1][...] = error


def small_errors(matrices, backs, basis):
    count, width, columns = matrices.shape
    return pl.pallas_call(
        small_error_kernel,
        out_shape=[jax.ShapeDtypeStruct((width, 2, columns), WIDE)] * (count - 1 > 0)
        + [jax.ShapeDtypeStruct((width, columns), WIDE)],
        compiler_params=params(32),
        cost_estimate=pl.CostEstimate(
            flops=48 * count * width * columns,
            bytes_accessed=8 * count * width * columns,
            transcendentals=0,
        ),
    )(matrices, backs, basis)


def table_error_kernel(bounds, *refs):
    highs, lows = refs[: len(bounds)], refs[len(bounds) : 2 * len(bounds)]
    back_ref, basis_ref, out_ref = refs[2 * len(bounds) :]
    step = pl.program_id(0)
    for (low, high), high_ref, low_ref in zip(bounds, highs, lows):

        @pl.when((step >= low) & (step < high))
        def _():
            whole = high_ref[...].astype(WIDE) + low_ref[...].astype(WIDE)
            out_ref[...] = whole - expand(basis_ref[...], back_ref[...])


def table_error(highs, lows, back, basis, columns):
    width = highs[0].shape[1]
    bounds, specs = table_specs(highs, width)
    return pl.pallas_call(
        functools.partial(table_error_kernel, bounds),
        grid=(basis.shape[1] // TILE,),
        in_specs=specs
        + specs
        + [
            pl.BlockSpec((RANK, width), lambda j: (0, 0)),
            pl.BlockSpec((RANK, TILE), lambda j: (0, j)),
        ],
        out_specs=pl.BlockSpec((TILE, width), lambda j: (j, 0)),
        out_shape=jax.ShapeDtypeStruct((columns, width), WIDE),
        compiler_params=params(24),
        cost_estimate=pl.CostEstimate(
            flops=48 * width * columns, bytes_accessed=8 * width * columns, transcendentals=0
        ),
    )(*highs, *lows, back, basis)


def normalize_keys(raw_keys):
    wide_keys = raw_keys.astype(WIDE)
    return (
        wide_keys * lax.rsqrt(jnp.sum(wide_keys * wide_keys, axis=-1, keepdims=True) + EPS)
    ).astype(NARROW)


def per_device(
    token_ids,
    seq_lengths,
    mask_slots,
    mask_targets,
    positive_rows,
    doc_ids,
    false_pairs,
    queue_docs,
    queue_embed,
    attend_weight,
    attend_moment,
    gate_up,
    gate_up_moment,
    down_weight,
    down_moment,
    embed_table,
    embed_moment,
    gains,
    gains_moment,
    attend_error,
    gate_up_error,
    down_error,
    embed_error,
    factors,
):
    tensor_count = lax.axis_size("tensor")
    tensor_rank = lax.axis_index("tensor")
    data_count = lax.axis_size("dp")
    data_rank = lax.axis_index("dp")
    groups, seq_len = token_ids.shape
    width = gains.shape[1]
    total_rows = groups * seq_len
    own_rows = total_rows // tensor_count
    slot_count = mask_slots.shape[2]
    seq_total = groups * data_count
    near = jnp.arange(tensor_count) ^ tensor_rank
    row_count = attend_weight.shape[0]

    tokens_all = lax.all_to_all(
        jnp.broadcast_to(token_ids, (data_count, seq_len)), "dp", 0, 0, tiled=True
    )
    vocab_own = embed_table.shape[1]
    vocab_start = tensor_rank * vocab_own
    ids = tokens_all - vocab_start
    ids = jnp.where((ids >= 0) & (ids < vocab_own), ids, vocab_own)
    table_local = embed_table.astype(NARROW)
    table_rows = turned_table(embed_table)
    ids = jnp.swapaxes(ids.reshape(data_count, tensor_count, own_rows), 0, 1).reshape(-1)
    looked, looked_sums = {}, {}
    for key in reversed(range(tensor_count)):
        start = ((tensor_rank ^ key) * (data_count * own_rows)).reshape(1)
        looked[key] = lookup(ids, table_rows, start, data_count, own_rows, row_count)
        if key == 1:
            for base in range(2, tensor_count, 2):
                looked_sums[base] = near_sum(looked[base], looked[base + 1])
            ids, looked_sums, looked[1] = lax.optimization_barrier((ids, looked_sums, looked[1]))
        elif key:
            ids, looked[key] = lax.optimization_barrier((ids, looked[key]))
    looked_sums[0] = near_sum(looked[0], looked[1])
    mine, _, got = far_sum(looked_sums)
    pieces = (mine + got).T.reshape(data_count, row_count, own_rows)
    soon = (jnp.minimum(data_rank, 0), token_ids, near)
    (none, near_ids, near_soon), pieces = lax.optimization_barrier((soon, pieces))
    near_tokens = picked_blocks(near_ids.reshape(tensor_count, own_rows), near_soon).reshape(1, -1)
    shifted = near_tokens - vocab_start
    tiles = -(-vocab_own // TILE)
    index = jnp.arange(total_rows)
    before = (shifted < shifted.T) | ((shifted == shifted.T) & (index[None, :] < index[:, None]))
    ranks = jnp.sum(before.astype(jnp.int32), axis=1)
    ordered = ranks[None, :] == index[:, None]
    sorted_ids = jnp.sum(jnp.where(ordered, shifted, 0), axis=1)[None, :]
    starts = jnp.sum(
        (shifted < jnp.minimum(jnp.arange(tiles + 1) * TILE, vocab_own)[:, None]).astype(jnp.int32),
        axis=1,
    )
    gate_error = lax.dynamic_slice_in_dim(gate_up_error[0], none, 1, 1)[:, 0]
    up_error = lax.dynamic_slice_in_dim(gate_up_error[0], none + 1, 1, 1)[:, 0]
    embedded = lax.all_to_all(pieces, "dp", 0, 0).reshape(width, own_rows).T

    attend_cols = attend_error.shape[2]
    queue_rows = queue_embed.shape[0] // tensor_count
    queue_own = lax.dynamic_slice_in_dim(queue_embed, tensor_rank * queue_rows, queue_rows, 0)
    joined = packed_weights(
        tensor_rank.astype(jnp.int32).reshape(1),
        attend_weight,
        gate_up,
        down_weight,
        queue_own.reshape(row_count, -1),
        attend_cols,
    )
    joined_b = lax.all_gather(joined, "dp", axis=0, tiled=True)
    table_local, _ = lax.optimization_barrier((table_local, looked[tensor_count - 1]))
    table_b = lax.all_gather(table_local, "dp", axis=0, tiled=True)

    x_zero, x_zero_b = norm_forward(gains[:1], embedded)
    side = (seq_lengths, mask_slots, mask_targets, positive_rows, doc_ids, false_pairs)
    side = side + (queue_docs, factors, data_rank, near)
    errors = (gate_error, up_error, ranks, sorted_ids, starts)
    x_zero_b, joined_b, side, errors = lax.optimization_barrier((x_zero_b, joined_b, side, errors))
    gate_error, up_error, ranks, sorted_ids, starts = errors
    ordered = ranks[None, :] == index[:, None]
    seq_lengths, mask_slots, mask_targets, positive_rows, doc_ids, false_pairs = side[:6]
    queue_docs, factors, data_rank, near = side[6:]
    x_blocks = spread_blocks(x_zero_b, "tensor")
    quarter_b, queue_near = joined_b[:, :attend_cols], joined_b[:, 4 * attend_cols :]
    attend_near = picked_blocks(spread_blocks(quarter_b, "tensor"), near)
    attend_b = jnp.concatenate([attend_near[k] for k in range(tensor_count)], axis=1)
    queue_near = normalize_keys(queue_near.reshape(data_count * queue_rows, width))

    every_rows = mask_slots + own_rows * jnp.arange(tensor_count)[None, :, None]
    every_len = seq_lengths[:, None, None]
    count = jnp.sum((every_rows < every_len).astype(WIDE))
    my_length = lax.dynamic_index_in_dim(seq_lengths, data_rank, 0, keepdims=False)
    group_valid = lax.dynamic_index_in_dim(every_rows < every_len, data_rank, 0, keepdims=False)
    own_slots = lax.dynamic_slice(
        mask_slots, (data_rank, tensor_rank, 0), (1, 1, slot_count)
    ).reshape(1, slot_count)
    own_length = (my_length - tensor_rank * own_rows).reshape(1)
    valid_rows = picked_blocks(group_valid, near).reshape(-1, 1).astype(WIDE)
    row_weight = valid_rows / count
    targets = picked_blocks(mask_targets[0], near).reshape(-1, 1) - vocab_start
    places = near[:, None] * own_rows + jnp.arange(own_rows)[None, :]
    keep_own = (places[0] < my_length)[:, None]
    cosine, sine = rotary_tables(places.reshape(-1))
    cosines, sines = row_blocks(cosine, tensor_count), row_blocks(sine, tensor_count)
    bias = jnp.where(places < my_length, 0.0, NEGATIVE).astype(NARROW)
    biases = [jnp.broadcast_to(bias[k][:, None], (own_rows, PAIR)) for k in range(tensor_count)]
    columns = jnp.arange(queue_docs.shape[0]).reshape(data_count, tensor_count, queue_rows)
    columns = picked_blocks(jnp.swapaxes(columns, 0, 1), near).reshape(-1)
    queue_docs = queue_docs.reshape(data_count, tensor_count, queue_rows)
    queue_docs = picked_blocks(jnp.swapaxes(queue_docs, 0, 1), near).reshape(-1)
    pick = lambda array: lax.dynamic_slice_in_dim(array, data_rank, 1, 0)
    target_c = columns[None, :] == pick(positive_rows)[:, None]
    blocked = (queue_docs[None, :] == pick(doc_ids)[:, None]) | jnp.any(
        pick(false_pairs)[:, :, None] == columns[None, None, :], axis=1
    )
    blocked = (blocked & jnp.logical_not(target_c)).astype(WIDE)
    target_c = target_c.astype(WIDE)

    factor_t = jnp.swapaxes(factors, 1, 2)
    factor_near = spread_blocks(factor_t[0], "tensor")
    error_p = partial_projections([attend_error[0]], [factor_t[0]])[0]

    queries, first_key, first_value = project(3, x_zero_b, attend_b, cosines[0], sines[0])
    keys, values = [first_key], [first_value]
    for k in range(1, tensor_count):
        key, value = project(2, x_blocks[k], attend_b, cosines[k], sines[k])
        keys.append(key)
        values.append(value)
    attended_t, log_total = attention_forward(queries, keys, values, biases)
    queue_near, _ = lax.optimization_barrier((queue_near, log_total))
    keys_hat = jnp.concatenate(spread_blocks(queue_near, "tensor"), axis=0)
    weight_out = attend_b[:, 3 * width :]
    attended_b, pre_one, hidden_in, hidden_in_b = merge_branch(
        attended_t, weight_out, x_zero, gains[1:2]
    )
    states, ffn_sums = paired(
        hidden_in_b, lambda index, first, second: ffn_forward(first, second, joined_b, attend_cols)
    )
    ffn_mine, _, ffn_got = far_sum(ffn_sums)
    final, _ = norm_forward(gains[2:], hidden_in, ffn_mine, ffn_got)

    ff_own = down_weight.shape[1]

    pool_part = jnp.sum(jnp.where(keep_own, final, 0.0), axis=0)
    picked = jnp.take(final, own_slots[0], axis=0).astype(NARROW)
    rows_all = jnp.concatenate(spread_blocks(picked, "tensor"), axis=0)
    logits, stats = vocab_logits(rows_all, table_b, targets)
    picks = rows_all.shape[0]
    pool_rows = jnp.pad(pool_part.reshape(-1, 128), ((0, 8 - width // 128), (0, 0)))
    stats = jnp.concatenate([stats, pool_rows], axis=0)
    for bit in axis_bits("tensor"):
        other = swap(stats, "tensor", bit)
        stats = whole_call(
            functools.partial(combine_kernel, tensor_count, slot_count, bit),
            [(stats.shape, WIDE)],
            20 * stats.size,
            stats,
            other,
        )[0]
    pooled_sum = stats[picks : picks + width // 128].reshape(1, width)
    own_stats = stats[:slot_count]
    cross = own_stats[:, 0] + jnp.log(own_stats[:, 1]) - own_stats[:, 2]
    masked_part = jnp.sum(valid_rows[:slot_count, 0] * cross)
    dlogits, row_part = vocab_back(logits, table_b, targets, stats[:picks], row_weight)
    row_grad = summed_block(row_blocks(row_part, tensor_count), "tensor", NARROW)

    weight_c = LAMBDA / seq_total
    first_rank = jnp.where(tensor_rank == 0, 1.0, 0.0)
    pooled_grad, contrast_row = contrast(
        weight_c, my_length.reshape(1), pooled_sum, keys_hat, blocked, target_c
    )
    contrast_part = contrast_row[0, 0] * first_rank

    pre_grad, pre_grad_b, gain_two = last_back(
        own_length, own_slots, row_grad, pooled_grad, hidden_in, ffn_mine, ffn_got, gains[2:]
    )
    backs, hidden_sums = paired(
        pre_grad_b,
        lambda index, first, second: ffn_backward(first, second, *states[index][:2], joined_b),
    )
    hidden_mine, hidden_sent, hidden_got = far_sum(hidden_sums)
    late = [(back[2], state[2], state[3], back[0], back[1]) for back, state in zip(backs, states)]
    late, _ = lax.optimization_barrier((late, hidden_sent))
    down_grad = sum(contract_rows(part[0], part[1]) for part in late)
    gate_w_grad = sum(contract_rows(part[2], part[3]) for part in late)
    up_w_grad = sum(contract_rows(part[2], part[4]) for part in late)
    ffn_grads = (down_grad, gate_w_grad, up_w_grad)
    ffn_grads, hidden_mine = lax.optimization_barrier((ffn_grads, hidden_mine))
    down_grad, gate_w_grad, up_w_grad = ffn_grads
    pre_one_grad, branch_grad, attended_grad, gain_one = branch_back(
        pre_grad, hidden_mine, hidden_got, pre_one, gains[1:2], weight_out
    )
    dq, dk, dv = attention_backward(
        queries, keys, values, biases, attended_grad, attended_t, log_total, cosines, sines
    )
    x_sums = {}
    for key in reversed(range(0, tensor_count, 2)):
        operands = (dk[key], dv[key], dk[key + 1], dv[key + 1])
        if x_sums:
            operands, _ = lax.optimization_barrier((operands, x_sums[key + 2]))
        x_sums[key] = near_sum(*input_grads(*operands, attend_b))
    x_mine, x_sent, x_got = far_sum(x_sums)
    late = (dq, dk, dv, branch_grad)
    late, _, x_mine = lax.optimization_barrier((late, x_sent, x_mine))
    dq_late, dk, dv, branch_grad = late
    attend_part = jnp.concatenate(
        [
            contract_rows(x_zero_b, dq_late),
            sum(contract_rows(x_blocks[k], dk[k]) for k in range(tensor_count)),
            sum(contract_rows(x_blocks[k], dv[k]) for k in range(tensor_count)),
            jnp.dot(attended_b, branch_grad, preferred_element_type=WIDE),
        ],
        axis=1,
    )
    attend_part, x_mine = lax.optimization_barrier((attend_part, x_mine))
    embedded_grad, gain_zero = first_back(
        pre_one_grad, dq, attend_b[:, :width], x_mine, x_got, embedded, gains[:1]
    )
    other_m, other_p = small_matrices(
        [gate_w_grad, up_w_grad, down_grad],
        [gate_error, up_error, down_error[0]],
        factor_t[1:4],
    )
    near_bit, *far_bits = axis_bits("tensor")
    held = {0: embedded_grad}
    for bit in reversed(far_bits):
        for key in sorted(held):
            held[key ^ bit] = swap(held[key], "tensor", bit)
    emb_blocks = dict(held)
    emb_blocks[1] = swap(held[0], "tensor", near_bit)
    rest = {key: held[key] for key in held if key}
    rest, other_p = lax.optimization_barrier((rest, other_p))
    for key in rest:
        emb_blocks[key] = rest[key]
        emb_blocks[key + 1] = swap(rest[key], "tensor", near_bit)
    emb_all = jnp.concatenate([emb_blocks[key] for key in range(tensor_count)], axis=0)
    emb_all = jnp.dot(ordered.astype(NARROW), emb_all)
    attend_blocks = [
        lax.dynamic_slice_in_dim(attend_part, near[k] * attend_cols, attend_cols, 1)
        for k in range(tensor_count)
    ]
    attend_p = partial_projections(
        [attend_blocks[k] for k in range(tensor_count)], factor_near
    )
    attend_p = summed_block([attend_p[k] for k in range(tensor_count)], "tensor", WIDE)
    attend_p = attend_p + error_p
    attend_held = dict(enumerate(attend_blocks[k] for k in range(tensor_count)))
    bits = axis_bits("tensor")
    for bit in bits[:-1]:
        for key in sorted((k for k in attend_held if not k & bit), reverse=True):
            attend_held[key] = attend_held[key] + swap(attend_held.pop(key ^ bit), "tensor", bit)
    emb_all, attend_held[bits[-1]] = lax.optimization_barrier((emb_all, attend_held[bits[-1]]))
    attend_got = [
        swap(piece, "tensor", bits[-1]) for piece in row_blocks(attend_held[bits[-1]], 2)
    ]

    other_sum = summed_all(jnp.concatenate([other_p[k] for k in range(3)], axis=1), "dp")
    cuts = sorted({0, tiles * 6 // 12, tiles * 10 // 12, tiles})
    table_parts, table_sums = [], []
    for bounds in zip(cuts, cuts[1:]):
        if table_parts:
            emb_all, table_parts[-1][2] = lax.optimization_barrier((emb_all, table_parts[-1][2]))
        if bounds[1] == tiles:
            emb_all, attend_got[0] = lax.optimization_barrier((emb_all, attend_got[0]))
        found = table_matrix(
            bounds, starts, emb_all, sorted_ids, rows_all, dlogits, embed_error[0].T, factor_t[4]
        )
        table_parts.append(list(found))
    for bounds, found in zip(zip(cuts, cuts[1:]), table_parts):
        piece = found[2]
        if bounds[1] == tiles:
            piece = jnp.concatenate([piece, attend_p], axis=1)
        table_sums.append(summed_all(piece, "dp"))
    highs, lows = [part[0] for part in table_parts], [part[1] for part in table_parts]
    parts = [table_sums[-1][:, -attend_cols:], other_sum] + table_sums[:-1]
    parts.append(table_sums[-1][:, :-attend_cols])
    sums = jnp.concatenate(parts, axis=1)
    attend_got[1], _ = lax.optimization_barrier((attend_got[1], sums))
    attend_got = jnp.concatenate(attend_got, axis=0)
    first_m = (attend_held[0] + attend_got + attend_error[0])[None]
    spans, start = [], 0
    for size in (attend_cols, ff_own, ff_own, ff_own, tiles * TILE):
        spans.append((start, size))
        start += size
    bases_t = bases_of(sums, spans)
    small_basis = jnp.stack([bases_t[:, at : at + size] for at, size in spans[:4]])
    table_basis = bases_t[:, spans[4][0] :]
    other_back = small_backs(other_m, small_basis[1:])
    tab_back = table_back(highs, lows, table_basis)
    gain_terms = jnp.concatenate([gain_zero, gain_one, gain_two], axis=0)
    loss_terms = jnp.stack([masked_part, contrast_part])
    loss_row = jnp.zeros((1, width), WIDE).at[0, :2].set(loss_terms)
    packed = jnp.concatenate(
        [other_back.reshape(-1, width), tab_back, gain_terms, loss_row], axis=0
    )
    packed = summed_all(packed, "dp")
    first_back_t = small_backs(first_m, small_basis[:1])
    first_sum = summed_all(first_back_t[0], "dp")
    errors = small_errors(first_m, first_back_t, small_basis[:1]) + small_errors(
        other_m, other_back, small_basis[1:]
    )
    new_table_error = table_error(highs, lows, tab_back, table_basis, vocab_own).T
    own_t = jnp.concatenate([first_sum, packed[: 4 * RANK]], axis=0).reshape(5, RANK, width)
    square = jnp.sum(own_t * own_t)
    tail = packed[4 * RANK :].at[3, 2].set(square)
    shared = jnp.concatenate(
        [own_t[0], tail, jnp.pad(small_basis[0], ((0, 0), (0, width - attend_cols)))], axis=0
    )
    shared = picked_blocks(spread_blocks(shared, "tensor"), near)
    tail_sum = jnp.sum(shared[:, RANK : RANK + 4], axis=0)
    gains_grad = tail_sum[:3]
    loss_sums = tail_sum[3, :2]
    clip_norm = jnp.sqrt(tail_sum[3, 2] + jnp.sum(gains_grad * gains_grad))
    shrink = CLIP / jnp.maximum(clip_norm, CLIP)
    row_start = data_rank * row_count

    def rows_of(factor):
        return lax.dynamic_slice_in_dim(factor, row_start, row_count, factor.ndim - 1)

    reduced_attend = jnp.einsum(
        "tkd,tkn->dtn",
        rows_of(shared[:, :RANK]),
        shared[:, RANK + 4 :, :attend_cols],
        precision=HIGH,
    ).reshape(row_count, -1)
    own_rows_t = rows_of(own_t)

    def reduced(index, basis):
        return dot_in(own_rows_t[index], basis, ((0,), (0,)), precision=HIGH)

    reduced_gate_up = jnp.stack(
        [reduced(1, small_basis[1]), reduced(2, small_basis[2])], axis=1
    )
    reduced_down = reduced(3, small_basis[3])
    reduced_table = reduced(4, table_basis[:, :vocab_own])

    def advance(weight, moment, grad):
        fresh = MOMENTUM * moment + shrink * grad
        return (weight - LRATE * fresh, fresh)

    new_attend, new_attend_moment = advance(attend_weight, attend_moment, reduced_attend)
    new_gate_up, new_gate_up_moment = advance(gate_up, gate_up_moment, reduced_gate_up)
    new_down, new_down_moment = advance(down_weight, down_moment, reduced_down)
    new_table, new_table_moment = advance(embed_table, embed_moment, reduced_table)
    new_gains, new_gains_moment = advance(gains, gains_moment, gains_grad)
    return (
        new_attend,
        new_attend_moment,
        new_gate_up,
        new_gate_up_moment,
        new_down,
        new_down_moment,
        new_table,
        new_table_moment,
        new_gains,
        new_gains_moment,
        errors[0][None],
        errors[1][None],
        errors[2][None],
        new_table_error[None],
        jnp.swapaxes(own_t, 1, 2),
        clip_norm,
        loss_sums[0],
        count,
        loss_sums[1],
    )


def solution(mesh):
    in_specs = (
        P("dp", None),
        P(),
        P(),
        P("dp", None, None),
        P(),
        P(),
        P(),
        P(),
        P("dp", None),
        P("dp", None),
        P("dp", None),
        P("dp", None, "tensor"),
        P("dp", None, "tensor"),
        P("dp", "tensor"),
        P("dp", "tensor"),
        P("dp", "tensor"),
        P("dp", "tensor"),
        P(),
        P(),
        P("dp", None, "tensor"),
        P("dp", None, None, "tensor"),
        P("dp", None, "tensor"),
        P("dp", None, "tensor"),
        P(None, None, "tensor"),
    )
    out_specs = (
        P("dp", None),
        P("dp", None),
        P("dp", None, "tensor"),
        P("dp", None, "tensor"),
        P("dp", "tensor"),
        P("dp", "tensor"),
        P("dp", "tensor"),
        P("dp", "tensor"),
        P(),
        P(),
        P("dp", None, "tensor"),
        P("dp", None, None, "tensor"),
        P("dp", None, "tensor"),
        P("dp", None, "tensor"),
        P(None, None, "tensor"),
        P(),
        P(),
        P(),
        P(),
    )
    return jax.shard_map(
        per_device, mesh=mesh, in_specs=in_specs, out_specs=out_specs, check_vma=False
    )
```
